32 devices in a mesh: dp: 8 (over z, y), tensor: 4 (over x, core).
Axes of the slice: x: 2, y: 2, z: 4, core: 2. Of those that a mesh axis runs over, the one named last changes fastest.
Arguments:
- block_input: bfloat16 [8192, 1792], P(('dp', 'tensor')), may hold values from -6 to 6
- cotangent: float32 [8192, 1792], P(('dp', 'tensor')), may hold values from -6 to 6
- teacher: bfloat16 [8192, 1792], P(('dp', 'tensor')), may hold values from -6 to 6
- segments: int32 [8192], P('dp'), may hold values from 0 to 8191, as said below
- valid_mask: int32 [8192], P(('dp', 'tensor')), may hold values from 0 to 1
- query_weight: bfloat16 [1792, 1792], P('dp', 'tensor'), may hold values from -0.125 to 0.125
- key_weight: bfloat16 [1792, 1792], P('dp', 'tensor'), may hold values from -0.125 to 0.125
- value_weight: bfloat16 [1792, 1792], P('dp', 'tensor'), may hold values from -0.125 to 0.125
- mixgate_weight: bfloat16 [1792, 1792], P('dp', 'tensor'), may hold values from -0.125 to 0.125
- output_weight: bfloat16 [1792, 1792], P('tensor', 'dp'), may hold values from -0.125 to 0.125
- conv_weight: float32 [3, 1792], replicated, may hold values from -3 to 3
- gain_mixer: float32 [1792], replicated, may hold values from 0.5 to 1.5
- gain_feed: float32 [1792], replicated, may hold values from 0.5 to 1.5
- gate_weight: bfloat16 [1792, 4864], P('dp', 'tensor'), may hold values from -0.125 to 0.125
- up_weight: bfloat16 [1792, 4864], P('dp', 'tensor'), may hold values from -0.125 to 0.125
- down_weight: bfloat16 [4864, 1792], P('tensor', 'dp'), may hold values from -0.078125 to 0.078125
Outputs:
- mean_loss: float32 [], replicated
- activations: float32 [8192, 1792], P(('dp', 'tensor'))
- input_grad: float32 [8192, 1792], P(('dp', 'tensor'))
- query_grad: float32 [1792, 1792], P('dp', 'tensor')
- key_grad: float32 [1792, 1792], P('dp', 'tensor')
- value_grad: float32 [1792, 1792], P('dp', 'tensor')
- mixgate_grad: float32 [1792, 1792], P('dp', 'tensor')
- output_grad: float32 [1792, 1792], P('tensor', 'dp')
- conv_grad: float32 [3, 1792], replicated
- gainmix_grad: float32 [1792], replicated
- gainfeed_grad: float32 [1792], replicated
- gate_grad: float32 [1792, 4864], P('dp', 'tensor')
- up_grad: float32 [1792, 4864], P('dp', 'tensor')
- down_grad: float32 [4864, 1792], P('tensor', 'dp')
The draws below stay inside these ranges and needn't reach their ends.
Inputs may be any that keep to these rules, and one draw needn't show every extreme that they name: `segments`: segment ids never fall; each sequence of 1024 tokens begins a new document, and one document of each sequence covers all its tokens but fewer than 128 at each end.
All inputs are finite; a program needn't handle non-finite values.
Results may differ from the reference program's by a relative error of at most 0.02.
Values may be sent and summed in bfloat16 or wider, within the bound.
A program may use at most 192 MiB of HBM per device.

```python
import jax
import jax.numpy as jnp
from jax import lax

D = 1792
HEAD_DIM = 64
FF = 4864
WINDOW = 64
CONV = 3
BLOCK = 512
LENGTH = 1024
TOKENS = 8192


def draw_segments(key, part):
    key = jax.random.fold_in(key, 7)
    first_key, second_key, third_key = jax.random.split(key, 3)
    seq_count = TOKENS // LENGTH
    reach = max(2, LENGTH // 8)
    head_len = jax.random.randint(first_key, (seq_count, 1), 1, reach)
    tail_len = jax.random.randint(second_key, (seq_count, 1), 1, reach)
    positions = jnp.arange(LENGTH, dtype=jnp.int32)[None, :]
    breaks = jax.random.randint(third_key, (seq_count, LENGTH), 0, 5) == 0
    outside = (positions < head_len) | (positions >= LENGTH - tail_len)
    break_marks = outside & breaks | (positions == head_len) | (positions == LENGTH - tail_len)
    break_marks = break_marks & (positions > 0)
    local_ids = jnp.cumsum(break_marks.astype(jnp.int32), axis=1)
    offsets = jnp.arange(seq_count, dtype=jnp.int32)[:, None] * LENGTH
    return (local_ids + offsets).reshape(TOKENS).astype(jnp.int32)


def draw_valid_mask(key, part):
    key = jax.random.fold_in(key, 8)
    random_levels = jax.random.randint(key, (TOKENS,), 0, 4 * TOKENS)
    return (random_levels < TOKENS + 2 * jnp.arange(TOKENS, dtype=jnp.int32)).astype(jnp.int32)


def strengthened(entries, rng, source, target, parts, factor):
    def block_of(axis_at):
        return (jnp.arange(entries.shape[axis_at]) // (entries.shape[axis_at] // parts)).reshape((-1,) + (1,) * (entries.ndim - 1 - axis_at))

    one_side = jax.random.permutation(rng, parts)[block_of(target)]
    far = (block_of(target) + parts // 2) % parts
    return jnp.where((block_of(source) == one_side) | (block_of(source) == far), factor * entries, entries)


def shard_levels(own_key, shape, shards, low, top_value):
    factor_of, own = 1.0, jax.random.fold_in(own_key, 6)
    for axis_at, blocks in shards:
        steps = jnp.exp(jax.random.uniform(jax.random.fold_in(own, axis_at), (blocks,), jnp.float32, low / len(shards), top_value / len(shards)))
        factor_of = factor_of * jnp.repeat(steps, shape[axis_at] // blocks).reshape([-1 if axis == axis_at else 1 for axis in range(len(shape))])
    return factor_of


def centred(key, shape, width, most, cuts=(), kind=jnp.bfloat16):
    entries = jax.random.normal(key, shape, jnp.float32) * width
    if len(cuts) > 0:
        entries = shard_levels(key, shape, cuts, -0.22, 0.18) * entries
    return jnp.clip(entries, min=-most, max=most).astype(kind)


def heavy_noise(rng, extent, width, most, cuts, heavy, kind=jnp.bfloat16):
    array = width * jax.random.normal(rng, extent, jnp.float32)
    if cuts:
        array = array * shard_levels(rng, extent, cuts, -0.22, 0.18)
    return jnp.clip(strengthened(array, jax.random.fold_in(rng, 3), *heavy), -most, most).astype(kind)


def setup_inputs(seed: int = 0) -> dict:
    seeds = jax.random.split(jax.random.key(seed), 17)
    block_input = centred(seeds[0], (TOKENS, D), 1.0, 6.0, ((0, 32),))
    cotangent = heavy_noise(seeds[1], (TOKENS, D), 1.0, 6.0, ((0, 32),), (0, 1, 32, 2.75), jnp.float32)
    teacher = centred(seeds[2], (TOKENS, D), 1.0, 6.0, ((0, 32),))
    segments = draw_segments(jax.random.fold_in(seeds[16], 71), 0)
    valid_mask = draw_valid_mask(jax.random.fold_in(seeds[16], 71), 0)
    query_weight = centred(seeds[5], (D, D), D ** -0.5, 0.125, ((0, 8), (1, 4)))
    key_weight = centred(seeds[6], (D, D), D ** -0.5, 0.125, ((0, 8), (1, 4)))
    value_weight = centred(seeds[7], (D, D), D ** -0.5, 0.125, ((0, 8), (1, 4)))
    mixgate_weight = centred(seeds[8], (D, D), D ** -0.5, 0.125, ((0, 8), (1, 4)))
    output_weight = centred(seeds[9], (D, D), D ** -0.5, 0.125, ((0, 4), (1, 8)))
    conv_weight = centred(seeds[10], (CONV, D), 0.5, 3.0, (), jnp.float32)
    gain_mixer = jnp.clip(1.0 + 0.1 * jax.random.normal(seeds[11], (D,), jnp.float32), 0.5, 1.5)
    gain_feed = jnp.clip(1.0 + 0.1 * jax.random.normal(seeds[12], (D,), jnp.float32), 0.5, 1.5)
    gate_weight = centred(seeds[13], (D, FF), D ** -0.5, 0.125, ((0, 8), (1, 4)))
    up_weight = centred(seeds[14], (D, FF), D ** -0.5, 0.125, ((0, 8), (1, 4)))
    down_weight = centred(seeds[15], (FF, D), FF ** -0.5, 0.078125, ((0, 4), (1, 8)))
    return {"block_input": block_input, "cotangent": cotangent, "teacher": teacher, "segments": segments, "valid_mask": valid_mask, "query_weight": query_weight, "key_weight": key_weight, "value_weight": value_weight, "mixgate_weight": mixgate_weight, "output_weight": output_weight, "conv_weight": conv_weight, "gain_mixer": gain_mixer, "gain_feed": gain_feed, "gate_weight": gate_weight, "up_weight": up_weight, "down_weight": down_weight}


EPS = 1e-05

@jax.custom_vjp
def low(v):
    return lax.optimization_barrier(v.astype(jnp.bfloat16)).astype(jnp.float32)

@jax.custom_vjp
def low_back(v):
    return v

def low_keep(v):
    return (low(v), None)

def low_pass(kept, grad):
    return (grad,)

def back_keep(v):
    return (v, None)

def back_low(kept, grad):
    return (low(grad),)
low.defvjp(low_keep, low_pass)
low_back.defvjp(back_keep, back_low)

def matmul(matrix_left, matrix_right):
    return jnp.dot(matrix_left, matrix_right, precision=lax.Precision.HIGHEST, preferred_element_type=jnp.float32)

def rms_norm(values, gain):
    scale_rows = lax.rsqrt(lax.optimization_barrier(jnp.mean(values * values, axis=1, keepdims=True)) + EPS)
    return values * scale_rows * gain

def same_shift(values, segments, offset):
    if offset == 0:
        return values
    shifted = jnp.concatenate([jnp.zeros((offset, values.shape[1]), values.dtype), values[:values.shape[0] - offset]], axis=0)
    same_doc = jnp.concatenate([jnp.zeros((offset,), bool), segments[offset:] == segments[:-offset]])
    return jnp.where(same_doc[:, None], shifted, 0.0)

def window_attention(queries, key_rows, value_rows, segments):
    head_count = D // HEAD_DIM
    score_scale = HEAD_DIM ** (-0.5)
    key_pad = jnp.concatenate([jnp.zeros((WINDOW, D), key_rows.dtype), key_rows], axis=0)
    value_pad = jnp.concatenate([jnp.zeros((WINDOW, D), value_rows.dtype), value_rows], axis=0)
    seg_pad = jnp.concatenate([jnp.full((WINDOW,), -1, jnp.int32), segments.astype(jnp.int32)])

    def one_block(block_index):
        row_start = (block_index * BLOCK).astype(jnp.int32)
        query_rows = lax.dynamic_slice_in_dim(queries, row_start, BLOCK, 0).reshape(BLOCK, head_count, HEAD_DIM)
        key_block = lax.dynamic_slice_in_dim(key_pad, row_start, BLOCK + WINDOW, 0).reshape(BLOCK + WINDOW, head_count, HEAD_DIM)
        value_block = lax.dynamic_slice_in_dim(value_pad, row_start, BLOCK + WINDOW, 0).reshape(BLOCK + WINDOW, head_count, HEAD_DIM)
        seg_rows = lax.dynamic_slice_in_dim(segments.astype(jnp.int32), row_start, BLOCK, 0)
        seg_keys = lax.dynamic_slice_in_dim(seg_pad, row_start, BLOCK + WINDOW, 0)
        scores = low_back(jnp.einsum('qhd,khd->hqk', query_rows, key_block, precision=lax.Precision.HIGHEST) * score_scale)
        distance = jnp.arange(BLOCK, dtype=jnp.int32)[:, None] + WINDOW - jnp.arange(BLOCK + WINDOW, dtype=jnp.int32)[None, :]
        allowed = (distance >= 0) & (distance < WINDOW) & (seg_rows[:, None] == seg_keys[None, :])
        scores = jnp.where(allowed[None], scores, -1e+30)
        attention = low(jax.nn.softmax(scores, axis=-1))
        mixed_rows = jnp.einsum('hqk,khd->qhd', attention, value_block, precision=lax.Precision.HIGHEST)
        return mixed_rows.reshape(BLOCK, D)
    blocks_out = lax.map(jax.checkpoint(one_block), jnp.arange(TOKENS // BLOCK, dtype=jnp.int32))
    return blocks_out.reshape(TOKENS, D)

def reference(block_input, cotangent, teacher, segments, valid_mask, query_weight, key_weight, value_weight, mixgate_weight, output_weight, conv_weight, gain_mixer, gain_feed, gate_weight, up_weight, down_weight):
    floats = [item.astype(jnp.float32) for item in (block_input, query_weight, key_weight, value_weight, mixgate_weight, output_weight, conv_weight, gain_mixer, gain_feed, gate_weight, up_weight, down_weight)]

    def forward(inputs, query_w, key_w, value_w, mixgate_w, output_w, conv_taps, gain_one, gain_two, gate_w, up_w, down_w):
        normed_one = low(rms_norm(inputs, gain_one))
        queries = low(low_back(matmul(normed_one, query_w)))
        key_rows = low(low_back(matmul(normed_one, key_w)))
        value_rows = low(low_back(matmul(normed_one, value_w)))
        mix_gate = low(low_back(matmul(normed_one, mixgate_w)))
        attended = window_attention(queries, key_rows, value_rows, segments)
        convolved = jnp.zeros_like(value_rows)
        for offset in range(CONV):
            convolved = convolved + conv_taps[offset] * same_shift(value_rows, segments, offset)
        mixer_out = low(low_back(attended + convolved * mix_gate))
        hidden = inputs + low_back(matmul(mixer_out, output_w))
        normed_two = low(rms_norm(hidden, gain_two))
        gate_value = low_back(matmul(normed_two, gate_w))
        up_value = low_back(matmul(normed_two, up_w))
        active = low(jax.nn.silu(gate_value) * up_value)
        return hidden + low_back(matmul(active, down_w))
    outputs, pullback = jax.vjp(forward, *floats)
    valid_rows = valid_mask.astype(jnp.float32)
    valid_total = jnp.sum(valid_rows)
    target = teacher.astype(jnp.float32)

    def penalty(result):
        return 0.5 * TOKENS / valid_total * jnp.sum(valid_rows[:, None] * (result - target) ** 2)
    penalty_value, penalty_pull = jax.vjp(penalty, outputs)
    extra_grad = penalty_pull(jnp.ones((), jnp.float32))[0]
    grads = pullback(cotangent.astype(jnp.float32) + extra_grad)
    mean_loss = jnp.sum(valid_rows[:, None] * (outputs - target) ** 2) / (valid_total * D)
    return (mean_loss, outputs, grads[0], grads[1], grads[2], grads[3], grads[4], grads[5], grads[6], grads[7], grads[8], grads[9], grads[10], grads[11])
```

```python
import jax
import jax.numpy as jnp
from jax import lax
from jax.sharding import PartitionSpec as P

D = 1792
HEAD_DIM = 64
WINDOW = 64
CONV = 3
BLOCK = 512


EPS = 1e-05


def rms_scale(values):
    return lax.rsqrt(jnp.mean(values * values, axis=1, keepdims=True) + EPS)


def rows_inner(matrix_left, matrix_right):
    return lax.dot_general(
        matrix_left, matrix_right, (((0,), (0,)), ((), ())), preferred_element_type=jnp.float32
    )


def cols_inner(matrix_left, matrix_right):
    return lax.dot_general(
        matrix_left, matrix_right, (((1,), (1,)), ((), ())), preferred_element_type=jnp.float32
    )


def shift_down(values, segments, offset):
    if offset == 0:
        return values
    shifted = jnp.concatenate(
        [jnp.zeros((offset, values.shape[1]), values.dtype), values[: values.shape[0] - offset]],
        axis=0,
    )
    same_doc = jnp.concatenate(
        [jnp.zeros((offset,), bool), segments[offset:] == segments[:-offset]]
    )
    return jnp.where(same_doc[:, None], shifted, 0.0)


def shift_up(values, segments, offset):
    if offset == 0:
        return values
    shifted = jnp.concatenate(
        [values[offset:], jnp.zeros((offset, values.shape[1]), values.dtype)], axis=0
    )
    same_doc = jnp.concatenate(
        [segments[:-offset] == segments[offset:], jnp.zeros((offset,), bool)]
    )
    return jnp.where(same_doc[:, None], shifted, 0.0)


def pad_front(array, fill_value):
    front = jnp.full((WINDOW,) + array.shape[1:], fill_value, array.dtype)
    return jnp.concatenate([front, array], axis=0)


def block_setup(queries, key_pad, seg_pad, segments, row_start, head_count):
    score_scale = HEAD_DIM ** (-0.5)
    query_rows = lax.dynamic_slice_in_dim(queries, row_start, BLOCK, 0).reshape(
        BLOCK, head_count, HEAD_DIM
    )
    key_block = lax.dynamic_slice_in_dim(key_pad, row_start, BLOCK + WINDOW, 0).reshape(
        BLOCK + WINDOW, head_count, HEAD_DIM
    )
    seg_rows = lax.dynamic_slice_in_dim(segments, row_start, BLOCK, 0)
    seg_keys = lax.dynamic_slice_in_dim(seg_pad, row_start, BLOCK + WINDOW, 0)
    distance = (
        jnp.arange(BLOCK, dtype=jnp.int32)[:, None]
        + WINDOW
        - jnp.arange(BLOCK + WINDOW, dtype=jnp.int32)[None, :]
    )
    allowed = (distance >= 0) & (distance < WINDOW) & (seg_rows[:, None] == seg_keys[None, :])
    scores = (
        jnp.einsum("qhd,khd->hqk", query_rows, key_block, preferred_element_type=jnp.float32)
        * score_scale
    )
    return (query_rows, key_block, jnp.where(allowed[None], scores, -1e30))


def attend_forward(queries, key_rows, value_rows, segments):
    group_rows, local_width = queries.shape
    head_count = local_width // HEAD_DIM
    key_pad = pad_front(key_rows, 0)
    value_pad = pad_front(value_rows, 0)
    seg_pad = pad_front(segments, -1)

    def one_block(block_index):
        row_start = block_index * BLOCK
        query_rows, key_block, scores = block_setup(
            queries, key_pad, seg_pad, segments, row_start, head_count
        )
        row_max = jnp.max(scores, axis=-1, keepdims=True)
        exponent = jnp.exp(scores - row_max)
        row_total = jnp.sum(exponent, axis=-1, keepdims=True)
        attention = (exponent / row_total).astype(jnp.bfloat16)
        value_block = lax.dynamic_slice_in_dim(value_pad, row_start, BLOCK + WINDOW, 0).reshape(
            BLOCK + WINDOW, head_count, HEAD_DIM
        )
        mixed_rows = jnp.einsum(
            "hqk,khd->qhd", attention, value_block, preferred_element_type=jnp.float32
        )
        return (
            mixed_rows.reshape(BLOCK, local_width),
            row_max[..., 0] + jnp.log(row_total[..., 0]),
        )

    blocks_out, log_totals = lax.map(one_block, jnp.arange(group_rows // BLOCK, dtype=jnp.int32))
    return (blocks_out.reshape(group_rows, local_width), log_totals)


def attend_backward(queries, key_rows, value_rows, segments, log_totals, grad_mixed):
    group_rows, local_width = queries.shape
    head_count = local_width // HEAD_DIM
    score_scale = HEAD_DIM ** (-0.5)
    key_pad = pad_front(key_rows, 0)
    value_pad = pad_front(value_rows, 0)
    seg_pad = pad_front(segments, -1)

    def one_block(accumulated, block_pair):
        block_index, log_block = block_pair
        row_start = block_index * BLOCK
        query_rows, key_block, scores = block_setup(
            queries, key_pad, seg_pad, segments, row_start, head_count
        )
        attention = jnp.exp(scores - log_block[..., None])
        value_block = lax.dynamic_slice_in_dim(value_pad, row_start, BLOCK + WINDOW, 0).reshape(
            BLOCK + WINDOW, head_count, HEAD_DIM
        )
        grad_block = lax.dynamic_slice_in_dim(grad_mixed, row_start, BLOCK, 0).reshape(
            BLOCK, head_count, HEAD_DIM
        )
        grad_attention = jnp.einsum(
            "qhd,khd->hqk", grad_block, value_block, preferred_element_type=jnp.float32
        )
        row_inner = jnp.sum(attention * grad_attention, axis=-1, keepdims=True)
        grad_scores = (attention * (grad_attention - row_inner)).astype(jnp.bfloat16)
        grad_query = (
            jnp.einsum("hqk,khd->qhd", grad_scores, key_block, preferred_element_type=jnp.float32)
            * score_scale
        )
        grad_key = (
            jnp.einsum("hqk,qhd->khd", grad_scores, query_rows, preferred_element_type=jnp.float32)
            * score_scale
        )
        grad_value = jnp.einsum(
            "hqk,qhd->khd",
            attention.astype(jnp.bfloat16),
            grad_block,
            preferred_element_type=jnp.float32,
        )
        key_acc, value_acc = accumulated
        key_acc = lax.dynamic_update_slice_in_dim(
            key_acc,
            lax.dynamic_slice_in_dim(key_acc, row_start, BLOCK + WINDOW, 0)
            + grad_key.reshape(BLOCK + WINDOW, local_width),
            row_start,
            0,
        )
        value_acc = lax.dynamic_update_slice_in_dim(
            value_acc,
            lax.dynamic_slice_in_dim(value_acc, row_start, BLOCK + WINDOW, 0)
            + grad_value.reshape(BLOCK + WINDOW, local_width),
            row_start,
            0,
        )
        return ((key_acc, value_acc), grad_query.astype(jnp.bfloat16).reshape(BLOCK, local_width))

    zeros_pad = jnp.zeros((group_rows + WINDOW, local_width), jnp.float32)
    block_ids = jnp.arange(group_rows // BLOCK, dtype=jnp.int32)
    (key_acc, value_acc), query_blocks = lax.scan(
        one_block, (zeros_pad, zeros_pad), (block_ids, log_totals)
    )
    return (query_blocks.reshape(group_rows, local_width), key_acc[WINDOW:], value_acc[WINDOW:])


def pairs_xor(size, mask):
    return [(i, i ^ mask) for i in range(size)]


def pairs_shift(size, step):
    return [(i, (i + step) % size) for i in range(size)]


def put(buffer, block, index):
    return lax.dynamic_update_slice_in_dim(buffer, block[None], index, 0)


def pick(blocks, index):
    return lax.dynamic_index_in_dim(blocks, index, 0, keepdims=False)


def gather_dp(own):
    size = lax.axis_size("dp")
    if size != 8:
        return lax.all_gather(own, "dp", axis=0)
    me = lax.axis_index("dp")
    over_y = pairs_xor(size, 1)
    up, down = pairs_shift(size, 2), pairs_shift(size, -2)
    mate = lax.ppermute(own, "dp", over_y)
    own_below = lax.ppermute(own, "dp", up)
    own_above = lax.ppermute(own, "dp", down)
    mate_below = lax.ppermute(mate, "dp", up)
    mate_above = lax.ppermute(mate, "dp", down)
    own_far = lax.ppermute(own_below, "dp", up)
    mate_far = lax.ppermute(mate_above, "dp", down)
    below, above, far = (me + 6) % size, (me + 2) % size, (me + 4) % size
    full = jnp.zeros((size,) + own.shape, own.dtype)
    for block, index in (
        (own, me),
        (mate, me ^ 1),
        (own_below, below),
        (own_above, above),
        (mate_below, below ^ 1),
        (mate_above, above ^ 1),
        (own_far, far),
        (mate_far, far ^ 1),
    ):
        full = put(full, block, index)
    return full


def scatter_dp(parts):
    size = lax.axis_size("dp")
    if size != 8:
        return lax.psum_scatter(parts, "dp", scatter_dimension=0).astype(jnp.float32)
    me = lax.axis_index("dp")
    over_y = pairs_xor(size, 1)
    up, down = pairs_shift(size, 2), pairs_shift(size, -2)
    below, above, far = (me + 6) % size, (me + 2) % size, (me + 4) % size

    def part(index):
        return pick(parts, index).astype(jnp.float32)

    low = jnp.bfloat16
    own_first = lax.ppermute(pick(parts, far), "dp", up)
    mate_first = lax.ppermute(pick(parts, far ^ 1), "dp", down)
    mate_from_below = lax.ppermute(pick(parts, above ^ 1), "dp", up)
    own_from_above = lax.ppermute(pick(parts, below), "dp", down)
    mate_from_above = lax.ppermute(
        (part(below ^ 1) + mate_first.astype(jnp.float32)).astype(low), "dp", down
    )
    own_from_below = lax.ppermute(
        (part(above) + own_first.astype(jnp.float32)).astype(low), "dp", up
    )
    mate_sum = (
        part(me ^ 1)
        + mate_from_below.astype(jnp.float32)
        + mate_from_above.astype(jnp.float32)
    )
    from_mate = lax.ppermute(mate_sum.astype(low), "dp", over_y)
    own_sum = part(me) + own_from_below.astype(jnp.float32) + own_from_above.astype(jnp.float32)
    return own_sum + from_mate.astype(jnp.float32)


def gather_tensor(own):
    size = lax.axis_size("tensor")
    if size != 4:
        return lax.all_gather(own, "tensor", axis=0, tiled=True)
    me = lax.axis_index("tensor")
    across = lax.ppermute(own, "tensor", pairs_xor(size, 2))
    beside = lax.ppermute(own, "tensor", pairs_xor(size, 1))
    beside_across = lax.ppermute(across, "tensor", pairs_xor(size, 1))
    full = jnp.zeros((size,) + own.shape, own.dtype)
    for block, index in ((own, me), (beside, me ^ 1), (across, me ^ 2), (beside_across, me ^ 3)):
        full = put(full, block, index)
    return full.reshape(size * own.shape[0], own.shape[1])


def scatter_tensor(parts):
    size = lax.axis_size("tensor")
    if size != 4:
        return lax.psum_scatter(
            parts.astype(jnp.bfloat16), "tensor", scatter_dimension=0, tiled=True
        ).astype(jnp.float32)
    me = lax.axis_index("tensor")
    low = jnp.bfloat16
    parts = parts.reshape(size, -1, parts.shape[1])
    beside = lax.ppermute(pick(parts, me ^ 3).astype(low), "tensor", pairs_xor(size, 1))
    sent = (pick(parts, me ^ 2).astype(jnp.float32) + beside.astype(jnp.float32)).astype(low)
    across = lax.ppermute(sent, "tensor", pairs_xor(size, 2))
    beside_own = lax.ppermute(pick(parts, me ^ 1).astype(low), "tensor", pairs_xor(size, 1))
    return (
        pick(parts, me).astype(jnp.float32)
        + beside_own.astype(jnp.float32)
        + across.astype(jnp.float32)
    )


def sum_all(values):
    dp_size, tensor_size = lax.axis_size("dp"), lax.axis_size("tensor")
    if dp_size != 8 or tensor_size != 4:
        return lax.psum(values, ("dp", "tensor"))
    for axis, size, mask in (
        ("tensor", tensor_size, 1),
        ("tensor", tensor_size, 2),
        ("dp", dp_size, 1),
        ("dp", dp_size, 2),
        ("dp", dp_size, 6),
    ):
        values = values + lax.ppermute(values, axis, pairs_xor(size, mask))
    return values


def on_device(
    block_input,
    cotangent,
    teacher,
    segments,
    valid_mask,
    query_weight,
    key_weight,
    value_weight,
    mixgate_weight,
    output_weight,
    conv_weight,
    gain_mixer,
    gain_feed,
    gate_weight,
    up_weight,
    down_weight,
):
    rows = block_input.shape[0]
    valid_rows = valid_mask.astype(jnp.float32)
    valid_total = sum_all(jnp.full((8, 128), jnp.sum(valid_rows), jnp.float32))[0, 0]
    local_width = query_weight.shape[1]
    local_hidden = gate_weight.shape[1]
    mixer_own = jnp.concatenate(
        [query_weight, key_weight, value_weight, mixgate_weight, output_weight.T], axis=1
    )
    feed_own = jnp.concatenate([gate_weight, up_weight], axis=1)
    mixer_all = gather_dp(mixer_own).reshape(D, -1)
    feed_all = gather_dp(feed_own).reshape(D, -1)
    full_down = gather_dp(down_weight.T).reshape(D, -1)
    full_query, full_key, full_value, full_mixgate, full_output = jnp.split(mixer_all, 5, axis=1)
    full_gate, full_upward = jnp.split(feed_all, 2, axis=1)
    column = lax.axis_index("tensor") * local_width
    conv_local = lax.dynamic_slice_in_dim(conv_weight, column, local_width, 1)
    inputs = block_input.astype(jnp.float32)
    scale_one = rms_scale(inputs)
    normed_one = inputs * scale_one
    group_one = gather_tensor((normed_one * gain_mixer).astype(jnp.bfloat16))
    queries = jnp.dot(group_one, full_query, preferred_element_type=jnp.float32).astype(
        jnp.bfloat16
    )
    key_rows = jnp.dot(group_one, full_key, preferred_element_type=jnp.float32).astype(jnp.bfloat16)
    value_rows = jnp.dot(group_one, full_value, preferred_element_type=jnp.float32).astype(
        jnp.bfloat16
    )
    mix_gate = jnp.dot(group_one, full_mixgate, preferred_element_type=jnp.float32).astype(
        jnp.bfloat16
    )
    attended, log_totals = attend_forward(queries, key_rows, value_rows, segments)
    value_float = value_rows.astype(jnp.float32)
    convolved = jnp.zeros_like(value_float)
    for offset in range(CONV):
        convolved = convolved + conv_local[offset] * shift_down(value_float, segments, offset)
    gate_float = mix_gate.astype(jnp.float32)
    mixer_out = (attended + convolved * gate_float).astype(jnp.bfloat16)
    mixer_part = cols_inner(mixer_out, full_output)
    hidden = inputs + scatter_tensor(mixer_part)
    scale_two = rms_scale(hidden)
    normed_two = hidden * scale_two
    group_two = gather_tensor((normed_two * gain_feed).astype(jnp.bfloat16))
    gate_value = jnp.dot(group_two, full_gate, preferred_element_type=jnp.float32)
    up_value = jnp.dot(group_two, full_upward, preferred_element_type=jnp.float32)
    sigmoid_gate = jax.nn.sigmoid(gate_value)
    silu_gate = gate_value * sigmoid_gate
    active = (silu_gate * up_value).astype(jnp.bfloat16)
    feed_part = cols_inner(active, full_down)
    outputs = hidden + scatter_tensor(feed_part)
    target = teacher.astype(jnp.float32)
    deviation = outputs - target
    squares = jnp.sum(valid_rows[:, None] * deviation * deviation)
    all_tokens = rows * lax.axis_size("dp") * lax.axis_size("tensor")
    grad_out = cotangent + valid_rows[:, None] * deviation * (all_tokens / valid_total)
    grad_feed = gather_tensor(grad_out.astype(jnp.bfloat16))
    down_part = rows_inner(grad_feed, active)
    down_grad = scatter_dp(down_part.astype(jnp.bfloat16).reshape(-1, down_weight.shape[1], local_hidden)).T
    grad_active = jnp.dot(grad_feed, full_down, preferred_element_type=jnp.float32)
    silu_slope = sigmoid_gate * (1.0 + gate_value * (1.0 - sigmoid_gate))
    grad_gate = (grad_active * up_value * silu_slope).astype(jnp.bfloat16)
    grad_upward = (grad_active * silu_gate).astype(jnp.bfloat16)
    grad_normed_two = cols_inner(grad_gate, full_gate) + cols_inner(grad_upward, full_upward)
    grad_rows_two = scatter_tensor(grad_normed_two)
    gate_part = rows_inner(group_two, grad_gate)
    up_part = rows_inner(group_two, grad_upward)
    shard = gate_weight.shape[0]
    gate_grad = scatter_dp(gate_part.astype(jnp.bfloat16).reshape(-1, shard, local_hidden))
    up_grad = scatter_dp(up_part.astype(jnp.bfloat16).reshape(-1, shard, local_hidden))
    gainfeed_part = jnp.sum(grad_rows_two * normed_two, axis=0)
    scaled_two = grad_rows_two * gain_feed
    grad_hidden = grad_out + scale_two * (
        scaled_two - normed_two * jnp.mean(scaled_two * normed_two, axis=1, keepdims=True)
    )
    grad_mixer = gather_tensor(grad_hidden.astype(jnp.bfloat16))
    output_part = rows_inner(grad_mixer, mixer_out)
    output_grad = scatter_dp(output_part.astype(jnp.bfloat16).reshape(-1, shard, local_width)).T
    grad_mixed = jnp.dot(grad_mixer, full_output, preferred_element_type=jnp.float32).astype(jnp.bfloat16)
    grad_mixed_float = grad_mixed.astype(jnp.float32)
    grad_mixgate = (grad_mixed_float * convolved).astype(jnp.bfloat16)
    grad_conv_out = grad_mixed_float * gate_float
    conv_rows = []
    value_from_conv = jnp.zeros_like(value_float)
    for offset in range(CONV):
        conv_rows.append(jnp.sum(grad_conv_out * shift_down(value_float, segments, offset), axis=0))
        value_from_conv = value_from_conv + conv_local[offset] * shift_up(
            grad_conv_out, segments, offset
        )
    grad_queries, key_float, value_attn = attend_backward(
        queries, key_rows, value_rows, segments, log_totals, grad_mixed
    )
    grad_keys = key_float.astype(jnp.bfloat16)
    grad_values = (value_attn + value_from_conv).astype(jnp.bfloat16)

    def project_grad(grads):
        part = rows_inner(group_one, grads).astype(jnp.bfloat16)
        return scatter_dp(part.reshape(-1, shard, local_width))

    query_grad = project_grad(grad_queries)
    key_grad = project_grad(grad_keys)
    value_grad = project_grad(grad_values)
    mixgate_grad = project_grad(grad_mixgate)
    grad_normed_one = (
        cols_inner(grad_queries, full_query)
        + cols_inner(grad_keys, full_key)
        + cols_inner(grad_values, full_value)
        + cols_inner(grad_mixgate, full_mixgate)
    )
    grad_rows_one = scatter_tensor(grad_normed_one)
    gainmix_part = jnp.sum(grad_rows_one * normed_one, axis=0)
    scaled_one = grad_rows_one * gain_mixer
    input_grad = grad_hidden + scale_one * (
        scaled_one - normed_one * jnp.mean(scaled_one * normed_one, axis=1, keepdims=True)
    )
    conv_full = lax.dynamic_update_slice_in_dim(
        jnp.zeros((CONV, D), jnp.float32), jnp.stack(conv_rows), column, 1
    )
    small = sum_all(
        jnp.concatenate(
            [
                conv_full,
                gainmix_part[None],
                gainfeed_part[None],
                jnp.full((1, D), squares, jnp.float32),
            ]
        )
    )
    conv_grad, gainmix_grad, gainfeed_grad = small[:CONV], small[CONV], small[CONV + 1]
    mean_loss = small[CONV + 2, 0] / (valid_total * D)
    return (
        mean_loss,
        outputs,
        input_grad,
        query_grad,
        key_grad,
        value_grad,
        mixgate_grad,
        output_grad,
        conv_grad,
        gainmix_grad,
        gainfeed_grad,
        gate_grad,
        up_grad,
        down_grad,
    )


def solution(mesh):
    return jax.shard_map(
        on_device,
        mesh=mesh,
        in_specs=(
            P(("dp", "tensor"), None),
            P(("dp", "tensor"), None),
            P(("dp", "tensor"), None),
            P("dp"),
            P(("dp", "tensor")),
            P("dp", "tensor"),
            P("dp", "tensor"),
            P("dp", "tensor"),
            P("dp", "tensor"),
            P("tensor", "dp"),
            P(),
            P(),
            P(),
            P("dp", "tensor"),
            P("dp", "tensor"),
            P("tensor", "dp"),
        ),
        out_specs=(
            P(),
            P(("dp", "tensor"), None),
            P(("dp", "tensor"), None),
            P("dp", "tensor"),
            P("dp", "tensor"),
            P("dp", "tensor"),
            P("dp", "tensor"),
            P("tensor", "dp"),
            P(),
            P(),
            P(),
            P("dp", "tensor"),
            P("dp", "tensor"),
            P("tensor", "dp"),
        ),
        check_vma=False,
    )
```

```python
import jax
import jax.numpy as jnp
from jax import lax
from jax.experimental import pallas as pl
from jax.experimental.pallas import tpu as pltpu
from jax.sharding import PartitionSpec as P

D = 1792
HEAD_DIM = 64
WINDOW = 64
CONV = 3
BLOCK = 512
EPS = 1e-05
MESH = pl.DeviceIdType.MESH
VMEM_LIMIT = 62 * 2**20


def rms_scale(values):
    return lax.rsqrt(jnp.mean(values * values, axis=1, keepdims=True) + EPS)


def rows_inner(matrix_left, matrix_right):
    return lax.dot_general(
        matrix_left, matrix_right, (((0,), (0,)), ((), ())), preferred_element_type=jnp.float32
    )


def cols_inner(matrix_left, matrix_right):
    return lax.dot_general(
        matrix_left, matrix_right, (((1,), (1,)), ((), ())), preferred_element_type=jnp.float32
    )


def shift_down(values, segments, offset):
    if offset == 0:
        return values
    shifted = jnp.concatenate(
        [jnp.zeros((offset, values.shape[1]), values.dtype), values[: values.shape[0] - offset]],
        axis=0,
    )
    same_doc = jnp.concatenate(
        [jnp.zeros((offset,), bool), segments[offset:] == segments[:-offset]]
    )
    return jnp.where(same_doc[:, None], shifted, 0.0)


def shift_up(values, segments, offset):
    if offset == 0:
        return values
    shifted = jnp.concatenate(
        [values[offset:], jnp.zeros((offset, values.shape[1]), values.dtype)], axis=0
    )
    same_doc = jnp.concatenate(
        [segments[:-offset] == segments[offset:], jnp.zeros((offset,), bool)]
    )
    return jnp.where(same_doc[:, None], shifted, 0.0)


def pad_front(array, fill_value):
    front = jnp.full((WINDOW,) + array.shape[1:], fill_value, array.dtype)
    return jnp.concatenate([front, array], axis=0)


def block_setup(queries, key_pad, seg_pad, segments, row_start, head_count):
    score_scale = HEAD_DIM ** (-0.5)
    query_rows = lax.dynamic_slice_in_dim(queries, row_start, BLOCK, 0).reshape(
        BLOCK, head_count, HEAD_DIM
    )
    key_block = lax.dynamic_slice_in_dim(key_pad, row_start, BLOCK + WINDOW, 0).reshape(
        BLOCK + WINDOW, head_count, HEAD_DIM
    )
    seg_rows = lax.dynamic_slice_in_dim(segments, row_start, BLOCK, 0)
    seg_keys = lax.dynamic_slice_in_dim(seg_pad, row_start, BLOCK + WINDOW, 0)
    distance = (
        jnp.arange(BLOCK, dtype=jnp.int32)[:, None]
        + WINDOW
        - jnp.arange(BLOCK + WINDOW, dtype=jnp.int32)[None, :]
    )
    allowed = (distance >= 0) & (distance < WINDOW) & (seg_rows[:, None] == seg_keys[None, :])
    scores = (
        jnp.einsum("qhd,khd->hqk", query_rows, key_block, preferred_element_type=jnp.float32)
        * score_scale
    )
    return (query_rows, key_block, jnp.where(allowed[None], scores, -1e30))


def attend_forward(queries, key_rows, value_rows, segments):
    group_rows, local_width = queries.shape
    head_count = local_width // HEAD_DIM
    key_pad = pad_front(key_rows, 0)
    value_pad = pad_front(value_rows, 0)
    seg_pad = pad_front(segments, -1)

    def one_block(block_index):
        row_start = block_index * BLOCK
        query_rows, key_block, scores = block_setup(
            queries, key_pad, seg_pad, segments, row_start, head_count
        )
        row_max = jnp.max(scores, axis=-1, keepdims=True)
        exponent = jnp.exp(scores - row_max)
        row_total = jnp.sum(exponent, axis=-1, keepdims=True)
        attention = (exponent / row_total).astype(jnp.bfloat16)
        value_block = lax.dynamic_slice_in_dim(value_pad, row_start, BLOCK + WINDOW, 0).reshape(
            BLOCK + WINDOW, head_count, HEAD_DIM
        )
        mixed_rows = jnp.einsum(
            "hqk,khd->qhd", attention, value_block, preferred_element_type=jnp.float32
        )
        return (
            mixed_rows.reshape(BLOCK, local_width),
            row_max[..., 0] + jnp.log(row_total[..., 0]),
        )

    blocks_out, log_totals = lax.map(one_block, jnp.arange(group_rows // BLOCK, dtype=jnp.int32))
    return (blocks_out.reshape(group_rows, local_width), log_totals)


def attend_backward(queries, key_rows, value_rows, segments, log_totals, grad_mixed):
    group_rows, local_width = queries.shape
    head_count = local_width // HEAD_DIM
    score_scale = HEAD_DIM ** (-0.5)
    key_pad = pad_front(key_rows, 0)
    value_pad = pad_front(value_rows, 0)
    seg_pad = pad_front(segments, -1)

    def one_block(accumulated, block_pair):
        block_index, log_block = block_pair
        row_start = block_index * BLOCK
        query_rows, key_block, scores = block_setup(
            queries, key_pad, seg_pad, segments, row_start, head_count
        )
        attention = jnp.exp(scores - log_block[..., None])
        value_block = lax.dynamic_slice_in_dim(value_pad, row_start, BLOCK + WINDOW, 0).reshape(
            BLOCK + WINDOW, head_count, HEAD_DIM
        )
        grad_block = lax.dynamic_slice_in_dim(grad_mixed, row_start, BLOCK, 0).reshape(
            BLOCK, head_count, HEAD_DIM
        )
        grad_attention = jnp.einsum(
            "qhd,khd->hqk", grad_block, value_block, preferred_element_type=jnp.float32
        )
        row_inner = jnp.sum(attention * grad_attention, axis=-1, keepdims=True)
        grad_scores = (attention * (grad_attention - row_inner)).astype(jnp.bfloat16)
        grad_query = (
            jnp.einsum("hqk,khd->qhd", grad_scores, key_block, preferred_element_type=jnp.float32)
            * score_scale
        )
        grad_key = (
            jnp.einsum("hqk,qhd->khd", grad_scores, query_rows, preferred_element_type=jnp.float32)
            * score_scale
        )
        grad_value = jnp.einsum(
            "hqk,qhd->khd",
            attention.astype(jnp.bfloat16),
            grad_block,
            preferred_element_type=jnp.float32,
        )
        key_acc, value_acc = accumulated
        key_acc = lax.dynamic_update_slice_in_dim(
            key_acc,
            lax.dynamic_slice_in_dim(key_acc, row_start, BLOCK + WINDOW, 0)
            + grad_key.reshape(BLOCK + WINDOW, local_width),
            row_start,
            0,
        )
        value_acc = lax.dynamic_update_slice_in_dim(
            value_acc,
            lax.dynamic_slice_in_dim(value_acc, row_start, BLOCK + WINDOW, 0)
            + grad_value.reshape(BLOCK + WINDOW, local_width),
            row_start,
            0,
        )
        return ((key_acc, value_acc), grad_query.astype(jnp.bfloat16).reshape(BLOCK, local_width))

    zeros_pad = jnp.zeros((group_rows + WINDOW, local_width), jnp.float32)
    block_ids = jnp.arange(group_rows // BLOCK, dtype=jnp.int32)
    (key_acc, value_acc), query_blocks = lax.scan(
        one_block, (zeros_pad, zeros_pad), (block_ids, log_totals)
    )
    return (query_blocks.reshape(group_rows, local_width), key_acc[WINDOW:], value_acc[WINDOW:])


def pairs_xor(size, mask):
    return [(i, i ^ mask) for i in range(size)]


def pairs_shift(size, step):
    return [(i, (i + step) % size) for i in range(size)]


def put(buffer, block, index):
    return lax.dynamic_update_slice_in_dim(buffer, block[None], index, 0)


def pick(blocks, index):
    return lax.dynamic_index_in_dim(blocks, index, 0, keepdims=False)


def gather_dp(own):
    size = lax.axis_size("dp")
    if size != 8:
        return lax.all_gather(own, "dp", axis=0)
    me = lax.axis_index("dp")
    over_y = pairs_xor(size, 1)
    up, down = pairs_shift(size, 2), pairs_shift(size, -2)
    mate = lax.ppermute(own, "dp", over_y)
    own_below = lax.ppermute(own, "dp", up)
    own_above = lax.ppermute(own, "dp", down)
    mate_below = lax.ppermute(mate, "dp", up)
    mate_above = lax.ppermute(mate, "dp", down)
    own_far = lax.ppermute(own_below, "dp", up)
    mate_far = lax.ppermute(mate_above, "dp", down)
    below, above, far = (me + 6) % size, (me + 2) % size, (me + 4) % size
    full = jnp.zeros((size,) + own.shape, own.dtype)
    for block, index in (
        (own, me),
        (mate, me ^ 1),
        (own_below, below),
        (own_above, above),
        (mate_below, below ^ 1),
        (mate_above, above ^ 1),
        (own_far, far),
        (mate_far, far ^ 1),
    ):
        full = put(full, block, index)
    return full


def scatter_dp(parts):
    size = lax.axis_size("dp")
    if size != 8:
        return lax.psum_scatter(parts, "dp", scatter_dimension=0).astype(jnp.float32)
    me = lax.axis_index("dp")
    over_y = pairs_xor(size, 1)
    up, down = pairs_shift(size, 2), pairs_shift(size, -2)
    below, above, far = (me + 6) % size, (me + 2) % size, (me + 4) % size

    def part(index):
        return pick(parts, index).astype(jnp.float32)

    low = jnp.bfloat16
    own_first = lax.ppermute(pick(parts, far), "dp", up)
    mate_first = lax.ppermute(pick(parts, far ^ 1), "dp", down)
    mate_from_below = lax.ppermute(pick(parts, above ^ 1), "dp", up)
    own_from_above = lax.ppermute(pick(parts, below), "dp", down)
    mate_from_above = lax.ppermute(
        (part(below ^ 1) + mate_first.astype(jnp.float32)).astype(low), "dp", down
    )
    own_from_below = lax.ppermute(
        (part(above) + own_first.astype(jnp.float32)).astype(low), "dp", up
    )
    mate_sum = (
        part(me ^ 1)
        + mate_from_below.astype(jnp.float32)
        + mate_from_above.astype(jnp.float32)
    )
    from_mate = lax.ppermute(mate_sum.astype(low), "dp", over_y)
    own_sum = part(me) + own_from_below.astype(jnp.float32) + own_from_above.astype(jnp.float32)
    return own_sum + from_mate.astype(jnp.float32)


def gather_tensor(own):
    size = lax.axis_size("tensor")
    if size != 4:
        return lax.all_gather(own, "tensor", axis=0, tiled=True)
    me = lax.axis_index("tensor")
    across = lax.ppermute(own, "tensor", pairs_xor(size, 2))
    beside = lax.ppermute(own, "tensor", pairs_xor(size, 1))
    beside_across = lax.ppermute(across, "tensor", pairs_xor(size, 1))
    full = jnp.zeros((size,) + own.shape, own.dtype)
    for block, index in ((own, me), (beside, me ^ 1), (across, me ^ 2), (beside_across, me ^ 3)):
        full = put(full, block, index)
    return full.reshape(size * own.shape[0], own.shape[1])


def scatter_tensor(parts):
    size = lax.axis_size("tensor")
    if size != 4:
        return lax.psum_scatter(
            parts.astype(jnp.bfloat16), "tensor", scatter_dimension=0, tiled=True
        ).astype(jnp.float32)
    me = lax.axis_index("tensor")
    low = jnp.bfloat16
    parts = parts.reshape(size, -1, parts.shape[1])
    beside = lax.ppermute(pick(parts, me ^ 3).astype(low), "tensor", pairs_xor(size, 1))
    sent = (pick(parts, me ^ 2).astype(jnp.float32) + beside.astype(jnp.float32)).astype(low)
    across = lax.ppermute(sent, "tensor", pairs_xor(size, 2))
    beside_own = lax.ppermute(pick(parts, me ^ 1).astype(low), "tensor", pairs_xor(size, 1))
    return (
        pick(parts, me).astype(jnp.float32)
        + beside_own.astype(jnp.float32)
        + across.astype(jnp.float32)
    )


def sum_all(values):
    dp_size, tensor_size = lax.axis_size("dp"), lax.axis_size("tensor")
    if dp_size != 8 or tensor_size != 4:
        return lax.psum(values, ("dp", "tensor"))
    for axis, size, mask in (
        ("tensor", tensor_size, 1),
        ("tensor", tensor_size, 2),
        ("dp", dp_size, 1),
        ("dp", dp_size, 2),
        ("dp", dp_size, 6),
    ):
        values = values + lax.ppermute(values, axis, pairs_xor(size, mask))
    return values


TILE = 64
LANES = 128


def neighbours():
    d, t = lax.axis_index("dp"), lax.axis_index("tensor")
    z, y = d // 2, lax.rem(d, 2)
    core = t + 1 - 2 * lax.rem(t, 2)
    place = z + y * (7 - 2 * z)

    def ring(offset):
        position = lax.rem(place + offset + 16, 8)
        side = position // 4
        return 2 * (position + side * (7 - 2 * position)) + side

    return dict(
        d=d,
        t=t,
        ring=ring,
        core=core,
        cross=lax.rem(t + 2, 4),
        cross_core=lax.rem(core + 2, 4),
        mate=d + 1 - 2 * y,
        z_pair=2 * (z + 1 - 2 * lax.rem(z, 2)) + y,
        z_mirror=2 * (3 - z) + y,
    )


def greet(at, everyone=False):
    d, t = at["d"], at["t"]
    devices = [(at["ring"](1), t), (at["ring"](-1), t), (d, at["core"]), (d, at["cross"])]
    if everyone:
        devices += [(at["mate"], t), (at["z_pair"], t), (at["z_mirror"], t)]
    barrier = pltpu.get_barrier_semaphore()
    for device in devices:
        pl.semaphore_signal(barrier, inc=1, device_id=device, device_id_type=MESH)
    pl.semaphore_wait(barrier, len(devices))


def remote(source, target, sems, index, device):
    return pltpu.make_async_remote_copy(
        src_ref=source,
        dst_ref=target,
        send_sem=sems[0].at[index],
        recv_sem=sems[1].at[index],
        device_id=device,
        device_id_type=MESH,
    )


class RingGather:
    def __init__(self, at, owns, slots, sems, base, local_sem):
        half = owns[0].shape[0] // 2
        ring, t = at["ring"], at["t"]
        self.local = [
            pltpu.make_async_copy(own, slot(at["d"], 0, 2 * half), local_sem.at[n])
            for n, (own, slot) in enumerate(zip(owns, slots))
        ]
        self.sends, self.receives, self.s = [], [], 0
        for s in range(7):
            sends, receives = [], []
            for way, sign in ((0, 1), (1, -1)):
                to = (ring(sign), t)
                for n, (own, slot) in enumerate(zip(owns, slots)):
                    index = base + (2 * s + way) * len(owns) + n
                    here = slot(ring(-sign * s), way * half, half)
                    there = slot(ring(-sign * (s + 1)), way * half, half)
                    source = own.at[pl.ds(way * half, half)] if s == 0 else here
                    sends.append(remote(source, here, sems, index, to))
                    receives.append(remote(there, there, sems, index, to))
            self.sends.append(sends)
            self.receives.append(receives)

    def start(self):
        for copy in self.sends[0] + self.local:
            copy.start()

    def step(self):
        for k, copy in enumerate(self.receives[self.s]):
            copy.wait_recv()
            if self.s < 6:
                self.sends[self.s + 1][k].start()
        self.s += 1

    def finish(self):
        while self.s < 7:
            self.step()
        for copy in self.local:
            copy.wait()

    def drain(self):
        for sends in self.sends:
            for copy in sends:
                copy.wait_send()


class RingScatter:
    def __init__(self, at, left, right, slots, term, out, sems, base):
        self.ring, self.left, self.right = at["ring"], left, right
        self.slots, self.term, self.out = slots, term, out
        self.half, self.columns = slots.shape[2], slots.shape[3]
        self.s = 0
        self.sends = [
            [
                remote(
                    slots.at[way, s], slots.at[way, s + 1], sems, base + 2 * s + way,
                    (at["ring"](sign), at["t"]),
                )
                for way, sign in ((0, 1), (1, -1))
            ]
            for s in range(7)
        ]

    def compute(self, away):
        half = self.half
        first = pl.multiple_of(self.ring(-away) * 2 * half, half)
        second = pl.multiple_of(self.ring(away) * 2 * half + half, half)
        width = 512
        whole = self.columns // width * width

        def block(lanes):
            left = jnp.concatenate(
                [self.left[pl.ds(first, half)], self.left[pl.ds(second, half)]], axis=0
            )
            self.term[:, lanes] = nn_dot(left, self.right[:, lanes])

        @pl.loop(0, whole // width)
        def _(i):
            block(pl.ds(pl.multiple_of(i * width, width), width))

        if whole < self.columns:
            block(pl.ds(whole, self.columns - whole))

    def start(self):
        self.compute(1)
        for way in range(2):
            rows = pl.ds(way * self.half, self.half)
            self.slots[way, 0] = self.term[rows, pl.ds(0, self.columns)].astype(jnp.bfloat16)
            self.sends[0][way].start()

    def step(self):
        s, half = self.s, self.half
        self.compute(s + 2)
        for way in range(2):
            rows = pl.ds(way * half, half)
            self.sends[s][way].wait_recv()
            total = self.slots[way, s + 1].astype(jnp.float32) + self.term[rows, pl.ds(0, self.columns)]
            if s < 6:
                self.slots[way, s + 1] = total.astype(jnp.bfloat16)
                self.sends[s + 1][way].start()
            else:
                self.out[rows] = total
        self.s += 1

    def finish(self):
        while self.s < 7:
            self.step()
        for sends in self.sends:
            for copy in sends:
                copy.wait_send()


class GatherTensor:
    def __init__(self, at, full, rows, sems, base):
        def block(index):
            return full.at[pl.ds(pl.multiple_of(index * rows, rows), rows)]

        mine, across = block(at["t"]), block(at["cross"])
        self.to_core = remote(mine, mine, sems, base, (at["d"], at["core"]))
        self.to_cross = remote(mine, mine, sems, base + 1, (at["d"], at["cross"]))
        self.relay_core = remote(across, across, sems, base + 2, (at["d"], at["core"]))
        places = (block(at["core"]), across, block(at["cross_core"]))
        self.receives = [
            remote(place, place, sems, base + k, (at["d"], at["core"]))
            for k, place in enumerate(places)
        ]

    def start(self):
        self.to_cross.start()
        self.to_core.start()

    def relay(self):
        self.receives[1].wait_recv()
        self.relay_core.start()

    def drain(self):
        for send in (self.to_core, self.to_cross, self.relay_core):
            send.wait_send()

    def finish(self):
        self.receives[0].wait_recv()
        self.receives[2].wait_recv()
        self.drain()


def sum_rows(at, block_part, send, receive, total, sems, base, idle=None):
    to_core, to_cross = (at["d"], at["core"]), (at["d"], at["cross"])
    low = jnp.bfloat16
    first = remote(send.at[0], receive.at[0], sems, base, to_core)
    second = remote(send.at[1], receive.at[1], sems, base + 1, to_cross)
    third = remote(send.at[2], receive.at[2], sems, base + 2, to_core)
    send[0] = block_part(at["cross_core"]).astype(low)
    first.start()
    total[...] = block_part(at["cross"])
    first.wait_recv()
    send[1] = (total[...] + receive[0].astype(jnp.float32)).astype(low)
    second.start()
    send[2] = block_part(at["core"]).astype(low)
    third.start()
    total[...] = block_part(at["t"])
    if idle is not None:
        idle()
    third.wait_recv()
    second.wait_recv()
    total[...] += receive[2].astype(jnp.float32) + receive[1].astype(jnp.float32)
    for copy in (first, second, third):
        copy.wait_send()


class SumAll:
    def __init__(self, at, value, received, sems, base):
        d, t = at["d"], at["t"]
        partners = ((d, at["core"]), (d, at["cross"]), (at["mate"], t), (at["z_pair"], t), (at["z_mirror"], t))
        self.value, self.received, self.s = value, received, 0
        self.copies = [
            remote(value.at[k], received.at[k], sems, base + k, partner)
            for k, partner in enumerate(partners)
        ]

    def start(self):
        self.copies[0].start()

    def step(self):
        s = self.s
        self.copies[s].wait_recv()
        self.value[s + 1] = self.value[s] + self.received[s]
        if s < 4:
            self.copies[s + 1].start()
        self.s += 1

    def finish(self):
        while self.s < 5:
            self.step()
        for copy in self.copies:
            copy.wait_send()


def nt_dot(left, right):
    return lax.dot_general(
        left, right, (((1,), (1,)), ((), ())), preferred_element_type=jnp.float32
    )


def nn_dot(left, right):
    return lax.dot_general(
        left, right, (((1,), (0,)), ((), ())), preferred_element_type=jnp.float32
    )


def tn_dot(left, right):
    return lax.dot_general(
        left, right, (((0,), (0,)), ((), ())), preferred_element_type=jnp.float32
    )


def head_groups(width):
    heads = width // HEAD_DIM
    return [(2 * HEAD_DIM * j, min(2, heads - 2 * j)) for j in range((heads + 1) // 2)]


def split_heads(tile, heads):
    if heads == 1:
        return tile
    lane = lax.broadcasted_iota(jnp.int32, tile.shape, 1)
    zero = jnp.zeros_like(tile)
    return jnp.concatenate(
        [jnp.where(lane < HEAD_DIM, tile, zero), jnp.where(lane < HEAD_DIM, zero, tile)], axis=0
    )


def join_heads(stacked, heads):
    if heads == 1:
        return stacked
    half = stacked.shape[0] // 2
    lane = lax.broadcasted_iota(jnp.int32, (half, stacked.shape[1]), 1)
    return jnp.where(lane < HEAD_DIM, stacked[:half], stacked[half:])


def convolve(window, taps, lanes, same_one, same_two):
    one = pltpu.roll(window, 1, axis=0)[TILE:] * same_one
    two = pltpu.roll(window, 2, axis=0)[TILE:] * same_two
    rows = (window[TILE:], one, two)
    return sum(taps[m : m + 1, lanes] * rows[m] for m in range(CONV)), rows


def attend_tile(i, q, k_pad, v_pad, u, seg_q, seg_k, same, taps, p_out, o):
    row = pl.multiple_of(i * TILE, TILE)
    at_row, at_window = pl.ds(row, TILE), pl.ds(row, 2 * TILE)
    distance = (
        lax.broadcasted_iota(jnp.int32, (TILE, 2 * TILE), 0)
        + TILE
        - lax.broadcasted_iota(jnp.int32, (TILE, 2 * TILE), 1)
    )
    allowed = (seg_q[at_row] == seg_k[i]) & (distance >= 0) & (distance < WINDOW)
    same_one, same_two = same[at_row, 0:1], same[at_row, 1:2]
    for lane, heads in head_groups(q.shape[1]):
        lanes = pl.ds(lane, heads * HEAD_DIM)
        values = v_pad[at_window, lanes]
        allow = jnp.concatenate([allowed] * heads, axis=0) if heads > 1 else allowed
        scores = nt_dot(split_heads(q[at_row, lanes], heads), k_pad[at_window, lanes])
        scores = jnp.where(allow, scores * (HEAD_DIM**-0.5), -1e30)
        exponent = jnp.exp(scores - jnp.max(scores, axis=1, keepdims=True))
        chance = exponent * (1.0 / jnp.sum(exponent, axis=1, keepdims=True))
        chance = chance.astype(jnp.bfloat16)
        p_out[i, pl.ds((lane // HEAD_DIM) * TILE, heads * TILE), :] = chance
        mixed = join_heads(nn_dot(chance, values), heads)
        convolved, _ = convolve(values.astype(jnp.float32), taps, lanes, same_one, same_two)
        o[at_row, lanes] = (mixed + convolved * u[at_row, lanes].astype(jnp.float32)).astype(
            jnp.bfloat16
        )


def attend_back_tile(
    i, q, k_pad, v_pad, u, p, same, taps, do, dq, du, dk, dv, conv_sum
):
    row = pl.multiple_of(i * TILE, TILE)
    at_row, at_window = pl.ds(row, TILE), pl.ds(row, 2 * TILE)
    same_one, same_two = same[at_row, 0:1], same[at_row, 1:2]
    for lane, heads in head_groups(q.shape[1]):
        lanes = pl.ds(lane, heads * HEAD_DIM)
        keys, values = k_pad[at_window, lanes], v_pad[at_window, lanes]
        grad = do[at_row, lanes]
        grad_heads = split_heads(grad, heads)
        chance_low = p[i, pl.ds((lane // HEAD_DIM) * TILE, heads * TILE), :]
        chance = chance_low.astype(jnp.float32)
        weighted = chance * nt_dot(grad_heads, values)
        slope = weighted - chance * jnp.sum(weighted, axis=1, keepdims=True)
        slope = (slope * (HEAD_DIM**-0.5)).astype(jnp.bfloat16)
        dq[at_row, lanes] = join_heads(nn_dot(slope, keys), heads).astype(jnp.bfloat16)
        dk[at_window, lanes] += tn_dot(slope, split_heads(q[at_row, lanes], heads))
        convolved, rows = convolve(values.astype(jnp.float32), taps, lanes, same_one, same_two)
        grad = grad.astype(jnp.float32)
        du[at_row, lanes] = (grad * convolved).astype(jnp.bfloat16)
        grad_conv = grad * u[at_row, lanes].astype(jnp.float32)
        back = tn_dot(chance_low, grad_heads)
        zero = jnp.zeros_like(grad_conv)
        for m, same_m in enumerate((None, same_one, same_two)):
            conv_sum[m : m + 1, lanes] += jnp.sum(grad_conv * rows[m], axis=0, keepdims=True)
            term = taps[m : m + 1, lanes] * grad_conv
            term = term if m == 0 else term * same_m
            term = jnp.concatenate([zero, term], axis=0)
            back = back + (term if m == 0 else pltpu.roll(term, 2 * TILE - m, axis=0))
        dv[at_window, lanes] += back


def norm_rows(values, gain):
    scale = lax.rsqrt(jnp.mean(values * values, axis=1, keepdims=True) + EPS)
    return (values * scale * gain).astype(jnp.bfloat16)


def norm_back(values, grad, gain):
    scale = lax.rsqrt(jnp.mean(values * values, axis=1, keepdims=True) + EPS)
    normed = values * scale
    scaled = grad * gain
    through = scale * (scaled - normed * jnp.mean(scaled * normed, axis=1, keepdims=True))
    return through, jnp.sum(grad * normed, axis=0, keepdims=True)


def chunks_of(rows, size=64):
    def run(body):
        @pl.loop(0, rows // size)
        def _(i):
            body(pl.multiple_of(i * size, size), size)

    return run


def mixer_forward_kernel(
    x, valid, gain_one, gain_two, seg_q, seg_k, same, taps, mix_own, out_own, feed_own,
    mix_out, last_out, feed, h1t_out, q_out, k_out, v_out, u_out, p_out, o_out, x1_out, h2_out, count_out,
    mix, last, h1, h1t, h2, q, k_pad, v_pad, u, p, o, send, receive, total, count, count_in,
    send_sems, recv_sems, local_sems, out_sems,
):
    at = neighbours()
    sems = (send_sems, recv_sems)
    rows, shard = x.shape[0], mix_own.shape[0]
    greet(at, everyone=True)

    def slot_of(full):
        return lambda i, first, size: full.at[pl.ds(pl.multiple_of(i * shard + first, 16), size)]

    early = RingGather(
        at, [mix_own, out_own], [slot_of(mix), slot_of(last)], sems, 0, local_sems.at[pl.ds(0, 2)]
    )
    late = RingGather(at, [feed_own], [slot_of(feed)], sems, 28, local_sems.at[pl.ds(2, 1)])
    group_one = GatherTensor(at, h1, rows, sems, 42)
    group_two = GatherTensor(at, h2, rows, sems, 45)
    counting = SumAll(at, count, count_in, sems, 51)
    local = q.shape[1]
    main = local // LANES * LANES
    tail = local - main
    keeps = []

    def keep(source, target):
        copy = pltpu.make_async_copy(source, target, out_sems.at[len(keeps)])
        copy.start()
        keeps.append(copy)

    early.start()

    @chunks_of(rows)
    def _(row, size):
        h1[pl.ds(pl.multiple_of(at["t"] * rows + row, size), size)] = norm_rows(
            x[pl.ds(row, size)].astype(jnp.float32), gain_one[...]
        )

    group_one.start()
    count[0] = jnp.full(count.shape[1:], jnp.sum(valid[...]), jnp.float32)
    counting.start()
    k_pad[pl.ds(0, TILE)] = jnp.zeros((TILE, local), k_pad.dtype)
    v_pad[pl.ds(0, TILE)] = jnp.zeros((TILE, local), v_pad.dtype)
    early.step()
    counting.step()
    early.step()
    counting.step()
    group_one.relay()
    early.step()
    counting.step()
    early.step()
    counting.step()
    group_one.finish()
    early.step()

    @pl.loop(0, 4)
    def _(j):
        here = pl.multiple_of(j * rows, rows)
        h1t[:, pl.ds(here, rows)] = h1[pl.ds(here, rows)].T

    keep(h1t, h1t_out)
    counting.finish()
    keep(count.at[5], count_out)
    early.step()
    late.start()
    early.finish()
    keep(mix, mix_out)
    keep(last, last_out)

    def project(j):
        here = pl.ds(pl.multiple_of(j * rows, rows), rows)
        there = pl.ds(pl.multiple_of(j * rows + TILE, TILE), rows)
        left = h1[here]
        low = jnp.bfloat16
        pair = nn_dot(left, mix[:, pl.ds(0, 2 * main)]).astype(low)
        q[here, pl.ds(0, main)] = pair[:, :main]
        k_pad[there, pl.ds(0, main)] = pair[:, main:]
        pair = nn_dot(left, mix[:, pl.ds(2 * main, 2 * main)]).astype(low)
        v_pad[there, pl.ds(0, main)] = pair[:, :main]
        u[here, pl.ds(0, main)] = pair[:, main:]
        ends = nn_dot(left, mix[:, pl.ds(4 * main, 4 * tail)])
        q[here, pl.ds(main, tail)] = ends[:, :tail].astype(low)
        k_pad[there, pl.ds(main, tail)] = ends[:, tail : 2 * tail].astype(low)
        v_pad[there, pl.ds(main, tail)] = ends[:, 2 * tail : 3 * tail].astype(low)
        u[here, pl.ds(main, tail)] = ends[:, 3 * tail :].astype(low)

    @pl.loop(0, h1.shape[0] // rows)
    def _(j):
        project(j)

    for source, target in ((q, q_out), (k_pad, k_out), (v_pad, v_out), (u, u_out)):
        keep(source, target)
    late.step()
    tiles = q.shape[0] // TILE

    def attend(first, last_tile):
        @pl.loop(first, last_tile)
        def _(i):
            attend_tile(i, q, k_pad, v_pad, u, seg_q, seg_k, same, taps, p, o)

    attend(0, tiles // 2)
    late.step()
    attend(tiles // 2, tiles)
    keep(p, p_out)
    keep(o, o_out)

    def part(block):
        return nt_dot(o[pl.ds(pl.multiple_of(block * rows, rows), rows)], last[...])

    def idle():
        late.step()

    sum_rows(at, part, send, receive, total, sems, 48, idle=idle)

    @chunks_of(rows)
    def _(row, size):
        here = pl.ds(row, size)
        hidden = total[here] + x[here].astype(jnp.float32)
        total[here] = hidden
        h2[pl.ds(pl.multiple_of(at["t"] * rows + row, size), size)] = norm_rows(hidden, gain_two[...])

    group_two.start()
    keep(total, x1_out)
    late.step()
    late.step()
    group_two.relay()
    group_two.finish()
    keep(h2, h2_out)
    late.finish()
    early.drain()
    late.drain()
    for copy in keeps:
        copy.wait()


def specs():
    return pl.BlockSpec(memory_space=pltpu.VMEM), pl.BlockSpec(memory_space=pl.ANY)


def shape(*dims, kind=jnp.bfloat16):
    return jax.ShapeDtypeStruct(dims, kind)


def params(identity):
    return pltpu.CompilerParams(
        collective_id=identity, has_side_effects=True, vmem_limit_bytes=VMEM_LIMIT
    )


def dma(count):
    return pltpu.SemaphoreType.DMA((count,))


def mixer_forward(x, valid, gain_one, gain_two, seg_q, seg_k, same, taps, mix_own, out_own, feed_own):
    rows, width = x.shape
    shard, local = out_own.shape
    everyone, depth = 4 * rows, 8 * shard
    low, wide = jnp.bfloat16, jnp.float32
    tiles, heads = everyone // TILE, local // HEAD_DIM
    vmem, hbm = specs()
    return pl.pallas_call(
        mixer_forward_kernel,
        out_shape=(
            shape(depth, mix_own.shape[1]),
            shape(depth, local),
            shape(depth, feed_own.shape[1]),
            shape(width, everyone),
            shape(everyone, local),
            shape(everyone + TILE, local),
            shape(everyone + TILE, local),
            shape(everyone, local),
            shape(tiles, heads * TILE, 2 * TILE),
            shape(everyone, local),
            shape(rows, width, kind=wide),
            shape(everyone, width),
            shape(8, LANES, kind=wide),
        ),
        in_specs=[vmem] * 8 + [hbm] * 3,
        out_specs=(hbm,) * 13,
        scratch_shapes=[
            pltpu.VMEM((depth, mix_own.shape[1]), low),
            pltpu.VMEM((depth, local), low),
            pltpu.VMEM((everyone, width), low),
            pltpu.VMEM((width, everyone), low),
            pltpu.VMEM((everyone, width), low),
            pltpu.VMEM((everyone, local), low),
            pltpu.VMEM((everyone + TILE, local), low),
            pltpu.VMEM((everyone + TILE, local), low),
            pltpu.VMEM((everyone, local), low),
            pltpu.VMEM((tiles, heads * TILE, 2 * TILE), low),
            pltpu.VMEM((everyone, local), low),
            pltpu.VMEM((3, rows, width), low),
            pltpu.VMEM((3, rows, width), low),
            pltpu.VMEM((rows, width), wide),
            pltpu.VMEM((6, 8, LANES), wide),
            pltpu.VMEM((5, 8, LANES), wide),
            dma(56),
            dma(56),
            dma(3),
            dma(12),
        ],
        compiler_params=params(1),
    )(x, valid, gain_one, gain_two, seg_q, seg_k, same, taps, mix_own, out_own, feed_own)


def feed_lanes(hidden):
    main = hidden // LANES * LANES
    cut = main // 2 // LANES * LANES
    parts = [(0, cut), (cut, main - cut)]
    return [(pl.ds(a, n), pl.ds(a, n), pl.ds(main + a, n)) for a, n in parts], main


def gated(gate, up):
    sigmoid = jax.nn.sigmoid(gate)
    silu = gate * sigmoid
    return silu * up, up * sigmoid * (1.0 + gate * (1.0 - sigmoid)), silu


def feed_forward_kernel(
    valid, count, h2_in, feed_in, x1_in, cotangent_in, teacher_in, down_own,
    down_out, slopes_out, active_out, act_out, dy_out, dyb_out, dybt_out, h2t_out, squares_out,
    h2, feed, down, slopes, active, x1, cotangent, teacher, dyb, turned, send, receive, total,
    send_sems, recv_sems, local_sems, load_sems, out_sems,
):
    at = neighbours()
    sems = (send_sems, recv_sems)
    rows, shard = x1.shape[0], down_own.shape[0]
    low = jnp.bfloat16
    greet(at)
    ring = RingGather(
        at, [down_own],
        [lambda i, first, size: down.at[pl.ds(pl.multiple_of(i * shard + first, 16), size)]],
        sems, 0, local_sems,
    )
    group = GatherTensor(at, dyb, rows, sems, 17)
    loads = [
        pltpu.make_async_copy(source, target, load_sems.at[n])
        for n, (source, target) in enumerate(
            ((h2_in, h2), (feed_in, feed), (x1_in, x1), (cotangent_in, cotangent), (teacher_in, teacher))
        )
    ]
    keeps = []

    def keep(source, target):
        copy = pltpu.make_async_copy(source, target, out_sems.at[len(keeps)])
        copy.start()
        keeps.append(copy)

    ring.start()
    for load in loads:
        load.start()
    hidden = active.shape[1]
    parts, main = feed_lanes(hidden)
    tail = hidden - main
    loads[0].wait()
    loads[1].wait()

    def widen(first, last):
        @pl.loop(first, last)
        def _(j):
            here = pl.ds(pl.multiple_of(j * rows, rows), rows)
            left = h2[here]
            for own, gate_lanes, up_lanes in parts:
                a, by_gate, by_up = gated(nn_dot(left, feed[:, gate_lanes]), nn_dot(left, feed[:, up_lanes]))
                active[here, own] = a.astype(low)
                slopes[here, gate_lanes] = by_gate.astype(low)
                slopes[here, up_lanes] = by_up.astype(low)
            both = nn_dot(left, feed[:, pl.ds(2 * main, 2 * tail)])
            a, by_gate, by_up = gated(both[:, :tail], both[:, tail:])
            active[here, pl.ds(main, tail)] = a.astype(low)
            slopes[here, pl.ds(2 * main, 2 * tail)] = jnp.concatenate([by_gate, by_up], axis=1).astype(low)

    ring.step()
    widen(0, 2)
    ring.step()
    widen(2, 4)
    keep(active, active_out)
    keep(slopes, slopes_out)
    ring.step()

    def turn(source, block):
        here = pl.multiple_of(block * rows, rows)
        turned[:, pl.ds(here, rows)] = source[pl.ds(here, rows)].T

    @pl.loop(0, 4)
    def _(j):
        turn(h2, j)

    keep(turned, h2t_out)
    ring.finish()
    keep(down, down_out)
    for load in loads[2:]:
        load.wait()

    def part(block):
        return nt_dot(active[pl.ds(pl.multiple_of(block * rows, rows), rows)], down[...])

    sum_rows(at, part, send, receive, total, sems, 14)
    weight = (rows * 4 * 8) / count[0:1, 0:1]
    squares_out[...] = jnp.zeros_like(squares_out)

    @chunks_of(rows, 32)
    def _(row, size):
        here = pl.ds(row, size)
        result = total[here] + x1[here]
        deviation = result - teacher[here].astype(jnp.float32)
        kept = valid[here, 0:1] * deviation
        total[here] = result
        squares_out[0:1] += jnp.sum(kept * deviation, axis=0, keepdims=True)
        grad = cotangent[here] + kept * weight
        x1[here] = grad
        dyb[pl.ds(pl.multiple_of(at["t"] * rows + row, size), size)] = grad.astype(low)

    group.start()
    keep(total, act_out)
    keep(x1, dy_out)
    keeps[2].wait()
    turn(dyb, at["t"])
    group.receives[0].wait_recv()
    turn(dyb, at["core"])
    group.relay()
    turn(dyb, at["cross"])
    group.receives[2].wait_recv()
    turn(dyb, at["cross_core"])
    group.drain()
    keep(dyb, dyb_out)
    keep(turned, dybt_out)
    ring.drain()
    for n, copy in enumerate(keeps):
        if n != 2:
            copy.wait()


def feed_forward(valid, count, h2, feed, x1, cotangent, teacher, down_own):
    rows, width = x1.shape
    shard, hidden = down_own.shape
    everyone, depth = 4 * rows, 8 * shard
    low, wide = jnp.bfloat16, jnp.float32
    vmem, hbm = specs()
    return pl.pallas_call(
        feed_forward_kernel,
        out_shape=(
            shape(depth, hidden),
            shape(everyone, 2 * hidden),
            shape(everyone, hidden),
            shape(rows, width, kind=wide),
            shape(rows, width, kind=wide),
            shape(everyone, width),
            shape(width, everyone),
            shape(width, everyone),
            shape(8, width, kind=wide),
        ),
        in_specs=[vmem] * 2 + [hbm] * 6,
        out_specs=(hbm,) * 8 + (vmem,),
        scratch_shapes=[
            pltpu.VMEM((everyone, width), low),
            pltpu.VMEM((depth, 2 * hidden), low),
            pltpu.VMEM((depth, hidden), low),
            pltpu.VMEM((everyone, 2 * hidden), low),
            pltpu.VMEM((everyone, hidden), low),
            pltpu.VMEM((rows, width), wide),
            pltpu.VMEM((rows, width), wide),
            pltpu.VMEM((rows, width), low),
            pltpu.VMEM((everyone, width), low),
            pltpu.VMEM((width, everyone), low),
            pltpu.VMEM((3, rows, width), low),
            pltpu.VMEM((3, rows, width), low),
            pltpu.VMEM((rows, width), wide),
            dma(20),
            dma(20),
            dma(1),
            dma(5),
            dma(8),
        ],
        compiler_params=params(2),
    )(valid, count, h2, feed, x1, cotangent, teacher, down_own)


def feed_backward_kernel(
    gain, dyb_in, dybt_in, h2t_in, down_in, feed_in, active_in, slopes_in, x1_in, dy_in,
    down_grad, feed_grad, gain_part, dx1_out, dx1b_out, dx1t_out,
    dyb, dybt, h2t, down, feed, active, slopes, side, total, down_slots, feed_slots, term, send, receive,
    send_sems, recv_sems, load_sems, out_sems,
):
    at = neighbours()
    sems = (send_sems, recv_sems)
    rows = total.shape[0]
    low = jnp.bfloat16
    loads = [
        pltpu.make_async_copy(source, target, load_sems.at[n])
        for n, (source, target) in enumerate(
            (
                (dybt_in, dybt), (active_in, active), (dyb_in, dyb), (down_in, down), (slopes_in, slopes),
                (feed_in, feed), (h2t_in, h2t), (x1_in, side), (dy_in, side),
            )
        )
    ]
    for load in loads[:-1]:
        load.start()
    greet(at)
    first = RingScatter(
        at, dybt, active, down_slots, term, down_grad, sems, 0
    )
    second = RingScatter(at, h2t, slopes, feed_slots, term, feed_grad, sems, 14)
    group = GatherTensor(at, dyb, rows, sems, 31)
    hidden = active.shape[1]
    parts, main = feed_lanes(hidden)
    tail = hidden - main
    loads[0].wait()
    loads[1].wait()
    first.start()
    for load in loads[2:5]:
        load.wait()

    def slope_back(first_block, last_block):
        @pl.loop(first_block, last_block)
        def _(j):
            here = pl.ds(pl.multiple_of(j * rows, rows), rows)
            left = dyb[here]
            for own, gate_lanes, up_lanes in parts:
                da = nn_dot(left, down[:, own])
                slopes[here, gate_lanes] = (da * slopes[here, gate_lanes].astype(jnp.float32)).astype(low)
                slopes[here, up_lanes] = (da * slopes[here, up_lanes].astype(jnp.float32)).astype(low)
            da = nn_dot(left, down[:, pl.ds(main, tail)])
            ends = pl.ds(2 * main, 2 * tail)
            both = jnp.concatenate([da, da], axis=1) * slopes[here, ends].astype(jnp.float32)
            slopes[here, ends] = both.astype(low)

    slope_back(0, 2)
    first.step()
    slope_back(2, 4)
    first.step()
    loads[6].wait()
    second.start()
    loads[5].wait()
    loads[7].wait()

    def part(block):
        return nt_dot(slopes[pl.ds(pl.multiple_of(block * rows, rows), rows)], feed[...])

    def idle():
        first.step()
        first.step()
        second.step()

    sum_rows(at, part, send, receive, total, sems, 28, idle=idle)
    gain_part[...] = jnp.zeros_like(gain_part)

    @chunks_of(rows, 32)
    def _(row, size):
        here = pl.ds(row, size)
        through, term_gain = norm_back(side[here], total[here], gain[...])
        gain_part[0:1] += term_gain
        total[here] = through

    loads[8].start()
    loads[8].wait()

    @chunks_of(rows, 32)
    def _(row, size):
        here = pl.ds(row, size)
        grad = total[here] + side[here]
        total[here] = grad
        dyb[pl.ds(pl.multiple_of(at["t"] * rows + row, size), size)] = grad.astype(low)

    group.start()
    keeps = [pltpu.make_async_copy(total, dx1_out, out_sems.at[0])]
    keeps[0].start()
    first.step()
    second.step()
    first.step()
    second.step()
    group.relay()
    first.finish()
    second.step()
    group.finish()

    @pl.loop(0, 4)
    def _(j):
        here = pl.multiple_of(j * rows, rows)
        dybt[:, pl.ds(here, rows)] = dyb[pl.ds(here, rows)].T

    for source, target in ((dyb, dx1b_out), (dybt, dx1t_out)):
        keeps.append(pltpu.make_async_copy(source, target, out_sems.at[len(keeps)]))
        keeps[-1].start()
    second.finish()
    for copy in keeps:
        copy.wait()


def feed_backward(gain, dyb, dybt, h2t, down, feed, active, slopes, x1, dy):
    rows, width = x1.shape
    depth, hidden = down.shape
    everyone, shard = 4 * rows, depth // 8
    low, wide = jnp.bfloat16, jnp.float32
    vmem, hbm = specs()
    return pl.pallas_call(
        feed_backward_kernel,
        out_shape=(
            shape(shard, hidden, kind=wide),
            shape(shard, 2 * hidden, kind=wide),
            shape(8, width, kind=wide),
            shape(rows, width, kind=wide),
            shape(everyone, width),
            shape(width, everyone),
        ),
        in_specs=[vmem] + [hbm] * 9,
        out_specs=(vmem,) * 3 + (hbm,) * 3,
        scratch_shapes=[
            pltpu.VMEM((everyone, width), low),
            pltpu.VMEM((width, everyone), low),
            pltpu.VMEM((width, everyone), low),
            pltpu.VMEM((depth, hidden), low),
            pltpu.VMEM((depth, 2 * hidden), low),
            pltpu.VMEM((everyone, hidden), low),
            pltpu.VMEM((everyone, 2 * hidden), low),
            pltpu.VMEM((rows, width), wide),
            pltpu.VMEM((rows, width), wide),
            pltpu.VMEM((2, 8, shard // 2, hidden), low),
            pltpu.VMEM((2, 8, shard // 2, 2 * hidden), low),
            pltpu.VMEM((shard, 2 * hidden), wide),
            pltpu.VMEM((3, rows, width), low),
            pltpu.VMEM((3, rows, width), low),
            dma(34),
            dma(34),
            dma(9),
            dma(3),
        ],
        compiler_params=params(3),
    )(gain, dyb, dybt, h2t, down, feed, active, slopes, x1, dy)


def mixer_backward_kernel(
    x, gain, same, taps, gain_part, squares,
    dx1b_in, dx1t_in, o_in, last_in, q_in, k_in, v_in, u_in, p_in, h1t_in, mix_in, dx1_in,
    out_grad, mix_grad, input_grad, small_out, conv_out,
    dx1b, dx1t, o, last, q, k_pad, v_pad, u, p, h1t, mix,
    do, dq, du, dk, dv, grads, out_slots, mix_slots, term, send, receive, total,
    small, small_in, conv, conv_in,
    send_sems, recv_sems, load_sems,
):
    at = neighbours()
    sems = (send_sems, recv_sems)
    rows = total.shape[0]
    low = jnp.bfloat16
    loads = [
        pltpu.make_async_copy(source, target, load_sems.at[n])
        for n, (source, target) in enumerate(
            (
                (dx1t_in, dx1t), (o_in, o), (dx1b_in, dx1b), (last_in, last), (q_in, q), (k_in, k_pad),
                (v_in, v_pad), (u_in, u), (p_in, p), (h1t_in, h1t), (mix_in, mix), (dx1_in, input_grad),
            )
        )
    ]
    for load in loads:
        load.start()
    greet(at, everyone=True)
    local = q.shape[1]
    main = local // LANES * LANES
    tail = local - main
    first = RingScatter(at, dx1t, o, out_slots, term, out_grad, sems, 0)
    second = RingScatter(at, h1t, grads, mix_slots, term, mix_grad, sems, 14)
    small_sum = SumAll(at, small, small_in, sems, 31)
    conv_all = SumAll(at, conv, conv_in, sems, 36)
    loads[0].wait()
    loads[1].wait()
    first.start()
    loads[2].wait()
    loads[3].wait()
    dk[...] = jnp.zeros_like(dk)
    dv[...] = jnp.zeros_like(dv)
    conv[0] = jnp.zeros(conv.shape[1:], jnp.float32)

    @pl.loop(0, 4)
    def _(j):
        here = pl.ds(pl.multiple_of(j * rows, rows), rows)
        do[here] = nn_dot(dx1b[here], last[...]).astype(low)

    first.step()
    for load in loads[4:9]:
        load.wait()
    tiles = q.shape[0] // TILE
    conv_sum = conv.at[0, at["t"]]

    def attend(a, b):
        @pl.loop(a, b)
        def _(i):
            attend_back_tile(i, q, k_pad, v_pad, u, p, same, taps, do, dq, du, dk, dv, conv_sum)

    for k in range(4):
        attend(k * tiles // 4, (k + 1) * tiles // 4)
        first.step()
    conv_all.start()

    @chunks_of(q.shape[0])
    def _(row, size):
        here, there = pl.ds(row, size), pl.ds(pl.multiple_of(row + TILE, TILE), size)
        four = [dq[here].astype(jnp.float32), dk[there], dv[there], du[here].astype(jnp.float32)]
        for n, value in enumerate(four):
            grads[here, pl.ds(n * main, main)] = value[:, :main].astype(low)
        ends = jnp.concatenate([value[:, main:] for value in four], axis=1)
        grads[here, pl.ds(4 * main, 4 * tail)] = ends.astype(low)

    loads[9].wait()
    second.start()
    first.finish()
    loads[10].wait()
    loads[11].wait()

    def part(block):
        return nt_dot(grads[pl.ds(pl.multiple_of(block * rows, rows), rows)], mix[...])

    def idle():
        second.step()
        conv_all.step()
        second.step()
        conv_all.step()

    sum_rows(at, part, send, receive, total, sems, 28, idle=idle)
    small[0, 0:1] = jnp.zeros((1, small.shape[2]), jnp.float32)
    small[0, 1:2] = gain_part[0:1]
    small[0, 2:3] = squares[0:1]
    small[0, 3:8] = jnp.zeros((5, small.shape[2]), jnp.float32)

    @chunks_of(rows, 32)
    def _(row, size):
        here = pl.ds(row, size)
        through, term_gain = norm_back(x[here].astype(jnp.float32), total[here], gain[...])
        small[0, 0:1] += term_gain
        input_grad[here] += through

    small_sum.start()
    while second.s < 6:
        second.step()
        if conv_all.s < 5:
            conv_all.step()
        small_sum.step()
    small_sum.finish()
    conv_all.finish()
    second.finish()
    small_out[...] = small[5]
    conv_out[...] = conv[5]


def mixer_backward(
    x, gain, same, taps, gain_part, squares, dx1b, dx1t, o, last, q, k_pad, v_pad, u, p, h1t, mix, dx1
):
    rows, width = x.shape
    depth, local = last.shape
    everyone, shard = 4 * rows, depth // 8
    low, wide = jnp.bfloat16, jnp.float32
    vmem, hbm = specs()
    arrays = (dx1b, dx1t, o, last, q, k_pad, v_pad, u, p, h1t, mix)
    return pl.pallas_call(
        mixer_backward_kernel,
        out_shape=(
            shape(shard, local, kind=wide),
            shape(shard, 4 * local, kind=wide),
            shape(rows, width, kind=wide),
            shape(8, width, kind=wide),
            shape(4, 8, local, kind=wide),
        ),
        in_specs=[vmem] * 6 + [hbm] * 12,
        out_specs=(vmem,) * 5,
        scratch_shapes=[pltpu.VMEM(array.shape, array.dtype) for array in arrays]
        + [
            pltpu.VMEM((everyone, local), low),
            pltpu.VMEM((everyone, local), low),
            pltpu.VMEM((everyone, local), low),
            pltpu.VMEM((everyone + TILE, local), wide),
            pltpu.VMEM((everyone + TILE, local), wide),
            pltpu.VMEM((everyone, 4 * local), low),
            pltpu.VMEM((2, 8, shard // 2, local), low),
            pltpu.VMEM((2, 8, shard // 2, 4 * local), low),
            pltpu.VMEM((shard, 4 * local), wide),
            pltpu.VMEM((3, rows, width), low),
            pltpu.VMEM((3, rows, width), low),
            pltpu.VMEM((rows, width), wide),
            pltpu.VMEM((6, 8, width), wide),
            pltpu.VMEM((5, 8, width), wide),
            pltpu.VMEM((6, 4, 8, local), wide),
            pltpu.VMEM((5, 4, 8, local), wide),
            dma(41),
            dma(41),
            dma(12),
        ],
        compiler_params=params(4),
    )(x, gain, same, taps, gain_part, squares, *arrays, dx1)


def segment_tables(segments):
    padded = jnp.concatenate([jnp.full((TILE,), -1, jnp.int32), segments])
    seg_k = jnp.concatenate(
        [padded[:-TILE].reshape(-1, 1, TILE), padded[TILE:].reshape(-1, 1, TILE)], axis=2
    )
    same = [
        jnp.concatenate(
            [jnp.zeros((m,), jnp.float32), (segments[m:] == segments[:-m]).astype(jnp.float32)]
        )
        for m in range(1, CONV)
    ]
    return segments[:, None], seg_k, jnp.stack(same, axis=1)


def pack(*weights):
    main = weights[0].shape[1] // LANES * LANES
    return jnp.concatenate([w[:, :main] for w in weights] + [w[:, main:] for w in weights], axis=1)


def unpack(packed, count):
    width = packed.shape[1] // count
    main = width // LANES * LANES
    tail = width - main
    return [
        jnp.concatenate(
            [
                packed[:, n * main : (n + 1) * main],
                packed[:, count * main + n * tail : count * main + (n + 1) * tail],
            ],
            axis=1,
        )
        for n in range(count)
    ]


def on_rings(
    block_input,
    cotangent,
    teacher,
    segments,
    valid_mask,
    query_weight,
    key_weight,
    value_weight,
    mixgate_weight,
    output_weight,
    conv_weight,
    gain_mixer,
    gain_feed,
    gate_weight,
    up_weight,
    down_weight,
):
    local = query_weight.shape[1]
    taps = lax.dynamic_slice_in_dim(conv_weight, lax.axis_index("tensor") * local, local, 1)
    seg_q, seg_k, same = segment_tables(segments)
    valid = valid_mask.astype(jnp.float32)
    mix_own = pack(query_weight, key_weight, value_weight, mixgate_weight)
    feed_own = pack(gate_weight, up_weight)
    gain_one, gain_two = gain_mixer[None], gain_feed[None]
    mix, last, feed, h1t, q, k_pad, v_pad, u, p, o, x1, h2, count = mixer_forward(
        block_input, valid.reshape(-1, LANES), gain_one, gain_two, seg_q, seg_k, same, taps,
        mix_own, output_weight.T, feed_own,
    )
    down, slopes, active, outputs, dy, dyb, dybt, h2t, squares = feed_forward(
        valid[:, None], count, h2, feed, x1, cotangent, teacher, down_weight.T
    )
    down_grad, feed_grad, gain_part, dx1, dx1b, dx1t = feed_backward(
        gain_two, dyb, dybt, h2t, down, feed, active, slopes, x1, dy
    )
    out_grad, mix_grad, input_grad, small, conv = mixer_backward(
        block_input, gain_one, same, taps, gain_part, squares, dx1b, dx1t, o, last, q, k_pad, v_pad,
        u, p, h1t, mix, dx1,
    )
    gate_grad, up_grad = unpack(feed_grad, 2)
    mean_loss = jnp.sum(small[2]) / (count[0, 0] * D)
    return (
        mean_loss,
        outputs,
        input_grad,
        *unpack(mix_grad, 4),
        out_grad.T,
        conv[:, :CONV].transpose(1, 0, 2).reshape(CONV, -1),
        small[0],
        small[1],
        gate_grad,
        up_grad,
        down_grad.T,
    )


def on_any_mesh(
    block_input,
    cotangent,
    teacher,
    segments,
    valid_mask,
    query_weight,
    key_weight,
    value_weight,
    mixgate_weight,
    output_weight,
    conv_weight,
    gain_mixer,
    gain_feed,
    gate_weight,
    up_weight,
    down_weight,
):
    rows = block_input.shape[0]
    valid_rows = valid_mask.astype(jnp.float32)
    valid_total = sum_all(jnp.full((8, 128), jnp.sum(valid_rows), jnp.float32))[0, 0]
    local_width = query_weight.shape[1]
    local_hidden = gate_weight.shape[1]
    mixer_own = jnp.concatenate(
        [query_weight, key_weight, value_weight, mixgate_weight, output_weight.T], axis=1
    )
    feed_own = jnp.concatenate([gate_weight, up_weight], axis=1)
    mixer_all = gather_dp(mixer_own).reshape(D, -1)
    feed_all = gather_dp(feed_own).reshape(D, -1)
    full_down = gather_dp(down_weight.T).reshape(D, -1)
    full_query, full_key, full_value, full_mixgate, full_output = jnp.split(mixer_all, 5, axis=1)
    full_gate, full_upward = jnp.split(feed_all, 2, axis=1)
    column = lax.axis_index("tensor") * local_width
    conv_local = lax.dynamic_slice_in_dim(conv_weight, column, local_width, 1)
    inputs = block_input.astype(jnp.float32)
    scale_one = rms_scale(inputs)
    normed_one = inputs * scale_one
    group_one = gather_tensor((normed_one * gain_mixer).astype(jnp.bfloat16))
    queries = jnp.dot(group_one, full_query, preferred_element_type=jnp.float32).astype(
        jnp.bfloat16
    )
    key_rows = jnp.dot(group_one, full_key, preferred_element_type=jnp.float32).astype(jnp.bfloat16)
    value_rows = jnp.dot(group_one, full_value, preferred_element_type=jnp.float32).astype(
        jnp.bfloat16
    )
    mix_gate = jnp.dot(group_one, full_mixgate, preferred_element_type=jnp.float32).astype(
        jnp.bfloat16
    )
    attended, log_totals = attend_forward(queries, key_rows, value_rows, segments)
    value_float = value_rows.astype(jnp.float32)
    convolved = jnp.zeros_like(value_float)
    for offset in range(CONV):
        convolved = convolved + conv_local[offset] * shift_down(value_float, segments, offset)
    gate_float = mix_gate.astype(jnp.float32)
    mixer_out = (attended + convolved * gate_float).astype(jnp.bfloat16)
    mixer_part = cols_inner(mixer_out, full_output)
    hidden = inputs + scatter_tensor(mixer_part)
    scale_two = rms_scale(hidden)
    normed_two = hidden * scale_two
    group_two = gather_tensor((normed_two * gain_feed).astype(jnp.bfloat16))
    gate_value = jnp.dot(group_two, full_gate, preferred_element_type=jnp.float32)
    up_value = jnp.dot(group_two, full_upward, preferred_element_type=jnp.float32)
    sigmoid_gate = jax.nn.sigmoid(gate_value)
    silu_gate = gate_value * sigmoid_gate
    active = (silu_gate * up_value).astype(jnp.bfloat16)
    feed_part = cols_inner(active, full_down)
    outputs = hidden + scatter_tensor(feed_part)
    target = teacher.astype(jnp.float32)
    deviation = outputs - target
    squares = jnp.sum(valid_rows[:, None] * deviation * deviation)
    all_tokens = rows * lax.axis_size("dp") * lax.axis_size("tensor")
    grad_out = cotangent + valid_rows[:, None] * deviation * (all_tokens / valid_total)
    grad_feed = gather_tensor(grad_out.astype(jnp.bfloat16))
    down_part = rows_inner(grad_feed, active)
    down_grad = scatter_dp(down_part.astype(jnp.bfloat16).reshape(-1, down_weight.shape[1], local_hidden)).T
    grad_active = jnp.dot(grad_feed, full_down, preferred_element_type=jnp.float32)
    silu_slope = sigmoid_gate * (1.0 + gate_value * (1.0 - sigmoid_gate))
    grad_gate = (grad_active * up_value * silu_slope).astype(jnp.bfloat16)
    grad_upward = (grad_active * silu_gate).astype(jnp.bfloat16)
    grad_normed_two = cols_inner(grad_gate, full_gate) + cols_inner(grad_upward, full_upward)
    grad_rows_two = scatter_tensor(grad_normed_two)
    gate_part = rows_inner(group_two, grad_gate)
    up_part = rows_inner(group_two, grad_upward)
    shard = gate_weight.shape[0]
    gate_grad = scatter_dp(gate_part.astype(jnp.bfloat16).reshape(-1, shard, local_hidden))
    up_grad = scatter_dp(up_part.astype(jnp.bfloat16).reshape(-1, shard, local_hidden))
    gainfeed_part = jnp.sum(grad_rows_two * normed_two, axis=0)
    scaled_two = grad_rows_two * gain_feed
    grad_hidden = grad_out + scale_two * (
        scaled_two - normed_two * jnp.mean(scaled_two * normed_two, axis=1, keepdims=True)
    )
    grad_mixer = gather_tensor(grad_hidden.astype(jnp.bfloat16))
    output_part = rows_inner(grad_mixer, mixer_out)
    output_grad = scatter_dp(output_part.astype(jnp.bfloat16).reshape(-1, shard, local_width)).T
    grad_mixed = jnp.dot(grad_mixer, full_output, preferred_element_type=jnp.float32).astype(jnp.bfloat16)
    grad_mixed_float = grad_mixed.astype(jnp.float32)
    grad_mixgate = (grad_mixed_float * convolved).astype(jnp.bfloat16)
    grad_conv_out = grad_mixed_float * gate_float
    conv_rows = []
    value_from_conv = jnp.zeros_like(value_float)
    for offset in range(CONV):
        conv_rows.append(jnp.sum(grad_conv_out * shift_down(value_float, segments, offset), axis=0))
        value_from_conv = value_from_conv + conv_local[offset] * shift_up(
            grad_conv_out, segments, offset
        )
    grad_queries, key_float, value_attn = attend_backward(
        queries, key_rows, value_rows, segments, log_totals, grad_mixed
    )
    grad_keys = key_float.astype(jnp.bfloat16)
    grad_values = (value_attn + value_from_conv).astype(jnp.bfloat16)

    def project_grad(grads):
        part = rows_inner(group_one, grads).astype(jnp.bfloat16)
        return scatter_dp(part.reshape(-1, shard, local_width))

    query_grad = project_grad(grad_queries)
    key_grad = project_grad(grad_keys)
    value_grad = project_grad(grad_values)
    mixgate_grad = project_grad(grad_mixgate)
    grad_normed_one = (
        cols_inner(grad_queries, full_query)
        + cols_inner(grad_keys, full_key)
        + cols_inner(grad_values, full_value)
        + cols_inner(grad_mixgate, full_mixgate)
    )
    grad_rows_one = scatter_tensor(grad_normed_one)
    gainmix_part = jnp.sum(grad_rows_one * normed_one, axis=0)
    scaled_one = grad_rows_one * gain_mixer
    input_grad = grad_hidden + scale_one * (
        scaled_one - normed_one * jnp.mean(scaled_one * normed_one, axis=1, keepdims=True)
    )
    conv_full = lax.dynamic_update_slice_in_dim(
        jnp.zeros((CONV, D), jnp.float32), jnp.stack(conv_rows), column, 1
    )
    small = sum_all(
        jnp.concatenate(
            [
                conv_full,
                gainmix_part[None],
                gainfeed_part[None],
                jnp.full((1, D), squares, jnp.float32),
            ]
        )
    )
    conv_grad, gainmix_grad, gainfeed_grad = small[:CONV], small[CONV], small[CONV + 1]
    mean_loss = small[CONV + 2, 0] / (valid_total * D)
    return (
        mean_loss,
        outputs,
        input_grad,
        query_grad,
        key_grad,
        value_grad,
        mixgate_grad,
        output_grad,
        conv_grad,
        gainmix_grad,
        gainfeed_grad,
        gate_grad,
        up_grad,
        down_grad,
    )


def solution(mesh):
    rings = mesh.shape["dp"] == 8 and mesh.shape["tensor"] == 4
    return jax.shard_map(
        on_rings if rings else on_any_mesh,
        mesh=mesh,
        in_specs=(
            P(("dp", "tensor"), None),
            P(("dp", "tensor"), None),
            P(("dp", "tensor"), None),
            P("dp"),
            P(("dp", "tensor")),
            P("dp", "tensor"),
            P("dp", "tensor"),
            P("dp", "tensor"),
            P("dp", "tensor"),
            P("tensor", "dp"),
            P(),
            P(),
            P(),
            P("dp", "tensor"),
            P("dp", "tensor"),
            P("tensor", "dp"),
        ),
        out_specs=(
            P(),
            P(("dp", "tensor"), None),
            P(("dp", "tensor"), None),
            P("dp", "tensor"),
            P("dp", "tensor"),
            P("dp", "tensor"),
            P("dp", "tensor"),
            P("tensor", "dp"),
            P(),
            P(),
            P(),
            P("dp", "tensor"),
            P("dp", "tensor"),
            P("tensor", "dp"),
        ),
        check_vma=False,
    )
```

```python
import jax
import jax.numpy as jnp
from jax import lax
from jax.experimental import pallas as pl
from jax.experimental.pallas import tpu as pltpu
from jax.sharding import PartitionSpec as P

D = 1792
HEAD_DIM = 64
WINDOW = 64
CONV = 3
BLOCK = 512
EPS = 1e-05
MESH = pl.DeviceIdType.MESH
VMEM_LIMIT = 63 * 2**20


def rms_scale(values):
    return lax.rsqrt(jnp.mean(values * values, axis=1, keepdims=True) + EPS)


def rows_inner(matrix_left, matrix_right):
    return lax.dot_general(
        matrix_left, matrix_right, (((0,), (0,)), ((), ())), preferred_element_type=jnp.float32
    )


def cols_inner(matrix_left, matrix_right):
    return lax.dot_general(
        matrix_left, matrix_right, (((1,), (1,)), ((), ())), preferred_element_type=jnp.float32
    )


def shift_down(values, segments, offset):
    if offset == 0:
        return values
    shifted = jnp.concatenate(
        [jnp.zeros((offset, values.shape[1]), values.dtype), values[: values.shape[0] - offset]],
        axis=0,
    )
    same_doc = jnp.concatenate(
        [jnp.zeros((offset,), bool), segments[offset:] == segments[:-offset]]
    )
    return jnp.where(same_doc[:, None], shifted, 0.0)


def shift_up(values, segments, offset):
    if offset == 0:
        return values
    shifted = jnp.concatenate(
        [values[offset:], jnp.zeros((offset, values.shape[1]), values.dtype)], axis=0
    )
    same_doc = jnp.concatenate(
        [segments[:-offset] == segments[offset:], jnp.zeros((offset,), bool)]
    )
    return jnp.where(same_doc[:, None], shifted, 0.0)


def pad_front(array, fill_value):
    front = jnp.full((WINDOW,) + array.shape[1:], fill_value, array.dtype)
    return jnp.concatenate([front, array], axis=0)


def block_setup(queries, key_pad, seg_pad, segments, row_start, head_count):
    score_scale = HEAD_DIM ** (-0.5)
    query_rows = lax.dynamic_slice_in_dim(queries, row_start, BLOCK, 0).reshape(
        BLOCK, head_count, HEAD_DIM
    )
    key_block = lax.dynamic_slice_in_dim(key_pad, row_start, BLOCK + WINDOW, 0).reshape(
        BLOCK + WINDOW, head_count, HEAD_DIM
    )
    seg_rows = lax.dynamic_slice_in_dim(segments, row_start, BLOCK, 0)
    seg_keys = lax.dynamic_slice_in_dim(seg_pad, row_start, BLOCK + WINDOW, 0)
    distance = (
        jnp.arange(BLOCK, dtype=jnp.int32)[:, None]
        + WINDOW
        - jnp.arange(BLOCK + WINDOW, dtype=jnp.int32)[None, :]
    )
    allowed = (distance >= 0) & (distance < WINDOW) & (seg_rows[:, None] == seg_keys[None, :])
    scores = (
        jnp.einsum("qhd,khd->hqk", query_rows, key_block, preferred_element_type=jnp.float32)
        * score_scale
    )
    return (query_rows, key_block, jnp.where(allowed[None], scores, -1e30))


def attend_forward(queries, key_rows, value_rows, segments):
    group_rows, local_width = queries.shape
    head_count = local_width // HEAD_DIM
    key_pad = pad_front(key_rows, 0)
    value_pad = pad_front(value_rows, 0)
    seg_pad = pad_front(segments, -1)

    def one_block(block_index):
        row_start = block_index * BLOCK
        query_rows, key_block, scores = block_setup(
            queries, key_pad, seg_pad, segments, row_start, head_count
        )
        row_max = jnp.max(scores, axis=-1, keepdims=True)
        exponent = jnp.exp(scores - row_max)
        row_total = jnp.sum(exponent, axis=-1, keepdims=True)
        attention = (exponent / row_total).astype(jnp.bfloat16)
        value_block = lax.dynamic_slice_in_dim(value_pad, row_start, BLOCK + WINDOW, 0).reshape(
            BLOCK + WINDOW, head_count, HEAD_DIM
        )
        mixed_rows = jnp.einsum(
            "hqk,khd->qhd", attention, value_block, preferred_element_type=jnp.float32
        )
        return (
            mixed_rows.reshape(BLOCK, local_width),
            row_max[..., 0] + jnp.log(row_total[..., 0]),
        )

    blocks_out, log_totals = lax.map(one_block, jnp.arange(group_rows // BLOCK, dtype=jnp.int32))
    return (blocks_out.reshape(group_rows, local_width), log_totals)


def attend_backward(queries, key_rows, value_rows, segments, log_totals, grad_mixed):
    group_rows, local_width = queries.shape
    head_count = local_width // HEAD_DIM
    score_scale = HEAD_DIM ** (-0.5)
    key_pad = pad_front(key_rows, 0)
    value_pad = pad_front(value_rows, 0)
    seg_pad = pad_front(segments, -1)

    def one_block(accumulated, block_pair):
        block_index, log_block = block_pair
        row_start = block_index * BLOCK
        query_rows, key_block, scores = block_setup(
            queries, key_pad, seg_pad, segments, row_start, head_count
        )
        attention = jnp.exp(scores - log_block[..., None])
        value_block = lax.dynamic_slice_in_dim(value_pad, row_start, BLOCK + WINDOW, 0).reshape(
            BLOCK + WINDOW, head_count, HEAD_DIM
        )
        grad_block = lax.dynamic_slice_in_dim(grad_mixed, row_start, BLOCK, 0).reshape(
            BLOCK, head_count, HEAD_DIM
        )
        grad_attention = jnp.einsum(
            "qhd,khd->hqk", grad_block, value_block, preferred_element_type=jnp.float32
        )
        row_inner = jnp.sum(attention * grad_attention, axis=-1, keepdims=True)
        grad_scores = (attention * (grad_attention - row_inner)).astype(jnp.bfloat16)
        grad_query = (
            jnp.einsum("hqk,khd->qhd", grad_scores, key_block, preferred_element_type=jnp.float32)
            * score_scale
        )
        grad_key = (
            jnp.einsum("hqk,qhd->khd", grad_scores, query_rows, preferred_element_type=jnp.float32)
            * score_scale
        )
        grad_value = jnp.einsum(
            "hqk,qhd->khd",
            attention.astype(jnp.bfloat16),
            grad_block,
            preferred_element_type=jnp.float32,
        )
        key_acc, value_acc = accumulated
        key_acc = lax.dynamic_update_slice_in_dim(
            key_acc,
            lax.dynamic_slice_in_dim(key_acc, row_start, BLOCK + WINDOW, 0)
            + grad_key.reshape(BLOCK + WINDOW, local_width),
            row_start,
            0,
        )
        value_acc = lax.dynamic_update_slice_in_dim(
            value_acc,
            lax.dynamic_slice_in_dim(value_acc, row_start, BLOCK + WINDOW, 0)
            + grad_value.reshape(BLOCK + WINDOW, local_width),
            row_start,
            0,
        )
        return ((key_acc, value_acc), grad_query.astype(jnp.bfloat16).reshape(BLOCK, local_width))

    zeros_pad = jnp.zeros((group_rows + WINDOW, local_width), jnp.float32)
    block_ids = jnp.arange(group_rows // BLOCK, dtype=jnp.int32)
    (key_acc, value_acc), query_blocks = lax.scan(
        one_block, (zeros_pad, zeros_pad), (block_ids, log_totals)
    )
    return (query_blocks.reshape(group_rows, local_width), key_acc[WINDOW:], value_acc[WINDOW:])


def pairs_xor(size, mask):
    return [(i, i ^ mask) for i in range(size)]


def pairs_shift(size, step):
    return [(i, (i + step) % size) for i in range(size)]


def put(buffer, block, index):
    return lax.dynamic_update_slice_in_dim(buffer, block[None], index, 0)


def pick(blocks, index):
    return lax.dynamic_index_in_dim(blocks, index, 0, keepdims=False)


def gather_dp(own):
    size = lax.axis_size("dp")
    if size != 8:
        return lax.all_gather(own, "dp", axis=0)
    me = lax.axis_index("dp")
    over_y = pairs_xor(size, 1)
    up, down = pairs_shift(size, 2), pairs_shift(size, -2)
    mate = lax.ppermute(own, "dp", over_y)
    own_below = lax.ppermute(own, "dp", up)
    own_above = lax.ppermute(own, "dp", down)
    mate_below = lax.ppermute(mate, "dp", up)
    mate_above = lax.ppermute(mate, "dp", down)
    own_far = lax.ppermute(own_below, "dp", up)
    mate_far = lax.ppermute(mate_above, "dp", down)
    below, above, far = (me + 6) % size, (me + 2) % size, (me + 4) % size
    full = jnp.zeros((size,) + own.shape, own.dtype)
    for block, index in (
        (own, me),
        (mate, me ^ 1),
        (own_below, below),
        (own_above, above),
        (mate_below, below ^ 1),
        (mate_above, above ^ 1),
        (own_far, far),
        (mate_far, far ^ 1),
    ):
        full = put(full, block, index)
    return full


def scatter_dp(parts):
    size = lax.axis_size("dp")
    if size != 8:
        return lax.psum_scatter(parts, "dp", scatter_dimension=0).astype(jnp.float32)
    me = lax.axis_index("dp")
    over_y = pairs_xor(size, 1)
    up, down = pairs_shift(size, 2), pairs_shift(size, -2)
    below, above, far = (me + 6) % size, (me + 2) % size, (me + 4) % size

    def part(index):
        return pick(parts, index).astype(jnp.float32)

    low = jnp.bfloat16
    own_first = lax.ppermute(pick(parts, far), "dp", up)
    mate_first = lax.ppermute(pick(parts, far ^ 1), "dp", down)
    mate_from_below = lax.ppermute(pick(parts, above ^ 1), "dp", up)
    own_from_above = lax.ppermute(pick(parts, below), "dp", down)
    mate_from_above = lax.ppermute(
        (part(below ^ 1) + mate_first.astype(jnp.float32)).astype(low), "dp", down
    )
    own_from_below = lax.ppermute(
        (part(above) + own_first.astype(jnp.float32)).astype(low), "dp", up
    )
    mate_sum = (
        part(me ^ 1)
        + mate_from_below.astype(jnp.float32)
        + mate_from_above.astype(jnp.float32)
    )
    from_mate = lax.ppermute(mate_sum.astype(low), "dp", over_y)
    own_sum = part(me) + own_from_below.astype(jnp.float32) + own_from_above.astype(jnp.float32)
    return own_sum + from_mate.astype(jnp.float32)


def gather_tensor(own):
    size = lax.axis_size("tensor")
    if size != 4:
        return lax.all_gather(own, "tensor", axis=0, tiled=True)
    me = lax.axis_index("tensor")
    across = lax.ppermute(own, "tensor", pairs_xor(size, 2))
    beside = lax.ppermute(own, "tensor", pairs_xor(size, 1))
    beside_across = lax.ppermute(across, "tensor", pairs_xor(size, 1))
    full = jnp.zeros((size,) + own.shape, own.dtype)
    for block, index in ((own, me), (beside, me ^ 1), (across, me ^ 2), (beside_across, me ^ 3)):
        full = put(full, block, index)
    return full.reshape(size * own.shape[0], own.shape[1])


def scatter_tensor(parts):
    size = lax.axis_size("tensor")
    if size != 4:
        return lax.psum_scatter(
            parts.astype(jnp.bfloat16), "tensor", scatter_dimension=0, tiled=True
        ).astype(jnp.float32)
    me = lax.axis_index("tensor")
    low = jnp.bfloat16
    parts = parts.reshape(size, -1, parts.shape[1])
    beside = lax.ppermute(pick(parts, me ^ 3).astype(low), "tensor", pairs_xor(size, 1))
    sent = (pick(parts, me ^ 2).astype(jnp.float32) + beside.astype(jnp.float32)).astype(low)
    across = lax.ppermute(sent, "tensor", pairs_xor(size, 2))
    beside_own = lax.ppermute(pick(parts, me ^ 1).astype(low), "tensor", pairs_xor(size, 1))
    return (
        pick(parts, me).astype(jnp.float32)
        + beside_own.astype(jnp.float32)
        + across.astype(jnp.float32)
    )


def sum_all(values):
    dp_size, tensor_size = lax.axis_size("dp"), lax.axis_size("tensor")
    if dp_size != 8 or tensor_size != 4:
        return lax.psum(values, ("dp", "tensor"))
    for axis, size, mask in (
        ("tensor", tensor_size, 1),
        ("tensor", tensor_size, 2),
        ("dp", dp_size, 1),
        ("dp", dp_size, 2),
        ("dp", dp_size, 6),
    ):
        values = values + lax.ppermute(values, axis, pairs_xor(size, mask))
    return values


TILE = 64
LANES = 128


def neighbours():
    d, t = lax.axis_index("dp"), lax.axis_index("tensor")
    z, y = d // 2, lax.rem(d, 2)
    core = t + 1 - 2 * lax.rem(t, 2)
    place = z + y * (7 - 2 * z)

    def ring(offset):
        position = lax.rem(place + offset + 16, 8)
        side = position // 4
        return 2 * (position + side * (7 - 2 * position)) + side

    return dict(
        d=d,
        t=t,
        ring=ring,
        core=core,
        cross=lax.rem(t + 2, 4),
        cross_core=lax.rem(core + 2, 4),
        mate=d + 1 - 2 * y,
        z_pair=2 * (z + 1 - 2 * lax.rem(z, 2)) + y,
        z_mirror=2 * (3 - z) + y,
    )


def greet(at, everyone=False):
    d, t = at["d"], at["t"]
    devices = [(at["ring"](1), t), (at["ring"](-1), t), (d, at["core"]), (d, at["cross"])]
    if everyone:
        devices += [(at["mate"], t), (at["z_pair"], t), (at["z_mirror"], t)]
    barrier = pltpu.get_barrier_semaphore()
    for device in devices:
        pl.semaphore_signal(barrier, inc=1, device_id=device, device_id_type=MESH)
    pl.semaphore_wait(barrier, len(devices))


def remote(source, target, sems, index, device):
    return pltpu.make_async_remote_copy(
        src_ref=source,
        dst_ref=target,
        send_sem=sems[0].at[index],
        recv_sem=sems[1].at[index],
        device_id=device,
        device_id_type=MESH,
    )


def pieces_of(half, count):
    if count == 1:
        return [(0, half)]
    first = (half // 2 + 15) // 16 * 16
    return [(0, first), (first, half - first)]


class RingGather:
    def __init__(self, at, own, slot, sems, base, local_sem, count=2):
        half = own.shape[0] // 2
        ring, t = at["ring"], at["t"]
        self.local = pltpu.make_async_copy(own, slot(at["d"], 0, 2 * half), local_sem)
        self.sends, self.receives, self.at = [], [], 0
        for s in range(7):
            for k, (first, size) in enumerate(pieces_of(half, count)):
                sends, receives = [], []
                for way, sign in ((0, 1), (1, -1)):
                    to, row = (ring(sign), t), way * half + first
                    index = base + (s * count + k) * 2 + way
                    here = slot(ring(-sign * s), row, size)
                    there = slot(ring(-sign * (s + 1)), row, size)
                    source = own.at[pl.ds(row, size)] if s == 0 else here
                    sends.append(remote(source, here, sems, index, to))
                    receives.append(remote(there, there, sems, index, to))
                self.sends.append(sends)
                self.receives.append(receives)
        self.count = count

    def start(self):
        for copies in self.sends[: self.count]:
            for copy in copies:
                copy.start()
        self.local.start()

    def tick(self):
        if self.at < len(self.receives):
            for way in range(2):
                self.receives[self.at][way].wait_recv()
                if self.at + self.count < len(self.sends):
                    self.sends[self.at + self.count][way].start()
            self.at += 1

    def finish(self):
        while self.at < len(self.receives):
            self.tick()
        self.local.wait()

    def drain(self):
        for sends in self.sends:
            for copy in sends:
                copy.wait_send()


class RingScatter:
    def __init__(self, at, left, right, slots, term, out, sems, base, count=2):
        self.ring, self.left, self.right = at["ring"], left, right
        self.slots, self.term, self.out = slots, term, out
        self.half, self.columns = slots.shape[2], slots.shape[3]
        self.pieces = pieces_of(self.half, count)
        self.at = 0
        self.sends = []
        for s in range(7):
            for k, (first, size) in enumerate(self.pieces):
                rows = pl.ds(first, size)
                self.sends.append(
                    [
                        remote(
                            slots.at[way, s, rows], slots.at[way, s + 1, rows], sems,
                            base + (s * count + k) * 2 + way, (at["ring"](sign), at["t"]),
                        )
                        for way, sign in ((0, 1), (1, -1))
                    ]
                )

    def compute(self, away):
        half = self.half
        first = pl.multiple_of(self.ring(-away) * 2 * half, half)
        second = pl.multiple_of(self.ring(away) * 2 * half + half, half)
        width = 512
        whole = self.columns // width * width

        def block(lanes):
            left = jnp.concatenate(
                [self.left[pl.ds(first, half)], self.left[pl.ds(second, half)]], axis=0
            )
            self.term[:, lanes] = nn_dot(left, self.right[:, lanes])

        @pl.loop(0, whole // width)
        def _(i):
            block(pl.ds(pl.multiple_of(i * width, width), width))

        if whole < self.columns:
            block(pl.ds(whole, self.columns - whole))

    def start(self):
        self.compute(1)
        for k, (first, size) in enumerate(self.pieces):
            for way in range(2):
                self.slots[way, 0, pl.ds(first, size)] = self.term[
                    pl.ds(way * self.half + first, size)
                ].astype(jnp.bfloat16)
                self.sends[k][way].start()
        self.compute(2)

    def tick(self):
        if self.at == len(self.sends):
            return
        count = len(self.pieces)
        s, k = divmod(self.at, count)
        first, size = self.pieces[k]
        for way in range(2):
            here, rows = pl.ds(first, size), pl.ds(way * self.half + first, size)
            self.sends[self.at][way].wait_recv()
            total = self.slots[way, s + 1, here].astype(jnp.float32) + self.term[rows]
            if s < 6:
                self.slots[way, s + 1, here] = total.astype(jnp.bfloat16)
                self.sends[self.at + count][way].start()
            else:
                self.out[rows] = total
        self.at += 1
        if k == count - 1 and s < 6:
            self.compute(s + 3)

    def finish(self):
        while self.at < len(self.sends):
            self.tick()
        for sends in self.sends:
            for copy in sends:
                copy.wait_send()


class GatherTensor:
    def __init__(self, at, full, rows, sems, base):
        def block(index):
            return full.at[pl.ds(pl.multiple_of(index * rows, rows), rows)]

        mine, across = block(at["t"]), block(at["cross"])
        self.to_core = remote(mine, mine, sems, base, (at["d"], at["core"]))
        self.to_cross = remote(mine, mine, sems, base + 1, (at["d"], at["cross"]))
        self.relay_core = remote(across, across, sems, base + 2, (at["d"], at["core"]))
        places = (block(at["core"]), across, block(at["cross_core"]))
        self.receives = [
            remote(place, place, sems, base + k, (at["d"], at["core"]))
            for k, place in enumerate(places)
        ]

    def start(self):
        self.to_cross.start()
        self.to_core.start()

    def relay(self):
        self.receives[1].wait_recv()
        self.relay_core.start()

    def drain(self):
        for send in (self.to_core, self.to_cross, self.relay_core):
            send.wait_send()

    def finish(self):
        self.receives[0].wait_recv()
        self.receives[2].wait_recv()
        self.drain()


def sum_rows(at, block_part, send, receive, total, sems, base, idle=lambda point: None):
    to_core, to_cross = (at["d"], at["core"]), (at["d"], at["cross"])
    low = jnp.bfloat16
    first = remote(send.at[0], receive.at[0], sems, base, to_core)
    second = remote(send.at[1], receive.at[1], sems, base + 1, to_cross)
    third = remote(send.at[2], receive.at[2], sems, base + 2, to_core)
    send[0] = block_part(at["cross_core"]).astype(low)
    first.start()
    total[...] = block_part(at["cross"])
    first.wait_recv()
    send[1] = (total[...] + receive[0].astype(jnp.float32)).astype(low)
    second.start()
    idle(0)
    send[2] = block_part(at["core"]).astype(low)
    third.start()
    idle(1)
    total[...] = block_part(at["t"])
    third.wait_recv()
    total[...] += receive[2].astype(jnp.float32)
    idle(2)
    second.wait_recv()
    total[...] += receive[1].astype(jnp.float32)
    for copy in (first, second, third):
        copy.wait_send()


class SumAll:
    def __init__(self, at, value, received, sems, base):
        d, t = at["d"], at["t"]
        partners = ((d, at["core"]), (d, at["cross"]), (at["mate"], t), (at["z_pair"], t), (at["z_mirror"], t))
        self.value, self.received, self.s = value, received, 0
        self.copies = [
            remote(value.at[k], received.at[k], sems, base + k, partner)
            for k, partner in enumerate(partners)
        ]

    def start(self):
        self.copies[0].start()

    def step(self):
        s = self.s
        self.copies[s].wait_recv()
        self.value[s + 1] = self.value[s] + self.received[s]
        if s < 4:
            self.copies[s + 1].start()
        self.s += 1

    def finish(self):
        while self.s < 5:
            self.step()
        for copy in self.copies:
            copy.wait_send()


def nt_dot(left, right):
    return lax.dot_general(
        left, right, (((1,), (1,)), ((), ())), preferred_element_type=jnp.float32
    )


def nn_dot(left, right):
    return lax.dot_general(
        left, right, (((1,), (0,)), ((), ())), preferred_element_type=jnp.float32
    )


def tn_dot(left, right):
    return lax.dot_general(
        left, right, (((0,), (0,)), ((), ())), preferred_element_type=jnp.float32
    )


def head_groups(width):
    heads = width // HEAD_DIM
    return [(2 * HEAD_DIM * j, min(2, heads - 2 * j)) for j in range((heads + 1) // 2)]


def split_heads(tile, heads):
    if heads == 1:
        return tile
    lane = lax.broadcasted_iota(jnp.int32, tile.shape, 1)
    zero = jnp.zeros_like(tile)
    return jnp.concatenate(
        [jnp.where(lane < HEAD_DIM, tile, zero), jnp.where(lane < HEAD_DIM, zero, tile)], axis=0
    )


def join_heads(stacked, heads):
    if heads == 1:
        return stacked
    half = stacked.shape[0] // 2
    lane = lax.broadcasted_iota(jnp.int32, (half, stacked.shape[1]), 1)
    return jnp.where(lane < HEAD_DIM, stacked[:half], stacked[half:])


def convolve(window, taps, lanes, same_one, same_two):
    one = pltpu.roll(window, 1, axis=0)[TILE:] * same_one
    two = pltpu.roll(window, 2, axis=0)[TILE:] * same_two
    rows = (window[TILE:], one, two)
    return sum(taps[m : m + 1, lanes] * rows[m] for m in range(CONV)), rows


def attend_tile(i, q, k_pad, v_pad, u, seg_q, seg_k, same, taps, p_out, o):
    row = pl.multiple_of(i * TILE, TILE)
    at_row, at_window = pl.ds(row, TILE), pl.ds(row, 2 * TILE)
    distance = (
        lax.broadcasted_iota(jnp.int32, (TILE, 2 * TILE), 0)
        + TILE
        - lax.broadcasted_iota(jnp.int32, (TILE, 2 * TILE), 1)
    )
    allowed = (seg_q[at_row] == seg_k[i]) & (distance >= 0) & (distance < WINDOW)
    same_one, same_two = same[at_row, 0:1], same[at_row, 1:2]
    for lane, heads in head_groups(q.shape[1]):
        lanes = pl.ds(lane, heads * HEAD_DIM)
        values = v_pad[at_window, lanes]
        allow = jnp.concatenate([allowed] * heads, axis=0) if heads > 1 else allowed
        scores = nt_dot(split_heads(q[at_row, lanes], heads), k_pad[at_window, lanes])
        scores = jnp.where(allow, scores * (HEAD_DIM**-0.5), -1e30)
        exponent = jnp.exp(scores - jnp.max(scores, axis=1, keepdims=True))
        chance = exponent * (1.0 / jnp.sum(exponent, axis=1, keepdims=True))
        chance = chance.astype(jnp.bfloat16)
        p_out[i, pl.ds((lane // HEAD_DIM) * TILE, heads * TILE), :] = chance
        mixed = join_heads(nn_dot(chance, values), heads)
        convolved, _ = convolve(values.astype(jnp.float32), taps, lanes, same_one, same_two)
        o[at_row, lanes] = (mixed + convolved * u[at_row, lanes].astype(jnp.float32)).astype(
            jnp.bfloat16
        )


def attend_back_tile(
    i, q, k_pad, v_pad, u, p, same, taps, do, dk, dv, conv_sum
):
    row = pl.multiple_of(i * TILE, TILE)
    at_row, at_window = pl.ds(row, TILE), pl.ds(row, 2 * TILE)
    same_one, same_two = same[at_row, 0:1], same[at_row, 1:2]
    for lane, heads in head_groups(q.shape[1]):
        lanes = pl.ds(lane, heads * HEAD_DIM)
        keys, values = k_pad[at_window, lanes], v_pad[at_window, lanes]
        grad = do[at_row, lanes]
        grad_heads = split_heads(grad, heads)
        chance_low = p[i, pl.ds((lane // HEAD_DIM) * TILE, heads * TILE), :]
        chance = chance_low.astype(jnp.float32)
        weighted = chance * nt_dot(grad_heads, values)
        slope = weighted - chance * jnp.sum(weighted, axis=1, keepdims=True)
        slope = (slope * (HEAD_DIM**-0.5)).astype(jnp.bfloat16)
        dk[at_window, lanes] += tn_dot(slope, split_heads(q[at_row, lanes], heads))
        q[at_row, lanes] = join_heads(nn_dot(slope, keys), heads).astype(jnp.bfloat16)
        convolved, rows = convolve(values.astype(jnp.float32), taps, lanes, same_one, same_two)
        grad = grad.astype(jnp.float32)
        do[at_row, lanes] = (grad * convolved).astype(jnp.bfloat16)
        grad_conv = grad * u[at_row, lanes].astype(jnp.float32)
        back = tn_dot(chance_low, grad_heads)
        zero = jnp.zeros_like(grad_conv)
        for m, same_m in enumerate((None, same_one, same_two)):
            conv_sum[m : m + 1, lanes] += jnp.sum(grad_conv * rows[m], axis=0, keepdims=True)
            term = taps[m : m + 1, lanes] * grad_conv
            term = term if m == 0 else term * same_m
            term = jnp.concatenate([zero, term], axis=0)
            back = back + (term if m == 0 else pltpu.roll(term, 2 * TILE - m, axis=0))
        dv[at_window, lanes] += back


def norm_rows(values, gain):
    scale = lax.rsqrt(jnp.mean(values * values, axis=1, keepdims=True) + EPS)
    return (values * scale * gain).astype(jnp.bfloat16)


def norm_back(values, grad, gain):
    scale = lax.rsqrt(jnp.mean(values * values, axis=1, keepdims=True) + EPS)
    normed = values * scale
    scaled = grad * gain
    through = scale * (scaled - normed * jnp.mean(scaled * normed, axis=1, keepdims=True))
    return through, jnp.sum(grad * normed, axis=0, keepdims=True)


def chunks_of(rows, size=64):
    def run(body):
        @pl.loop(0, rows // size)
        def _(i):
            body(pl.multiple_of(i * size, size), size)

    return run


def mixer_forward_kernel(
    x, valid, gain_one, gain_two, seg_q, seg_k, same, taps, mix_own, out_own, feed_own,
    mix_out, last_out, feed, h1t_out, q_out, k_out, v_out, u_out, p_out, o_out, x1_out, h2_out, count_out,
    mix, last, h1, h1t, h2, q, k_pad, v_pad, u, p, o, send, receive, total, count, count_in,
    send_sems, recv_sems, local_sems, out_sems,
):
    at = neighbours()
    sems = (send_sems, recv_sems)
    rows, shard = x.shape[0], mix_own.shape[0]
    greet(at, everyone=True)

    def slot_of(full):
        return lambda i, first, size: full.at[pl.ds(pl.multiple_of(i * shard + first, 16), size)]

    early = RingGather(at, mix_own, slot_of(mix), sems, 0, local_sems.at[0])
    middle = RingGather(at, out_own, slot_of(last), sems, 28, local_sems.at[1], count=1)
    late = RingGather(at, feed_own, slot_of(feed), sems, 42, local_sems.at[2])
    group_one = GatherTensor(at, h1, rows, sems, 70)
    group_two = GatherTensor(at, h2, rows, sems, 73)
    counting = SumAll(at, count, count_in, sems, 79)
    local = q.shape[1]
    main = local // LANES * LANES
    tail = local - main
    keeps = []

    def keep(source, target):
        copy = pltpu.make_async_copy(source, target, out_sems.at[len(keeps)])
        copy.start()
        keeps.append(copy)

    early.start()

    @chunks_of(rows)
    def _(row, size):
        h1[pl.ds(pl.multiple_of(at["t"] * rows + row, size), size)] = norm_rows(
            x[pl.ds(row, size)].astype(jnp.float32), gain_one[...]
        )

    group_one.start()
    count[0] = jnp.full(count.shape[1:], jnp.sum(valid[...]), jnp.float32)
    counting.start()
    k_pad[pl.ds(0, TILE)] = jnp.zeros((TILE, local), k_pad.dtype)
    v_pad[pl.ds(0, TILE)] = jnp.zeros((TILE, local), v_pad.dtype)
    early.tick()
    early.tick()
    counting.step()
    early.tick()
    early.tick()
    counting.step()
    early.tick()
    group_one.relay()
    early.tick()
    counting.step()
    early.tick()
    early.tick()
    counting.step()
    group_one.finish()
    early.tick()

    @pl.loop(0, 4)
    def _(j):
        here = pl.multiple_of(j * rows, rows)
        h1t[:, pl.ds(here, rows)] = h1[pl.ds(here, rows)].T

    keep(h1t, h1t_out)
    early.tick()
    counting.finish()
    keep(count.at[5], count_out)
    middle.start()
    early.tick()
    early.tick()
    middle.tick()
    late.start()
    early.tick()
    middle.tick()
    early.finish()
    middle.tick()
    keep(mix, mix_out)

    def project(j):
        here = pl.ds(pl.multiple_of(j * rows, rows), rows)
        there = pl.ds(pl.multiple_of(j * rows + TILE, TILE), rows)
        left = h1[here]
        low = jnp.bfloat16
        pair = nn_dot(left, mix[:, pl.ds(0, 2 * main)]).astype(low)
        q[here, pl.ds(0, main)] = pair[:, :main]
        k_pad[there, pl.ds(0, main)] = pair[:, main:]
        pair = nn_dot(left, mix[:, pl.ds(2 * main, 2 * main)]).astype(low)
        v_pad[there, pl.ds(0, main)] = pair[:, :main]
        u[here, pl.ds(0, main)] = pair[:, main:]
        ends = nn_dot(left, mix[:, pl.ds(4 * main, 4 * tail)])
        q[here, pl.ds(main, tail)] = ends[:, :tail].astype(low)
        k_pad[there, pl.ds(main, tail)] = ends[:, tail : 2 * tail].astype(low)
        v_pad[there, pl.ds(main, tail)] = ends[:, 2 * tail : 3 * tail].astype(low)
        u[here, pl.ds(main, tail)] = ends[:, 3 * tail :].astype(low)

    def projects(first, last_block):
        @pl.loop(first, last_block)
        def _(j):
            project(j)

    def tick():
        late.tick()
        middle.tick()

    projects(0, 2)
    tick()
    projects(2, 4)
    for source, target in ((q, q_out), (k_pad, k_out), (v_pad, v_out), (u, u_out)):
        keep(source, target)
    tick()
    tiles = q.shape[0] // TILE

    def attend(first, last_tile):
        @pl.loop(first, last_tile)
        def _(i):
            attend_tile(i, q, k_pad, v_pad, u, seg_q, seg_k, same, taps, p, o)

    for k in range(4):
        attend(k * tiles // 4, (k + 1) * tiles // 4)
        tick()
    middle.finish()
    keep(last, last_out)
    keep(p, p_out)
    keep(o, o_out)

    def part(block):
        return nt_dot(o[pl.ds(pl.multiple_of(block * rows, rows), rows)], last[...])

    def idle(point):
        late.tick()
        if point == 2:
            late.tick()

    sum_rows(at, part, send, receive, total, sems, 76, idle=idle)

    @chunks_of(rows)
    def _(row, size):
        here = pl.ds(row, size)
        hidden = total[here] + x[here].astype(jnp.float32)
        total[here] = hidden
        h2[pl.ds(pl.multiple_of(at["t"] * rows + row, size), size)] = norm_rows(hidden, gain_two[...])

    group_two.start()
    keep(total, x1_out)
    for _ in range(3):
        late.tick()
    group_two.relay()
    late.tick()
    group_two.finish()
    keep(h2, h2_out)
    late.finish()
    for ring in (early, middle, late):
        ring.drain()
    for copy in keeps:
        copy.wait()


def specs():
    return pl.BlockSpec(memory_space=pltpu.VMEM), pl.BlockSpec(memory_space=pl.ANY)


def shape(*dims, kind=jnp.bfloat16):
    return jax.ShapeDtypeStruct(dims, kind)


def params(identity):
    return pltpu.CompilerParams(
        collective_id=identity, has_side_effects=True, vmem_limit_bytes=VMEM_LIMIT
    )


def dma(count):
    return pltpu.SemaphoreType.DMA((count,))


def mixer_forward(x, valid, gain_one, gain_two, seg_q, seg_k, same, taps, mix_own, out_own, feed_own):
    rows, width = x.shape
    shard, local = out_own.shape
    everyone, depth = 4 * rows, 8 * shard
    low, wide = jnp.bfloat16, jnp.float32
    tiles, heads = everyone // TILE, local // HEAD_DIM
    vmem, hbm = specs()
    return pl.pallas_call(
        mixer_forward_kernel,
        out_shape=(
            shape(depth, mix_own.shape[1]),
            shape(depth, local),
            shape(depth, feed_own.shape[1]),
            shape(width, everyone),
            shape(everyone, local),
            shape(everyone + TILE, local),
            shape(everyone + TILE, local),
            shape(everyone, local),
            shape(tiles, heads * TILE, 2 * TILE),
            shape(everyone, local),
            shape(rows, width, kind=wide),
            shape(everyone, width),
            shape(8, LANES, kind=wide),
        ),
        in_specs=[vmem] * 8 + [hbm] * 3,
        out_specs=(hbm,) * 13,
        scratch_shapes=[
            pltpu.VMEM((depth, mix_own.shape[1]), low),
            pltpu.VMEM((depth, local), low),
            pltpu.VMEM((everyone, width), low),
            pltpu.VMEM((width, everyone), low),
            pltpu.VMEM((everyone, width), low),
            pltpu.VMEM((everyone, local), low),
            pltpu.VMEM((everyone + TILE, local), low),
            pltpu.VMEM((everyone + TILE, local), low),
            pltpu.VMEM((everyone, local), low),
            pltpu.VMEM((tiles, heads * TILE, 2 * TILE), low),
            pltpu.VMEM((everyone, local), low),
            pltpu.VMEM((3, rows, width), low),
            pltpu.VMEM((3, rows, width), low),
            pltpu.VMEM((rows, width), wide),
            pltpu.VMEM((6, 8, LANES), wide),
            pltpu.VMEM((5, 8, LANES), wide),
            dma(84),
            dma(84),
            dma(3),
            dma(12),
        ],
        compiler_params=params(1),
    )(x, valid, gain_one, gain_two, seg_q, seg_k, same, taps, mix_own, out_own, feed_own)


def feed_lanes(hidden):
    main = hidden // LANES * LANES
    cut = main // 2 // LANES * LANES
    parts = [(0, cut), (cut, main - cut)]
    return [(pl.ds(a, n), pl.ds(a, n), pl.ds(main + a, n)) for a, n in parts], main


def gated(gate, up):
    sigmoid = jax.nn.sigmoid(gate)
    silu = gate * sigmoid
    return silu * up, up * sigmoid * (1.0 + gate * (1.0 - sigmoid)), silu


def feed_forward_kernel(
    valid, count, h2_in, feed_in, x1_in, cotangent_in, teacher_in, down_own,
    down_out, slopes_out, active_out, act_out, dy_out, dyb_out, dybt_out, h2t_out, squares_out,
    h2, feed, down, slopes, active, x1, cotangent, teacher, dyb, turned, send, receive, total,
    send_sems, recv_sems, local_sems, load_sems, out_sems,
):
    at = neighbours()
    sems = (send_sems, recv_sems)
    rows, shard = x1.shape[0], down_own.shape[0]
    low = jnp.bfloat16
    greet(at)
    ring = RingGather(
        at, down_own, lambda i, first, size: down.at[pl.ds(pl.multiple_of(i * shard + first, 16), size)],
        sems, 0, local_sems.at[0],
    )
    group = GatherTensor(at, dyb, rows, sems, 31)
    loads = [
        pltpu.make_async_copy(source, target, load_sems.at[n])
        for n, (source, target) in enumerate(
            ((h2_in, h2), (feed_in, feed), (x1_in, x1), (cotangent_in, cotangent), (teacher_in, teacher))
        )
    ]
    keeps = []

    def keep(source, target):
        copy = pltpu.make_async_copy(source, target, out_sems.at[len(keeps)])
        copy.start()
        keeps.append(copy)

    ring.start()
    for load in loads:
        load.start()
    hidden = active.shape[1]
    parts, main = feed_lanes(hidden)
    tail = hidden - main
    loads[0].wait()
    loads[1].wait()

    def widen(first, last):
        @pl.loop(first, last)
        def _(j):
            here = pl.ds(pl.multiple_of(j * rows, rows), rows)
            left = h2[here]
            for own, gate_lanes, up_lanes in parts:
                a, by_gate, by_up = gated(nn_dot(left, feed[:, gate_lanes]), nn_dot(left, feed[:, up_lanes]))
                active[here, own] = a.astype(low)
                slopes[here, gate_lanes] = by_gate.astype(low)
                slopes[here, up_lanes] = by_up.astype(low)
            both = nn_dot(left, feed[:, pl.ds(2 * main, 2 * tail)])
            a, by_gate, by_up = gated(both[:, :tail], both[:, tail:])
            active[here, pl.ds(main, tail)] = a.astype(low)
            slopes[here, pl.ds(2 * main, 2 * tail)] = jnp.concatenate([by_gate, by_up], axis=1).astype(low)

    ring.tick()
    for k in range(4):
        widen(k, k + 1)
        ring.tick()
    keep(active, active_out)
    keep(slopes, slopes_out)
    ring.tick()

    def turn(source, block):
        here = pl.multiple_of(block * rows, rows)
        turned[:, pl.ds(here, rows)] = source[pl.ds(here, rows)].T

    @pl.loop(0, 4)
    def _(j):
        turn(h2, j)

    keep(turned, h2t_out)
    ring.finish()
    keep(down, down_out)
    for load in loads[2:]:
        load.wait()

    def part(block):
        return nt_dot(active[pl.ds(pl.multiple_of(block * rows, rows), rows)], down[...])

    sum_rows(at, part, send, receive, total, sems, 28)
    weight = (rows * 4 * 8) / count[0:1, 0:1]
    squares_out[...] = jnp.zeros_like(squares_out)

    @chunks_of(rows, 32)
    def _(row, size):
        here = pl.ds(row, size)
        result = total[here] + x1[here]
        deviation = result - teacher[here].astype(jnp.float32)
        kept = valid[here, 0:1] * deviation
        total[here] = result
        squares_out[0:1] += jnp.sum(kept * deviation, axis=0, keepdims=True)
        grad = cotangent[here] + kept * weight
        x1[here] = grad
        dyb[pl.ds(pl.multiple_of(at["t"] * rows + row, size), size)] = grad.astype(low)

    group.start()
    keep(total, act_out)
    keep(x1, dy_out)
    keeps[2].wait()
    turn(dyb, at["t"])
    group.receives[0].wait_recv()
    turn(dyb, at["core"])
    group.relay()
    turn(dyb, at["cross"])
    group.receives[2].wait_recv()
    turn(dyb, at["cross_core"])
    group.drain()
    keep(dyb, dyb_out)
    keep(turned, dybt_out)
    ring.drain()
    for n, copy in enumerate(keeps):
        if n != 2:
            copy.wait()


def feed_forward(valid, count, h2, feed, x1, cotangent, teacher, down_own):
    rows, width = x1.shape
    shard, hidden = down_own.shape
    everyone, depth = 4 * rows, 8 * shard
    low, wide = jnp.bfloat16, jnp.float32
    vmem, hbm = specs()
    return pl.pallas_call(
        feed_forward_kernel,
        out_shape=(
            shape(depth, hidden),
            shape(everyone, 2 * hidden),
            shape(everyone, hidden),
            shape(rows, width, kind=wide),
            shape(rows, width, kind=wide),
            shape(everyone, width),
            shape(width, everyone),
            shape(width, everyone),
            shape(8, width, kind=wide),
        ),
        in_specs=[vmem] * 2 + [hbm] * 6,
        out_specs=(hbm,) * 8 + (vmem,),
        scratch_shapes=[
            pltpu.VMEM((everyone, width), low),
            pltpu.VMEM((depth, 2 * hidden), low),
            pltpu.VMEM((depth, hidden), low),
            pltpu.VMEM((everyone, 2 * hidden), low),
            pltpu.VMEM((everyone, hidden), low),
            pltpu.VMEM((rows, width), wide),
            pltpu.VMEM((rows, width), wide),
            pltpu.VMEM((rows, width), low),
            pltpu.VMEM((everyone, width), low),
            pltpu.VMEM((width, everyone), low),
            pltpu.VMEM((3, rows, width), low),
            pltpu.VMEM((3, rows, width), low),
            pltpu.VMEM((rows, width), wide),
            dma(34),
            dma(34),
            dma(1),
            dma(5),
            dma(8),
        ],
        compiler_params=params(2),
    )(valid, count, h2, feed, x1, cotangent, teacher, down_own)


def feed_backward_kernel(
    gain, dyb_in, dybt_in, h2t_in, down_in, feed_in, active_in, slopes_in, last_in, x1_in, dy_in,
    down_grad, gate_grad, gain_part, dx1_out, dx1t_out, do_out, slopes_out,
    dyb, dybt, h2t, down, feed, active, slopes, last, do, side, total, down_slots, gate_slots,
    down_term, gate_term, send, receive,
    send_sems, recv_sems, load_sems, out_sems,
):
    at = neighbours()
    sems = (send_sems, recv_sems)
    rows = total.shape[0]
    low = jnp.bfloat16
    loads = [
        pltpu.make_async_copy(source, target, load_sems.at[n])
        for n, (source, target) in enumerate(
            (
                (dybt_in, dybt), (active_in, active), (dyb_in, dyb), (down_in, down), (slopes_in, slopes),
                (h2t_in, h2t), (feed_in, feed), (last_in, last), (x1_in, side), (dy_in, side),
            )
        )
    ]
    for load in loads[:-1]:
        load.start()
    greet(at)
    hidden = active.shape[1]
    parts, main = feed_lanes(hidden)
    tail = hidden - main
    first = RingScatter(at, dybt, active, down_slots, down_term, down_grad, sems, 0)
    second = RingScatter(
        at, h2t, slopes.at[:, pl.ds(0, main)], gate_slots, gate_term, gate_grad, sems, 28
    )
    group = GatherTensor(at, dyb, rows, sems, 59)
    keeps = []

    def keep(source, target):
        copy = pltpu.make_async_copy(source, target, out_sems.at[len(keeps)])
        copy.start()
        keeps.append(copy)

    loads[0].wait()
    loads[1].wait()
    first.start()
    for load in loads[2:5]:
        load.wait()

    def slope_back(first_block, last_block):
        @pl.loop(first_block, last_block)
        def _(j):
            here = pl.ds(pl.multiple_of(j * rows, rows), rows)
            left = dyb[here]
            for own, gate_lanes, up_lanes in parts:
                da = nn_dot(left, down[:, own])
                slopes[here, gate_lanes] = (da * slopes[here, gate_lanes].astype(jnp.float32)).astype(low)
                slopes[here, up_lanes] = (da * slopes[here, up_lanes].astype(jnp.float32)).astype(low)
            da = nn_dot(left, down[:, pl.ds(main, tail)])
            ends = pl.ds(2 * main, 2 * tail)
            both = jnp.concatenate([da, da], axis=1) * slopes[here, ends].astype(jnp.float32)
            slopes[here, ends] = both.astype(low)

    for k in range(4):
        slope_back(k, k + 1)
        first.tick()
    keep(slopes.at[:, pl.ds(main, 2 * hidden - main)], slopes_out)
    loads[5].wait()
    second.start()
    loads[6].wait()
    loads[8].wait()

    def part(block):
        return nt_dot(slopes[pl.ds(pl.multiple_of(block * rows, rows), rows)], feed[...])

    def idle(point):
        first.tick()
        second.tick()
        if point == 2:
            first.tick()
            second.tick()

    sum_rows(at, part, send, receive, total, sems, 56, idle=idle)
    gain_part[...] = jnp.zeros_like(gain_part)

    @chunks_of(rows, 32)
    def _(row, size):
        here = pl.ds(row, size)
        through, term_gain = norm_back(side[here], total[here], gain[...])
        gain_part[0:1] += term_gain
        total[here] = through

    loads[9].start()
    first.tick()
    second.tick()
    loads[9].wait()

    @chunks_of(rows, 32)
    def _(row, size):
        here = pl.ds(row, size)
        grad = total[here] + side[here]
        total[here] = grad
        dyb[pl.ds(pl.multiple_of(at["t"] * rows + row, size), size)] = grad.astype(low)

    group.start()
    keep(total, dx1_out)
    loads[7].wait()

    def spread(block):
        here = pl.ds(pl.multiple_of(block * rows, rows), rows)
        dybt[:, here] = dyb[here].T
        do[here] = nn_dot(dyb[here], last[...]).astype(low)

    while first.at < len(first.sends):
        first.tick()
        second.tick()
    spread(at["t"])
    second.tick()
    group.receives[0].wait_recv()
    spread(at["core"])
    second.tick()
    group.relay()
    second.tick()
    spread(at["cross"])
    group.receives[2].wait_recv()
    spread(at["cross_core"])
    group.drain()
    keep(dybt, dx1t_out)
    keep(do, do_out)
    second.finish()
    first.finish()
    for copy in keeps:
        copy.wait()


def feed_backward(gain, dyb, dybt, h2t, down, feed, active, slopes, last, x1, dy):
    rows, width = x1.shape
    depth, hidden = down.shape
    local = last.shape[1]
    main = hidden // LANES * LANES
    everyone, shard = 4 * rows, depth // 8
    low, wide = jnp.bfloat16, jnp.float32
    vmem, hbm = specs()
    return pl.pallas_call(
        feed_backward_kernel,
        out_shape=(
            shape(shard, hidden, kind=wide),
            shape(shard, main, kind=wide),
            shape(8, width, kind=wide),
            shape(rows, width, kind=wide),
            shape(width, everyone),
            shape(everyone, local),
            shape(everyone, 2 * hidden - main),
        ),
        in_specs=[vmem] + [hbm] * 10,
        out_specs=(vmem,) * 3 + (hbm,) * 4,
        scratch_shapes=[
            pltpu.VMEM((everyone, width), low),
            pltpu.VMEM((width, everyone), low),
            pltpu.VMEM((width, everyone), low),
            pltpu.VMEM((depth, hidden), low),
            pltpu.VMEM((depth, 2 * hidden), low),
            pltpu.VMEM((everyone, hidden), low),
            pltpu.VMEM((everyone, 2 * hidden), low),
            pltpu.VMEM((depth, local), low),
            pltpu.VMEM((everyone, local), low),
            pltpu.VMEM((rows, width), wide),
            pltpu.VMEM((rows, width), wide),
            pltpu.VMEM((2, 8, shard // 2, hidden), low),
            pltpu.VMEM((2, 8, shard // 2, main), low),
            pltpu.VMEM((shard, hidden), wide),
            pltpu.VMEM((shard, main), wide),
            pltpu.VMEM((3, rows, width), low),
            pltpu.VMEM((3, rows, width), low),
            dma(62),
            dma(62),
            dma(10),
            dma(4),
        ],
        compiler_params=params(3),
    )(gain, dyb, dybt, h2t, down, feed, active, slopes, last, x1, dy)


def mixer_backward_kernel(
    x, gain, same, taps, gain_part, squares,
    dx1t_in, o_in, h2t_in, slopes_in, q_in, k_in, v_in, u_in, p_in, do_in, mix_in, h1t_in, dx1_in,
    out_grad, up_grad, mix_grad, input_grad, small_out, conv_out,
    turned, o, h2t, slopes, q, k_pad, v_pad, u, p, do, mix,
    dk, dv, grads, out_slots, up_slots, mix_slots, out_term, up_term, mix_term, send, receive, total,
    small, small_in, conv, conv_in,
    send_sems, recv_sems, load_sems,
):
    at = neighbours()
    sems = (send_sems, recv_sems)
    rows = total.shape[0]
    low = jnp.bfloat16
    loads = [
        pltpu.make_async_copy(source, target, load_sems.at[n])
        for n, (source, target) in enumerate(
            (
                (dx1t_in, turned), (o_in, o), (h2t_in, h2t), (slopes_in, slopes), (q_in, q), (k_in, k_pad),
                (v_in, v_pad), (u_in, u), (p_in, p), (do_in, do), (mix_in, mix), (dx1_in, input_grad),
                (h1t_in, turned),
            )
        )
    ]
    for load in loads[:-1]:
        load.start()
    greet(at, everyone=True)
    local = q.shape[1]
    main = local // LANES * LANES
    tail = local - main
    first = RingScatter(at, turned, o, out_slots, out_term, out_grad, sems, 0, count=1)
    second = RingScatter(at, h2t, slopes, up_slots, up_term, up_grad, sems, 14)
    third = RingScatter(at, turned, grads, mix_slots, mix_term, mix_grad, sems, 42)
    small_sum = SumAll(at, small, small_in, sems, 73)
    conv_all = SumAll(at, conv, conv_in, sems, 78)
    loads[0].wait()
    loads[1].wait()
    first.start()
    loads[2].wait()
    loads[3].wait()
    second.start()
    dk[...] = jnp.zeros_like(dk)
    dv[...] = jnp.zeros_like(dv)
    conv[0] = jnp.zeros(conv.shape[1:], jnp.float32)
    first.tick()
    for load in loads[4:10]:
        load.wait()
    tiles = q.shape[0] // TILE
    conv_sum = conv.at[0, at["t"]]

    def attend(a, b):
        @pl.loop(a, b)
        def _(i):
            attend_back_tile(i, q, k_pad, v_pad, u, p, same, taps, do, dk, dv, conv_sum)

    for k in range(4):
        attend(k * tiles // 4, (k + 1) * tiles // 4)
        first.tick()
        second.tick()
    conv_all.start()

    @chunks_of(q.shape[0])
    def _(row, size):
        here, there = pl.ds(row, size), pl.ds(pl.multiple_of(row + TILE, TILE), size)
        four = [q[here].astype(jnp.float32), dk[there], dv[there], do[here].astype(jnp.float32)]
        for n, value in enumerate(four):
            grads[here, pl.ds(n * main, main)] = value[:, :main].astype(low)
        ends = jnp.concatenate([value[:, main:] for value in four], axis=1)
        grads[here, pl.ds(4 * main, 4 * tail)] = ends.astype(low)

    first.finish()
    loads[12].start()
    second.tick()
    second.tick()
    loads[12].wait()
    loads[10].wait()
    loads[11].wait()
    third.start()

    def part(block):
        return nt_dot(grads[pl.ds(pl.multiple_of(block * rows, rows), rows)], mix[...])

    def idle(point):
        second.tick()
        third.tick()
        if point == 2:
            second.tick()
            conv_all.step()

    sum_rows(at, part, send, receive, total, sems, 70, idle=idle)
    small[0, 0:1] = jnp.zeros((1, small.shape[2]), jnp.float32)
    small[0, 1:2] = gain_part[0:1]
    small[0, 2:3] = squares[0:1]
    small[0, 3:8] = jnp.zeros((5, small.shape[2]), jnp.float32)

    @chunks_of(rows, 32)
    def _(row, size):
        here = pl.ds(row, size)
        through, term_gain = norm_back(x[here].astype(jnp.float32), total[here], gain[...])
        small[0, 0:1] += term_gain
        input_grad[here] += through

    small_sum.start()
    for k in range(4):
        second.tick()
        third.tick()
        conv_all.step()
        second.tick()
        third.tick()
        small_sum.step()
    small_sum.finish()
    conv_all.finish()
    second.finish()
    third.finish()
    small_out[...] = small[5]
    conv_out[...] = conv[5]


def mixer_backward(
    x, gain, same, taps, gain_part, squares, dx1t, o, h2t, slopes, q, k_pad, v_pad, u, p, do, mix, h1t, dx1
):
    rows, width = x.shape
    everyone, local = o.shape
    shard, ups = width // 8, slopes.shape[1]
    low, wide = jnp.bfloat16, jnp.float32
    vmem, hbm = specs()
    arrays = (dx1t, o, h2t, slopes, q, k_pad, v_pad, u, p, do, mix)
    return pl.pallas_call(
        mixer_backward_kernel,
        out_shape=(
            shape(shard, local, kind=wide),
            shape(shard, ups, kind=wide),
            shape(shard, 4 * local, kind=wide),
            shape(rows, width, kind=wide),
            shape(8, width, kind=wide),
            shape(4, 8, local, kind=wide),
        ),
        in_specs=[vmem] * 6 + [hbm] * 13,
        out_specs=(vmem,) * 6,
        scratch_shapes=[pltpu.VMEM(array.shape, array.dtype) for array in arrays]
        + [
            pltpu.VMEM((everyone + TILE, local), wide),
            pltpu.VMEM((everyone + TILE, local), wide),
            pltpu.VMEM((everyone, 4 * local), low),
            pltpu.VMEM((2, 8, shard // 2, local), low),
            pltpu.VMEM((2, 8, shard // 2, ups), low),
            pltpu.VMEM((2, 8, shard // 2, 4 * local), low),
            pltpu.VMEM((shard, local), wide),
            pltpu.VMEM((shard, ups), wide),
            pltpu.VMEM((shard, 4 * local), wide),
            pltpu.VMEM((3, rows, width), low),
            pltpu.VMEM((3, rows, width), low),
            pltpu.VMEM((rows, width), wide),
            pltpu.VMEM((6, 8, width), wide),
            pltpu.VMEM((5, 8, width), wide),
            pltpu.VMEM((6, 4, 8, local), wide),
            pltpu.VMEM((5, 4, 8, local), wide),
            dma(83),
            dma(83),
            dma(13),
        ],
        compiler_params=params(4),
    )(x, gain, same, taps, gain_part, squares, *arrays, h1t, dx1)


def segment_tables(segments):
    padded = jnp.concatenate([jnp.full((TILE,), -1, jnp.int32), segments])
    seg_k = jnp.concatenate(
        [padded[:-TILE].reshape(-1, 1, TILE), padded[TILE:].reshape(-1, 1, TILE)], axis=2
    )
    same = [
        jnp.concatenate(
            [jnp.zeros((m,), jnp.float32), (segments[m:] == segments[:-m]).astype(jnp.float32)]
        )
        for m in range(1, CONV)
    ]
    return segments[:, None], seg_k, jnp.stack(same, axis=1)


def pack(*weights):
    main = weights[0].shape[1] // LANES * LANES
    return jnp.concatenate([w[:, :main] for w in weights] + [w[:, main:] for w in weights], axis=1)


def unpack(packed, count):
    width = packed.shape[1] // count
    main = width // LANES * LANES
    tail = width - main
    return [
        jnp.concatenate(
            [
                packed[:, n * main : (n + 1) * main],
                packed[:, count * main + n * tail : count * main + (n + 1) * tail],
            ],
            axis=1,
        )
        for n in range(count)
    ]


def on_rings(
    block_input,
    cotangent,
    teacher,
    segments,
    valid_mask,
    query_weight,
    key_weight,
    value_weight,
    mixgate_weight,
    output_weight,
    conv_weight,
    gain_mixer,
    gain_feed,
    gate_weight,
    up_weight,
    down_weight,
):
    local = query_weight.shape[1]
    taps = lax.dynamic_slice_in_dim(conv_weight, lax.axis_index("tensor") * local, local, 1)
    seg_q, seg_k, same = segment_tables(segments)
    valid = valid_mask.astype(jnp.float32)
    mix_own = pack(query_weight, key_weight, value_weight, mixgate_weight)
    feed_own = pack(gate_weight, up_weight)
    gain_one, gain_two = gain_mixer[None], gain_feed[None]
    mix, last, feed, h1t, q, k_pad, v_pad, u, p, o, x1, h2, count = mixer_forward(
        block_input, valid.reshape(-1, LANES), gain_one, gain_two, seg_q, seg_k, same, taps,
        mix_own, output_weight.T, feed_own,
    )
    down, slopes, active, outputs, dy, dyb, dybt, h2t, squares = feed_forward(
        valid[:, None], count, h2, feed, x1, cotangent, teacher, down_weight.T
    )
    down_grad, gate_main, gain_part, dx1, dx1t, do, slopes_up = feed_backward(
        gain_two, dyb, dybt, h2t, down, feed, active, slopes, last, x1, dy
    )
    out_grad, up_rest, mix_grad, input_grad, small, conv = mixer_backward(
        block_input, gain_one, same, taps, gain_part, squares, dx1t, o, h2t, slopes_up, q, k_pad, v_pad,
        u, p, do, mix, h1t, dx1,
    )
    main = gate_main.shape[1]
    tail = gate_weight.shape[1] - main
    gate_grad = jnp.concatenate([gate_main, up_rest[:, main : main + tail]], axis=1)
    up_grad = jnp.concatenate([up_rest[:, :main], up_rest[:, main + tail :]], axis=1)
    mean_loss = jnp.sum(small[2]) / (count[0, 0] * D)
    return (
        mean_loss,
        outputs,
        input_grad,
        *unpack(mix_grad, 4),
        out_grad.T,
        conv[:, :CONV].transpose(1, 0, 2).reshape(CONV, -1),
        small[0],
        small[1],
        gate_grad,
        up_grad,
        down_grad.T,
    )


def on_any_mesh(
    block_input,
    cotangent,
    teacher,
    segments,
    valid_mask,
    query_weight,
    key_weight,
    value_weight,
    mixgate_weight,
    output_weight,
    conv_weight,
    gain_mixer,
    gain_feed,
    gate_weight,
    up_weight,
    down_weight,
):
    rows = block_input.shape[0]
    valid_rows = valid_mask.astype(jnp.float32)
    valid_total = sum_all(jnp.full((8, 128), jnp.sum(valid_rows), jnp.float32))[0, 0]
    local_width = query_weight.shape[1]
    local_hidden = gate_weight.shape[1]
    mixer_own = jnp.concatenate(
        [query_weight, key_weight, value_weight, mixgate_weight, output_weight.T], axis=1
    )
    feed_own = jnp.concatenate([gate_weight, up_weight], axis=1)
    mixer_all = gather_dp(mixer_own).reshape(D, -1)
    feed_all = gather_dp(feed_own).reshape(D, -1)
    full_down = gather_dp(down_weight.T).reshape(D, -1)
    full_query, full_key, full_value, full_mixgate, full_output = jnp.split(mixer_all, 5, axis=1)
    full_gate, full_upward = jnp.split(feed_all, 2, axis=1)
    column = lax.axis_index("tensor") * local_width
    conv_local = lax.dynamic_slice_in_dim(conv_weight, column, local_width, 1)
    inputs = block_input.astype(jnp.float32)
    scale_one = rms_scale(inputs)
    normed_one = inputs * scale_one
    group_one = gather_tensor((normed_one * gain_mixer).astype(jnp.bfloat16))
    queries = jnp.dot(group_one, full_query, preferred_element_type=jnp.float32).astype(
        jnp.bfloat16
    )
    key_rows = jnp.dot(group_one, full_key, preferred_element_type=jnp.float32).astype(jnp.bfloat16)
    value_rows = jnp.dot(group_one, full_value, preferred_element_type=jnp.float32).astype(
        jnp.bfloat16
    )
    mix_gate = jnp.dot(group_one, full_mixgate, preferred_element_type=jnp.float32).astype(
        jnp.bfloat16
    )
    attended, log_totals = attend_forward(queries, key_rows, value_rows, segments)
    value_float = value_rows.astype(jnp.float32)
    convolved = jnp.zeros_like(value_float)
    for offset in range(CONV):
        convolved = convolved + conv_local[offset] * shift_down(value_float, segments, offset)
    gate_float = mix_gate.astype(jnp.float32)
    mixer_out = (attended + convolved * gate_float).astype(jnp.bfloat16)
    mixer_part = cols_inner(mixer_out, full_output)
    hidden = inputs + scatter_tensor(mixer_part)
    scale_two = rms_scale(hidden)
    normed_two = hidden * scale_two
    group_two = gather_tensor((normed_two * gain_feed).astype(jnp.bfloat16))
    gate_value = jnp.dot(group_two, full_gate, preferred_element_type=jnp.float32)
    up_value = jnp.dot(group_two, full_upward, preferred_element_type=jnp.float32)
    sigmoid_gate = jax.nn.sigmoid(gate_value)
    silu_gate = gate_value * sigmoid_gate
    active = (silu_gate * up_value).astype(jnp.bfloat16)
    feed_part = cols_inner(active, full_down)
    outputs = hidden + scatter_tensor(feed_part)
    target = teacher.astype(jnp.float32)
    deviation = outputs - target
    squares = jnp.sum(valid_rows[:, None] * deviation * deviation)
    all_tokens = rows * lax.axis_size("dp") * lax.axis_size("tensor")
    grad_out = cotangent + valid_rows[:, None] * deviation * (all_tokens / valid_total)
    grad_feed = gather_tensor(grad_out.astype(jnp.bfloat16))
    down_part = rows_inner(grad_feed, active)
    down_grad = scatter_dp(down_part.astype(jnp.bfloat16).reshape(-1, down_weight.shape[1], local_hidden)).T
    grad_active = jnp.dot(grad_feed, full_down, preferred_element_type=jnp.float32)
    silu_slope = sigmoid_gate * (1.0 + gate_value * (1.0 - sigmoid_gate))
    grad_gate = (grad_active * up_value * silu_slope).astype(jnp.bfloat16)
    grad_upward = (grad_active * silu_gate).astype(jnp.bfloat16)
    grad_normed_two = cols_inner(grad_gate, full_gate) + cols_inner(grad_upward, full_upward)
    grad_rows_two = scatter_tensor(grad_normed_two)
    gate_part = rows_inner(group_two, grad_gate)
    up_part = rows_inner(group_two, grad_upward)
    shard = gate_weight.shape[0]
    gate_grad = scatter_dp(gate_part.astype(jnp.bfloat16).reshape(-1, shard, local_hidden))
    up_grad = scatter_dp(up_part.astype(jnp.bfloat16).reshape(-1, shard, local_hidden))
    gainfeed_part = jnp.sum(grad_rows_two * normed_two, axis=0)
    scaled_two = grad_rows_two * gain_feed
    grad_hidden = grad_out + scale_two * (
        scaled_two - normed_two * jnp.mean(scaled_two * normed_two, axis=1, keepdims=True)
    )
    grad_mixer = gather_tensor(grad_hidden.astype(jnp.bfloat16))
    output_part = rows_inner(grad_mixer, mixer_out)
    output_grad = scatter_dp(output_part.astype(jnp.bfloat16).reshape(-1, shard, local_width)).T
    grad_mixed = jnp.dot(grad_mixer, full_output, preferred_element_type=jnp.float32).astype(jnp.bfloat16)
    grad_mixed_float = grad_mixed.astype(jnp.float32)
    grad_mixgate = (grad_mixed_float * convolved).astype(jnp.bfloat16)
    grad_conv_out = grad_mixed_float * gate_float
    conv_rows = []
    value_from_conv = jnp.zeros_like(value_float)
    for offset in range(CONV):
        conv_rows.append(jnp.sum(grad_conv_out * shift_down(value_float, segments, offset), axis=0))
        value_from_conv = value_from_conv + conv_local[offset] * shift_up(
            grad_conv_out, segments, offset
        )
    grad_queries, key_float, value_attn = attend_backward(
        queries, key_rows, value_rows, segments, log_totals, grad_mixed
    )
    grad_keys = key_float.astype(jnp.bfloat16)
    grad_values = (value_attn + value_from_conv).astype(jnp.bfloat16)

    def project_grad(grads):
        part = rows_inner(group_one, grads).astype(jnp.bfloat16)
        return scatter_dp(part.reshape(-1, shard, local_width))

    query_grad = project_grad(grad_queries)
    key_grad = project_grad(grad_keys)
    value_grad = project_grad(grad_values)
    mixgate_grad = project_grad(grad_mixgate)
    grad_normed_one = (
        cols_inner(grad_queries, full_query)
        + cols_inner(grad_keys, full_key)
        + cols_inner(grad_values, full_value)
        + cols_inner(grad_mixgate, full_mixgate)
    )
    grad_rows_one = scatter_tensor(grad_normed_one)
    gainmix_part = jnp.sum(grad_rows_one * normed_one, axis=0)
    scaled_one = grad_rows_one * gain_mixer
    input_grad = grad_hidden + scale_one * (
        scaled_one - normed_one * jnp.mean(scaled_one * normed_one, axis=1, keepdims=True)
    )
    conv_full = lax.dynamic_update_slice_in_dim(
        jnp.zeros((CONV, D), jnp.float32), jnp.stack(conv_rows), column, 1
    )
    small = sum_all(
        jnp.concatenate(
            [
                conv_full,
                gainmix_part[None],
                gainfeed_part[None],
                jnp.full((1, D), squares, jnp.float32),
            ]
        )
    )
    conv_grad, gainmix_grad, gainfeed_grad = small[:CONV], small[CONV], small[CONV + 1]
    mean_loss = small[CONV + 2, 0] / (valid_total * D)
    return (
        mean_loss,
        outputs,
        input_grad,
        query_grad,
        key_grad,
        value_grad,
        mixgate_grad,
        output_grad,
        conv_grad,
        gainmix_grad,
        gainfeed_grad,
        gate_grad,
        up_grad,
        down_grad,
    )


def solution(mesh):
    rings = mesh.shape["dp"] == 8 and mesh.shape["tensor"] == 4
    return jax.shard_map(
        on_rings if rings else on_any_mesh,
        mesh=mesh,
        in_specs=(
            P(("dp", "tensor"), None),
            P(("dp", "tensor"), None),
            P(("dp", "tensor"), None),
            P("dp"),
            P(("dp", "tensor")),
            P("dp", "tensor"),
            P("dp", "tensor"),
            P("dp", "tensor"),
            P("dp", "tensor"),
            P("tensor", "dp"),
            P(),
            P(),
            P(),
            P("dp", "tensor"),
            P("dp", "tensor"),
            P("tensor", "dp"),
        ),
        out_specs=(
            P(),
            P(("dp", "tensor"), None),
            P(("dp", "tensor"), None),
            P("dp", "tensor"),
            P("dp", "tensor"),
            P("dp", "tensor"),
            P("dp", "tensor"),
            P("tensor", "dp"),
            P(),
            P(),
            P(),
            P("dp", "tensor"),
            P("dp", "tensor"),
            P("tensor", "dp"),
        ),
        check_vma=False,
    )
```

```python
import jax
import jax.numpy as jnp
from jax import lax
from jax.experimental import pallas as pl
from jax.experimental.pallas import tpu as pltpu
from jax.sharding import PartitionSpec as P

D = 1792
HEAD_DIM = 64
WINDOW = 64
CONV = 3
BLOCK = 512
EPS = 1e-05
MESH = pl.DeviceIdType.MESH
VMEM_LIMIT = 63 * 2**20


def rms_scale(values):
    return lax.rsqrt(jnp.mean(values * values, axis=1, keepdims=True) + EPS)


def rows_inner(matrix_left, matrix_right):
    return lax.dot_general(
        matrix_left, matrix_right, (((0,), (0,)), ((), ())), preferred_element_type=jnp.float32
    )


def cols_inner(matrix_left, matrix_right):
    return lax.dot_general(
        matrix_left, matrix_right, (((1,), (1,)), ((), ())), preferred_element_type=jnp.float32
    )


def shift_down(values, segments, offset):
    if offset == 0:
        return values
    shifted = jnp.concatenate(
        [jnp.zeros((offset, values.shape[1]), values.dtype), values[: values.shape[0] - offset]],
        axis=0,
    )
    same_doc = jnp.concatenate(
        [jnp.zeros((offset,), bool), segments[offset:] == segments[:-offset]]
    )
    return jnp.where(same_doc[:, None], shifted, 0.0)


def shift_up(values, segments, offset):
    if offset == 0:
        return values
    shifted = jnp.concatenate(
        [values[offset:], jnp.zeros((offset, values.shape[1]), values.dtype)], axis=0
    )
    same_doc = jnp.concatenate(
        [segments[:-offset] == segments[offset:], jnp.zeros((offset,), bool)]
    )
    return jnp.where(same_doc[:, None], shifted, 0.0)


def pad_front(array, fill_value):
    front = jnp.full((WINDOW,) + array.shape[1:], fill_value, array.dtype)
    return jnp.concatenate([front, array], axis=0)


def block_setup(queries, key_pad, seg_pad, segments, row_start, head_count):
    score_scale = HEAD_DIM ** (-0.5)
    query_rows = lax.dynamic_slice_in_dim(queries, row_start, BLOCK, 0).reshape(
        BLOCK, head_count, HEAD_DIM
    )
    key_block = lax.dynamic_slice_in_dim(key_pad, row_start, BLOCK + WINDOW, 0).reshape(
        BLOCK + WINDOW, head_count, HEAD_DIM
    )
    seg_rows = lax.dynamic_slice_in_dim(segments, row_start, BLOCK, 0)
    seg_keys = lax.dynamic_slice_in_dim(seg_pad, row_start, BLOCK + WINDOW, 0)
    distance = (
        jnp.arange(BLOCK, dtype=jnp.int32)[:, None]
        + WINDOW
        - jnp.arange(BLOCK + WINDOW, dtype=jnp.int32)[None, :]
    )
    allowed = (distance >= 0) & (distance < WINDOW) & (seg_rows[:, None] == seg_keys[None, :])
    scores = (
        jnp.einsum("qhd,khd->hqk", query_rows, key_block, preferred_element_type=jnp.float32)
        * score_scale
    )
    return (query_rows, key_block, jnp.where(allowed[None], scores, -1e30))


def attend_forward(queries, key_rows, value_rows, segments):
    group_rows, local_width = queries.shape
    head_count = local_width // HEAD_DIM
    key_pad = pad_front(key_rows, 0)
    value_pad = pad_front(value_rows, 0)
    seg_pad = pad_front(segments, -1)

    def one_block(block_index):
        row_start = block_index * BLOCK
        query_rows, key_block, scores = block_setup(
            queries, key_pad, seg_pad, segments, row_start, head_count
        )
        row_max = jnp.max(scores, axis=-1, keepdims=True)
        exponent = jnp.exp(scores - row_max)
        row_total = jnp.sum(exponent, axis=-1, keepdims=True)
        attention = (exponent / row_total).astype(jnp.bfloat16)
        value_block = lax.dynamic_slice_in_dim(value_pad, row_start, BLOCK + WINDOW, 0).reshape(
            BLOCK + WINDOW, head_count, HEAD_DIM
        )
        mixed_rows = jnp.einsum(
            "hqk,khd->qhd", attention, value_block, preferred_element_type=jnp.float32
        )
        return (
            mixed_rows.reshape(BLOCK, local_width),
            row_max[..., 0] + jnp.log(row_total[..., 0]),
        )

    blocks_out, log_totals = lax.map(one_block, jnp.arange(group_rows // BLOCK, dtype=jnp.int32))
    return (blocks_out.reshape(group_rows, local_width), log_totals)


def attend_backward(queries, key_rows, value_rows, segments, log_totals, grad_mixed):
    group_rows, local_width = queries.shape
    head_count = local_width // HEAD_DIM
    score_scale = HEAD_DIM ** (-0.5)
    key_pad = pad_front(key_rows, 0)
    value_pad = pad_front(value_rows, 0)
    seg_pad = pad_front(segments, -1)

    def one_block(accumulated, block_pair):
        block_index, log_block = block_pair
        row_start = block_index * BLOCK
        query_rows, key_block, scores = block_setup(
            queries, key_pad, seg_pad, segments, row_start, head_count
        )
        attention = jnp.exp(scores - log_block[..., None])
        value_block = lax.dynamic_slice_in_dim(value_pad, row_start, BLOCK + WINDOW, 0).reshape(
            BLOCK + WINDOW, head_count, HEAD_DIM
        )
        grad_block = lax.dynamic_slice_in_dim(grad_mixed, row_start, BLOCK, 0).reshape(
            BLOCK, head_count, HEAD_DIM
        )
        grad_attention = jnp.einsum(
            "qhd,khd->hqk", grad_block, value_block, preferred_element_type=jnp.float32
        )
        row_inner = jnp.sum(attention * grad_attention, axis=-1, keepdims=True)
        grad_scores = (attention * (grad_attention - row_inner)).astype(jnp.bfloat16)
        grad_query = (
            jnp.einsum("hqk,khd->qhd", grad_scores, key_block, preferred_element_type=jnp.float32)
            * score_scale
        )
        grad_key = (
            jnp.einsum("hqk,qhd->khd", grad_scores, query_rows, preferred_element_type=jnp.float32)
            * score_scale
        )
        grad_value = jnp.einsum(
            "hqk,qhd->khd",
            attention.astype(jnp.bfloat16),
            grad_block,
            preferred_element_type=jnp.float32,
        )
        key_acc, value_acc = accumulated
        key_acc = lax.dynamic_update_slice_in_dim(
            key_acc,
            lax.dynamic_slice_in_dim(key_acc, row_start, BLOCK + WINDOW, 0)
            + grad_key.reshape(BLOCK + WINDOW, local_width),
            row_start,
            0,
        )
        value_acc = lax.dynamic_update_slice_in_dim(
            value_acc,
            lax.dynamic_slice_in_dim(value_acc, row_start, BLOCK + WINDOW, 0)
            + grad_value.reshape(BLOCK + WINDOW, local_width),
            row_start,
            0,
        )
        return ((key_acc, value_acc), grad_query.astype(jnp.bfloat16).reshape(BLOCK, local_width))

    zeros_pad = jnp.zeros((group_rows + WINDOW, local_width), jnp.float32)
    block_ids = jnp.arange(group_rows // BLOCK, dtype=jnp.int32)
    (key_acc, value_acc), query_blocks = lax.scan(
        one_block, (zeros_pad, zeros_pad), (block_ids, log_totals)
    )
    return (query_blocks.reshape(group_rows, local_width), key_acc[WINDOW:], value_acc[WINDOW:])


def pairs_xor(size, mask):
    return [(i, i ^ mask) for i in range(size)]


def pairs_shift(size, step):
    return [(i, (i + step) % size) for i in range(size)]


def put(buffer, block, index):
    return lax.dynamic_update_slice_in_dim(buffer, block[None], index, 0)


def pick(blocks, index):
    return lax.dynamic_index_in_dim(blocks, index, 0, keepdims=False)


def gather_dp(own):
    size = lax.axis_size("dp")
    if size != 8:
        return lax.all_gather(own, "dp", axis=0)
    me = lax.axis_index("dp")
    over_y = pairs_xor(size, 1)
    up, down = pairs_shift(size, 2), pairs_shift(size, -2)
    mate = lax.ppermute(own, "dp", over_y)
    own_below = lax.ppermute(own, "dp", up)
    own_above = lax.ppermute(own, "dp", down)
    mate_below = lax.ppermute(mate, "dp", up)
    mate_above = lax.ppermute(mate, "dp", down)
    own_far = lax.ppermute(own_below, "dp", up)
    mate_far = lax.ppermute(mate_above, "dp", down)
    below, above, far = (me + 6) % size, (me + 2) % size, (me + 4) % size
    full = jnp.zeros((size,) + own.shape, own.dtype)
    for block, index in (
        (own, me),
        (mate, me ^ 1),
        (own_below, below),
        (own_above, above),
        (mate_below, below ^ 1),
        (mate_above, above ^ 1),
        (own_far, far),
        (mate_far, far ^ 1),
    ):
        full = put(full, block, index)
    return full


def scatter_dp(parts):
    size = lax.axis_size("dp")
    if size != 8:
        return lax.psum_scatter(parts, "dp", scatter_dimension=0).astype(jnp.float32)
    me = lax.axis_index("dp")
    over_y = pairs_xor(size, 1)
    up, down = pairs_shift(size, 2), pairs_shift(size, -2)
    below, above, far = (me + 6) % size, (me + 2) % size, (me + 4) % size

    def part(index):
        return pick(parts, index).astype(jnp.float32)

    low = jnp.bfloat16
    own_first = lax.ppermute(pick(parts, far), "dp", up)
    mate_first = lax.ppermute(pick(parts, far ^ 1), "dp", down)
    mate_from_below = lax.ppermute(pick(parts, above ^ 1), "dp", up)
    own_from_above = lax.ppermute(pick(parts, below), "dp", down)
    mate_from_above = lax.ppermute(
        (part(below ^ 1) + mate_first.astype(jnp.float32)).astype(low), "dp", down
    )
    own_from_below = lax.ppermute(
        (part(above) + own_first.astype(jnp.float32)).astype(low), "dp", up
    )
    mate_sum = (
        part(me ^ 1)
        + mate_from_below.astype(jnp.float32)
        + mate_from_above.astype(jnp.float32)
    )
    from_mate = lax.ppermute(mate_sum.astype(low), "dp", over_y)
    own_sum = part(me) + own_from_below.astype(jnp.float32) + own_from_above.astype(jnp.float32)
    return own_sum + from_mate.astype(jnp.float32)


def gather_tensor(own):
    size = lax.axis_size("tensor")
    if size != 4:
        return lax.all_gather(own, "tensor", axis=0, tiled=True)
    me = lax.axis_index("tensor")
    across = lax.ppermute(own, "tensor", pairs_xor(size, 2))
    beside = lax.ppermute(own, "tensor", pairs_xor(size, 1))
    beside_across = lax.ppermute(across, "tensor", pairs_xor(size, 1))
    full = jnp.zeros((size,) + own.shape, own.dtype)
    for block, index in ((own, me), (beside, me ^ 1), (across, me ^ 2), (beside_across, me ^ 3)):
        full = put(full, block, index)
    return full.reshape(size * own.shape[0], own.shape[1])


def scatter_tensor(parts):
    size = lax.axis_size("tensor")
    if size != 4:
        return lax.psum_scatter(
            parts.astype(jnp.bfloat16), "tensor", scatter_dimension=0, tiled=True
        ).astype(jnp.float32)
    me = lax.axis_index("tensor")
    low = jnp.bfloat16
    parts = parts.reshape(size, -1, parts.shape[1])
    beside = lax.ppermute(pick(parts, me ^ 3).astype(low), "tensor", pairs_xor(size, 1))
    sent = (pick(parts, me ^ 2).astype(jnp.float32) + beside.astype(jnp.float32)).astype(low)
    across = lax.ppermute(sent, "tensor", pairs_xor(size, 2))
    beside_own = lax.ppermute(pick(parts, me ^ 1).astype(low), "tensor", pairs_xor(size, 1))
    return (
        pick(parts, me).astype(jnp.float32)
        + beside_own.astype(jnp.float32)
        + across.astype(jnp.float32)
    )


def sum_all(values):
    dp_size, tensor_size = lax.axis_size("dp"), lax.axis_size("tensor")
    if dp_size != 8 or tensor_size != 4:
        return lax.psum(values, ("dp", "tensor"))
    for axis, size, mask in (
        ("tensor", tensor_size, 1),
        ("tensor", tensor_size, 2),
        ("dp", dp_size, 1),
        ("dp", dp_size, 2),
        ("dp", dp_size, 6),
    ):
        values = values + lax.ppermute(values, axis, pairs_xor(size, mask))
    return values


TILE = 64
LANES = 128


def neighbours():
    d, t = lax.axis_index("dp"), lax.axis_index("tensor")
    z, y = d // 2, lax.rem(d, 2)
    core = t + 1 - 2 * lax.rem(t, 2)
    place = z + y * (7 - 2 * z)

    def ring(offset):
        position = lax.rem(place + offset + 16, 8)
        side = position // 4
        return 2 * (position + side * (7 - 2 * position)) + side

    return dict(
        d=d,
        t=t,
        ring=ring,
        core=core,
        cross=lax.rem(t + 2, 4),
        cross_core=lax.rem(core + 2, 4),
        mate=d + 1 - 2 * y,
        z_pair=2 * (z + 1 - 2 * lax.rem(z, 2)) + y,
        z_mirror=2 * (3 - z) + y,
    )


def greet(at, everyone=False):
    d, t = at["d"], at["t"]
    devices = [(at["ring"](1), t), (at["ring"](-1), t), (d, at["core"]), (d, at["cross"])]
    if everyone:
        devices += [(at["mate"], t), (at["z_pair"], t), (at["z_mirror"], t)]
    barrier = pltpu.get_barrier_semaphore()
    for device in devices:
        pl.semaphore_signal(barrier, inc=1, device_id=device, device_id_type=MESH)
    pl.semaphore_wait(barrier, len(devices))


def remote(source, target, sems, index, device):
    return pltpu.make_async_remote_copy(
        src_ref=source,
        dst_ref=target,
        send_sem=sems[0].at[index],
        recv_sem=sems[1].at[index],
        device_id=device,
        device_id_type=MESH,
    )


def pieces_of(half, count):
    if count == 1:
        return [(0, half)]
    first = (half // 2 + 15) // 16 * 16
    return [(0, first), (first, half - first)]


class RingGather:
    def __init__(self, at, own, slot, sems, base, local_sem, count=2):
        half = own.shape[0] // 2
        ring, t = at["ring"], at["t"]
        self.local = pltpu.make_async_copy(own, slot(at["d"], 0, 2 * half), local_sem)
        self.sends, self.receives, self.at = [], [], 0
        for s in range(7):
            for k, (first, size) in enumerate(pieces_of(half, count)):
                sends, receives = [], []
                for way, sign in ((0, 1), (1, -1)):
                    to, row = (ring(sign), t), way * half + first
                    index = base + (s * count + k) * 2 + way
                    here = slot(ring(-sign * s), row, size)
                    there = slot(ring(-sign * (s + 1)), row, size)
                    source = own.at[pl.ds(row, size)] if s == 0 else here
                    sends.append(remote(source, here, sems, index, to))
                    receives.append(remote(there, there, sems, index, to))
                self.sends.append(sends)
                self.receives.append(receives)
        self.count = count

    def start(self):
        for copies in self.sends[: self.count]:
            for copy in copies:
                copy.start()
        self.local.start()

    def tick(self):
        if self.at < len(self.receives):
            for way in range(2):
                self.receives[self.at][way].wait_recv()
                if self.at + self.count < len(self.sends):
                    self.sends[self.at + self.count][way].start()
            self.at += 1

    def finish(self):
        while self.at < len(self.receives):
            self.tick()
        self.local.wait()

    def drain(self):
        for sends in self.sends:
            for copy in sends:
                copy.wait_send()


class RingScatter:
    def __init__(self, at, left, right, slots, term, out, sems, base, count=2):
        self.ring, self.left, self.right = at["ring"], left, right
        self.slots, self.term, self.out = slots, term, out
        self.half, self.columns = slots.shape[2], slots.shape[3]
        self.pieces = pieces_of(self.half, count)
        self.at = 0
        self.sends = []
        for s in range(7):
            for k, (first, size) in enumerate(self.pieces):
                rows = pl.ds(first, size)
                self.sends.append(
                    [
                        remote(
                            slots.at[way, s, rows], slots.at[way, s + 1, rows], sems,
                            base + (s * count + k) * 2 + way, (at["ring"](sign), at["t"]),
                        )
                        for way, sign in ((0, 1), (1, -1))
                    ]
                )

    def compute(self, away):
        half = self.half
        first = pl.multiple_of(self.ring(-away) * 2 * half, half)
        second = pl.multiple_of(self.ring(away) * 2 * half + half, half)
        width = 512
        whole = self.columns // width * width

        def block(lanes):
            left = jnp.concatenate(
                [self.left[pl.ds(first, half)], self.left[pl.ds(second, half)]], axis=0
            )
            self.term[:, lanes] = nn_dot(left, self.right[:, lanes])

        @pl.loop(0, whole // width)
        def _(i):
            block(pl.ds(pl.multiple_of(i * width, width), width))

        if whole < self.columns:
            block(pl.ds(whole, self.columns - whole))

    def start(self):
        self.compute(1)
        for k, (first, size) in enumerate(self.pieces):
            for way in range(2):
                self.slots[way, 0, pl.ds(first, size)] = self.term[
                    pl.ds(way * self.half + first, size)
                ].astype(jnp.bfloat16)
                self.sends[k][way].start()
        self.compute(2)

    def tick(self):
        if self.at == len(self.sends):
            return
        count = len(self.pieces)
        s, k = divmod(self.at, count)
        first, size = self.pieces[k]
        for way in range(2):
            here, rows = pl.ds(first, size), pl.ds(way * self.half + first, size)
            self.sends[self.at][way].wait_recv()
            total = self.slots[way, s + 1, here].astype(jnp.float32) + self.term[rows]
            if s < 6:
                self.slots[way, s + 1, here] = total.astype(jnp.bfloat16)
                self.sends[self.at + count][way].start()
            else:
                self.out[rows] = total
        self.at += 1
        if k == count - 1 and s < 6:
            self.compute(s + 3)

    def finish(self):
        while self.at < len(self.sends):
            self.tick()
        for sends in self.sends:
            for copy in sends:
                copy.wait_send()


class GatherTensor:
    def __init__(self, at, full, rows, sems, base):
        def block(index):
            return full.at[pl.ds(pl.multiple_of(index * rows, rows), rows)]

        mine, across = block(at["t"]), block(at["cross"])
        self.to_core = remote(mine, mine, sems, base, (at["d"], at["core"]))
        self.to_cross = remote(mine, mine, sems, base + 1, (at["d"], at["cross"]))
        self.relay_core = remote(across, across, sems, base + 2, (at["d"], at["core"]))
        places = (block(at["core"]), across, block(at["cross_core"]))
        self.receives = [
            remote(place, place, sems, base + k, (at["d"], at["core"]))
            for k, place in enumerate(places)
        ]

    def start(self):
        self.to_cross.start()
        self.to_core.start()

    def relay(self):
        self.receives[1].wait_recv()
        self.relay_core.start()

    def drain(self):
        for send in (self.to_core, self.to_cross, self.relay_core):
            send.wait_send()

    def finish(self):
        self.receives[0].wait_recv()
        self.receives[2].wait_recv()
        self.drain()


def sum_rows(at, block_part, send, receive, total, sems, base, idle=lambda point: None):
    to_core, to_cross = (at["d"], at["core"]), (at["d"], at["cross"])
    low = jnp.bfloat16
    first = remote(send.at[0], receive.at[0], sems, base, to_core)
    second = remote(send.at[1], receive.at[1], sems, base + 1, to_cross)
    third = remote(send.at[2], receive.at[2], sems, base + 2, to_core)
    send[0] = block_part(at["cross_core"]).astype(low)
    first.start()
    total[...] = block_part(at["cross"])
    first.wait_recv()
    send[1] = (total[...] + receive[0].astype(jnp.float32)).astype(low)
    second.start()
    idle(0)
    send[2] = block_part(at["core"]).astype(low)
    third.start()
    idle(1)
    total[...] = block_part(at["t"])
    third.wait_recv()
    total[...] += receive[2].astype(jnp.float32)
    idle(2)
    second.wait_recv()
    total[...] += receive[1].astype(jnp.float32)
    for copy in (first, second, third):
        copy.wait_send()


class SumAll:
    def __init__(self, at, value, received, sems, base):
        d, t = at["d"], at["t"]
        partners = ((d, at["core"]), (d, at["cross"]), (at["mate"], t), (at["z_pair"], t), (at["z_mirror"], t))
        self.value, self.received, self.s = value, received, 0
        self.copies = [
            remote(value.at[k], received.at[k], sems, base + k, partner)
            for k, partner in enumerate(partners)
        ]

    def start(self):
        self.copies[0].start()

    def step(self):
        s = self.s
        self.copies[s].wait_recv()
        self.value[s + 1] = self.value[s] + self.received[s]
        if s < 4:
            self.copies[s + 1].start()
        self.s += 1

    def finish(self):
        while self.s < 5:
            self.step()
        for copy in self.copies:
            copy.wait_send()


def nt_dot(left, right):
    return lax.dot_general(
        left, right, (((1,), (1,)), ((), ())), preferred_element_type=jnp.float32
    )


def nn_dot(left, right):
    return lax.dot_general(
        left, right, (((1,), (0,)), ((), ())), preferred_element_type=jnp.float32
    )


def tn_dot(left, right):
    return lax.dot_general(
        left, right, (((0,), (0,)), ((), ())), preferred_element_type=jnp.float32
    )


def head_groups(width):
    heads = width // HEAD_DIM
    return [(2 * HEAD_DIM * j, min(2, heads - 2 * j)) for j in range((heads + 1) // 2)]


def split_heads(tile, heads):
    if heads == 1:
        return tile
    lane = lax.broadcasted_iota(jnp.int32, tile.shape, 1)
    zero = jnp.zeros_like(tile)
    return jnp.concatenate(
        [jnp.where(lane < HEAD_DIM, tile, zero), jnp.where(lane < HEAD_DIM, zero, tile)], axis=0
    )


def join_heads(stacked, heads):
    if heads == 1:
        return stacked
    half = stacked.shape[0] // 2
    lane = lax.broadcasted_iota(jnp.int32, (half, stacked.shape[1]), 1)
    return jnp.where(lane < HEAD_DIM, stacked[:half], stacked[half:])


def convolve(window, taps, lanes, same_one, same_two):
    one = pltpu.roll(window, 1, axis=0)[TILE:] * same_one
    two = pltpu.roll(window, 2, axis=0)[TILE:] * same_two
    rows = (window[TILE:], one, two)
    return sum(taps[m : m + 1, lanes] * rows[m] for m in range(CONV)), rows


def attend_tile(i, q, k_pad, v_pad, u, seg_q, seg_k, same, taps, p_out, o):
    row = pl.multiple_of(i * TILE, TILE)
    at_row, at_window = pl.ds(row, TILE), pl.ds(row, 2 * TILE)
    distance = (
        lax.broadcasted_iota(jnp.int32, (TILE, 2 * TILE), 0)
        + TILE
        - lax.broadcasted_iota(jnp.int32, (TILE, 2 * TILE), 1)
    )
    allowed = (seg_q[at_row] == seg_k[i]) & (distance >= 0) & (distance < WINDOW)
    same_one, same_two = same[at_row, 0:1], same[at_row, 1:2]
    for lane, heads in head_groups(q.shape[1]):
        lanes = pl.ds(lane, heads * HEAD_DIM)
        values = v_pad[at_window, lanes]
        allow = jnp.concatenate([allowed] * heads, axis=0) if heads > 1 else allowed
        scores = nt_dot(split_heads(q[at_row, lanes], heads), k_pad[at_window, lanes])
        scores = jnp.where(allow, scores * (HEAD_DIM**-0.5), -1e30)
        exponent = jnp.exp(scores - jnp.max(scores, axis=1, keepdims=True))
        chance = exponent * (1.0 / jnp.sum(exponent, axis=1, keepdims=True))
        chance = chance.astype(jnp.bfloat16)
        p_out[i, pl.ds((lane // HEAD_DIM) * TILE, heads * TILE), :] = chance
        mixed = join_heads(nn_dot(chance, values), heads)
        convolved, _ = convolve(values.astype(jnp.float32), taps, lanes, same_one, same_two)
        o[at_row, lanes] = (mixed + convolved * u[at_row, lanes].astype(jnp.float32)).astype(
            jnp.bfloat16
        )


def attend_back_tile(
    i, q, k_pad, v_pad, u, p, same, taps, do, dk, dv, conv_sum
):
    row = pl.multiple_of(i * TILE, TILE)
    at_row, at_window = pl.ds(row, TILE), pl.ds(row, 2 * TILE)
    same_one, same_two = same[at_row, 0:1], same[at_row, 1:2]
    for lane, heads in head_groups(q.shape[1]):
        lanes = pl.ds(lane, heads * HEAD_DIM)
        keys, values = k_pad[at_window, lanes], v_pad[at_window, lanes]
        grad = do[at_row, lanes]
        grad_heads = split_heads(grad, heads)
        chance_low = p[i, pl.ds((lane // HEAD_DIM) * TILE, heads * TILE), :]
        chance = chance_low.astype(jnp.float32)
        weighted = chance * nt_dot(grad_heads, values)
        slope = weighted - chance * jnp.sum(weighted, axis=1, keepdims=True)
        slope = (slope * (HEAD_DIM**-0.5)).astype(jnp.bfloat16)
        dk[at_window, lanes] += tn_dot(slope, split_heads(q[at_row, lanes], heads))
        q[at_row, lanes] = join_heads(nn_dot(slope, keys), heads).astype(jnp.bfloat16)
        convolved, rows = convolve(values.astype(jnp.float32), taps, lanes, same_one, same_two)
        grad = grad.astype(jnp.float32)
        do[at_row, lanes] = (grad * convolved).astype(jnp.bfloat16)
        grad_conv = grad * u[at_row, lanes].astype(jnp.float32)
        back = tn_dot(chance_low, grad_heads)
        zero = jnp.zeros_like(grad_conv)
        for m, same_m in enumerate((None, same_one, same_two)):
            conv_sum[m : m + 1, lanes] += jnp.sum(grad_conv * rows[m], axis=0, keepdims=True)
            term = taps[m : m + 1, lanes] * grad_conv
            term = term if m == 0 else term * same_m
            term = jnp.concatenate([zero, term], axis=0)
            back = back + (term if m == 0 else pltpu.roll(term, 2 * TILE - m, axis=0))
        dv[at_window, lanes] += back


def rolled(values, offset):
    turned = pltpu.roll(values, offset, axis=1)
    lane = lax.broadcasted_iota(jnp.int32, values.shape, 1)
    return jnp.where(lane < offset, pltpu.roll(turned, 1, axis=0), turned)


def make_tables(segments, seg_q, seg_k, same):
    values = segments[...]
    row = lax.broadcasted_iota(jnp.int32, values.shape, 0)
    lane = lax.broadcasted_iota(jnp.int32, values.shape, 1)
    columns = values.T
    matches = [
        jnp.where((values == rolled(values, m)) & ((row > 0) | (lane >= m)), 1.0, 0.0).astype(jnp.float32).T
        for m in range(1, CONV)
    ]
    crossing = rolled(values, TILE)
    crossing = jnp.where((row == 0) & (lane < TILE), -1, crossing)
    for n in range(values.shape[0]):
        rows = pl.ds(n * LANES, LANES)
        seg_q[rows] = columns[:, n : n + 1]
        for m, match in enumerate(matches):
            same[rows, m : m + 1] = match[:, n : n + 1]
        seg_k[2 * n] = crossing[n : n + 1]
        seg_k[2 * n + 1] = values[n : n + 1]


def norm_rows(values, gain):
    scale = lax.rsqrt(jnp.mean(values * values, axis=1, keepdims=True) + EPS)
    return (values * scale * gain).astype(jnp.bfloat16)


def norm_back(values, grad, gain):
    scale = lax.rsqrt(jnp.mean(values * values, axis=1, keepdims=True) + EPS)
    normed = values * scale
    scaled = grad * gain
    through = scale * (scaled - normed * jnp.mean(scaled * normed, axis=1, keepdims=True))
    return through, jnp.sum(grad * normed, axis=0, keepdims=True)


def chunks_of(rows, size=64):
    def run(body):
        @pl.loop(0, rows // size)
        def _(i):
            body(pl.multiple_of(i * size, size), size)

    return run


def forward_kernel(
    x, valid_lanes, gains, segments, taps,
    mix_own, out_own, feed_own, down_own, cotangent_in, teacher_in,
    mix_out, last_out, feed_out, down_out, h1t_out, h2t_out, dybt_out, q_out, k_out, v_out, u_out, p_out,
    o_out, x1_out, dyb_out, slopes_out, active_out, act_out, dy_out, count_out, squares_out, same,
    valid, seg_q, seg_k, mix, last, feed, down, h1, turned, h2, q, k_pad, v_pad, u, p, o, slopes, active, x1, side, teacher,
    send, receive, total, count, count_in,
    send_sems, recv_sems, local_sems, load_sems, out_sems,
):
    at = neighbours()
    sems = (send_sems, recv_sems)
    rows, shard = x.shape[0], mix_own.shape[0]
    low = jnp.bfloat16
    greet(at, everyone=True)

    def slot_of(full):
        return lambda i, first, size: full.at[pl.ds(pl.multiple_of(i * shard + first, 16), size)]

    mix_ring = RingGather(at, mix_own, slot_of(mix), sems, 0, local_sems.at[0])
    last_ring = RingGather(at, out_own, slot_of(last), sems, 28, local_sems.at[1], count=1)
    feed_ring = RingGather(at, feed_own, slot_of(feed), sems, 42, local_sems.at[2])
    down_ring = RingGather(at, down_own, slot_of(down), sems, 70, local_sems.at[3])
    dyb = h1
    group_one = GatherTensor(at, h1, rows, sems, 98)
    group_two = GatherTensor(at, h2, rows, sems, 101)
    group_back = GatherTensor(at, dyb, rows, sems, 104)
    counting = SumAll(at, count, count_in, sems, 113)
    local = q.shape[1]
    main = local // LANES * LANES
    tail = local - main
    keeps = []

    def keep(source, target):
        copy = pltpu.make_async_copy(source, target, out_sems.at[len(keeps)])
        copy.start()
        keeps.append(copy)
        return copy

    def tick():
        last_ring.tick()
        if feed_ring.at < len(feed_ring.receives):
            feed_ring.tick()
            if feed_ring.at == len(feed_ring.receives) - 2:
                down_ring.start()
        else:
            down_ring.tick()

    def turn(source, block):
        here = pl.ds(pl.multiple_of(block * rows, rows), rows)
        turned[:, here] = source[here].T

    mix_ring.start()

    @chunks_of(rows)
    def _(row, size):
        h1[pl.ds(pl.multiple_of(at["t"] * rows + row, size), size)] = norm_rows(
            x[pl.ds(row, size)].astype(jnp.float32), gains[0:1]
        )

    group_one.start()
    flags = valid_lanes[...].astype(jnp.float32)
    count[0] = jnp.full(count.shape[1:], jnp.sum(flags), jnp.float32)
    counting.start()
    load_teacher = pltpu.make_async_copy(teacher_in, teacher, load_sems.at[0])
    load_cotangent = pltpu.make_async_copy(cotangent_in, side, load_sems.at[1])
    load_teacher.start()
    load_cotangent.start()
    k_pad[pl.ds(0, TILE)] = jnp.zeros((TILE, local), k_pad.dtype)
    v_pad[pl.ds(0, TILE)] = jnp.zeros((TILE, local), v_pad.dtype)
    make_tables(segments, seg_q, seg_k, same)
    spare = jnp.zeros((8 - flags.shape[0], LANES), jnp.float32)
    columns = jnp.concatenate([flags, spare], axis=0).T
    for n in range(flags.shape[0]):
        valid[pl.ds(n * LANES, LANES)] = columns[:, n : n + 1]
    mix_ring.tick()
    mix_ring.tick()
    counting.step()
    mix_ring.tick()
    mix_ring.tick()
    counting.step()
    mix_ring.tick()
    group_one.relay()
    mix_ring.tick()
    counting.step()
    mix_ring.tick()
    mix_ring.tick()
    counting.step()
    group_one.finish()
    mix_ring.tick()

    @pl.loop(0, 4)
    def _(j):
        turn(h1, j)

    keep_h1t = keep(turned, h1t_out)
    mix_ring.tick()
    counting.finish()
    keep(count.at[5], count_out)
    last_ring.start()
    mix_ring.tick()
    mix_ring.tick()
    last_ring.tick()
    feed_ring.start()
    mix_ring.tick()
    last_ring.tick()
    mix_ring.finish()
    last_ring.tick()
    keep(mix, mix_out)

    def project(j):
        here = pl.ds(pl.multiple_of(j * rows, rows), rows)
        there = pl.ds(pl.multiple_of(j * rows + TILE, TILE), rows)
        left = h1[here]
        pair = nn_dot(left, mix[:, pl.ds(0, 2 * main)]).astype(low)
        q[here, pl.ds(0, main)] = pair[:, :main]
        k_pad[there, pl.ds(0, main)] = pair[:, main:]
        pair = nn_dot(left, mix[:, pl.ds(2 * main, 2 * main)]).astype(low)
        v_pad[there, pl.ds(0, main)] = pair[:, :main]
        u[here, pl.ds(0, main)] = pair[:, main:]
        ends = nn_dot(left, mix[:, pl.ds(4 * main, 4 * tail)])
        q[here, pl.ds(main, tail)] = ends[:, :tail].astype(low)
        k_pad[there, pl.ds(main, tail)] = ends[:, tail : 2 * tail].astype(low)
        v_pad[there, pl.ds(main, tail)] = ends[:, 2 * tail : 3 * tail].astype(low)
        u[here, pl.ds(main, tail)] = ends[:, 3 * tail :].astype(low)

    def projects(first, last_block):
        @pl.loop(first, last_block)
        def _(j):
            project(j)

    projects(0, 2)
    tick()
    projects(2, 4)
    for source, target in ((q, q_out), (k_pad, k_out), (v_pad, v_out), (u, u_out)):
        keep(source, target)
    tick()
    tiles = q.shape[0] // TILE

    def attend(first, last_tile):
        @pl.loop(first, last_tile)
        def _(i):
            attend_tile(i, q, k_pad, v_pad, u, seg_q, seg_k, same, taps, p, o)

    for k in range(4):
        attend(k * tiles // 4, (k + 1) * tiles // 4)
        tick()
    last_ring.finish()
    keep(last, last_out)
    keep(p, p_out)
    keep(o, o_out)

    def mixed_part(block):
        return nt_dot(o[pl.ds(pl.multiple_of(block * rows, rows), rows)], last[...])

    def idle(point):
        tick()
        if point == 2:
            tick()

    sum_rows(at, mixed_part, send, receive, total, sems, 107, idle=idle)

    @chunks_of(rows)
    def _(row, size):
        here = pl.ds(row, size)
        hidden = total[here] + x[here].astype(jnp.float32)
        x1[here] = hidden
        h2[pl.ds(pl.multiple_of(at["t"] * rows + row, size), size)] = norm_rows(hidden, gains[1:2])

    group_two.start()
    keep(x1, x1_out)
    for _ in range(3):
        tick()
    group_two.relay()
    tick()
    group_two.finish()
    while feed_ring.at < len(feed_ring.receives):
        tick()
    feed_ring.finish()
    keep(feed, feed_out)
    width = active.shape[1]
    parts, cut = feed_lanes(width)
    rest = width - cut

    def widen(j):
        here = pl.ds(pl.multiple_of(j * rows, rows), rows)
        left = h2[here]
        for own, gate_lanes, up_lanes in parts:
            a, by_gate, by_up = gated(nn_dot(left, feed[:, gate_lanes]), nn_dot(left, feed[:, up_lanes]))
            active[here, own] = a.astype(low)
            slopes[here, gate_lanes] = by_gate.astype(low)
            slopes[here, up_lanes] = by_up.astype(low)
        both = nn_dot(left, feed[:, pl.ds(2 * cut, 2 * rest)])
        a, by_gate, by_up = gated(both[:, :rest], both[:, rest:])
        active[here, pl.ds(cut, rest)] = a.astype(low)
        slopes[here, pl.ds(2 * cut, 2 * rest)] = jnp.concatenate([by_gate, by_up], axis=1).astype(low)

    for k in range(4):

        @pl.loop(k, k + 1)
        def _(j):
            widen(j)

        tick()
    keep(active, active_out)
    keep(slopes, slopes_out)
    keep_h1t.wait()

    @pl.loop(0, 4)
    def _(j):
        turn(h2, j)

    keep_h2t = keep(turned, h2t_out)
    tick()
    down_ring.finish()
    keep(down, down_out)
    load_teacher.wait()
    load_cotangent.wait()

    def fed_part(block):
        return nt_dot(active[pl.ds(pl.multiple_of(block * rows, rows), rows)], down[...])

    sum_rows(at, fed_part, send, receive, total, sems, 110)
    weight = (rows * 4 * 8) / count[5, 0:1, 0:1]
    squares_out[...] = jnp.zeros_like(squares_out)

    @chunks_of(rows, 32)
    def _(row, size):
        here = pl.ds(row, size)
        result = total[here] + x1[here]
        deviation = result - teacher[here].astype(jnp.float32)
        kept = valid[here, 0:1] * deviation
        total[here] = result
        squares_out[0:1] += jnp.sum(kept * deviation, axis=0, keepdims=True)
        grad = side[here] + kept * weight
        side[here] = grad
        dyb[pl.ds(pl.multiple_of(at["t"] * rows + row, size), size)] = grad.astype(low)

    group_back.start()
    keep(total, act_out)
    keep(side, dy_out)
    keep_h2t.wait()
    turn(dyb, at["t"])
    group_back.receives[0].wait_recv()
    turn(dyb, at["core"])
    group_back.relay()
    turn(dyb, at["cross"])
    group_back.receives[2].wait_recv()
    turn(dyb, at["cross_core"])
    group_back.drain()
    keep(dyb, dyb_out)
    keep(turned, dybt_out)
    for ring in (mix_ring, last_ring, feed_ring, down_ring):
        ring.drain()
    for copy in keeps:
        if copy is not keep_h1t and copy is not keep_h2t:
            copy.wait()


def specs():
    return pl.BlockSpec(memory_space=pltpu.VMEM), pl.BlockSpec(memory_space=pl.ANY)


def shape(*dims, kind=jnp.bfloat16):
    return jax.ShapeDtypeStruct(dims, kind)


def params(identity):
    return pltpu.CompilerParams(
        collective_id=identity, has_side_effects=True, vmem_limit_bytes=VMEM_LIMIT
    )


def dma(count):
    return pltpu.SemaphoreType.DMA((count,))


def forward(
    x, valid_lanes, gains, segments, taps, mix_own, out_own, feed_own, down_own, cotangent, teacher
):
    rows, width = x.shape
    shard, local = out_own.shape
    hidden = down_own.shape[1]
    everyone, depth = 4 * rows, 8 * shard
    low, wide = jnp.bfloat16, jnp.float32
    tiles, heads = everyone // TILE, local // HEAD_DIM
    vmem, hbm = specs()
    return pl.pallas_call(
        forward_kernel,
        out_shape=(
            shape(depth, 4 * local),
            shape(depth, local),
            shape(depth, 2 * hidden),
            shape(depth, hidden),
            shape(width, everyone),
            shape(width, everyone),
            shape(width, everyone),
            shape(everyone, local),
            shape(everyone + TILE, local),
            shape(everyone + TILE, local),
            shape(everyone, local),
            shape(tiles, heads * TILE, 2 * TILE),
            shape(everyone, local),
            shape(rows, width, kind=wide),
            shape(everyone, width),
            shape(everyone, 2 * hidden),
            shape(everyone, hidden),
            shape(rows, width, kind=wide),
            shape(rows, width, kind=wide),
            shape(8, LANES, kind=wide),
            shape(8, width, kind=wide),
            shape(everyone, CONV - 1, kind=wide),
        ),
        in_specs=[vmem] * 5 + [hbm] * 6,
        out_specs=(hbm,) * 20 + (vmem,) * 2,
        scratch_shapes=[
            pltpu.VMEM((rows, 1), wide),
            pltpu.VMEM((everyone, 1), jnp.int32),
            pltpu.VMEM((tiles, 1, 2 * TILE), jnp.int32),
            pltpu.VMEM((depth, 4 * local), low),
            pltpu.VMEM((depth, local), low),
            pltpu.VMEM((depth, 2 * hidden), low),
            pltpu.VMEM((depth, hidden), low),
            pltpu.VMEM((everyone, width), low),
            pltpu.VMEM((width, everyone), low),
            pltpu.VMEM((everyone, width), low),
            pltpu.VMEM((everyone, local), low),
            pltpu.VMEM((everyone + TILE, local), low),
            pltpu.VMEM((everyone + TILE, local), low),
            pltpu.VMEM((everyone, local), low),
            pltpu.VMEM((tiles, heads * TILE, 2 * TILE), low),
            pltpu.VMEM((everyone, local), low),
            pltpu.VMEM((everyone, 2 * hidden), low),
            pltpu.VMEM((everyone, hidden), low),
            pltpu.VMEM((rows, width), wide),
            pltpu.VMEM((rows, width), wide),
            pltpu.VMEM((rows, width), low),
            pltpu.VMEM((3, rows, width), low),
            pltpu.VMEM((3, rows, width), low),
            pltpu.VMEM((rows, width), wide),
            pltpu.VMEM((6, 8, LANES), wide),
            pltpu.VMEM((5, 8, LANES), wide),
            dma(118),
            dma(118),
            dma(4),
            dma(2),
            dma(20),
        ],
        compiler_params=params(1),
    )(
        x, valid_lanes, gains, segments, taps, mix_own, out_own, feed_own, down_own, cotangent, teacher
    )


def feed_lanes(hidden):
    main = hidden // LANES * LANES
    cut = main // 2 // LANES * LANES
    parts = [(0, cut), (cut, main - cut)]
    return [(pl.ds(a, n), pl.ds(a, n), pl.ds(main + a, n)) for a, n in parts], main


def gated(gate, up):
    sigmoid = jax.nn.sigmoid(gate)
    silu = gate * sigmoid
    return silu * up, up * sigmoid * (1.0 + gate * (1.0 - sigmoid)), silu


def feed_backward_kernel(
    gains, dyb_in, dybt_in, h2t_in, down_in, feed_in, active_in, slopes_in, last_in, x1_in, dy_in,
    down_grad, gate_grad, gain_part, dx1_out, dx1t_out, do_out, slopes_out,
    dyb, dybt, h2t, down, feed, active, slopes, last, do, side, total, down_slots, gate_slots,
    down_term, gate_term, send, receive,
    send_sems, recv_sems, load_sems, out_sems,
):
    at = neighbours()
    sems = (send_sems, recv_sems)
    rows = total.shape[0]
    low = jnp.bfloat16
    loads = [
        pltpu.make_async_copy(source, target, load_sems.at[n])
        for n, (source, target) in enumerate(
            (
                (dybt_in, dybt), (active_in, active), (dyb_in, dyb), (down_in, down), (slopes_in, slopes),
                (h2t_in, h2t), (feed_in, feed), (last_in, last), (x1_in, side), (dy_in, side),
            )
        )
    ]
    for load in loads[:2]:
        load.start()
    greet(at)
    hidden = active.shape[1]
    parts, main = feed_lanes(hidden)
    tail = hidden - main
    first = RingScatter(at, dybt, active, down_slots, down_term, down_grad, sems, 0)
    second = RingScatter(
        at, h2t, slopes.at[:, pl.ds(0, main)], gate_slots, gate_term, gate_grad, sems, 28
    )
    group = GatherTensor(at, dyb, rows, sems, 59)
    keeps = []

    def keep(source, target):
        copy = pltpu.make_async_copy(source, target, out_sems.at[len(keeps)])
        copy.start()
        keeps.append(copy)

    loads[0].wait()
    loads[1].wait()
    for load in loads[2:-1]:
        load.start()
    first.start()
    for load in loads[2:5]:
        load.wait()

    def slope_back(first_block, last_block):
        @pl.loop(first_block, last_block)
        def _(j):
            here = pl.ds(pl.multiple_of(j * rows, rows), rows)
            left = dyb[here]
            for own, gate_lanes, up_lanes in parts:
                da = nn_dot(left, down[:, own])
                slopes[here, gate_lanes] = (da * slopes[here, gate_lanes].astype(jnp.float32)).astype(low)
                slopes[here, up_lanes] = (da * slopes[here, up_lanes].astype(jnp.float32)).astype(low)
            da = nn_dot(left, down[:, pl.ds(main, tail)])
            ends = pl.ds(2 * main, 2 * tail)
            both = jnp.concatenate([da, da], axis=1) * slopes[here, ends].astype(jnp.float32)
            slopes[here, ends] = both.astype(low)

    for k in range(4):
        slope_back(k, k + 1)
        first.tick()
    keep(slopes.at[:, pl.ds(main, 2 * hidden - main)], slopes_out)
    loads[5].wait()
    second.start()
    loads[6].wait()
    loads[8].wait()

    def part(block):
        return nt_dot(slopes[pl.ds(pl.multiple_of(block * rows, rows), rows)], feed[...])

    def idle(point):
        first.tick()
        second.tick()
        if point == 2:
            first.tick()
            second.tick()

    sum_rows(at, part, send, receive, total, sems, 56, idle=idle)
    gain_part[...] = jnp.zeros_like(gain_part)

    @chunks_of(rows, 32)
    def _(row, size):
        here = pl.ds(row, size)
        through, term_gain = norm_back(side[here], total[here], gains[1:2])
        gain_part[0:1] += term_gain
        total[here] = through

    loads[9].start()
    first.tick()
    second.tick()
    loads[9].wait()

    @chunks_of(rows, 32)
    def _(row, size):
        here = pl.ds(row, size)
        grad = total[here] + side[here]
        total[here] = grad
        dyb[pl.ds(pl.multiple_of(at["t"] * rows + row, size), size)] = grad.astype(low)

    group.start()
    keep(total, dx1_out)
    loads[7].wait()

    def spread(block):
        here = pl.ds(pl.multiple_of(block * rows, rows), rows)
        dybt[:, here] = dyb[here].T
        do[here] = nn_dot(dyb[here], last[...]).astype(low)

    while first.at < len(first.sends):
        first.tick()
        second.tick()
    spread(at["t"])
    second.tick()
    group.receives[0].wait_recv()
    spread(at["core"])
    second.tick()
    group.relay()
    second.tick()
    spread(at["cross"])
    group.receives[2].wait_recv()
    spread(at["cross_core"])
    group.drain()
    keep(dybt, dx1t_out)
    keep(do, do_out)
    second.finish()
    first.finish()
    for copy in keeps:
        copy.wait()


def feed_backward(gains, dyb, dybt, h2t, down, feed, active, slopes, last, x1, dy):
    rows, width = x1.shape
    depth, hidden = down.shape
    local = last.shape[1]
    main = hidden // LANES * LANES
    everyone, shard = 4 * rows, depth // 8
    low, wide = jnp.bfloat16, jnp.float32
    vmem, hbm = specs()
    return pl.pallas_call(
        feed_backward_kernel,
        out_shape=(
            shape(shard, hidden, kind=wide),
            shape(shard, main, kind=wide),
            shape(8, width, kind=wide),
            shape(rows, width, kind=wide),
            shape(width, everyone),
            shape(everyone, local),
            shape(everyone, 2 * hidden - main),
        ),
        in_specs=[vmem] + [hbm] * 10,
        out_specs=(vmem,) * 3 + (hbm,) * 4,
        scratch_shapes=[
            pltpu.VMEM((everyone, width), low),
            pltpu.VMEM((width, everyone), low),
            pltpu.VMEM((width, everyone), low),
            pltpu.VMEM((depth, hidden), low),
            pltpu.VMEM((depth, 2 * hidden), low),
            pltpu.VMEM((everyone, hidden), low),
            pltpu.VMEM((everyone, 2 * hidden), low),
            pltpu.VMEM((depth, local), low),
            pltpu.VMEM((everyone, local), low),
            pltpu.VMEM((rows, width), wide),
            pltpu.VMEM((rows, width), wide),
            pltpu.VMEM((2, 8, shard // 2, hidden), low),
            pltpu.VMEM((2, 8, shard // 2, main), low),
            pltpu.VMEM((shard, hidden), wide),
            pltpu.VMEM((shard, main), wide),
            pltpu.VMEM((3, rows, width), low),
            pltpu.VMEM((3, rows, width), low),
            dma(62),
            dma(62),
            dma(10),
            dma(4),
        ],
        compiler_params=params(3),
    )(gains, dyb, dybt, h2t, down, feed, active, slopes, last, x1, dy)


def mixer_backward_kernel(
    x, gains, same, taps, gain_part, squares,
    dx1t_in, o_in, h2t_in, slopes_in, q_in, k_in, v_in, u_in, p_in, do_in, mix_in, h1t_in, dx1_in,
    out_grad, up_grad, mix_grad, input_grad, small_out, conv_out,
    turned, o, h2t, slopes, q, k_pad, v_pad, u, p, do, mix,
    dk, dv, grads, out_slots, up_slots, mix_slots, out_term, up_term, mix_term, send, receive, total,
    small, small_in, conv, conv_in,
    send_sems, recv_sems, load_sems,
):
    at = neighbours()
    sems = (send_sems, recv_sems)
    rows = total.shape[0]
    low = jnp.bfloat16
    loads = [
        pltpu.make_async_copy(source, target, load_sems.at[n])
        for n, (source, target) in enumerate(
            (
                (dx1t_in, turned), (o_in, o), (h2t_in, h2t), (slopes_in, slopes), (q_in, q), (k_in, k_pad),
                (v_in, v_pad), (u_in, u), (p_in, p), (do_in, do), (mix_in, mix), (dx1_in, input_grad),
                (h1t_in, turned),
            )
        )
    ]
    for load in loads[:4]:
        load.start()
    greet(at, everyone=True)
    local = q.shape[1]
    main = local // LANES * LANES
    tail = local - main
    first = RingScatter(at, turned, o, out_slots, out_term, out_grad, sems, 0, count=1)
    second = RingScatter(at, h2t, slopes, up_slots, up_term, up_grad, sems, 14)
    third = RingScatter(at, turned, grads, mix_slots, mix_term, mix_grad, sems, 42)
    small_sum = SumAll(at, small, small_in, sems, 73)
    conv_all = SumAll(at, conv, conv_in, sems, 78)
    loads[0].wait()
    loads[1].wait()
    first.start()
    loads[2].wait()
    loads[3].wait()
    for load in loads[4:-1]:
        load.start()
    second.start()
    dk[...] = jnp.zeros_like(dk)
    dv[...] = jnp.zeros_like(dv)
    conv[0] = jnp.zeros(conv.shape[1:], jnp.float32)
    first.tick()
    for load in loads[4:10]:
        load.wait()
    tiles = q.shape[0] // TILE
    conv_sum = conv.at[0, at["t"]]

    def attend(a, b):
        @pl.loop(a, b)
        def _(i):
            attend_back_tile(i, q, k_pad, v_pad, u, p, same, taps, do, dk, dv, conv_sum)

    for k in range(8):
        attend(k * tiles // 8, (k + 1) * tiles // 8)
        first.tick()
        second.tick()
    conv_all.start()

    first.finish()
    loads[12].start()
    second.tick()

    @chunks_of(q.shape[0])
    def _(row, size):
        here, there = pl.ds(row, size), pl.ds(pl.multiple_of(row + TILE, TILE), size)
        four = [q[here].astype(jnp.float32), dk[there], dv[there], do[here].astype(jnp.float32)]
        for n, value in enumerate(four):
            grads[here, pl.ds(n * main, main)] = value[:, :main].astype(low)
        ends = jnp.concatenate([value[:, main:] for value in four], axis=1)
        grads[here, pl.ds(4 * main, 4 * tail)] = ends.astype(low)

    second.tick()
    loads[12].wait()
    third.start()
    loads[10].wait()
    loads[11].wait()

    def part(block):
        return nt_dot(grads[pl.ds(pl.multiple_of(block * rows, rows), rows)], mix[...])

    def idle(point):
        second.tick()
        third.tick()
        if point == 2:
            second.tick()
            conv_all.step()

    sum_rows(at, part, send, receive, total, sems, 70, idle=idle)
    small[0, 0:1] = jnp.zeros((1, small.shape[2]), jnp.float32)
    small[0, 1:2] = gain_part[0:1]
    small[0, 2:3] = squares[0:1]
    small[0, 3:8] = jnp.zeros((5, small.shape[2]), jnp.float32)

    @chunks_of(rows, 32)
    def _(row, size):
        here = pl.ds(row, size)
        through, term_gain = norm_back(x[here].astype(jnp.float32), total[here], gains[0:1])
        small[0, 0:1] += term_gain
        input_grad[here] += through

    small_sum.start()
    for k in range(4):
        second.tick()
        third.tick()
        conv_all.step()
        second.tick()
        third.tick()
        small_sum.step()
    small_sum.finish()
    conv_all.finish()
    second.finish()
    third.finish()
    small_out[...] = small[5]
    conv_out[...] = conv[5]


def mixer_backward(
    x, gains, same, taps, gain_part, squares, dx1t, o, h2t, slopes, q, k_pad, v_pad, u, p, do, mix, h1t, dx1
):
    rows, width = x.shape
    everyone, local = o.shape
    shard, ups = width // 8, slopes.shape[1]
    low, wide = jnp.bfloat16, jnp.float32
    vmem, hbm = specs()
    arrays = (dx1t, o, h2t, slopes, q, k_pad, v_pad, u, p, do, mix)
    return pl.pallas_call(
        mixer_backward_kernel,
        out_shape=(
            shape(shard, local, kind=wide),
            shape(shard, ups, kind=wide),
            shape(shard, 4 * local, kind=wide),
            shape(rows, width, kind=wide),
            shape(8, width, kind=wide),
            shape(4, 8, local, kind=wide),
        ),
        in_specs=[vmem] * 6 + [hbm] * 13,
        out_specs=(vmem,) * 6,
        scratch_shapes=[pltpu.VMEM(array.shape, array.dtype) for array in arrays]
        + [
            pltpu.VMEM((everyone + TILE, local), wide),
            pltpu.VMEM((everyone + TILE, local), wide),
            pltpu.VMEM((everyone, 4 * local), low),
            pltpu.VMEM((2, 8, shard // 2, local), low),
            pltpu.VMEM((2, 8, shard // 2, ups), low),
            pltpu.VMEM((2, 8, shard // 2, 4 * local), low),
            pltpu.VMEM((shard, local), wide),
            pltpu.VMEM((shard, ups), wide),
            pltpu.VMEM((shard, 4 * local), wide),
            pltpu.VMEM((3, rows, width), low),
            pltpu.VMEM((3, rows, width), low),
            pltpu.VMEM((rows, width), wide),
            pltpu.VMEM((6, 8, width), wide),
            pltpu.VMEM((5, 8, width), wide),
            pltpu.VMEM((6, 4, 8, local), wide),
            pltpu.VMEM((5, 4, 8, local), wide),
            dma(83),
            dma(83),
            dma(13),
        ],
        compiler_params=params(4),
    )(x, gains, same, taps, gain_part, squares, *arrays, h1t, dx1)


def finish_kernel(
    count, down_grad, gate_main, up_rest, mix_grad, out_grad, small, conv, act_in, input_in,
    loss, act, input_grad, query, key, value, mixgate, output, conv_grad, gain_one, gain_two, gate, up, down,
):
    act[...] = act_in[...]
    input_grad[...] = input_in[...]
    local = query.shape[1]
    main = local // LANES * LANES
    tail = local - main
    for n, target in enumerate((query, key, value, mixgate)):
        target[:, pl.ds(0, main)] = mix_grad[:, pl.ds(n * main, main)]
        target[:, pl.ds(main, tail)] = mix_grad[:, pl.ds(4 * main, 4 * tail)][:, n * tail : (n + 1) * tail]
    cut = gate_main.shape[1]
    rest = gate.shape[1] - cut
    ends = up_rest[:, pl.ds(cut, 2 * rest)]
    gate[:, pl.ds(0, cut)] = gate_main[...]
    gate[:, pl.ds(cut, rest)] = ends[:, :rest]
    up[:, pl.ds(0, cut)] = up_rest[:, pl.ds(0, cut)]
    up[:, pl.ds(cut, rest)] = ends[:, rest:]
    output[...] = out_grad[...].T
    down[...] = down_grad[...].T
    conv_grad[...] = jnp.concatenate([conv[n, 0:CONV] for n in range(conv.shape[0])], axis=1)
    gain_one[...] = small[0]
    gain_two[...] = small[1]
    total = jnp.sum(small[2:3], axis=1, keepdims=True) / (count[0:1, 0:1] * D)
    loss[...] = jnp.broadcast_to(total, loss.shape)


def finish(count, down_grad, gate_main, up_rest, mix_grad, out_grad, small, conv, act, input_grad):
    vmem, _ = specs()
    wide = jnp.float32
    shard, hidden = down_grad.shape
    local, width = out_grad.shape[1], small.shape[1]
    square = shape(shard, local, kind=wide)
    broad = shape(shard, hidden, kind=wide)
    return pl.pallas_call(
        finish_kernel,
        out_shape=(
            shape(8, LANES, kind=wide),
            shape(*act.shape, kind=wide),
            shape(*input_grad.shape, kind=wide),
            square,
            square,
            square,
            square,
            shape(local, shard, kind=wide),
            shape(CONV, width, kind=wide),
            shape(width, kind=wide),
            shape(width, kind=wide),
            broad,
            broad,
            shape(hidden, shard, kind=wide),
        ),
        in_specs=[vmem] * 10,
        out_specs=(vmem,) * 14,
        compiler_params=pltpu.CompilerParams(vmem_limit_bytes=VMEM_LIMIT),
    )(count, down_grad, gate_main, up_rest, mix_grad, out_grad, small, conv, act, input_grad)


def pack(*weights):
    main = weights[0].shape[1] // LANES * LANES
    return jnp.concatenate([w[:, :main] for w in weights] + [w[:, main:] for w in weights], axis=1)


def on_rings(
    block_input,
    cotangent,
    teacher,
    segments,
    valid_mask,
    query_weight,
    key_weight,
    value_weight,
    mixgate_weight,
    output_weight,
    conv_weight,
    gain_mixer,
    gain_feed,
    gate_weight,
    up_weight,
    down_weight,
):
    local = query_weight.shape[1]
    taps = lax.dynamic_slice_in_dim(conv_weight, lax.axis_index("tensor") * local, local, 1)
    gains = jnp.stack([gain_mixer, gain_feed])
    (
        mix, last, feed, down, h1t, h2t, dybt, q, k_pad, v_pad, u, p, o, x1, dyb, slopes, active,
        outputs, dy, count, squares, same,
    ) = forward(
        block_input, valid_mask.reshape(-1, LANES), gains, segments.reshape(-1, LANES), taps,
        pack(query_weight, key_weight, value_weight, mixgate_weight), output_weight.T,
        pack(gate_weight, up_weight), down_weight.T, cotangent, teacher,
    )
    down_grad, gate_main, gain_part, dx1, dx1t, do, slopes_up = feed_backward(
        gains, dyb, dybt, h2t, down, feed, active, slopes, last, x1, dy
    )
    out_grad, up_rest, mix_grad, input_grad, small, conv = mixer_backward(
        block_input, gains, same, taps, gain_part, squares, dx1t, o, h2t, slopes_up, q, k_pad, v_pad,
        u, p, do, mix, h1t, dx1,
    )
    loss, *rest = finish(
        count, down_grad, gate_main, up_rest, mix_grad, out_grad, small, conv, outputs, input_grad
    )
    return (loss[0, 0], *rest)


def on_any_mesh(
    block_input,
    cotangent,
    teacher,
    segments,
    valid_mask,
    query_weight,
    key_weight,
    value_weight,
    mixgate_weight,
    output_weight,
    conv_weight,
    gain_mixer,
    gain_feed,
    gate_weight,
    up_weight,
    down_weight,
):
    rows = block_input.shape[0]
    valid_rows = valid_mask.astype(jnp.float32)
    valid_total = sum_all(jnp.full((8, 128), jnp.sum(valid_rows), jnp.float32))[0, 0]
    local_width = query_weight.shape[1]
    local_hidden = gate_weight.shape[1]
    mixer_own = jnp.concatenate(
        [query_weight, key_weight, value_weight, mixgate_weight, output_weight.T], axis=1
    )
    feed_own = jnp.concatenate([gate_weight, up_weight], axis=1)
    mixer_all = gather_dp(mixer_own).reshape(D, -1)
    feed_all = gather_dp(feed_own).reshape(D, -1)
    full_down = gather_dp(down_weight.T).reshape(D, -1)
    full_query, full_key, full_value, full_mixgate, full_output = jnp.split(mixer_all, 5, axis=1)
    full_gate, full_upward = jnp.split(feed_all, 2, axis=1)
    column = lax.axis_index("tensor") * local_width
    conv_local = lax.dynamic_slice_in_dim(conv_weight, column, local_width, 1)
    inputs = block_input.astype(jnp.float32)
    scale_one = rms_scale(inputs)
    normed_one = inputs * scale_one
    group_one = gather_tensor((normed_one * gain_mixer).astype(jnp.bfloat16))
    queries = jnp.dot(group_one, full_query, preferred_element_type=jnp.float32).astype(
        jnp.bfloat16
    )
    key_rows = jnp.dot(group_one, full_key, preferred_element_type=jnp.float32).astype(jnp.bfloat16)
    value_rows = jnp.dot(group_one, full_value, preferred_element_type=jnp.float32).astype(
        jnp.bfloat16
    )
    mix_gate = jnp.dot(group_one, full_mixgate, preferred_element_type=jnp.float32).astype(
        jnp.bfloat16
    )
    attended, log_totals = attend_forward(queries, key_rows, value_rows, segments)
    value_float = value_rows.astype(jnp.float32)
    convolved = jnp.zeros_like(value_float)
    for offset in range(CONV):
        convolved = convolved + conv_local[offset] * shift_down(value_float, segments, offset)
    gate_float = mix_gate.astype(jnp.float32)
    mixer_out = (attended + convolved * gate_float).astype(jnp.bfloat16)
    mixer_part = cols_inner(mixer_out, full_output)
    hidden = inputs + scatter_tensor(mixer_part)
    scale_two = rms_scale(hidden)
    normed_two = hidden * scale_two
    group_two = gather_tensor((normed_two * gain_feed).astype(jnp.bfloat16))
    gate_value = jnp.dot(group_two, full_gate, preferred_element_type=jnp.float32)
    up_value = jnp.dot(group_two, full_upward, preferred_element_type=jnp.float32)
    sigmoid_gate = jax.nn.sigmoid(gate_value)
    silu_gate = gate_value * sigmoid_gate
    active = (silu_gate * up_value).astype(jnp.bfloat16)
    feed_part = cols_inner(active, full_down)
    outputs = hidden + scatter_tensor(feed_part)
    target = teacher.astype(jnp.float32)
    deviation = outputs - target
    squares = jnp.sum(valid_rows[:, None] * deviation * deviation)
    all_tokens = rows * lax.axis_size("dp") * lax.axis_size("tensor")
    grad_out = cotangent + valid_rows[:, None] * deviation * (all_tokens / valid_total)
    grad_feed = gather_tensor(grad_out.astype(jnp.bfloat16))
    down_part = rows_inner(grad_feed, active)
    down_grad = scatter_dp(down_part.astype(jnp.bfloat16).reshape(-1, down_weight.shape[1], local_hidden)).T
    grad_active = jnp.dot(grad_feed, full_down, preferred_element_type=jnp.float32)
    silu_slope = sigmoid_gate * (1.0 + gate_value * (1.0 - sigmoid_gate))
    grad_gate = (grad_active * up_value * silu_slope).astype(jnp.bfloat16)
    grad_upward = (grad_active * silu_gate).astype(jnp.bfloat16)
    grad_normed_two = cols_inner(grad_gate, full_gate) + cols_inner(grad_upward, full_upward)
    grad_rows_two = scatter_tensor(grad_normed_two)
    gate_part = rows_inner(group_two, grad_gate)
    up_part = rows_inner(group_two, grad_upward)
    shard = gate_weight.shape[0]
    gate_grad = scatter_dp(gate_part.astype(jnp.bfloat16).reshape(-1, shard, local_hidden))
    up_grad = scatter_dp(up_part.astype(jnp.bfloat16).reshape(-1, shard, local_hidden))
    gainfeed_part = jnp.sum(grad_rows_two * normed_two, axis=0)
    scaled_two = grad_rows_two * gain_feed
    grad_hidden = grad_out + scale_two * (
        scaled_two - normed_two * jnp.mean(scaled_two * normed_two, axis=1, keepdims=True)
    )
    grad_mixer = gather_tensor(grad_hidden.astype(jnp.bfloat16))
    output_part = rows_inner(grad_mixer, mixer_out)
    output_grad = scatter_dp(output_part.astype(jnp.bfloat16).reshape(-1, shard, local_width)).T
    grad_mixed = jnp.dot(grad_mixer, full_output, preferred_element_type=jnp.float32).astype(jnp.bfloat16)
    grad_mixed_float = grad_mixed.astype(jnp.float32)
    grad_mixgate = (grad_mixed_float * convolved).astype(jnp.bfloat16)
    grad_conv_out = grad_mixed_float * gate_float
    conv_rows = []
    value_from_conv = jnp.zeros_like(value_float)
    for offset in range(CONV):
        conv_rows.append(jnp.sum(grad_conv_out * shift_down(value_float, segments, offset), axis=0))
        value_from_conv = value_from_conv + conv_local[offset] * shift_up(
            grad_conv_out, segments, offset
        )
    grad_queries, key_float, value_attn = attend_backward(
        queries, key_rows, value_rows, segments, log_totals, grad_mixed
    )
    grad_keys = key_float.astype(jnp.bfloat16)
    grad_values = (value_attn + value_from_conv).astype(jnp.bfloat16)

    def project_grad(grads):
        part = rows_inner(group_one, grads).astype(jnp.bfloat16)
        return scatter_dp(part.reshape(-1, shard, local_width))

    query_grad = project_grad(grad_queries)
    key_grad = project_grad(grad_keys)
    value_grad = project_grad(grad_values)
    mixgate_grad = project_grad(grad_mixgate)
    grad_normed_one = (
        cols_inner(grad_queries, full_query)
        + cols_inner(grad_keys, full_key)
        + cols_inner(grad_values, full_value)
        + cols_inner(grad_mixgate, full_mixgate)
    )
    grad_rows_one = scatter_tensor(grad_normed_one)
    gainmix_part = jnp.sum(grad_rows_one * normed_one, axis=0)
    scaled_one = grad_rows_one * gain_mixer
    input_grad = grad_hidden + scale_one * (
        scaled_one - normed_one * jnp.mean(scaled_one * normed_one, axis=1, keepdims=True)
    )
    conv_full = lax.dynamic_update_slice_in_dim(
        jnp.zeros((CONV, D), jnp.float32), jnp.stack(conv_rows), column, 1
    )
    small = sum_all(
        jnp.concatenate(
            [
                conv_full,
                gainmix_part[None],
                gainfeed_part[None],
                jnp.full((1, D), squares, jnp.float32),
            ]
        )
    )
    conv_grad, gainmix_grad, gainfeed_grad = small[:CONV], small[CONV], small[CONV + 1]
    mean_loss = small[CONV + 2, 0] / (valid_total * D)
    return (
        mean_loss,
        outputs,
        input_grad,
        query_grad,
        key_grad,
        value_grad,
        mixgate_grad,
        output_grad,
        conv_grad,
        gainmix_grad,
        gainfeed_grad,
        gate_grad,
        up_grad,
        down_grad,
    )


def solution(mesh):
    rings = mesh.shape["dp"] == 8 and mesh.shape["tensor"] == 4
    return jax.shard_map(
        on_rings if rings else on_any_mesh,
        mesh=mesh,
        in_specs=(
            P(("dp", "tensor"), None),
            P(("dp", "tensor"), None),
            P(("dp", "tensor"), None),
            P("dp"),
            P(("dp", "tensor")),
            P("dp", "tensor"),
            P("dp", "tensor"),
            P("dp", "tensor"),
            P("dp", "tensor"),
            P("tensor", "dp"),
            P(),
            P(),
            P(),
            P("dp", "tensor"),
            P("dp", "tensor"),
            P("tensor", "dp"),
        ),
        out_specs=(
            P(),
            P(("dp", "tensor"), None),
            P(("dp", "tensor"), None),
            P("dp", "tensor"),
            P("dp", "tensor"),
            P("dp", "tensor"),
            P("dp", "tensor"),
            P("tensor", "dp"),
            P(),
            P(),
            P(),
            P("dp", "tensor"),
            P("dp", "tensor"),
            P("tensor", "dp"),
        ),
        check_vma=False,
    )
```

```python
import jax
import jax.numpy as jnp
from jax import lax
from jax.experimental import pallas as pl
from jax.experimental.pallas import tpu as pltpu
from jax.sharding import PartitionSpec as P

D = 1792
HEAD_DIM = 64
WINDOW = 64
CONV = 3
BLOCK = 512
EPS = 1e-05
MESH = pl.DeviceIdType.MESH
VMEM_LIMIT = 63 * 2**20


def rms_scale(values):
    return lax.rsqrt(jnp.mean(values * values, axis=1, keepdims=True) + EPS)


def rows_inner(matrix_left, matrix_right):
    return lax.dot_general(
        matrix_left, matrix_right, (((0,), (0,)), ((), ())), preferred_element_type=jnp.float32
    )


def cols_inner(matrix_left, matrix_right):
    return lax.dot_general(
        matrix_left, matrix_right, (((1,), (1,)), ((), ())), preferred_element_type=jnp.float32
    )


def shift_down(values, segments, offset):
    if offset == 0:
        return values
    shifted = jnp.concatenate(
        [jnp.zeros((offset, values.shape[1]), values.dtype), values[: values.shape[0] - offset]],
        axis=0,
    )
    same_doc = jnp.concatenate(
        [jnp.zeros((offset,), bool), segments[offset:] == segments[:-offset]]
    )
    return jnp.where(same_doc[:, None], shifted, 0.0)


def shift_up(values, segments, offset):
    if offset == 0:
        return values
    shifted = jnp.concatenate(
        [values[offset:], jnp.zeros((offset, values.shape[1]), values.dtype)], axis=0
    )
    same_doc = jnp.concatenate(
        [segments[:-offset] == segments[offset:], jnp.zeros((offset,), bool)]
    )
    return jnp.where(same_doc[:, None], shifted, 0.0)


def pad_front(array, fill_value):
    front = jnp.full((WINDOW,) + array.shape[1:], fill_value, array.dtype)
    return jnp.concatenate([front, array], axis=0)


def block_setup(queries, key_pad, seg_pad, segments, row_start, head_count):
    score_scale = HEAD_DIM ** (-0.5)
    query_rows = lax.dynamic_slice_in_dim(queries, row_start, BLOCK, 0).reshape(
        BLOCK, head_count, HEAD_DIM
    )
    key_block = lax.dynamic_slice_in_dim(key_pad, row_start, BLOCK + WINDOW, 0).reshape(
        BLOCK + WINDOW, head_count, HEAD_DIM
    )
    seg_rows = lax.dynamic_slice_in_dim(segments, row_start, BLOCK, 0)
    seg_keys = lax.dynamic_slice_in_dim(seg_pad, row_start, BLOCK + WINDOW, 0)
    distance = (
        jnp.arange(BLOCK, dtype=jnp.int32)[:, None]
        + WINDOW
        - jnp.arange(BLOCK + WINDOW, dtype=jnp.int32)[None, :]
    )
    allowed = (distance >= 0) & (distance < WINDOW) & (seg_rows[:, None] == seg_keys[None, :])
    scores = (
        jnp.einsum("qhd,khd->hqk", query_rows, key_block, preferred_element_type=jnp.float32)
        * score_scale
    )
    return (query_rows, key_block, jnp.where(allowed[None], scores, -1e30))


def attend_forward(queries, key_rows, value_rows, segments):
    group_rows, local_width = queries.shape
    head_count = local_width // HEAD_DIM
    key_pad = pad_front(key_rows, 0)
    value_pad = pad_front(value_rows, 0)
    seg_pad = pad_front(segments, -1)

    def one_block(block_index):
        row_start = block_index * BLOCK
        query_rows, key_block, scores = block_setup(
            queries, key_pad, seg_pad, segments, row_start, head_count
        )
        row_max = jnp.max(scores, axis=-1, keepdims=True)
        exponent = jnp.exp(scores - row_max)
        row_total = jnp.sum(exponent, axis=-1, keepdims=True)
        attention = (exponent / row_total).astype(jnp.bfloat16)
        value_block = lax.dynamic_slice_in_dim(value_pad, row_start, BLOCK + WINDOW, 0).reshape(
            BLOCK + WINDOW, head_count, HEAD_DIM
        )
        mixed_rows = jnp.einsum(
            "hqk,khd->qhd", attention, value_block, preferred_element_type=jnp.float32
        )
        return (
            mixed_rows.reshape(BLOCK, local_width),
            row_max[..., 0] + jnp.log(row_total[..., 0]),
        )

    blocks_out, log_totals = lax.map(one_block, jnp.arange(group_rows // BLOCK, dtype=jnp.int32))
    return (blocks_out.reshape(group_rows, local_width), log_totals)


def attend_backward(queries, key_rows, value_rows, segments, log_totals, grad_mixed):
    group_rows, local_width = queries.shape
    head_count = local_width // HEAD_DIM
    score_scale = HEAD_DIM ** (-0.5)
    key_pad = pad_front(key_rows, 0)
    value_pad = pad_front(value_rows, 0)
    seg_pad = pad_front(segments, -1)

    def one_block(accumulated, block_pair):
        block_index, log_block = block_pair
        row_start = block_index * BLOCK
        query_rows, key_block, scores = block_setup(
            queries, key_pad, seg_pad, segments, row_start, head_count
        )
        attention = jnp.exp(scores - log_block[..., None])
        value_block = lax.dynamic_slice_in_dim(value_pad, row_start, BLOCK + WINDOW, 0).reshape(
            BLOCK + WINDOW, head_count, HEAD_DIM
        )
        grad_block = lax.dynamic_slice_in_dim(grad_mixed, row_start, BLOCK, 0).reshape(
            BLOCK, head_count, HEAD_DIM
        )
        grad_attention = jnp.einsum(
            "qhd,khd->hqk", grad_block, value_block, preferred_element_type=jnp.float32
        )
        row_inner = jnp.sum(attention * grad_attention, axis=-1, keepdims=True)
        grad_scores = (attention * (grad_attention - row_inner)).astype(jnp.bfloat16)
        grad_query = (
            jnp.einsum("hqk,khd->qhd", grad_scores, key_block, preferred_element_type=jnp.float32)
            * score_scale
        )
        grad_key = (
            jnp.einsum("hqk,qhd->khd", grad_scores, query_rows, preferred_element_type=jnp.float32)
            * score_scale
        )
        grad_value = jnp.einsum(
            "hqk,qhd->khd",
            attention.astype(jnp.bfloat16),
            grad_block,
            preferred_element_type=jnp.float32,
        )
        key_acc, value_acc = accumulated
        key_acc = lax.dynamic_update_slice_in_dim(
            key_acc,
            lax.dynamic_slice_in_dim(key_acc, row_start, BLOCK + WINDOW, 0)
            + grad_key.reshape(BLOCK + WINDOW, local_width),
            row_start,
            0,
        )
        value_acc = lax.dynamic_update_slice_in_dim(
            value_acc,
            lax.dynamic_slice_in_dim(value_acc, row_start, BLOCK + WINDOW, 0)
            + grad_value.reshape(BLOCK + WINDOW, local_width),
            row_start,
            0,
        )
        return ((key_acc, value_acc), grad_query.astype(jnp.bfloat16).reshape(BLOCK, local_width))

    zeros_pad = jnp.zeros((group_rows + WINDOW, local_width), jnp.float32)
    block_ids = jnp.arange(group_rows // BLOCK, dtype=jnp.int32)
    (key_acc, value_acc), query_blocks = lax.scan(
        one_block, (zeros_pad, zeros_pad), (block_ids, log_totals)
    )
    return (query_blocks.reshape(group_rows, local_width), key_acc[WINDOW:], value_acc[WINDOW:])


def pairs_xor(size, mask):
    return [(i, i ^ mask) for i in range(size)]


def pairs_shift(size, step):
    return [(i, (i + step) % size) for i in range(size)]


def put(buffer, block, index):
    return lax.dynamic_update_slice_in_dim(buffer, block[None], index, 0)


def pick(blocks, index):
    return lax.dynamic_index_in_dim(blocks, index, 0, keepdims=False)


def gather_dp(own):
    size = lax.axis_size("dp")
    if size != 8:
        return lax.all_gather(own, "dp", axis=0)
    me = lax.axis_index("dp")
    over_y = pairs_xor(size, 1)
    up, down = pairs_shift(size, 2), pairs_shift(size, -2)
    mate = lax.ppermute(own, "dp", over_y)
    own_below = lax.ppermute(own, "dp", up)
    own_above = lax.ppermute(own, "dp", down)
    mate_below = lax.ppermute(mate, "dp", up)
    mate_above = lax.ppermute(mate, "dp", down)
    own_far = lax.ppermute(own_below, "dp", up)
    mate_far = lax.ppermute(mate_above, "dp", down)
    below, above, far = (me + 6) % size, (me + 2) % size, (me + 4) % size
    full = jnp.zeros((size,) + own.shape, own.dtype)
    for block, index in (
        (own, me),
        (mate, me ^ 1),
        (own_below, below),
        (own_above, above),
        (mate_below, below ^ 1),
        (mate_above, above ^ 1),
        (own_far, far),
        (mate_far, far ^ 1),
    ):
        full = put(full, block, index)
    return full


def scatter_dp(parts):
    size = lax.axis_size("dp")
    if size != 8:
        return lax.psum_scatter(parts, "dp", scatter_dimension=0).astype(jnp.float32)
    me = lax.axis_index("dp")
    over_y = pairs_xor(size, 1)
    up, down = pairs_shift(size, 2), pairs_shift(size, -2)
    below, above, far = (me + 6) % size, (me + 2) % size, (me + 4) % size

    def part(index):
        return pick(parts, index).astype(jnp.float32)

    low = jnp.bfloat16
    own_first = lax.ppermute(pick(parts, far), "dp", up)
    mate_first = lax.ppermute(pick(parts, far ^ 1), "dp", down)
    mate_from_below = lax.ppermute(pick(parts, above ^ 1), "dp", up)
    own_from_above = lax.ppermute(pick(parts, below), "dp", down)
    mate_from_above = lax.ppermute(
        (part(below ^ 1) + mate_first.astype(jnp.float32)).astype(low), "dp", down
    )
    own_from_below = lax.ppermute(
        (part(above) + own_first.astype(jnp.float32)).astype(low), "dp", up
    )
    mate_sum = (
        part(me ^ 1)
        + mate_from_below.astype(jnp.float32)
        + mate_from_above.astype(jnp.float32)
    )
    from_mate = lax.ppermute(mate_sum.astype(low), "dp", over_y)
    own_sum = part(me) + own_from_below.astype(jnp.float32) + own_from_above.astype(jnp.float32)
    return own_sum + from_mate.astype(jnp.float32)


def gather_tensor(own):
    size = lax.axis_size("tensor")
    if size != 4:
        return lax.all_gather(own, "tensor", axis=0, tiled=True)
    me = lax.axis_index("tensor")
    across = lax.ppermute(own, "tensor", pairs_xor(size, 2))
    beside = lax.ppermute(own, "tensor", pairs_xor(size, 1))
    beside_across = lax.ppermute(across, "tensor", pairs_xor(size, 1))
    full = jnp.zeros((size,) + own.shape, own.dtype)
    for block, index in ((own, me), (beside, me ^ 1), (across, me ^ 2), (beside_across, me ^ 3)):
        full = put(full, block, index)
    return full.reshape(size * own.shape[0], own.shape[1])


def scatter_tensor(parts):
    size = lax.axis_size("tensor")
    if size != 4:
        return lax.psum_scatter(
            parts.astype(jnp.bfloat16), "tensor", scatter_dimension=0, tiled=True
        ).astype(jnp.float32)
    me = lax.axis_index("tensor")
    low = jnp.bfloat16
    parts = parts.reshape(size, -1, parts.shape[1])
    beside = lax.ppermute(pick(parts, me ^ 3).astype(low), "tensor", pairs_xor(size, 1))
    sent = (pick(parts, me ^ 2).astype(jnp.float32) + beside.astype(jnp.float32)).astype(low)
    across = lax.ppermute(sent, "tensor", pairs_xor(size, 2))
    beside_own = lax.ppermute(pick(parts, me ^ 1).astype(low), "tensor", pairs_xor(size, 1))
    return (
        pick(parts, me).astype(jnp.float32)
        + beside_own.astype(jnp.float32)
        + across.astype(jnp.float32)
    )


def sum_all(values):
    dp_size, tensor_size = lax.axis_size("dp"), lax.axis_size("tensor")
    if dp_size != 8 or tensor_size != 4:
        return lax.psum(values, ("dp", "tensor"))
    for axis, size, mask in (
        ("tensor", tensor_size, 1),
        ("tensor", tensor_size, 2),
        ("dp", dp_size, 1),
        ("dp", dp_size, 2),
        ("dp", dp_size, 6),
    ):
        values = values + lax.ppermute(values, axis, pairs_xor(size, mask))
    return values


TILE = 64
LANES = 128
PIECES = 4


def neighbours():
    d, t = lax.axis_index("dp"), lax.axis_index("tensor")
    z, y = d // 2, lax.rem(d, 2)
    core = t + 1 - 2 * lax.rem(t, 2)
    place = z + y * (7 - 2 * z)

    def ring(offset):
        position = lax.rem(place + offset + 16, 8)
        side = position // 4
        return 2 * (position + side * (7 - 2 * position)) + side

    return dict(
        d=d,
        t=t,
        ring=ring,
        core=core,
        cross=lax.rem(t + 2, 4),
        cross_core=lax.rem(core + 2, 4),
        mate=d + 1 - 2 * y,
        z_pair=2 * (z + 1 - 2 * lax.rem(z, 2)) + y,
        z_mirror=2 * (3 - z) + y,
    )


def greet(at, everyone=False):
    d, t = at["d"], at["t"]
    devices = [(at["ring"](1), t), (at["ring"](-1), t), (d, at["core"]), (d, at["cross"])]
    if everyone:
        devices += [(at["mate"], t), (at["z_pair"], t), (at["z_mirror"], t)]
    barrier = pltpu.get_barrier_semaphore()
    for device in devices:
        pl.semaphore_signal(barrier, inc=1, device_id=device, device_id_type=MESH)
    pl.semaphore_wait(barrier, len(devices))


def remote(source, target, sems, index, device):
    return pltpu.make_async_remote_copy(
        src_ref=source,
        dst_ref=target,
        send_sem=sems[0].at[index],
        recv_sem=sems[1].at[index],
        device_id=device,
        device_id_type=MESH,
    )


def pieces_of(half, count):
    if count == 1:
        return [(0, half)]
    first = (half // 2 + 15) // 16 * 16
    return [(0, first), (first, half - first)]


class RingGather:
    def __init__(self, at, own, slot, sems, base, local_sem, count=2):
        half = own.shape[0] // 2
        ring, t = at["ring"], at["t"]
        self.local = pltpu.make_async_copy(own, slot(at["d"], 0, 2 * half), local_sem)
        self.sends, self.receives, self.at = [], [], 0
        for s in range(7):
            for k, (first, size) in enumerate(pieces_of(half, count)):
                sends, receives = [], []
                for way, sign in ((0, 1), (1, -1)):
                    to, row = (ring(sign), t), way * half + first
                    index = base + (s * count + k) * 2 + way
                    here = slot(ring(-sign * s), row, size)
                    there = slot(ring(-sign * (s + 1)), row, size)
                    source = own.at[pl.ds(row, size)] if s == 0 else here
                    sends.append(remote(source, here, sems, index, to))
                    receives.append(remote(there, there, sems, index, to))
                self.sends.append(sends)
                self.receives.append(receives)
        self.count = count

    def start(self):
        for copies in self.sends[: self.count]:
            for copy in copies:
                copy.start()
        self.local.start()

    def tick(self):
        if self.at < len(self.receives):
            for way in range(2):
                self.receives[self.at][way].wait_recv()
                if self.at + self.count < len(self.sends):
                    self.sends[self.at + self.count][way].start()
            self.at += 1

    def finish(self):
        while self.at < len(self.receives):
            self.tick()
        self.local.wait()

    def drain(self):
        for sends in self.sends:
            for copy in sends:
                copy.wait_send()


class RingScatter:
    def __init__(self, at, left, right, slots, term, out, sems, base, count=2):
        self.ring, self.left, self.right = at["ring"], left, right
        self.slots, self.term, self.out = slots, term, out
        self.half, self.columns = slots.shape[2], slots.shape[3]
        self.pieces = pieces_of(self.half, count)
        self.at = 0
        self.sends = []
        for s in range(7):
            for k, (first, size) in enumerate(self.pieces):
                rows = pl.ds(first, size)
                self.sends.append(
                    [
                        remote(
                            slots.at[way, s, rows], slots.at[way, s + 1, rows], sems,
                            base + (s * count + k) * 2 + way, (at["ring"](sign), at["t"]),
                        )
                        for way, sign in ((0, 1), (1, -1))
                    ]
                )

    def compute(self, away):
        half = self.half
        first = pl.multiple_of(self.ring(-away) * 2 * half, half)
        second = pl.multiple_of(self.ring(away) * 2 * half + half, half)
        width = 512
        whole = self.columns // width * width

        def block(lanes):
            left = jnp.concatenate(
                [self.left[pl.ds(first, half)], self.left[pl.ds(second, half)]], axis=0
            )
            self.term[:, lanes] = nn_dot(left, self.right[:, lanes])

        @pl.loop(0, whole // width)
        def _(i):
            block(pl.ds(pl.multiple_of(i * width, width), width))

        if whole < self.columns:
            block(pl.ds(whole, self.columns - whole))

    def start(self):
        self.compute(1)
        for k, (first, size) in enumerate(self.pieces):
            for way in range(2):
                self.slots[way, 0, pl.ds(first, size)] = self.term[
                    pl.ds(way * self.half + first, size)
                ].astype(jnp.bfloat16)
                self.sends[k][way].start()
        self.compute(2)

    def tick(self):
        if self.at == len(self.sends):
            return
        count = len(self.pieces)
        s, k = divmod(self.at, count)
        first, size = self.pieces[k]
        for way in range(2):
            here, rows = pl.ds(first, size), pl.ds(way * self.half + first, size)
            self.sends[self.at][way].wait_recv()
            total = self.slots[way, s + 1, here].astype(jnp.float32) + self.term[rows]
            if s < 6:
                self.slots[way, s + 1, here] = total.astype(jnp.bfloat16)
                self.sends[self.at + count][way].start()
            else:
                self.out[rows] = total
        self.at += 1
        if k == count - 1 and s < 6:
            self.compute(s + 3)

    def finish(self):
        while self.at < len(self.sends):
            self.tick()
        for sends in self.sends:
            for copy in sends:
                copy.wait_send()


class GatherTensor:
    def __init__(self, at, full, rows, sems, base):
        def block(index):
            return full.at[pl.ds(pl.multiple_of(index * rows, rows), rows)]

        mine, across = block(at["t"]), block(at["cross"])
        self.to_core = remote(mine, mine, sems, base, (at["d"], at["core"]))
        self.to_cross = remote(mine, mine, sems, base + 1, (at["d"], at["cross"]))
        self.relay_core = remote(across, across, sems, base + 2, (at["d"], at["core"]))
        places = (block(at["core"]), across, block(at["cross_core"]))
        self.receives = [
            remote(place, place, sems, base + k, (at["d"], at["core"]))
            for k, place in enumerate(places)
        ]

    def start(self):
        self.to_cross.start()
        self.to_core.start()

    def relay(self):
        self.receives[1].wait_recv()
        self.relay_core.start()

    def drain(self):
        for send in (self.to_core, self.to_cross, self.relay_core):
            send.wait_send()

    def finish(self):
        self.receives[0].wait_recv()
        self.receives[2].wait_recv()
        self.drain()


def sum_rows(at, block_part, send, receive, total, sems, base, idle=lambda point: None):
    to_core, to_cross = (at["d"], at["core"]), (at["d"], at["cross"])
    low = jnp.bfloat16
    first = remote(send.at[0], receive.at[0], sems, base, to_core)
    second = remote(send.at[1], receive.at[1], sems, base + 1, to_cross)
    third = remote(send.at[2], receive.at[2], sems, base + 2, to_core)
    send[0] = block_part(at["cross_core"]).astype(low)
    first.start()
    total[...] = block_part(at["cross"])
    first.wait_recv()
    send[1] = (total[...] + receive[0].astype(jnp.float32)).astype(low)
    second.start()
    idle(0)
    send[2] = block_part(at["core"]).astype(low)
    third.start()
    idle(1)
    total[...] = block_part(at["t"])
    third.wait_recv()
    total[...] += receive[2].astype(jnp.float32)
    idle(2)
    second.wait_recv()
    total[...] += receive[1].astype(jnp.float32)
    for copy in (first, second, third):
        copy.wait_send()


class GatherPieces:
    def __init__(self, at, full, rows, count, sems, base):
        size = rows // count
        to_core, to_cross = (at["d"], at["core"]), (at["d"], at["cross"])

        def place(block, c):
            return full.at[pl.ds(pl.multiple_of(block * rows + c * size, size), size)]

        def copies(k, block, to):
            return [
                remote(place(block, c), place(block, c), sems, base + k * count + c, to)
                for c in range(count)
            ]

        self.to_core = copies(0, at["t"], to_core)
        self.to_cross = copies(1, at["t"], to_cross)
        self.relay_core = copies(2, at["cross"], to_core)
        self.receives = [
            copies(k, block, to_core) for k, block in enumerate((at["core"], at["cross"], at["cross_core"]))
        ]

    def start(self, c):
        self.to_cross[c].start()
        self.to_core[c].start()

    def relay(self):
        for receive, send in zip(self.receives[1], self.relay_core):
            receive.wait_recv()
            send.start()

    def wait(self, k):
        for receive in self.receives[k]:
            receive.wait_recv()

    def drain(self):
        for send in self.to_core + self.to_cross + self.relay_core:
            send.wait_send()


def sum_pieces(at, block_part, send, receive, total, sems, base, count, done):
    to_core, to_cross = (at["d"], at["core"]), (at["d"], at["cross"])
    low = jnp.bfloat16
    size = total.shape[0] // count
    pieces = [pl.ds(c * size, size) for c in range(count)]

    def copies(k, to):
        return [
            remote(send.at[k, piece], receive.at[k, piece], sems, base + k * count + c, to)
            for c, piece in enumerate(pieces)
        ]

    first, second, third = copies(0, to_core), copies(1, to_cross), copies(2, to_core)
    send[0] = block_part(at["cross_core"]).astype(low)
    for copy in first:
        copy.start()
    total[...] = block_part(at["cross"])
    for c, piece in enumerate(pieces):
        first[c].wait_recv()
        send[1, piece] = (total[piece] + receive[0, piece].astype(jnp.float32)).astype(low)
        second[c].start()
    send[2] = block_part(at["core"]).astype(low)
    for copy in third:
        copy.start()
    total[...] = block_part(at["t"])
    for c, piece in enumerate(pieces):
        third[c].wait_recv()
        second[c].wait_recv()
        total[piece] += receive[2, piece].astype(jnp.float32) + receive[1, piece].astype(jnp.float32)
        done(c)
    for copy in first + second + third:
        copy.wait_send()


class SumAll:
    def __init__(self, at, value, received, sems, base):
        d, t = at["d"], at["t"]
        partners = ((d, at["core"]), (d, at["cross"]), (at["mate"], t), (at["z_pair"], t), (at["z_mirror"], t))
        self.value, self.received, self.s = value, received, 0
        self.copies = [
            remote(value.at[k], received.at[k], sems, base + k, partner)
            for k, partner in enumerate(partners)
        ]

    def start(self):
        self.copies[0].start()

    def step(self):
        s = self.s
        self.copies[s].wait_recv()
        self.value[s + 1] = self.value[s] + self.received[s]
        if s < 4:
            self.copies[s + 1].start()
        self.s += 1

    def finish(self):
        while self.s < 5:
            self.step()
        for copy in self.copies:
            copy.wait_send()


def nt_dot(left, right):
    return lax.dot_general(
        left, right, (((1,), (1,)), ((), ())), preferred_element_type=jnp.float32
    )


def nn_dot(left, right):
    return lax.dot_general(
        left, right, (((1,), (0,)), ((), ())), preferred_element_type=jnp.float32
    )


def tn_dot(left, right):
    return lax.dot_general(
        left, right, (((0,), (0,)), ((), ())), preferred_element_type=jnp.float32
    )


def head_groups(width):
    heads = width // HEAD_DIM
    return [(2 * HEAD_DIM * j, min(2, heads - 2 * j)) for j in range((heads + 1) // 2)]


def split_heads(tile, heads):
    if heads == 1:
        return tile
    lane = lax.broadcasted_iota(jnp.int32, tile.shape, 1)
    zero = jnp.zeros_like(tile)
    return jnp.concatenate(
        [jnp.where(lane < HEAD_DIM, tile, zero), jnp.where(lane < HEAD_DIM, zero, tile)], axis=0
    )


def join_heads(stacked, heads):
    if heads == 1:
        return stacked
    half = stacked.shape[0] // 2
    lane = lax.broadcasted_iota(jnp.int32, (half, stacked.shape[1]), 1)
    return jnp.where(lane < HEAD_DIM, stacked[:half], stacked[half:])


def convolve(window, taps, lanes, same_one, same_two):
    one = pltpu.roll(window, 1, axis=0)[TILE:] * same_one
    two = pltpu.roll(window, 2, axis=0)[TILE:] * same_two
    rows = (window[TILE:], one, two)
    return sum(taps[m : m + 1, lanes] * rows[m] for m in range(CONV)), rows


def attend_tile(i, q, k_pad, v_pad, u, seg_q, seg_k, same, taps, p_out, o):
    row = pl.multiple_of(i * TILE, TILE)
    at_row, at_window = pl.ds(row, TILE), pl.ds(row, 2 * TILE)
    distance = (
        lax.broadcasted_iota(jnp.int32, (TILE, 2 * TILE), 0)
        + TILE
        - lax.broadcasted_iota(jnp.int32, (TILE, 2 * TILE), 1)
    )
    allowed = (seg_q[at_row] == seg_k[i]) & (distance >= 0) & (distance < WINDOW)
    same_one, same_two = same[at_row, 0:1], same[at_row, 1:2]
    for lane, heads in head_groups(q.shape[1]):
        lanes = pl.ds(lane, heads * HEAD_DIM)
        values = v_pad[at_window, lanes]
        allow = jnp.concatenate([allowed] * heads, axis=0) if heads > 1 else allowed
        scores = nt_dot(split_heads(q[at_row, lanes], heads), k_pad[at_window, lanes])
        scores = jnp.where(allow, scores * (HEAD_DIM**-0.5), -1e30)
        exponent = jnp.exp(scores - jnp.max(scores, axis=1, keepdims=True))
        chance = exponent * (1.0 / jnp.sum(exponent, axis=1, keepdims=True))
        chance = chance.astype(jnp.bfloat16)
        p_out[i, pl.ds((lane // HEAD_DIM) * TILE, heads * TILE), :] = chance
        mixed = join_heads(nn_dot(chance, values), heads)
        convolved, _ = convolve(values.astype(jnp.float32), taps, lanes, same_one, same_two)
        o[at_row, lanes] = (mixed + convolved * u[at_row, lanes].astype(jnp.float32)).astype(
            jnp.bfloat16
        )


def attend_back_tile(
    i, q, k_pad, v_pad, u, p, same, taps, do, dk, dv, conv_sum
):
    row = pl.multiple_of(i * TILE, TILE)
    at_row, at_window = pl.ds(row, TILE), pl.ds(row, 2 * TILE)
    same_one, same_two = same[at_row, 0:1], same[at_row, 1:2]
    for lane, heads in head_groups(q.shape[1]):
        lanes = pl.ds(lane, heads * HEAD_DIM)
        keys, values = k_pad[at_window, lanes], v_pad[at_window, lanes]
        grad = do[at_row, lanes]
        grad_heads = split_heads(grad, heads)
        chance_low = p[i, pl.ds((lane // HEAD_DIM) * TILE, heads * TILE), :]
        chance = chance_low.astype(jnp.float32)
        weighted = chance * nt_dot(grad_heads, values)
        slope = weighted - chance * jnp.sum(weighted, axis=1, keepdims=True)
        slope = (slope * (HEAD_DIM**-0.5)).astype(jnp.bfloat16)
        dk[at_window, lanes] += tn_dot(slope, split_heads(q[at_row, lanes], heads))
        q[at_row, lanes] = join_heads(nn_dot(slope, keys), heads).astype(jnp.bfloat16)
        convolved, rows = convolve(values.astype(jnp.float32), taps, lanes, same_one, same_two)
        grad = grad.astype(jnp.float32)
        do[at_row, lanes] = (grad * convolved).astype(jnp.bfloat16)
        grad_conv = grad * u[at_row, lanes].astype(jnp.float32)
        back = tn_dot(chance_low, grad_heads)
        zero = jnp.zeros_like(grad_conv)
        for m, same_m in enumerate((None, same_one, same_two)):
            conv_sum[m : m + 1, lanes] += jnp.sum(grad_conv * rows[m], axis=0, keepdims=True)
            term = taps[m : m + 1, lanes] * grad_conv
            term = term if m == 0 else term * same_m
            term = jnp.concatenate([zero, term], axis=0)
            back = back + (term if m == 0 else pltpu.roll(term, 2 * TILE - m, axis=0))
        dv[at_window, lanes] += back


def rolled(values, offset):
    turned = pltpu.roll(values, offset, axis=1)
    lane = lax.broadcasted_iota(jnp.int32, values.shape, 1)
    return jnp.where(lane < offset, pltpu.roll(turned, 1, axis=0), turned)


def make_tables(segments, seg_q, seg_k, same):
    values = segments[...]
    row = lax.broadcasted_iota(jnp.int32, values.shape, 0)
    lane = lax.broadcasted_iota(jnp.int32, values.shape, 1)
    columns = values.T
    matches = [
        jnp.where((values == rolled(values, m)) & ((row > 0) | (lane >= m)), 1.0, 0.0).astype(jnp.float32).T
        for m in range(1, CONV)
    ]
    crossing = rolled(values, TILE)
    crossing = jnp.where((row == 0) & (lane < TILE), -1, crossing)
    for n in range(values.shape[0]):
        rows = pl.ds(n * LANES, LANES)
        seg_q[rows] = columns[:, n : n + 1]
        for m, match in enumerate(matches):
            same[rows, m : m + 1] = match[:, n : n + 1]
        seg_k[2 * n] = crossing[n : n + 1]
        seg_k[2 * n + 1] = values[n : n + 1]


def row_of(gain):
    return gain[...].reshape(1, -1)


def norm_rows(values, gain):
    scale = lax.rsqrt(jnp.mean(values * values, axis=1, keepdims=True) + EPS)
    return (values * scale * gain).astype(jnp.bfloat16)


def norm_back(values, grad, gain):
    scale = lax.rsqrt(jnp.mean(values * values, axis=1, keepdims=True) + EPS)
    normed = values * scale
    scaled = grad * gain
    through = scale * (scaled - normed * jnp.mean(scaled * normed, axis=1, keepdims=True))
    return through, jnp.sum(grad * normed, axis=0, keepdims=True)


def chunks_of(rows, size=64):
    def run(body):
        @pl.loop(0, rows // size)
        def _(i):
            body(pl.multiple_of(i * size, size), size)

    return run


def forward_kernel(
    x, valid_lanes, gain_one, gain_two, segments, taps,
    gate_own, up_own, mix_own, out_own, down_own, cotangent_in, teacher_in,
    mix_out, last_out, feed_out, down_out, h1t_out, h2t_out, dybt_out, q_out, k_out, v_out, u_out, p_out,
    o_out, x1_out, dyb_out, slopes_out, active_out, act_out, dy_out, count_out, squares_out, same,
    valid, seg_q, seg_k, feed_own, mix, last, feed, down, h1, turned, h2, q, k_pad, v_pad, u, p, o, slopes, active, x1, side, teacher,
    send, receive, total, count, count_in,
    send_sems, recv_sems, local_sems, load_sems, out_sems,
):
    at = neighbours()
    sems = (send_sems, recv_sems)
    rows, shard = x.shape[0], mix_own.shape[0]
    low = jnp.bfloat16
    greet(at, everyone=True)

    def slot_of(full):
        return lambda i, first, size: full.at[pl.ds(pl.multiple_of(i * shard + first, 16), size)]

    mix_ring = RingGather(at, mix_own, slot_of(mix), sems, 0, local_sems.at[0])
    last_ring = RingGather(at, out_own, slot_of(last), sems, 28, local_sems.at[1], count=1)
    feed_ring = RingGather(at, feed_own, slot_of(feed), sems, 42, local_sems.at[2])
    down_ring = RingGather(
        at, down_own.at[:, pl.ds(0, down.shape[1])], slot_of(down), sems, 70, local_sems.at[3]
    )
    dyb = h1
    group_one = GatherTensor(at, h1, rows, sems, 98)
    group_two = GatherTensor(at, h2, rows, sems, 101)
    group_back = GatherPieces(at, dyb, rows, PIECES, sems, 115)
    counting = SumAll(at, count, count_in, sems, 110)
    local = q.shape[1]
    main = local // LANES * LANES
    tail = local - main
    keeps = []

    def keep(source, target):
        copy = pltpu.make_async_copy(source, target, out_sems.at[len(keeps)])
        copy.start()
        keeps.append(copy)
        return copy

    def tick():
        last_ring.tick()
        if feed_ring.at < len(feed_ring.receives):
            feed_ring.tick()
            if feed_ring.at == len(feed_ring.receives) - 2:
                down_ring.start()
        else:
            down_ring.tick()

    def turn(source, block):
        here = pl.ds(pl.multiple_of(block * rows, rows), rows)
        turned[:, here] = source[here].T

    mix_ring.start()

    @chunks_of(rows)
    def _(row, size):
        h1[pl.ds(pl.multiple_of(at["t"] * rows + row, size), size)] = norm_rows(
            x[pl.ds(row, size)].astype(jnp.float32), row_of(gain_one)
        )

    group_one.start()
    flags = valid_lanes[...].astype(jnp.float32)
    count[0] = jnp.full(count.shape[1:], jnp.sum(flags), jnp.float32)
    counting.start()
    load_teacher = pltpu.make_async_copy(teacher_in, teacher, load_sems.at[0])
    load_cotangent = pltpu.make_async_copy(cotangent_in, side, load_sems.at[1])
    load_teacher.start()
    load_cotangent.start()
    k_pad[pl.ds(0, TILE)] = jnp.zeros((TILE, local), k_pad.dtype)
    v_pad[pl.ds(0, TILE)] = jnp.zeros((TILE, local), v_pad.dtype)
    make_tables(segments, seg_q, seg_k, same)
    width = gate_own.shape[1]
    cut = width // LANES * LANES
    rest = width - cut
    feed_own[:, pl.ds(0, cut)] = gate_own[:, pl.ds(0, cut)]
    feed_own[:, pl.ds(cut, cut)] = up_own[:, pl.ds(0, cut)]
    ends = [own[:, pl.ds(cut, rest)].astype(jnp.float32) for own in (gate_own, up_own)]
    feed_own[:, pl.ds(2 * cut, 2 * rest)] = jnp.concatenate(ends, axis=1).astype(low)
    spare = jnp.zeros((8 - flags.shape[0], LANES), jnp.float32)
    columns = jnp.concatenate([flags, spare], axis=0).T
    for n in range(flags.shape[0]):
        valid[pl.ds(n * LANES, LANES)] = columns[:, n : n + 1]
    for _ in range(6):
        mix_ring.tick()
    group_one.relay()
    mix_ring.tick()
    mix_ring.tick()
    group_one.finish()
    mix_ring.tick()
    for k in range(2):

        @pl.loop(2 * k, 2 * k + 2)
        def _(j):
            turn(h1, j)

        mix_ring.tick()
    keep_h1t = keep(turned, h1t_out)
    last_ring.start()
    mix_ring.tick()
    last_ring.tick()
    feed_ring.start()
    mix_ring.tick()
    last_ring.tick()
    mix_ring.finish()
    last_ring.tick()
    keep(mix, mix_out)

    def project(j):
        here = pl.ds(pl.multiple_of(j * rows, rows), rows)
        there = pl.ds(pl.multiple_of(j * rows + TILE, TILE), rows)
        left = h1[here]
        pair = nn_dot(left, mix[:, pl.ds(0, 2 * main)]).astype(low)
        q[here, pl.ds(0, main)] = pair[:, :main]
        k_pad[there, pl.ds(0, main)] = pair[:, main:]
        pair = nn_dot(left, mix[:, pl.ds(2 * main, 2 * main)]).astype(low)
        v_pad[there, pl.ds(0, main)] = pair[:, :main]
        u[here, pl.ds(0, main)] = pair[:, main:]
        ends = nn_dot(left, mix[:, pl.ds(4 * main, 4 * tail)])
        q[here, pl.ds(main, tail)] = ends[:, :tail].astype(low)
        k_pad[there, pl.ds(main, tail)] = ends[:, tail : 2 * tail].astype(low)
        v_pad[there, pl.ds(main, tail)] = ends[:, 2 * tail : 3 * tail].astype(low)
        u[here, pl.ds(main, tail)] = ends[:, 3 * tail :].astype(low)

    def projects(first, last_block):
        @pl.loop(first, last_block)
        def _(j):
            project(j)

    projects(0, 2)
    tick()
    counting.step()
    projects(2, 4)
    for source, target in ((q, q_out), (k_pad, k_out), (v_pad, v_out), (u, u_out)):
        keep(source, target)
    tick()
    tiles = q.shape[0] // TILE

    def attend(first, last_tile):
        @pl.loop(first, last_tile)
        def _(i):
            attend_tile(i, q, k_pad, v_pad, u, seg_q, seg_k, same, taps, p, o)

    for k in range(4):
        attend(k * tiles // 4, (k + 1) * tiles // 4)
        tick()
        if k % 2:
            counting.step()
    last_ring.finish()
    keep(last, last_out)
    keep(p, p_out)
    keep(o, o_out)

    def mixed_part(block):
        return nt_dot(o[pl.ds(pl.multiple_of(block * rows, rows), rows)], last[:, pl.ds(0, local)])

    def idle(point):
        tick()
        if point == 2:
            tick()

    sum_rows(at, mixed_part, send, receive, total, sems, 107, idle=idle)

    @chunks_of(rows)
    def _(row, size):
        here = pl.ds(row, size)
        hidden = total[here] + x[here].astype(jnp.float32)
        x1[here] = hidden
        h2[pl.ds(pl.multiple_of(at["t"] * rows + row, size), size)] = norm_rows(hidden, row_of(gain_two))

    group_two.start()
    keep(x1, x1_out)
    for _ in range(3):
        tick()
    counting.step()
    tick()
    group_two.relay()
    tick()
    counting.finish()
    keep(count.at[5], count_out)
    group_two.finish()
    while feed_ring.at < len(feed_ring.receives):
        tick()
    feed_ring.finish()
    keep(feed, feed_out)
    parts, _ = feed_lanes(width)

    def widen(j):
        here = pl.ds(pl.multiple_of(j * (rows // 2), rows // 2), rows // 2)
        left = h2[here]
        for own, gate_lanes, up_lanes in parts:
            a, by_gate, by_up = gated(nn_dot(left, feed[:, gate_lanes]), nn_dot(left, feed[:, up_lanes]))
            active[here, own] = a.astype(low)
            slopes[here, gate_lanes] = by_gate.astype(low)
            slopes[here, up_lanes] = by_up.astype(low)
        both = nn_dot(left, feed[:, pl.ds(2 * cut, 2 * rest)])
        a, by_gate, by_up = gated(both[:, :rest], both[:, rest:])
        active[here, pl.ds(cut, rest)] = a.astype(low)
        slopes[here, pl.ds(2 * cut, 2 * rest)] = jnp.concatenate([by_gate, by_up], axis=1).astype(low)

    for k in range(8):

        @pl.loop(k, k + 1)
        def _(j):
            widen(j)

        tick()
    keep(active, active_out)
    keep(slopes, slopes_out)
    keep_h1t.wait()
    for k in range(4):

        @pl.loop(k, k + 1)
        def _(j):
            turn(h2, j)

        tick()
    keep_h2t = keep(turned, h2t_out)
    down_ring.finish()
    keep(down, down_out)
    load_teacher.wait()
    load_cotangent.wait()

    def fed_part(block):
        here = pl.ds(pl.multiple_of(block * rows, rows), rows)
        ends = nt_dot(active[here, pl.ds(cut, rest)], last[:, pl.ds(local, rest)])
        return ends + nt_dot(active[here, pl.ds(0, cut)], down[...])

    weight = (rows * 4 * 8) / count[5, 0:1, 0:1]
    squares_out[...] = jnp.zeros_like(squares_out)
    piece, step = rows // PIECES, 32

    def judge(c):
        @pl.loop(0, piece // step)
        def _(i):
            row = pl.multiple_of(c * piece + i * step, step)
            here = pl.ds(row, step)
            result = total[here] + x1[here]
            deviation = result - teacher[here].astype(jnp.float32)
            kept = valid[here, 0:1] * deviation
            total[here] = result
            squares_out[0:1] += jnp.sum(kept * deviation, axis=0, keepdims=True)
            grad = side[here] + kept * weight
            side[here] = grad
            dyb[pl.ds(pl.multiple_of(at["t"] * rows + row, step), step)] = grad.astype(low)

        group_back.start(c)

    sum_pieces(at, fed_part, send, receive, total, sems, 115 + 3 * PIECES, PIECES, judge)
    keep(total, act_out)
    keep(side, dy_out)
    keep_h2t.wait()

    def spread(block):
        here = pl.ds(pl.multiple_of(block * rows, rows), rows)
        turn(dyb, block)
        keep(dyb.at[here], dyb_out.at[here])
        keep(turned.at[:, here], dybt_out.at[:, here])

    spread(at["t"])
    group_back.wait(0)
    spread(at["core"])
    group_back.relay()
    spread(at["cross"])
    group_back.wait(2)
    spread(at["cross_core"])
    group_back.drain()
    for ring in (mix_ring, last_ring, feed_ring, down_ring):
        ring.drain()
    for copy in keeps:
        if copy is not keep_h1t and copy is not keep_h2t:
            copy.wait()


def specs():
    return pl.BlockSpec(memory_space=pltpu.VMEM), pl.BlockSpec(memory_space=pl.ANY)


def shape(*dims, kind=jnp.bfloat16):
    return jax.ShapeDtypeStruct(dims, kind)


def params(identity):
    return pltpu.CompilerParams(
        collective_id=identity, has_side_effects=True, vmem_limit_bytes=VMEM_LIMIT
    )


def dma(count):
    return pltpu.SemaphoreType.DMA((count,))


def forward(
    x, valid_lanes, gain_one, gain_two, segments, taps, mix_own, out_own, gate_own, up_own, down_own, cotangent,
    teacher,
):
    rows, width = x.shape
    shard = out_own.shape[0]
    local, hidden = mix_own.shape[1] // 4, gate_own.shape[1]
    cut = hidden // LANES * LANES
    everyone, depth = 4 * rows, 8 * shard
    low, wide = jnp.bfloat16, jnp.float32
    tiles, heads = everyone // TILE, local // HEAD_DIM
    vmem, hbm = specs()
    return pl.pallas_call(
        forward_kernel,
        out_shape=(
            shape(depth, 4 * local),
            shape(depth, out_own.shape[1]),
            shape(depth, 2 * hidden),
            shape(depth, cut),
            shape(width, everyone),
            shape(width, everyone),
            shape(width, everyone),
            shape(everyone, local),
            shape(everyone + TILE, local),
            shape(everyone + TILE, local),
            shape(everyone, local),
            shape(tiles, heads * TILE, 2 * TILE),
            shape(everyone, local),
            shape(rows, width, kind=wide),
            shape(everyone, width),
            shape(everyone, 2 * hidden),
            shape(everyone, hidden),
            shape(rows, width, kind=wide),
            shape(rows, width, kind=wide),
            shape(8, LANES, kind=wide),
            shape(8, width, kind=wide),
            shape(everyone, CONV - 1, kind=wide),
        ),
        in_specs=[vmem] * 8 + [hbm] * 5,
        out_specs=(hbm,) * 20 + (vmem,) * 2,
        scratch_shapes=[
            pltpu.VMEM((rows, 1), wide),
            pltpu.VMEM((everyone, 1), jnp.int32),
            pltpu.VMEM((tiles, 1, 2 * TILE), jnp.int32),
            pltpu.VMEM((shard, 2 * hidden), low),
            pltpu.VMEM((depth, 4 * local), low),
            pltpu.VMEM((depth, out_own.shape[1]), low),
            pltpu.VMEM((depth, 2 * hidden), low),
            pltpu.VMEM((depth, cut), low),
            pltpu.VMEM((everyone, width), low),
            pltpu.VMEM((width, everyone), low),
            pltpu.VMEM((everyone, width), low),
            pltpu.VMEM((everyone, local), low),
            pltpu.VMEM((everyone + TILE, local), low),
            pltpu.VMEM((everyone + TILE, local), low),
            pltpu.VMEM((everyone, local), low),
            pltpu.VMEM((tiles, heads * TILE, 2 * TILE), low),
            pltpu.VMEM((everyone, local), low),
            pltpu.VMEM((everyone, 2 * hidden), low),
            pltpu.VMEM((everyone, hidden), low),
            pltpu.VMEM((rows, width), wide),
            pltpu.VMEM((rows, width), wide),
            pltpu.VMEM((rows, width), low),
            pltpu.VMEM((3, rows, width), low),
            pltpu.VMEM((3, rows, width), low),
            pltpu.VMEM((rows, width), wide),
            pltpu.VMEM((6, 8, LANES), wide),
            pltpu.VMEM((5, 8, LANES), wide),
            dma(115 + 6 * PIECES),
            dma(115 + 6 * PIECES),
            dma(4),
            dma(2),
            dma(26),
        ],
        compiler_params=params(1),
    )(
        x, valid_lanes, gain_one, gain_two, segments, taps, gate_own, up_own, mix_own, out_own, down_own,
        cotangent, teacher,
    )


def feed_lanes(hidden):
    main = hidden // LANES * LANES
    cut = main // 2 // LANES * LANES
    parts = [(0, cut), (cut, main - cut)]
    return [(pl.ds(a, n), pl.ds(a, n), pl.ds(main + a, n)) for a, n in parts], main


def gated(gate, up):
    sigmoid = jax.nn.sigmoid(gate)
    silu = gate * sigmoid
    return silu * up, up * sigmoid * (1.0 + gate * (1.0 - sigmoid)), silu


def feed_backward_kernel(
    gain, dyb_in, dybt_in, h2t_in, down_in, feed_in, active_in, slopes_in, last_in, x1_in, dy_in,
    down_grad, gate_grad, gain_part, dx1_out, dx1t_out, do_out, slopes_out,
    dyb, dybt, h2t, down, feed, active, slopes, last, do, side, total, down_slots, gate_slots,
    down_term, gate_term, send, receive,
    send_sems, recv_sems, load_sems, out_sems,
):
    at = neighbours()
    sems = (send_sems, recv_sems)
    rows = total.shape[0]
    low = jnp.bfloat16
    loads = [
        pltpu.make_async_copy(source, target, load_sems.at[n])
        for n, (source, target) in enumerate(
            (
                (dybt_in, dybt), (active_in, active), (dyb_in, dyb), (down_in, down), (slopes_in, slopes),
                (last_in, last), (h2t_in, h2t), (feed_in, feed), (x1_in, side), (dy_in, side),
            )
        )
    ]
    for load in loads[:2]:
        load.start()
    greet(at)
    hidden = active.shape[1]
    parts, main = feed_lanes(hidden)
    tail = hidden - main
    first = RingScatter(at, dybt, active, down_slots, down_term, down_grad, sems, 0)
    second = RingScatter(
        at, h2t, slopes.at[:, pl.ds(0, main)], gate_slots, gate_term, gate_grad, sems, 28
    )
    group = GatherTensor(at, dyb, rows, sems, 59)
    keeps = []

    def keep(source, target):
        copy = pltpu.make_async_copy(source, target, out_sems.at[len(keeps)])
        copy.start()
        keeps.append(copy)

    loads[0].wait()
    loads[1].wait()
    for load in loads[2:-1]:
        load.start()
    first.start()
    for load in loads[2:6]:
        load.wait()

    def slope_back(first_block, last_block):
        @pl.loop(first_block, last_block)
        def _(j):
            here = pl.ds(pl.multiple_of(j * rows, rows), rows)
            left = dyb[here]
            for own, gate_lanes, up_lanes in parts:
                da = nn_dot(left, down[:, own])
                slopes[here, gate_lanes] = (da * slopes[here, gate_lanes].astype(jnp.float32)).astype(low)
                slopes[here, up_lanes] = (da * slopes[here, up_lanes].astype(jnp.float32)).astype(low)
            da = nn_dot(left, last[:, pl.ds(last.shape[1] - tail, tail)])
            ends = pl.ds(2 * main, 2 * tail)
            both = jnp.concatenate([da, da], axis=1) * slopes[here, ends].astype(jnp.float32)
            slopes[here, ends] = both.astype(low)

    for k in range(4):
        slope_back(k, k + 1)
        first.tick()
    keep(slopes.at[:, pl.ds(main, 2 * hidden - main)], slopes_out)
    loads[6].wait()
    second.start()
    loads[7].wait()
    loads[8].wait()

    def part(block):
        return nt_dot(slopes[pl.ds(pl.multiple_of(block * rows, rows), rows)], feed[...])

    def idle(point):
        first.tick()
        second.tick()
        if point == 2:
            first.tick()
            second.tick()

    sum_rows(at, part, send, receive, total, sems, 56, idle=idle)
    gain_part[...] = jnp.zeros_like(gain_part)

    @chunks_of(rows, 32)
    def _(row, size):
        here = pl.ds(row, size)
        through, term_gain = norm_back(side[here], total[here], row_of(gain))
        gain_part[0:1] += term_gain
        total[here] = through

    loads[9].start()
    first.tick()
    second.tick()
    loads[9].wait()

    @chunks_of(rows, 32)
    def _(row, size):
        here = pl.ds(row, size)
        grad = total[here] + side[here]
        total[here] = grad
        dyb[pl.ds(pl.multiple_of(at["t"] * rows + row, size), size)] = grad.astype(low)

    group.start()
    keep(total, dx1_out)

    def spread(block):
        here = pl.ds(pl.multiple_of(block * rows, rows), rows)
        dybt[:, here] = dyb[here].T
        do[here] = nn_dot(dyb[here], last[:, pl.ds(0, do.shape[1])]).astype(low)

    while first.at < len(first.sends):
        first.tick()
        second.tick()
    spread(at["t"])
    second.tick()
    group.receives[0].wait_recv()
    spread(at["core"])
    second.tick()
    group.relay()
    second.tick()
    spread(at["cross"])
    group.receives[2].wait_recv()
    spread(at["cross_core"])
    group.drain()
    keep(dybt, dx1t_out)
    keep(do, do_out)
    second.finish()
    first.finish()
    for copy in keeps:
        copy.wait()


def feed_backward(gain, dyb, dybt, h2t, down, feed, active, slopes, last, x1, dy):
    rows, width = x1.shape
    depth, main = down.shape
    hidden = active.shape[1]
    local = last.shape[1] - (hidden - main)
    everyone, shard = 4 * rows, depth // 8
    low, wide = jnp.bfloat16, jnp.float32
    vmem, hbm = specs()
    return pl.pallas_call(
        feed_backward_kernel,
        out_shape=(
            shape(shard, hidden, kind=wide),
            shape(shard, main, kind=wide),
            shape(8, width, kind=wide),
            shape(rows, width, kind=wide),
            shape(width, everyone),
            shape(everyone, local),
            shape(everyone, 2 * hidden - main),
        ),
        in_specs=[vmem] + [hbm] * 10,
        out_specs=(vmem,) * 3 + (hbm,) * 4,
        scratch_shapes=[
            pltpu.VMEM((everyone, width), low),
            pltpu.VMEM((width, everyone), low),
            pltpu.VMEM((width, everyone), low),
            pltpu.VMEM((depth, main), low),
            pltpu.VMEM((depth, 2 * hidden), low),
            pltpu.VMEM((everyone, hidden), low),
            pltpu.VMEM((everyone, 2 * hidden), low),
            pltpu.VMEM(last.shape, low),
            pltpu.VMEM((everyone, local), low),
            pltpu.VMEM((rows, width), wide),
            pltpu.VMEM((rows, width), wide),
            pltpu.VMEM((2, 8, shard // 2, hidden), low),
            pltpu.VMEM((2, 8, shard // 2, main), low),
            pltpu.VMEM((shard, hidden), wide),
            pltpu.VMEM((shard, main), wide),
            pltpu.VMEM((3, rows, width), low),
            pltpu.VMEM((3, rows, width), low),
            dma(62),
            dma(62),
            dma(10),
            dma(4),
        ],
        compiler_params=params(3),
    )(gain, dyb, dybt, h2t, down, feed, active, slopes, last, x1, dy)


def mixer_backward_kernel(
    x, gain, same, taps, gain_part, squares,
    dx1t_in, o_in, h2t_in, slopes_in, q_in, k_in, v_in, u_in, p_in, do_in, mix_in, h1t_in, dx1_in,
    out_grad, up_grad, mix_grad, input_grad, small_out, conv_out,
    turned, o, h2t, slopes, q, k_pad, v_pad, u, p, do, mix,
    dk, dv, grads, out_slots, up_slots, mix_slots, out_term, up_term, mix_term, send, receive, total,
    small, small_in, conv, conv_in,
    send_sems, recv_sems, load_sems,
):
    at = neighbours()
    sems = (send_sems, recv_sems)
    rows = total.shape[0]
    low = jnp.bfloat16
    loads = [
        pltpu.make_async_copy(source, target, load_sems.at[n])
        for n, (source, target) in enumerate(
            (
                (dx1t_in, turned), (o_in, o), (h2t_in, h2t), (slopes_in, slopes), (q_in, q), (k_in, k_pad),
                (v_in, v_pad), (u_in, u), (p_in, p), (do_in, do), (mix_in, mix), (dx1_in, input_grad),
                (h1t_in, turned),
            )
        )
    ]
    for load in loads[:4]:
        load.start()
    greet(at, everyone=True)
    local = q.shape[1]
    main = local // LANES * LANES
    tail = local - main
    first = RingScatter(at, turned, o, out_slots, out_term, out_grad, sems, 0, count=1)
    second = RingScatter(at, h2t, slopes, up_slots, up_term, up_grad, sems, 14)
    third = RingScatter(at, turned, grads, mix_slots, mix_term, mix_grad, sems, 42)
    small_sum = SumAll(at, small, small_in, sems, 73)
    conv_all = SumAll(at, conv, conv_in, sems, 78)
    loads[0].wait()
    loads[1].wait()
    first.start()
    loads[2].wait()
    loads[3].wait()
    for load in loads[4:-1]:
        load.start()
    second.start()
    dk[...] = jnp.zeros_like(dk)
    dv[...] = jnp.zeros_like(dv)
    conv[0] = jnp.zeros(conv.shape[1:], jnp.float32)
    first.tick()
    for load in loads[4:10]:
        load.wait()
    tiles = q.shape[0] // TILE
    conv_sum = conv.at[0, at["t"]]

    def attend(a, b):
        @pl.loop(a, b)
        def _(i):
            attend_back_tile(i, q, k_pad, v_pad, u, p, same, taps, do, dk, dv, conv_sum)

    for k in range(8):
        attend(k * tiles // 8, (k + 1) * tiles // 8)
        first.tick()
        second.tick()
    conv_all.start()

    first.finish()
    loads[12].start()
    second.tick()

    @chunks_of(q.shape[0])
    def _(row, size):
        here, there = pl.ds(row, size), pl.ds(pl.multiple_of(row + TILE, TILE), size)
        four = [q[here].astype(jnp.float32), dk[there], dv[there], do[here].astype(jnp.float32)]
        for n, value in enumerate(four):
            grads[here, pl.ds(n * main, main)] = value[:, :main].astype(low)
        ends = jnp.concatenate([value[:, main:] for value in four], axis=1)
        grads[here, pl.ds(4 * main, 4 * tail)] = ends.astype(low)

    second.tick()
    loads[12].wait()
    third.start()
    loads[10].wait()
    loads[11].wait()

    def part(block):
        return nt_dot(grads[pl.ds(pl.multiple_of(block * rows, rows), rows)], mix[...])

    def idle(point):
        second.tick()
        third.tick()
        if point == 2:
            second.tick()
            conv_all.step()

    sum_rows(at, part, send, receive, total, sems, 70, idle=idle)
    small[0, 0:1] = jnp.zeros((1, small.shape[2]), jnp.float32)
    small[0, 1:2] = gain_part[0:1]
    small[0, 2:3] = squares[0:1]
    small[0, 3:8] = jnp.zeros((5, small.shape[2]), jnp.float32)

    @chunks_of(rows, 32)
    def _(row, size):
        here = pl.ds(row, size)
        through, term_gain = norm_back(x[here].astype(jnp.float32), total[here], row_of(gain))
        small[0, 0:1] += term_gain
        input_grad[here] += through

    small_sum.start()
    second.finish()
    for k in range(5):
        third.tick()
        if k > 0:
            conv_all.step()
        third.tick()
        small_sum.step()
    third.finish()
    small_sum.finish()
    conv_all.finish()
    small_out[...] = small[5]
    conv_out[...] = conv[5]


def mixer_backward(
    x, gain, same, taps, gain_part, squares, dx1t, o, h2t, slopes, q, k_pad, v_pad, u, p, do, mix, h1t, dx1
):
    rows, width = x.shape
    everyone, local = o.shape
    shard, ups = width // 8, slopes.shape[1]
    low, wide = jnp.bfloat16, jnp.float32
    vmem, hbm = specs()
    arrays = (dx1t, o, h2t, slopes, q, k_pad, v_pad, u, p, do, mix)
    return pl.pallas_call(
        mixer_backward_kernel,
        out_shape=(
            shape(shard, local, kind=wide),
            shape(shard, ups, kind=wide),
            shape(shard, 4 * local, kind=wide),
            shape(rows, width, kind=wide),
            shape(8, width, kind=wide),
            shape(4, 8, local, kind=wide),
        ),
        in_specs=[vmem] * 6 + [hbm] * 13,
        out_specs=(vmem,) * 6,
        scratch_shapes=[pltpu.VMEM(array.shape, array.dtype) for array in arrays]
        + [
            pltpu.VMEM((everyone + TILE, local), wide),
            pltpu.VMEM((everyone + TILE, local), wide),
            pltpu.VMEM((everyone, 4 * local), low),
            pltpu.VMEM((2, 8, shard // 2, local), low),
            pltpu.VMEM((2, 8, shard // 2, ups), low),
            pltpu.VMEM((2, 8, shard // 2, 4 * local), low),
            pltpu.VMEM((shard, local), wide),
            pltpu.VMEM((shard, ups), wide),
            pltpu.VMEM((shard, 4 * local), wide),
            pltpu.VMEM((3, rows, width), low),
            pltpu.VMEM((3, rows, width), low),
            pltpu.VMEM((rows, width), wide),
            pltpu.VMEM((6, 8, width), wide),
            pltpu.VMEM((5, 8, width), wide),
            pltpu.VMEM((6, 4, 8, local), wide),
            pltpu.VMEM((5, 4, 8, local), wide),
            dma(83),
            dma(83),
            dma(13),
        ],
        compiler_params=params(4),
    )(x, gain, same, taps, gain_part, squares, *arrays, h1t, dx1)


def finish_kernel(
    count, down_grad, gate_main, up_rest, mix_grad, out_grad, small, conv, act_in, input_in,
    loss, act, input_grad, query, key, value, mixgate, output, conv_grad, gain_one, gain_two, gate, up, down,
):
    act[...] = act_in[...]
    input_grad[...] = input_in[...]
    local = query.shape[1]
    main = local // LANES * LANES
    tail = local - main
    for n, target in enumerate((query, key, value, mixgate)):
        target[:, pl.ds(0, main)] = mix_grad[:, pl.ds(n * main, main)]
        target[:, pl.ds(main, tail)] = mix_grad[:, pl.ds(4 * main, 4 * tail)][:, n * tail : (n + 1) * tail]
    cut = gate_main.shape[1]
    rest = gate.shape[1] - cut
    ends = up_rest[:, pl.ds(cut, 2 * rest)]
    gate[:, pl.ds(0, cut)] = gate_main[...]
    gate[:, pl.ds(cut, rest)] = ends[:, :rest]
    up[:, pl.ds(0, cut)] = up_rest[:, pl.ds(0, cut)]
    up[:, pl.ds(cut, rest)] = ends[:, rest:]
    output[...] = out_grad[...].T
    down[...] = down_grad[...]
    conv_grad[...] = jnp.concatenate([conv[n, 0:CONV] for n in range(conv.shape[0])], axis=1)
    gain_one[...] = small[0]
    gain_two[...] = small[1]
    total = jnp.sum(small[2:3], axis=1, keepdims=True) / (count[0:1, 0:1] * D)
    loss[...] = total


def finish(count, down_grad, gate_main, up_rest, mix_grad, out_grad, small, conv, act, input_grad):
    vmem, _ = specs()
    wide = jnp.float32
    shard, hidden = down_grad.shape
    local, width = out_grad.shape[1], small.shape[1]
    square = shape(shard, local, kind=wide)
    broad = shape(shard, hidden, kind=wide)
    return pl.pallas_call(
        finish_kernel,
        out_shape=(
            shape(1, 1, kind=wide),
            shape(*act.shape, kind=wide),
            shape(*input_grad.shape, kind=wide),
            square,
            square,
            square,
            square,
            shape(local, shard, kind=wide),
            shape(CONV, width, kind=wide),
            shape(width, kind=wide),
            shape(width, kind=wide),
            broad,
            broad,
            broad,
        ),
        in_specs=[vmem] * 10,
        out_specs=(vmem,) * 14,
        compiler_params=pltpu.CompilerParams(vmem_limit_bytes=VMEM_LIMIT),
    )(count, down_grad, gate_main, up_rest, mix_grad, out_grad, small, conv, act, input_grad)


def pack(*weights):
    main = weights[0].shape[1] // LANES * LANES
    return jnp.concatenate([w[:, :main] for w in weights] + [w[:, main:] for w in weights], axis=1)


def on_rings(
    block_input,
    cotangent,
    teacher,
    segments,
    valid_mask,
    query_weight,
    key_weight,
    value_weight,
    mixgate_weight,
    output_weight,
    conv_weight,
    gain_mixer,
    gain_feed,
    gate_weight,
    up_weight,
    down_weight,
):
    local = query_weight.shape[1]
    taps = lax.dynamic_slice_in_dim(conv_weight, lax.axis_index("tensor") * local, local, 1)
    cut = down_weight.shape[0] // LANES * LANES
    down_own = down_weight.T
    (
        mix, last, feed, down, h1t, h2t, dybt, q, k_pad, v_pad, u, p, o, x1, dyb, slopes, active,
        outputs, dy, count, squares, same,
    ) = forward(
        block_input, valid_mask.reshape(-1, LANES), gain_mixer, gain_feed, segments.reshape(-1, LANES), taps,
        pack(query_weight, key_weight, value_weight, mixgate_weight),
        jnp.concatenate([output_weight.T, down_own[:, cut:]], axis=1), gate_weight, up_weight, down_own,
        cotangent, teacher,
    )
    down_grad, gate_main, gain_part, dx1, dx1t, do, slopes_up = feed_backward(
        gain_feed, dyb, dybt, h2t, down, feed, active, slopes, last, x1, dy
    )
    out_grad, up_rest, mix_grad, input_grad, small, conv = mixer_backward(
        block_input, gain_mixer, same, taps, gain_part, squares, dx1t, o, h2t, slopes_up, q, k_pad, v_pad,
        u, p, do, mix, h1t, dx1,
    )
    loss, *rest, down_turned = finish(
        count, down_grad, gate_main, up_rest, mix_grad, out_grad, small, conv, outputs, input_grad
    )
    return (loss.reshape(()), *rest, down_turned.T)


def on_any_mesh(
    block_input,
    cotangent,
    teacher,
    segments,
    valid_mask,
    query_weight,
    key_weight,
    value_weight,
    mixgate_weight,
    output_weight,
    conv_weight,
    gain_mixer,
    gain_feed,
    gate_weight,
    up_weight,
    down_weight,
):
    rows = block_input.shape[0]
    valid_rows = valid_mask.astype(jnp.float32)
    valid_total = sum_all(jnp.full((8, 128), jnp.sum(valid_rows), jnp.float32))[0, 0]
    local_width = query_weight.shape[1]
    local_hidden = gate_weight.shape[1]
    mixer_own = jnp.concatenate(
        [query_weight, key_weight, value_weight, mixgate_weight, output_weight.T], axis=1
    )
    feed_own = jnp.concatenate([gate_weight, up_weight], axis=1)
    mixer_all = gather_dp(mixer_own).reshape(D, -1)
    feed_all = gather_dp(feed_own).reshape(D, -1)
    full_down = gather_dp(down_weight.T).reshape(D, -1)
    full_query, full_key, full_value, full_mixgate, full_output = jnp.split(mixer_all, 5, axis=1)
    full_gate, full_upward = jnp.split(feed_all, 2, axis=1)
    column = lax.axis_index("tensor") * local_width
    conv_local = lax.dynamic_slice_in_dim(conv_weight, column, local_width, 1)
    inputs = block_input.astype(jnp.float32)
    scale_one = rms_scale(inputs)
    normed_one = inputs * scale_one
    group_one = gather_tensor((normed_one * gain_mixer).astype(jnp.bfloat16))
    queries = jnp.dot(group_one, full_query, preferred_element_type=jnp.float32).astype(
        jnp.bfloat16
    )
    key_rows = jnp.dot(group_one, full_key, preferred_element_type=jnp.float32).astype(jnp.bfloat16)
    value_rows = jnp.dot(group_one, full_value, preferred_element_type=jnp.float32).astype(
        jnp.bfloat16
    )
    mix_gate = jnp.dot(group_one, full_mixgate, preferred_element_type=jnp.float32).astype(
        jnp.bfloat16
    )
    attended, log_totals = attend_forward(queries, key_rows, value_rows, segments)
    value_float = value_rows.astype(jnp.float32)
    convolved = jnp.zeros_like(value_float)
    for offset in range(CONV):
        convolved = convolved + conv_local[offset] * shift_down(value_float, segments, offset)
    gate_float = mix_gate.astype(jnp.float32)
    mixer_out = (attended + convolved * gate_float).astype(jnp.bfloat16)
    mixer_part = cols_inner(mixer_out, full_output)
    hidden = inputs + scatter_tensor(mixer_part)
    scale_two = rms_scale(hidden)
    normed_two = hidden * scale_two
    group_two = gather_tensor((normed_two * gain_feed).astype(jnp.bfloat16))
    gate_value = jnp.dot(group_two, full_gate, preferred_element_type=jnp.float32)
    up_value = jnp.dot(group_two, full_upward, preferred_element_type=jnp.float32)
    sigmoid_gate = jax.nn.sigmoid(gate_value)
    silu_gate = gate_value * sigmoid_gate
    active = (silu_gate * up_value).astype(jnp.bfloat16)
    feed_part = cols_inner(active, full_down)
    outputs = hidden + scatter_tensor(feed_part)
    target = teacher.astype(jnp.float32)
    deviation = outputs - target
    squares = jnp.sum(valid_rows[:, None] * deviation * deviation)
    all_tokens = rows * lax.axis_size("dp") * lax.axis_size("tensor")
    grad_out = cotangent + valid_rows[:, None] * deviation * (all_tokens / valid_total)
    grad_feed = gather_tensor(grad_out.astype(jnp.bfloat16))
    down_part = rows_inner(grad_feed, active)
    down_grad = scatter_dp(down_part.astype(jnp.bfloat16).reshape(-1, down_weight.shape[1], local_hidden)).T
    grad_active = jnp.dot(grad_feed, full_down, preferred_element_type=jnp.float32)
    silu_slope = sigmoid_gate * (1.0 + gate_value * (1.0 - sigmoid_gate))
    grad_gate = (grad_active * up_value * silu_slope).astype(jnp.bfloat16)
    grad_upward = (grad_active * silu_gate).astype(jnp.bfloat16)
    grad_normed_two = cols_inner(grad_gate, full_gate) + cols_inner(grad_upward, full_upward)
    grad_rows_two = scatter_tensor(grad_normed_two)
    gate_part = rows_inner(group_two, grad_gate)
    up_part = rows_inner(group_two, grad_upward)
    shard = gate_weight.shape[0]
    gate_grad = scatter_dp(gate_part.astype(jnp.bfloat16).reshape(-1, shard, local_hidden))
    up_grad = scatter_dp(up_part.astype(jnp.bfloat16).reshape(-1, shard, local_hidden))
    gainfeed_part = jnp.sum(grad_rows_two * normed_two, axis=0)
    scaled_two = grad_rows_two * gain_feed
    grad_hidden = grad_out + scale_two * (
        scaled_two - normed_two * jnp.mean(scaled_two * normed_two, axis=1, keepdims=True)
    )
    grad_mixer = gather_tensor(grad_hidden.astype(jnp.bfloat16))
    output_part = rows_inner(grad_mixer, mixer_out)
    output_grad = scatter_dp(output_part.astype(jnp.bfloat16).reshape(-1, shard, local_width)).T
    grad_mixed = jnp.dot(grad_mixer, full_output, preferred_element_type=jnp.float32).astype(jnp.bfloat16)
    grad_mixed_float = grad_mixed.astype(jnp.float32)
    grad_mixgate = (grad_mixed_float * convolved).astype(jnp.bfloat16)
    grad_conv_out = grad_mixed_float * gate_float
    conv_rows = []
    value_from_conv = jnp.zeros_like(value_float)
    for offset in range(CONV):
        conv_rows.append(jnp.sum(grad_conv_out * shift_down(value_float, segments, offset), axis=0))
        value_from_conv = value_from_conv + conv_local[offset] * shift_up(
            grad_conv_out, segments, offset
        )
    grad_queries, key_float, value_attn = attend_backward(
        queries, key_rows, value_rows, segments, log_totals, grad_mixed
    )
    grad_keys = key_float.astype(jnp.bfloat16)
    grad_values = (value_attn + value_from_conv).astype(jnp.bfloat16)

    def project_grad(grads):
        part = rows_inner(group_one, grads).astype(jnp.bfloat16)
        return scatter_dp(part.reshape(-1, shard, local_width))

    query_grad = project_grad(grad_queries)
    key_grad = project_grad(grad_keys)
    value_grad = project_grad(grad_values)
    mixgate_grad = project_grad(grad_mixgate)
    grad_normed_one = (
        cols_inner(grad_queries, full_query)
        + cols_inner(grad_keys, full_key)
        + cols_inner(grad_values, full_value)
        + cols_inner(grad_mixgate, full_mixgate)
    )
    grad_rows_one = scatter_tensor(grad_normed_one)
    gainmix_part = jnp.sum(grad_rows_one * normed_one, axis=0)
    scaled_one = grad_rows_one * gain_mixer
    input_grad = grad_hidden + scale_one * (
        scaled_one - normed_one * jnp.mean(scaled_one * normed_one, axis=1, keepdims=True)
    )
    conv_full = lax.dynamic_update_slice_in_dim(
        jnp.zeros((CONV, D), jnp.float32), jnp.stack(conv_rows), column, 1
    )
    small = sum_all(
        jnp.concatenate(
            [
                conv_full,
                gainmix_part[None],
                gainfeed_part[None],
                jnp.full((1, D), squares, jnp.float32),
            ]
        )
    )
    conv_grad, gainmix_grad, gainfeed_grad = small[:CONV], small[CONV], small[CONV + 1]
    mean_loss = small[CONV + 2, 0] / (valid_total * D)
    return (
        mean_loss,
        outputs,
        input_grad,
        query_grad,
        key_grad,
        value_grad,
        mixgate_grad,
        output_grad,
        conv_grad,
        gainmix_grad,
        gainfeed_grad,
        gate_grad,
        up_grad,
        down_grad,
    )


def solution(mesh):
    rings = mesh.shape["dp"] == 8 and mesh.shape["tensor"] == 4
    return jax.shard_map(
        on_rings if rings else on_any_mesh,
        mesh=mesh,
        in_specs=(
            P(("dp", "tensor"), None),
            P(("dp", "tensor"), None),
            P(("dp", "tensor"), None),
            P("dp"),
            P(("dp", "tensor")),
            P("dp", "tensor"),
            P("dp", "tensor"),
            P("dp", "tensor"),
            P("dp", "tensor"),
            P("tensor", "dp"),
            P(),
            P(),
            P(),
            P("dp", "tensor"),
            P("dp", "tensor"),
            P("tensor", "dp"),
        ),
        out_specs=(
            P(),
            P(("dp", "tensor"), None),
            P(("dp", "tensor"), None),
            P("dp", "tensor"),
            P("dp", "tensor"),
            P("dp", "tensor"),
            P("dp", "tensor"),
            P("tensor", "dp"),
            P(),
            P(),
            P(),
            P("dp", "tensor"),
            P("dp", "tensor"),
            P("tensor", "dp"),
        ),
        check_vma=False,
    )
```

```python
import jax
import jax.numpy as jnp
from jax import lax
from jax.experimental import pallas as pl
from jax.experimental.pallas import tpu as pltpu
from jax.sharding import PartitionSpec as P

D = 1792
HEAD_DIM = 64
WINDOW = 64
CONV = 3
BLOCK = 512
EPS = 1e-05
MESH = pl.DeviceIdType.MESH
VMEM_LIMIT = 63 * 2**20


def rms_scale(values):
    return lax.rsqrt(jnp.mean(values * values, axis=1, keepdims=True) + EPS)


def rows_inner(matrix_left, matrix_right):
    return lax.dot_general(
        matrix_left, matrix_right, (((0,), (0,)), ((), ())), preferred_element_type=jnp.float32
    )


def cols_inner(matrix_left, matrix_right):
    return lax.dot_general(
        matrix_left, matrix_right, (((1,), (1,)), ((), ())), preferred_element_type=jnp.float32
    )


def shift_down(values, segments, offset):
    if offset == 0:
        return values
    shifted = jnp.concatenate(
        [jnp.zeros((offset, values.shape[1]), values.dtype), values[: values.shape[0] - offset]],
        axis=0,
    )
    same_doc = jnp.concatenate(
        [jnp.zeros((offset,), bool), segments[offset:] == segments[:-offset]]
    )
    return jnp.where(same_doc[:, None], shifted, 0.0)


def shift_up(values, segments, offset):
    if offset == 0:
        return values
    shifted = jnp.concatenate(
        [values[offset:], jnp.zeros((offset, values.shape[1]), values.dtype)], axis=0
    )
    same_doc = jnp.concatenate(
        [segments[:-offset] == segments[offset:], jnp.zeros((offset,), bool)]
    )
    return jnp.where(same_doc[:, None], shifted, 0.0)


def pad_front(array, fill_value):
    front = jnp.full((WINDOW,) + array.shape[1:], fill_value, array.dtype)
    return jnp.concatenate([front, array], axis=0)


def block_setup(queries, key_pad, seg_pad, segments, row_start, head_count):
    score_scale = HEAD_DIM ** (-0.5)
    query_rows = lax.dynamic_slice_in_dim(queries, row_start, BLOCK, 0).reshape(
        BLOCK, head_count, HEAD_DIM
    )
    key_block = lax.dynamic_slice_in_dim(key_pad, row_start, BLOCK + WINDOW, 0).reshape(
        BLOCK + WINDOW, head_count, HEAD_DIM
    )
    seg_rows = lax.dynamic_slice_in_dim(segments, row_start, BLOCK, 0)
    seg_keys = lax.dynamic_slice_in_dim(seg_pad, row_start, BLOCK + WINDOW, 0)
    distance = (
        jnp.arange(BLOCK, dtype=jnp.int32)[:, None]
        + WINDOW
        - jnp.arange(BLOCK + WINDOW, dtype=jnp.int32)[None, :]
    )
    allowed = (distance >= 0) & (distance < WINDOW) & (seg_rows[:, None] == seg_keys[None, :])
    scores = (
        jnp.einsum("qhd,khd->hqk", query_rows, key_block, preferred_element_type=jnp.float32)
        * score_scale
    )
    return (query_rows, key_block, jnp.where(allowed[None], scores, -1e30))


def attend_forward(queries, key_rows, value_rows, segments):
    group_rows, local_width = queries.shape
    head_count = local_width // HEAD_DIM
    key_pad = pad_front(key_rows, 0)
    value_pad = pad_front(value_rows, 0)
    seg_pad = pad_front(segments, -1)

    def one_block(block_index):
        row_start = block_index * BLOCK
        query_rows, key_block, scores = block_setup(
            queries, key_pad, seg_pad, segments, row_start, head_count
        )
        row_max = jnp.max(scores, axis=-1, keepdims=True)
        exponent = jnp.exp(scores - row_max)
        row_total = jnp.sum(exponent, axis=-1, keepdims=True)
        attention = (exponent / row_total).astype(jnp.bfloat16)
        value_block = lax.dynamic_slice_in_dim(value_pad, row_start, BLOCK + WINDOW, 0).reshape(
            BLOCK + WINDOW, head_count, HEAD_DIM
        )
        mixed_rows = jnp.einsum(
            "hqk,khd->qhd", attention, value_block, preferred_element_type=jnp.float32
        )
        return (
            mixed_rows.reshape(BLOCK, local_width),
            row_max[..., 0] + jnp.log(row_total[..., 0]),
        )

    blocks_out, log_totals = lax.map(one_block, jnp.arange(group_rows // BLOCK, dtype=jnp.int32))
    return (blocks_out.reshape(group_rows, local_width), log_totals)


def attend_backward(queries, key_rows, value_rows, segments, log_totals, grad_mixed):
    group_rows, local_width = queries.shape
    head_count = local_width // HEAD_DIM
    score_scale = HEAD_DIM ** (-0.5)
    key_pad = pad_front(key_rows, 0)
    value_pad = pad_front(value_rows, 0)
    seg_pad = pad_front(segments, -1)

    def one_block(accumulated, block_pair):
        block_index, log_block = block_pair
        row_start = block_index * BLOCK
        query_rows, key_block, scores = block_setup(
            queries, key_pad, seg_pad, segments, row_start, head_count
        )
        attention = jnp.exp(scores - log_block[..., None])
        value_block = lax.dynamic_slice_in_dim(value_pad, row_start, BLOCK + WINDOW, 0).reshape(
            BLOCK + WINDOW, head_count, HEAD_DIM
        )
        grad_block = lax.dynamic_slice_in_dim(grad_mixed, row_start, BLOCK, 0).reshape(
            BLOCK, head_count, HEAD_DIM
        )
        grad_attention = jnp.einsum(
            "qhd,khd->hqk", grad_block, value_block, preferred_element_type=jnp.float32
        )
        row_inner = jnp.sum(attention * grad_attention, axis=-1, keepdims=True)
        grad_scores = (attention * (grad_attention - row_inner)).astype(jnp.bfloat16)
        grad_query = (
            jnp.einsum("hqk,khd->qhd", grad_scores, key_block, preferred_element_type=jnp.float32)
            * score_scale
        )
        grad_key = (
            jnp.einsum("hqk,qhd->khd", grad_scores, query_rows, preferred_element_type=jnp.float32)
            * score_scale
        )
        grad_value = jnp.einsum(
            "hqk,qhd->khd",
            attention.astype(jnp.bfloat16),
            grad_block,
            preferred_element_type=jnp.float32,
        )
        key_acc, value_acc = accumulated
        key_acc = lax.dynamic_update_slice_in_dim(
            key_acc,
            lax.dynamic_slice_in_dim(key_acc, row_start, BLOCK + WINDOW, 0)
            + grad_key.reshape(BLOCK + WINDOW, local_width),
            row_start,
            0,
        )
        value_acc = lax.dynamic_update_slice_in_dim(
            value_acc,
            lax.dynamic_slice_in_dim(value_acc, row_start, BLOCK + WINDOW, 0)
            + grad_value.reshape(BLOCK + WINDOW, local_width),
            row_start,
            0,
        )
        return ((key_acc, value_acc), grad_query.astype(jnp.bfloat16).reshape(BLOCK, local_width))

    zeros_pad = jnp.zeros((group_rows + WINDOW, local_width), jnp.float32)
    block_ids = jnp.arange(group_rows // BLOCK, dtype=jnp.int32)
    (key_acc, value_acc), query_blocks = lax.scan(
        one_block, (zeros_pad, zeros_pad), (block_ids, log_totals)
    )
    return (query_blocks.reshape(group_rows, local_width), key_acc[WINDOW:], value_acc[WINDOW:])


def pairs_xor(size, mask):
    return [(i, i ^ mask) for i in range(size)]


def pairs_shift(size, step):
    return [(i, (i + step) % size) for i in range(size)]


def put(buffer, block, index):
    return lax.dynamic_update_slice_in_dim(buffer, block[None], index, 0)


def pick(blocks, index):
    return lax.dynamic_index_in_dim(blocks, index, 0, keepdims=False)


def gather_dp(own):
    size = lax.axis_size("dp")
    if size != 8:
        return lax.all_gather(own, "dp", axis=0)
    me = lax.axis_index("dp")
    over_y = pairs_xor(size, 1)
    up, down = pairs_shift(size, 2), pairs_shift(size, -2)
    mate = lax.ppermute(own, "dp", over_y)
    own_below = lax.ppermute(own, "dp", up)
    own_above = lax.ppermute(own, "dp", down)
    mate_below = lax.ppermute(mate, "dp", up)
    mate_above = lax.ppermute(mate, "dp", down)
    own_far = lax.ppermute(own_below, "dp", up)
    mate_far = lax.ppermute(mate_above, "dp", down)
    below, above, far = (me + 6) % size, (me + 2) % size, (me + 4) % size
    full = jnp.zeros((size,) + own.shape, own.dtype)
    for block, index in (
        (own, me),
        (mate, me ^ 1),
        (own_below, below),
        (own_above, above),
        (mate_below, below ^ 1),
        (mate_above, above ^ 1),
        (own_far, far),
        (mate_far, far ^ 1),
    ):
        full = put(full, block, index)
    return full


def scatter_dp(parts):
    size = lax.axis_size("dp")
    if size != 8:
        return lax.psum_scatter(parts, "dp", scatter_dimension=0).astype(jnp.float32)
    me = lax.axis_index("dp")
    over_y = pairs_xor(size, 1)
    up, down = pairs_shift(size, 2), pairs_shift(size, -2)
    below, above, far = (me + 6) % size, (me + 2) % size, (me + 4) % size

    def part(index):
        return pick(parts, index).astype(jnp.float32)

    low = jnp.bfloat16
    own_first = lax.ppermute(pick(parts, far), "dp", up)
    mate_first = lax.ppermute(pick(parts, far ^ 1), "dp", down)
    mate_from_below = lax.ppermute(pick(parts, above ^ 1), "dp", up)
    own_from_above = lax.ppermute(pick(parts, below), "dp", down)
    mate_from_above = lax.ppermute(
        (part(below ^ 1) + mate_first.astype(jnp.float32)).astype(low), "dp", down
    )
    own_from_below = lax.ppermute(
        (part(above) + own_first.astype(jnp.float32)).astype(low), "dp", up
    )
    mate_sum = (
        part(me ^ 1)
        + mate_from_below.astype(jnp.float32)
        + mate_from_above.astype(jnp.float32)
    )
    from_mate = lax.ppermute(mate_sum.astype(low), "dp", over_y)
    own_sum = part(me) + own_from_below.astype(jnp.float32) + own_from_above.astype(jnp.float32)
    return own_sum + from_mate.astype(jnp.float32)


def gather_tensor(own):
    size = lax.axis_size("tensor")
    if size != 4:
        return lax.all_gather(own, "tensor", axis=0, tiled=True)
    me = lax.axis_index("tensor")
    across = lax.ppermute(own, "tensor", pairs_xor(size, 2))
    beside = lax.ppermute(own, "tensor", pairs_xor(size, 1))
    beside_across = lax.ppermute(across, "tensor", pairs_xor(size, 1))
    full = jnp.zeros((size,) + own.shape, own.dtype)
    for block, index in ((own, me), (beside, me ^ 1), (across, me ^ 2), (beside_across, me ^ 3)):
        full = put(full, block, index)
    return full.reshape(size * own.shape[0], own.shape[1])


def scatter_tensor(parts):
    size = lax.axis_size("tensor")
    if size != 4:
        return lax.psum_scatter(
            parts.astype(jnp.bfloat16), "tensor", scatter_dimension=0, tiled=True
        ).astype(jnp.float32)
    me = lax.axis_index("tensor")
    low = jnp.bfloat16
    parts = parts.reshape(size, -1, parts.shape[1])
    beside = lax.ppermute(pick(parts, me ^ 3).astype(low), "tensor", pairs_xor(size, 1))
    sent = (pick(parts, me ^ 2).astype(jnp.float32) + beside.astype(jnp.float32)).astype(low)
    across = lax.ppermute(sent, "tensor", pairs_xor(size, 2))
    beside_own = lax.ppermute(pick(parts, me ^ 1).astype(low), "tensor", pairs_xor(size, 1))
    return (
        pick(parts, me).astype(jnp.float32)
        + beside_own.astype(jnp.float32)
        + across.astype(jnp.float32)
    )


def sum_all(values):
    dp_size, tensor_size = lax.axis_size("dp"), lax.axis_size("tensor")
    if dp_size != 8 or tensor_size != 4:
        return lax.psum(values, ("dp", "tensor"))
    for axis, size, mask in (
        ("tensor", tensor_size, 1),
        ("tensor", tensor_size, 2),
        ("dp", dp_size, 1),
        ("dp", dp_size, 2),
        ("dp", dp_size, 6),
    ):
        values = values + lax.ppermute(values, axis, pairs_xor(size, mask))
    return values


TILE = 64
LANES = 128
PIECES = 4
SHARE = 2


def neighbours():
    d, t = lax.axis_index("dp"), lax.axis_index("tensor")
    z, y = d // 2, lax.rem(d, 2)
    core = t + 1 - 2 * lax.rem(t, 2)
    place = z + y * (7 - 2 * z)

    def ring(offset):
        position = lax.rem(place + offset + 16, 8)
        side = position // 4
        return 2 * (position + side * (7 - 2 * position)) + side

    return dict(
        d=d,
        t=t,
        ring=ring,
        core=core,
        cross=lax.rem(t + 2, 4),
        cross_core=lax.rem(core + 2, 4),
        mate=d + 1 - 2 * y,
        z_pair=2 * (z + 1 - 2 * lax.rem(z, 2)) + y,
        z_mirror=2 * (3 - z) + y,
    )


def hail(at, everyone=False):
    d, t = at["d"], at["t"]
    devices = [(at["ring"](1), t), (at["ring"](-1), t), (d, at["core"]), (d, at["cross"])]
    if everyone:
        devices += [(at["mate"], t), (at["z_pair"], t), (at["z_mirror"], t)]
    for device in devices:
        pl.semaphore_signal(
            pltpu.get_barrier_semaphore(), inc=1, device_id=device, device_id_type=MESH
        )
    return len(devices)


def meet(number):
    pl.semaphore_wait(pltpu.get_barrier_semaphore(), number)


def remote(source, target, sems, index, device):
    return pltpu.make_async_remote_copy(
        src_ref=source,
        dst_ref=target,
        send_sem=sems[0].at[index],
        recv_sem=sems[1].at[index],
        device_id=device,
        device_id_type=MESH,
    )


def pieces_of(half, count):
    if count == 1:
        return [(0, half)]
    first = (half // 2 + 15) // 16 * 16
    return [(0, first), (first, half - first)]


class RingGather:
    def __init__(self, at, own, slot, sems, base, local_sem, count=2):
        half = own.shape[0] // 2
        ring, t = at["ring"], at["t"]
        self.local = pltpu.make_async_copy(own, slot(at["d"], 0, 2 * half), local_sem)
        self.sends, self.receives, self.at = [], [], 0
        for s in range(7):
            for k, (first, size) in enumerate(pieces_of(half, count)):
                sends, receives = [], []
                for way, sign in ((0, 1), (1, -1)):
                    to, row = (ring(sign), t), way * half + first
                    index = base + (s * count + k) * 2 + way
                    here = slot(ring(-sign * s), row, size)
                    there = slot(ring(-sign * (s + 1)), row, size)
                    source = own.at[pl.ds(row, size)] if s == 0 else here
                    sends.append(remote(source, here, sems, index, to))
                    receives.append(remote(there, there, sems, index, to))
                self.sends.append(sends)
                self.receives.append(receives)
        self.count = count

    def start(self):
        for copies in self.sends[: self.count]:
            for copy in copies:
                copy.start()
        self.local.start()

    def tick(self):
        if self.at < len(self.receives):
            for way in range(2):
                self.receives[self.at][way].wait_recv()
                if self.at + self.count < len(self.sends):
                    self.sends[self.at + self.count][way].start()
            self.at += 1

    def finish(self):
        while self.at < len(self.receives):
            self.tick()
        self.local.wait()

    def drain(self):
        for sends in self.sends:
            for copy in sends:
                copy.wait_send()


class RingScatter:
    def __init__(self, at, left, right, slots, term, out, sems, base, count=2, side=None):
        self.ring, self.left, self.right, self.side = at["ring"], left, right, side
        self.slots, self.term, self.out = slots, term, out
        self.half, self.columns = slots.shape[2], slots.shape[3]
        self.pieces = pieces_of(self.half, count)
        self.at = 0
        self.sends = []
        for s in range(7):
            for k, (first, size) in enumerate(self.pieces):
                rows = pl.ds(first, size)
                self.sends.append(
                    [
                        remote(
                            slots.at[way, s, rows], slots.at[way, s + 1, rows], sems,
                            base + (s * count + k) * 2 + way, (at["ring"](sign), at["t"]),
                        )
                        for way, sign in ((0, 1), (1, -1))
                    ]
                )

    def compute(self, away):
        half = self.half
        first = pl.multiple_of(self.ring(-away) * 2 * half, half)
        second = pl.multiple_of(self.ring(away) * 2 * half + half, half)
        if self.side is not None:
            left, beside = [
                jnp.concatenate([ref[pl.ds(first, half)], ref[pl.ds(second, half)]], axis=0)
                for ref in (self.left, self.side)
            ]
            self.term[...] = jnp.concatenate(
                [nn_dot(left, self.right[...]), beside.astype(jnp.float32)], axis=1
            )
            return
        width = 512
        whole = self.columns // width * width

        def block(lanes):
            left = jnp.concatenate(
                [self.left[pl.ds(first, half)], self.left[pl.ds(second, half)]], axis=0
            )
            self.term[:, lanes] = nn_dot(left, self.right[:, lanes])

        @pl.loop(0, whole // width)
        def _(i):
            block(pl.ds(pl.multiple_of(i * width, width), width))

        if whole < self.columns:
            block(pl.ds(whole, self.columns - whole))

    def prepare(self):
        self.compute(1)
        for way in range(2):
            self.slots[way, 0] = self.term[pl.ds(way * self.half, self.half)].astype(jnp.bfloat16)

    def launch(self):
        for k in range(len(self.pieces)):
            for way in range(2):
                self.sends[k][way].start()

    def start(self):
        self.prepare()
        self.launch()
        self.compute(2)

    def tick(self):
        if self.at == len(self.sends):
            return
        count = len(self.pieces)
        s, k = divmod(self.at, count)
        first, size = self.pieces[k]
        for way in range(2):
            here, rows = pl.ds(first, size), pl.ds(way * self.half + first, size)
            self.sends[self.at][way].wait_recv()
            total = self.slots[way, s + 1, here].astype(jnp.float32) + self.term[rows]
            if s < 6:
                self.slots[way, s + 1, here] = total.astype(jnp.bfloat16)
                self.sends[self.at + count][way].start()
            else:
                self.out[rows] = total
        self.at += 1
        if k == count - 1 and s < 6:
            self.compute(s + 3)

    def finish(self):
        while self.at < len(self.sends):
            self.tick()
        for sends in self.sends:
            for copy in sends:
                copy.wait_send()


class GatherTensor:
    def __init__(self, at, full, rows, sems, base):
        def block(index):
            return full.at[pl.ds(pl.multiple_of(index * rows, rows), rows)]

        mine, across = block(at["t"]), block(at["cross"])
        self.to_core = remote(mine, mine, sems, base, (at["d"], at["core"]))
        self.to_cross = remote(mine, mine, sems, base + 1, (at["d"], at["cross"]))
        self.relay_core = remote(across, across, sems, base + 2, (at["d"], at["core"]))
        places = (block(at["core"]), across, block(at["cross_core"]))
        self.receives = [
            remote(place, place, sems, base + k, (at["d"], at["core"]))
            for k, place in enumerate(places)
        ]

    def start(self):
        self.to_cross.start()
        self.to_core.start()

    def relay(self):
        self.receives[1].wait_recv()
        self.relay_core.start()

    def drain(self):
        for send in (self.to_core, self.to_cross, self.relay_core):
            send.wait_send()

    def finish(self):
        self.receives[0].wait_recv()
        self.receives[2].wait_recv()
        self.drain()


def sum_rows(at, block_part, send, receive, total, sems, base, idle=lambda point: None):
    to_core, to_cross = (at["d"], at["core"]), (at["d"], at["cross"])
    low = jnp.bfloat16
    first = remote(send.at[0], receive.at[0], sems, base, to_core)
    second = remote(send.at[1], receive.at[1], sems, base + 1, to_cross)
    third = remote(send.at[2], receive.at[2], sems, base + 2, to_core)
    send[0] = block_part(at["cross_core"]).astype(low)
    first.start()
    total[...] = block_part(at["cross"])
    first.wait_recv()
    send[1] = (total[...] + receive[0].astype(jnp.float32)).astype(low)
    second.start()
    idle(0)
    send[2] = block_part(at["core"]).astype(low)
    third.start()
    idle(1)
    total[...] = block_part(at["t"])
    third.wait_recv()
    total[...] += receive[2].astype(jnp.float32)
    idle(2)
    second.wait_recv()
    total[...] += receive[1].astype(jnp.float32)
    for copy in (first, second, third):
        copy.wait_send()


class GatherPieces:
    def __init__(self, at, full, rows, count, sems, base):
        size = rows // count
        to_core, to_cross = (at["d"], at["core"]), (at["d"], at["cross"])

        def place(block, c):
            return full.at[pl.ds(pl.multiple_of(block * rows + c * size, size), size)]

        def copies(k, block, to):
            return [
                remote(place(block, c), place(block, c), sems, base + k * count + c, to)
                for c in range(count)
            ]

        self.to_core = copies(0, at["t"], to_core)
        self.to_cross = copies(1, at["t"], to_cross)
        self.relay_core = copies(2, at["cross"], to_core)
        self.receives = [
            copies(k, block, to_core) for k, block in enumerate((at["core"], at["cross"], at["cross_core"]))
        ]

    def start(self, c):
        self.to_cross[c].start()
        self.to_core[c].start()

    def relay(self):
        for receive, send in zip(self.receives[1], self.relay_core):
            receive.wait_recv()
            send.start()

    def wait(self, k):
        for receive in self.receives[k]:
            receive.wait_recv()

    def drain(self):
        for send in self.to_core + self.to_cross + self.relay_core:
            send.wait_send()


def sum_pieces(
    at, block_part, send, receive, total, sems, base, count, done, idle=lambda: None
):
    to_core, to_cross = (at["d"], at["core"]), (at["d"], at["cross"])
    low = jnp.bfloat16
    size = total.shape[0] // count
    pieces = [pl.ds(c * size, size) for c in range(count)]

    def copies(k, to):
        return [
            remote(send.at[k, piece], receive.at[k, piece], sems, base + k * count + c, to)
            for c, piece in enumerate(pieces)
        ]

    first, second, third = copies(0, to_core), copies(1, to_cross), copies(2, to_core)
    send[0] = block_part(at["cross_core"]).astype(low)
    for copy in first:
        copy.start()
    total[...] = block_part(at["cross"])
    for c, piece in enumerate(pieces):
        first[c].wait_recv()
        send[1, piece] = (total[piece] + receive[0, piece].astype(jnp.float32)).astype(low)
        second[c].start()
    idle()
    send[2] = block_part(at["core"]).astype(low)
    for copy in third:
        copy.start()
    total[...] = block_part(at["t"])
    for c, piece in enumerate(pieces):
        idle()
        third[c].wait_recv()
        second[c].wait_recv()
        total[piece] += receive[2, piece].astype(jnp.float32) + receive[1, piece].astype(jnp.float32)
        done(c)
    for copy in first + second + third:
        copy.wait_send()


class SumAll:
    def __init__(self, at, value, received, sems, base, over=("core", "cross", "mate", "z_pair", "z_mirror")):
        d, t = at["d"], at["t"]
        self.value, self.received, self.s = value, received, 0
        self.copies = [
            remote(
                value.at[k], received.at[k], sems, base + k,
                (d, at[name]) if name in ("core", "cross") else (at[name], t),
            )
            for k, name in enumerate(over)
        ]

    def start(self):
        self.copies[0].start()

    def step(self):
        s = self.s
        if s == len(self.copies):
            return
        self.copies[s].wait_recv()
        self.value[s + 1] = self.value[s] + self.received[s]
        if s + 1 < len(self.copies):
            self.copies[s + 1].start()
        self.s += 1

    def finish(self):
        while self.s < len(self.copies):
            self.step()
        for copy in self.copies:
            copy.wait_send()


def nt_dot(left, right):
    return lax.dot_general(
        left, right, (((1,), (1,)), ((), ())), preferred_element_type=jnp.float32
    )


def nn_dot(left, right):
    return lax.dot_general(
        left, right, (((1,), (0,)), ((), ())), preferred_element_type=jnp.float32
    )


def tn_dot(left, right):
    return lax.dot_general(
        left, right, (((0,), (0,)), ((), ())), preferred_element_type=jnp.float32
    )


def head_groups(width):
    heads = width // HEAD_DIM
    return [(2 * HEAD_DIM * j, min(2, heads - 2 * j)) for j in range((heads + 1) // 2)]


def split_heads(tile, heads):
    if heads == 1:
        return tile
    lane = lax.broadcasted_iota(jnp.int32, tile.shape, 1)
    zero = jnp.zeros_like(tile)
    return jnp.concatenate(
        [jnp.where(lane < HEAD_DIM, tile, zero), jnp.where(lane < HEAD_DIM, zero, tile)], axis=0
    )


def join_heads(stacked, heads):
    if heads == 1:
        return stacked
    half = stacked.shape[0] // 2
    lane = lax.broadcasted_iota(jnp.int32, (half, stacked.shape[1]), 1)
    return jnp.where(lane < HEAD_DIM, stacked[:half], stacked[half:])


def convolve(window, taps, lanes, same_one, same_two):
    one = pltpu.roll(window, 1, axis=0)[TILE:] * same_one
    two = pltpu.roll(window, 2, axis=0)[TILE:] * same_two
    rows = (window[TILE:], one, two)
    return sum(taps[m : m + 1, lanes] * rows[m] for m in range(CONV)), rows


def attend_tile(i, q, k_pad, v_pad, u, seg_q, seg_k, same, taps, p_out, o):
    row = pl.multiple_of(i * TILE, TILE)
    at_row, at_window = pl.ds(row, TILE), pl.ds(row, 2 * TILE)
    distance = (
        lax.broadcasted_iota(jnp.int32, (TILE, 2 * TILE), 0)
        + TILE
        - lax.broadcasted_iota(jnp.int32, (TILE, 2 * TILE), 1)
    )
    allowed = (seg_q[at_row] == seg_k[i]) & (distance >= 0) & (distance < WINDOW)
    same_one, same_two = same[at_row, 0:1], same[at_row, 1:2]
    for lane, heads in head_groups(q.shape[1]):
        lanes = pl.ds(lane, heads * HEAD_DIM)
        values = v_pad[at_window, lanes]
        allow = jnp.concatenate([allowed] * heads, axis=0) if heads > 1 else allowed
        scores = nt_dot(split_heads(q[at_row, lanes], heads), k_pad[at_window, lanes])
        scores = jnp.where(allow, scores * (HEAD_DIM**-0.5), -1e30)
        exponent = jnp.exp(scores - jnp.max(scores, axis=1, keepdims=True))
        chance = exponent * (1.0 / jnp.sum(exponent, axis=1, keepdims=True))
        chance = chance.astype(jnp.bfloat16)
        p_out[i, pl.ds((lane // HEAD_DIM) * TILE, heads * TILE), :] = chance
        mixed = join_heads(nn_dot(chance, values), heads)
        convolved, _ = convolve(values.astype(jnp.float32), taps, lanes, same_one, same_two)
        o[at_row, lanes] = (mixed + convolved * u[at_row, lanes].astype(jnp.float32)).astype(
            jnp.bfloat16
        )


def attend_back_tile(
    i, q, k_pad, v_pad, u, p, same, taps, do, dk, dv, conv_sum
):
    row = pl.multiple_of(i * TILE, TILE)
    at_row, at_window = pl.ds(row, TILE), pl.ds(row, 2 * TILE)
    same_one, same_two = same[at_row, 0:1], same[at_row, 1:2]
    for lane, heads in head_groups(q.shape[1]):
        lanes = pl.ds(lane, heads * HEAD_DIM)
        keys, values = k_pad[at_window, lanes], v_pad[at_window, lanes]
        grad = do[at_row, lanes]
        grad_heads = split_heads(grad, heads)
        chance_low = p[i, pl.ds((lane // HEAD_DIM) * TILE, heads * TILE), :]
        chance = chance_low.astype(jnp.float32)
        weighted = chance * nt_dot(grad_heads, values)
        slope = weighted - chance * jnp.sum(weighted, axis=1, keepdims=True)
        slope = (slope * (HEAD_DIM**-0.5)).astype(jnp.bfloat16)
        dk[at_window, lanes] += tn_dot(slope, split_heads(q[at_row, lanes], heads))
        q[at_row, lanes] = join_heads(nn_dot(slope, keys), heads).astype(jnp.bfloat16)
        convolved, rows = convolve(values.astype(jnp.float32), taps, lanes, same_one, same_two)
        grad = grad.astype(jnp.float32)
        do[at_row, lanes] = (grad * convolved).astype(jnp.bfloat16)
        grad_conv = grad * u[at_row, lanes].astype(jnp.float32)
        back = tn_dot(chance_low, grad_heads)
        zero = jnp.zeros_like(grad_conv)
        for m, same_m in enumerate((None, same_one, same_two)):
            conv_sum[m, :, lanes] += jnp.sum(grad_conv * rows[m], axis=0, keepdims=True)
            term = taps[m : m + 1, lanes] * grad_conv
            term = term if m == 0 else term * same_m
            term = jnp.concatenate([zero, term], axis=0)
            back = back + (term if m == 0 else pltpu.roll(term, 2 * TILE - m, axis=0))
        dv[at_window, lanes] += back


def rolled(values, offset):
    turned = pltpu.roll(values, offset, axis=1)
    lane = lax.broadcasted_iota(jnp.int32, values.shape, 1)
    return jnp.where(lane < offset, pltpu.roll(turned, 1, axis=0), turned)


def make_tables(segments, seg_q, seg_k, same):
    values = segments[...]
    row = lax.broadcasted_iota(jnp.int32, values.shape, 0)
    lane = lax.broadcasted_iota(jnp.int32, values.shape, 1)
    columns = values.T
    matches = [
        jnp.where((values == rolled(values, m)) & ((row > 0) | (lane >= m)), 1.0, 0.0).astype(jnp.float32).T
        for m in range(1, CONV)
    ]
    crossing = rolled(values, TILE)
    crossing = jnp.where((row == 0) & (lane < TILE), -1, crossing)
    for n in range(values.shape[0]):
        rows = pl.ds(n * LANES, LANES)
        seg_q[rows] = columns[:, n : n + 1]
        for m, match in enumerate(matches):
            same[rows, m : m + 1] = match[:, n : n + 1]
        seg_k[2 * n] = crossing[n : n + 1]
        seg_k[2 * n + 1] = values[n : n + 1]


def row_of(gain):
    return gain[...].reshape(1, -1)


def norm_rows(values, gain):
    scale = lax.rsqrt(jnp.mean(values * values, axis=1, keepdims=True) + EPS)
    return (values * scale * gain).astype(jnp.bfloat16)


def norm_back(values, grad, gain):
    scale = lax.rsqrt(jnp.mean(values * values, axis=1, keepdims=True) + EPS)
    normed = values * scale
    scaled = grad * gain
    through = scale * (scaled - normed * jnp.mean(scaled * normed, axis=1, keepdims=True))
    return through, jnp.sum(grad * normed, axis=0, keepdims=True)


def chunks_of(rows, size=64):
    def run(body):
        @pl.loop(0, rows // size)
        def _(i):
            body(pl.multiple_of(i * size, size), size)

    return run


def forward_kernel(
    x, valid_lanes, gain_one, gain_two, segments, taps,
    gate_own, up_own, out_turned, down_own, mix_own, cotangent_in, teacher_in,
    mix_out, last_out, feed_out, down_out, h1t_out, h2t_out, dybt_out, q_out, k_out, v_out, u_out, p_out,
    o_out, x1_out, dyb_out, slopes_out, active_out, act_out, dy_out, count_out, squares_out, same,
    valid, seg_q, seg_k, feed_own, out_own, mix, last, feed, down, h1, turned, h2, q, k_pad, v_pad, u, p, o, slopes, active, x1, side, teacher,
    send, receive, total, count, count_in,
    send_sems, recv_sems, local_sems, load_sems, out_sems,
):
    at = neighbours()
    sems = (send_sems, recv_sems)
    rows, shard = x.shape[0], mix_own.shape[0]
    low = jnp.bfloat16
    meet(hail(at, everyone=True))

    def slot_of(full):
        return lambda i, first, size: full.at[pl.ds(pl.multiple_of(i * shard + first, 16), size)]

    mix_ring = RingGather(at, mix_own, slot_of(mix), sems, 0, local_sems.at[0])
    last_ring = RingGather(at, out_own, slot_of(last), sems, 28, local_sems.at[1], count=1)
    feed_ring = RingGather(at, feed_own, slot_of(feed), sems, 42, local_sems.at[2])
    down_ring = RingGather(
        at, down_own.at[:, pl.ds(0, down.shape[1])], slot_of(down), sems, 70, local_sems.at[3]
    )
    dyb = h1
    group_one = GatherTensor(at, h1, rows, sems, 98)
    group_two = GatherTensor(at, h2, rows, sems, 101)
    group_back = GatherPieces(at, dyb, rows, PIECES, sems, 115)
    counting = SumAll(at, count, count_in, sems, 110)
    local = q.shape[1]
    main = local // LANES * LANES
    tail = local - main
    keeps = []

    def keep(source, target):
        copy = pltpu.make_async_copy(source, target, out_sems.at[len(keeps)])
        copy.start()
        keeps.append(copy)
        return copy

    def tick():
        last_ring.tick()
        if feed_ring.at < len(feed_ring.receives):
            feed_ring.tick()
            if feed_ring.at == len(feed_ring.receives) - 2:
                down_ring.start()
        else:
            down_ring.tick()

    def turn(source, block):
        here = pl.ds(pl.multiple_of(block * rows, rows), rows)
        turned[:, here] = source[here].T

    mix_ring.start()

    @chunks_of(rows)
    def _(row, size):
        h1[pl.ds(pl.multiple_of(at["t"] * rows + row, size), size)] = norm_rows(
            x[pl.ds(row, size)].astype(jnp.float32), row_of(gain_one)
        )

    group_one.start()
    flags = valid_lanes[...].astype(jnp.float32)
    count[0] = jnp.full(count.shape[1:], jnp.sum(flags), jnp.float32)
    counting.start()
    load_teacher = pltpu.make_async_copy(teacher_in, teacher, load_sems.at[0])
    load_cotangent = pltpu.make_async_copy(cotangent_in, side, load_sems.at[1])
    load_teacher.start()
    load_cotangent.start()
    k_pad[pl.ds(0, TILE)] = jnp.zeros((TILE, local), k_pad.dtype)
    v_pad[pl.ds(0, TILE)] = jnp.zeros((TILE, local), v_pad.dtype)
    make_tables(segments, seg_q, seg_k, same)
    width = gate_own.shape[1]
    cut = width // LANES * LANES
    rest = width - cut
    feed_own[:, pl.ds(0, cut)] = gate_own[:, pl.ds(0, cut)]
    feed_own[:, pl.ds(cut, cut)] = up_own[:, pl.ds(0, cut)]
    ends = [own[:, pl.ds(cut, rest)].astype(jnp.float32) for own in (gate_own, up_own)]
    feed_own[:, pl.ds(2 * cut, 2 * rest)] = jnp.concatenate(ends, axis=1).astype(low)
    ends = [out_turned[...].astype(jnp.float32).T, down_own[:, pl.ds(cut, rest)].astype(jnp.float32)]
    out_own[...] = jnp.concatenate(ends, axis=1).astype(low)
    spare = jnp.zeros((8 - flags.shape[0], LANES), jnp.float32)
    columns = jnp.concatenate([flags, spare], axis=0).T
    for n in range(flags.shape[0]):
        valid[pl.ds(n * LANES, LANES)] = columns[:, n : n + 1]
    for _ in range(6):
        mix_ring.tick()
    group_one.relay()
    mix_ring.tick()
    mix_ring.tick()
    group_one.finish()
    mix_ring.tick()
    for k in range(2):

        @pl.loop(2 * k, 2 * k + 2)
        def _(j):
            turn(h1, j)

        mix_ring.tick()
    keep_h1t = keep(turned, h1t_out)
    last_ring.start()
    mix_ring.tick()
    last_ring.tick()
    feed_ring.start()
    mix_ring.tick()
    last_ring.tick()
    mix_ring.finish()
    last_ring.tick()
    keep(mix, mix_out)

    def project(j):
        here = pl.ds(pl.multiple_of(j * rows, rows), rows)
        there = pl.ds(pl.multiple_of(j * rows + TILE, TILE), rows)
        left = h1[here]
        pair = nn_dot(left, mix[:, pl.ds(0, 2 * main)]).astype(low)
        q[here, pl.ds(0, main)] = pair[:, :main]
        k_pad[there, pl.ds(0, main)] = pair[:, main:]
        pair = nn_dot(left, mix[:, pl.ds(2 * main, 2 * main)]).astype(low)
        v_pad[there, pl.ds(0, main)] = pair[:, :main]
        u[here, pl.ds(0, main)] = pair[:, main:]
        ends = nn_dot(left, mix[:, pl.ds(4 * main, 4 * tail)])
        q[here, pl.ds(main, tail)] = ends[:, :tail].astype(low)
        k_pad[there, pl.ds(main, tail)] = ends[:, tail : 2 * tail].astype(low)
        v_pad[there, pl.ds(main, tail)] = ends[:, 2 * tail : 3 * tail].astype(low)
        u[here, pl.ds(main, tail)] = ends[:, 3 * tail :].astype(low)

    def projects(first, last_block):
        @pl.loop(first, last_block)
        def _(j):
            project(j)

    projects(0, 2)
    tick()
    counting.step()
    projects(2, 4)
    for source, target in ((q, q_out), (k_pad, k_out), (v_pad, v_out), (u, u_out)):
        keep(source, target)
    tick()
    tiles = q.shape[0] // TILE

    def attend(first, last_tile):
        @pl.loop(first, last_tile)
        def _(i):
            attend_tile(i, q, k_pad, v_pad, u, seg_q, seg_k, same, taps, p, o)

    for k in range(4):
        attend(k * tiles // 4, (k + 1) * tiles // 4)
        tick()
        if k % 2:
            counting.step()
    last_ring.finish()
    keep(last, last_out)
    keep(p, p_out)
    keep(o, o_out)

    def mixed_part(block):
        return nt_dot(o[pl.ds(pl.multiple_of(block * rows, rows), rows)], last[:, pl.ds(0, local)])

    def idle(point):
        tick()
        if point == 2:
            tick()

    sum_rows(at, mixed_part, send, receive, total, sems, 107, idle=idle)

    @chunks_of(rows)
    def _(row, size):
        here = pl.ds(row, size)
        hidden = total[here] + x[here].astype(jnp.float32)
        x1[here] = hidden
        h2[pl.ds(pl.multiple_of(at["t"] * rows + row, size), size)] = norm_rows(hidden, row_of(gain_two))

    group_two.start()
    keep(x1, x1_out)
    for _ in range(3):
        tick()
    counting.step()
    tick()
    group_two.relay()
    tick()
    counting.finish()
    keep(count.at[5], count_out)
    group_two.finish()
    while feed_ring.at < len(feed_ring.receives):
        tick()
    feed_ring.finish()
    keep(feed, feed_out)
    parts, _ = feed_lanes(width)

    def widen(j):
        here = pl.ds(pl.multiple_of(j * (rows // 2), rows // 2), rows // 2)
        left = h2[here]
        for own, gate_lanes, up_lanes in parts:
            a, by_gate, by_up = gated(nn_dot(left, feed[:, gate_lanes]), nn_dot(left, feed[:, up_lanes]))
            active[here, own] = a.astype(low)
            slopes[here, gate_lanes] = by_gate.astype(low)
            slopes[here, up_lanes] = by_up.astype(low)
        both = nn_dot(left, feed[:, pl.ds(2 * cut, 2 * rest)])
        a, by_gate, by_up = gated(both[:, :rest], both[:, rest:])
        active[here, pl.ds(cut, rest)] = a.astype(low)
        slopes[here, pl.ds(2 * cut, 2 * rest)] = jnp.concatenate([by_gate, by_up], axis=1).astype(low)

    for k in range(8):

        @pl.loop(k, k + 1)
        def _(j):
            widen(j)

        tick()
    keep(active, active_out)
    keep(slopes, slopes_out)
    keep_h1t.wait()
    for k in range(4):

        @pl.loop(k, k + 1)
        def _(j):
            turn(h2, j)

        tick()
    keep_h2t = keep(turned, h2t_out)
    down_ring.finish()
    keep(down, down_out)
    load_teacher.wait()
    load_cotangent.wait()

    def fed_part(block):
        here = pl.ds(pl.multiple_of(block * rows, rows), rows)
        ends = nt_dot(active[here, pl.ds(cut, rest)], last[:, pl.ds(local, rest)])
        return ends + nt_dot(active[here, pl.ds(0, cut)], down[...])

    weight = (rows * 4 * 8) / count[5, 0:1, 0:1]
    squares_out[...] = jnp.zeros_like(squares_out)
    piece, step = rows // PIECES, 32

    def judge(c):
        @pl.loop(0, piece // step)
        def _(i):
            row = pl.multiple_of(c * piece + i * step, step)
            here = pl.ds(row, step)
            result = total[here] + x1[here]
            deviation = result - teacher[here].astype(jnp.float32)
            kept = valid[here, 0:1] * deviation
            total[here] = result
            squares_out[0:1] += jnp.sum(kept * deviation, axis=0, keepdims=True)
            grad = side[here] + kept * weight
            side[here] = grad
            dyb[pl.ds(pl.multiple_of(at["t"] * rows + row, step), step)] = grad.astype(low)

        group_back.start(c)

    sum_pieces(at, fed_part, send, receive, total, sems, 115 + 3 * PIECES, PIECES, judge)
    keep(total, act_out)
    keep(side, dy_out)
    keep_h2t.wait()

    def spread(block):
        here = pl.ds(pl.multiple_of(block * rows, rows), rows)
        turn(dyb, block)
        keep(dyb.at[here], dyb_out.at[here])
        keep(turned.at[:, here], dybt_out.at[:, here])

    spread(at["t"])
    group_back.wait(0)
    spread(at["core"])
    group_back.relay()
    spread(at["cross"])
    group_back.wait(2)
    spread(at["cross_core"])
    group_back.drain()
    for ring in (mix_ring, last_ring, feed_ring, down_ring):
        ring.drain()
    for copy in keeps:
        if copy is not keep_h1t and copy is not keep_h2t:
            copy.wait()


def specs():
    return pl.BlockSpec(memory_space=pltpu.VMEM), pl.BlockSpec(memory_space=pl.ANY)


def shape(*dims, kind=jnp.bfloat16):
    return jax.ShapeDtypeStruct(dims, kind)


def params(identity):
    return pltpu.CompilerParams(
        collective_id=identity, has_side_effects=True, vmem_limit_bytes=VMEM_LIMIT
    )


def dma(count):
    return pltpu.SemaphoreType.DMA((count,))


def forward(
    x, valid_lanes, gain_one, gain_two, segments, taps, mix_own, output_weight, gate_own, up_own, down_own,
    cotangent, teacher,
):
    rows, width = x.shape
    shard = mix_own.shape[0]
    local, hidden = mix_own.shape[1] // 4, gate_own.shape[1]
    cut = hidden // LANES * LANES
    both = local + hidden - cut
    everyone, depth = 4 * rows, 8 * shard
    low, wide = jnp.bfloat16, jnp.float32
    tiles, heads = everyone // TILE, local // HEAD_DIM
    vmem, hbm = specs()
    return pl.pallas_call(
        forward_kernel,
        out_shape=(
            shape(depth, 4 * local),
            shape(depth, both),
            shape(depth, 2 * hidden),
            shape(depth, cut),
            shape(width, everyone),
            shape(width, everyone),
            shape(width, everyone),
            shape(everyone, local),
            shape(everyone + TILE, local),
            shape(everyone + TILE, local),
            shape(everyone, local),
            shape(tiles, heads * TILE, 2 * TILE),
            shape(everyone, local),
            shape(rows, width, kind=wide),
            shape(everyone, width),
            shape(everyone, 2 * hidden),
            shape(everyone, hidden),
            shape(rows, width, kind=wide),
            shape(rows, width, kind=wide),
            shape(8, LANES, kind=wide),
            shape(8, width, kind=wide),
            shape(everyone, CONV - 1, kind=wide),
        ),
        in_specs=[vmem] * 10 + [hbm] * 3,
        out_specs=(hbm,) * 20 + (vmem,) * 2,
        scratch_shapes=[
            pltpu.VMEM((rows, 1), wide),
            pltpu.VMEM((everyone, 1), jnp.int32),
            pltpu.VMEM((tiles, 1, 2 * TILE), jnp.int32),
            pltpu.VMEM((shard, 2 * hidden), low),
            pltpu.VMEM((shard, both), low),
            pltpu.VMEM((depth, 4 * local), low),
            pltpu.VMEM((depth, both), low),
            pltpu.VMEM((depth, 2 * hidden), low),
            pltpu.VMEM((depth, cut), low),
            pltpu.VMEM((everyone, width), low),
            pltpu.VMEM((width, everyone), low),
            pltpu.VMEM((everyone, width), low),
            pltpu.VMEM((everyone, local), low),
            pltpu.VMEM((everyone + TILE, local), low),
            pltpu.VMEM((everyone + TILE, local), low),
            pltpu.VMEM((everyone, local), low),
            pltpu.VMEM((tiles, heads * TILE, 2 * TILE), low),
            pltpu.VMEM((everyone, local), low),
            pltpu.VMEM((everyone, 2 * hidden), low),
            pltpu.VMEM((everyone, hidden), low),
            pltpu.VMEM((rows, width), wide),
            pltpu.VMEM((rows, width), wide),
            pltpu.VMEM((rows, width), low),
            pltpu.VMEM((3, rows, width), low),
            pltpu.VMEM((3, rows, width), low),
            pltpu.VMEM((rows, width), wide),
            pltpu.VMEM((6, 8, LANES), wide),
            pltpu.VMEM((5, 8, LANES), wide),
            dma(115 + 6 * PIECES),
            dma(115 + 6 * PIECES),
            dma(4),
            dma(2),
            dma(26),
        ],
        compiler_params=params(1),
    )(
        x, valid_lanes, gain_one, gain_two, segments, taps, gate_own, up_own, output_weight, down_own, mix_own,
        cotangent, teacher,
    )


def feed_lanes(hidden):
    main = hidden // LANES * LANES
    cut = main // 2 // LANES * LANES
    parts = [(0, cut), (cut, main - cut)]
    return [(pl.ds(a, n), pl.ds(a, n), pl.ds(main + a, n)) for a, n in parts], main


def gated(gate, up):
    sigmoid = jax.nn.sigmoid(gate)
    silu = gate * sigmoid
    return silu * up, up * sigmoid * (1.0 + gate * (1.0 - sigmoid)), silu


def feed_backward_kernel(
    gain, dyb_in, dybt_in, h2t_in, down_in, feed_in, active_in, slopes_in, last_in, x1_in, dy_in,
    down_grad, gate_grad, gain_part, dx1_out, dx1t_out, do_out, slopes_out, ends_out,
    dyb, dybt, h2t, down, feed, active, slopes, last, do, x1, dy, total, down_slots, gate_slots,
    down_term, gate_term, ends, send, receive,
    send_sems, recv_sems, load_sems, out_sems,
):
    at = neighbours()
    sems = (send_sems, recv_sems)
    rows = total.shape[0]
    low = jnp.bfloat16
    loads = [
        pltpu.make_async_copy(source, target, load_sems.at[n])
        for n, (source, target) in enumerate(
            (
                (dybt_in, dybt), (active_in, active), (dyb_in, dyb), (down_in, down), (slopes_in, slopes),
                (last_in, last), (h2t_in, h2t), (feed_in, feed), (x1_in, x1), (dy_in, dy),
            )
        )
    ]
    for load in loads[:2]:
        load.start()
    number = hail(at)
    hidden = active.shape[1]
    parts, main = feed_lanes(hidden)
    tail, share = hidden - main, gate_slots.shape[3]
    first = RingScatter(
        at, dybt, active.at[:, pl.ds(0, main)], down_slots, down_term, down_grad, sems, 0
    )
    second = RingScatter(
        at, h2t, slopes.at[:, pl.ds(0, share)], gate_slots, gate_term, gate_grad, sems, 28
    )
    group = GatherPieces(at, dyb, rows, PIECES, sems, 56)
    keeps = []

    def keep(source, target):
        copy = pltpu.make_async_copy(source, target, out_sems.at[len(keeps)])
        copy.start()
        keeps.append(copy)

    loads[0].wait()
    loads[1].wait()
    for load in loads[2:]:
        load.start()
    first.prepare()
    meet(number)
    first.launch()
    first.compute(2)
    for load in loads[2:6]:
        load.wait()

    def slope_back(first_block, last_block):
        @pl.loop(first_block, last_block)
        def _(j):
            here = pl.ds(pl.multiple_of(j * (rows // 2), rows // 2), rows // 2)
            left = dyb[here]
            for own, gate_lanes, up_lanes in parts:
                da = nn_dot(left, down[:, own])
                slopes[here, gate_lanes] = (da * slopes[here, gate_lanes].astype(jnp.float32)).astype(low)
                slopes[here, up_lanes] = (da * slopes[here, up_lanes].astype(jnp.float32)).astype(low)
            da = nn_dot(left, last[:, pl.ds(last.shape[1] - tail, tail)])
            last_lanes = pl.ds(2 * main, 2 * tail)
            both = jnp.concatenate([da, da], axis=1) * slopes[here, last_lanes].astype(jnp.float32)
            slopes[here, last_lanes] = both.astype(low)

    for k in range(8):
        slope_back(k, k + 1)
        if k % 2 or k > 3:
            first.tick()
    loads[6].wait()
    second.start()
    first.tick()
    keep(slopes.at[:, pl.ds(share, 2 * hidden - share)], slopes_out)

    @pl.loop(0, dybt.shape[0] // rows)
    def _(j):
        here = pl.ds(pl.multiple_of(j * rows, rows), rows)
        ends[here] = nn_dot(dybt[here], active[:, pl.ds(main, tail)]).astype(low)

    keep(ends, ends_out)
    first.tick()
    loads[7].wait()
    loads[8].wait()

    def part(block):
        return nt_dot(slopes[pl.ds(pl.multiple_of(block * rows, rows), rows)], feed[...])

    def idle():
        first.tick()
        second.tick()

    gain_part[...] = jnp.zeros_like(gain_part)
    loads[9].wait()
    piece, step = rows // PIECES, 32

    def through_norm(c):
        @pl.loop(0, piece // step)
        def _(i):
            row = pl.multiple_of(c * piece + i * step, step)
            here = pl.ds(row, step)
            through, term_gain = norm_back(x1[here], total[here], row_of(gain))
            gain_part[0:1] += term_gain
            grad = dy[here] + through
            total[here] = grad
            dyb[pl.ds(pl.multiple_of(at["t"] * rows + row, step), step)] = grad.astype(low)

        group.start(c)

    sum_pieces(
        at, part, send, receive, total, sems, 56 + 3 * PIECES, PIECES, through_norm, idle=idle
    )
    keep(total, dx1_out)

    def spread(block):
        here = pl.ds(pl.multiple_of(block * rows, rows), rows)
        dybt[:, here] = dyb[here].T
        do[here] = nn_dot(dyb[here], last[:, pl.ds(0, do.shape[1])]).astype(low)

    while first.at < len(first.sends):
        first.tick()
        second.tick()
    spread(at["t"])
    second.tick()
    group.wait(0)
    spread(at["core"])
    second.tick()
    group.relay()
    second.tick()
    spread(at["cross"])
    group.wait(2)
    spread(at["cross_core"])
    group.drain()
    keep(dybt, dx1t_out)
    keep(do, do_out)
    second.finish()
    first.finish()
    for copy in keeps:
        copy.wait()


def feed_backward(gain, dyb, dybt, h2t, down, feed, active, slopes, last, x1, dy):
    rows, width = x1.shape
    depth, main = down.shape
    hidden = active.shape[1]
    share = main + SHARE * LANES
    local = last.shape[1] - (hidden - main)
    everyone, shard = 4 * rows, depth // 8
    low, wide = jnp.bfloat16, jnp.float32
    vmem, hbm = specs()
    return pl.pallas_call(
        feed_backward_kernel,
        out_shape=(
            shape(shard, main, kind=wide),
            shape(shard, share, kind=wide),
            shape(8, width, kind=wide),
            shape(rows, width, kind=wide),
            shape(width, everyone),
            shape(everyone, local),
            shape(everyone, 2 * hidden - share),
            shape(width, hidden - main),
        ),
        in_specs=[vmem] + [hbm] * 10,
        out_specs=(vmem,) * 3 + (hbm,) * 5,
        scratch_shapes=[
            pltpu.VMEM((everyone, width), low),
            pltpu.VMEM((width, everyone), low),
            pltpu.VMEM((width, everyone), low),
            pltpu.VMEM((depth, main), low),
            pltpu.VMEM((depth, 2 * hidden), low),
            pltpu.VMEM((everyone, hidden), low),
            pltpu.VMEM((everyone, 2 * hidden), low),
            pltpu.VMEM(last.shape, low),
            pltpu.VMEM((everyone, local), low),
            pltpu.VMEM((rows, width), wide),
            pltpu.VMEM((rows, width), wide),
            pltpu.VMEM((rows, width), wide),
            pltpu.VMEM((2, 8, shard // 2, main), low),
            pltpu.VMEM((2, 8, shard // 2, share), low),
            pltpu.VMEM((shard, main), wide),
            pltpu.VMEM((shard, share), wide),
            pltpu.VMEM((width, hidden - main), low),
            pltpu.VMEM((3, rows, width), low),
            pltpu.VMEM((3, rows, width), low),
            dma(56 + 6 * PIECES),
            dma(56 + 6 * PIECES),
            dma(10),
            dma(5),
        ],
        compiler_params=params(3),
    )(gain, dyb, dybt, h2t, down, feed, active, slopes, last, x1, dy)


def mixer_backward_kernel(
    x, gain, same, taps, gain_part, squares,
    dx1t_in, o_in, h2t_in, slopes_in, ends_in, q_in, k_in, v_in, u_in, p_in, do_in, mix_in, h1t_in, dx1_in,
    out_grad, up_grad, mix_grad, input_grad, small_out, conv_out,
    turned, o, h2t, slopes, ends, q, k_pad, v_pad, u, p, do, mix,
    dk, dv, grads, out_slots, up_slots, mix_slots, out_term, up_term, mix_term, send, receive, total,
    small, small_in, conv, conv_in, conv_all,
    send_sems, recv_sems, load_sems,
):
    at = neighbours()
    sems = (send_sems, recv_sems)
    rows = total.shape[0]
    low = jnp.bfloat16
    loads = [
        pltpu.make_async_copy(source, target, load_sems.at[n])
        for n, (source, target) in enumerate(
            (
                (dx1t_in, turned), (o_in, o), (h2t_in, h2t), (slopes_in, slopes), (ends_in, ends), (q_in, q), (k_in, k_pad),
                (v_in, v_pad), (u_in, u), (p_in, p), (do_in, do), (mix_in, mix), (dx1_in, input_grad),
                (h1t_in, turned),
            )
        )
    ]
    for load in loads[:5]:
        load.start()
    number = hail(at, everyone=True)
    local = q.shape[1]
    main = local // LANES * LANES
    tail = local - main
    first = RingScatter(
        at, turned, o, out_slots, out_term, out_grad, sems, 0, count=1, side=ends
    )
    second = RingScatter(at, h2t, slopes, up_slots, up_term, up_grad, sems, 14)
    third = RingScatter(at, turned, grads, mix_slots, mix_term, mix_grad, sems, 42)
    small_sum = SumAll(at, small, small_in, sems, 73)
    conv_sum = SumAll(at, conv, conv_in, sems, 78, over=("mate", "z_pair", "z_mirror"))
    conv_group = GatherTensor(at, conv_all, 1, sems, 81)
    loads[0].wait()
    loads[1].wait()
    loads[4].wait()
    first.prepare()
    meet(number)
    first.launch()
    loads[2].wait()
    loads[3].wait()
    for load in loads[5:-1]:
        load.start()
    second.prepare()
    second.launch()
    first.compute(2)
    second.compute(2)
    dk[...] = jnp.zeros_like(dk)
    dv[...] = jnp.zeros_like(dv)
    conv[0] = jnp.zeros(conv.shape[1:], jnp.float32)
    first.tick()
    for load in loads[5:11]:
        load.wait()
    tiles = q.shape[0] // TILE

    def attend(a, b):
        @pl.loop(a, b)
        def _(i):
            attend_back_tile(i, q, k_pad, v_pad, u, p, same, taps, do, dk, dv, conv.at[0])

    for k in range(8):
        attend(k * tiles // 8, (k + 1) * tiles // 8)
        first.tick()
        second.tick()
    conv_sum.start()

    first.finish()
    loads[13].start()
    second.tick()

    @chunks_of(q.shape[0])
    def _(row, size):
        here, there = pl.ds(row, size), pl.ds(pl.multiple_of(row + TILE, TILE), size)
        four = [q[here].astype(jnp.float32), dk[there], dv[there], do[here].astype(jnp.float32)]
        for n, value in enumerate(four):
            grads[here, pl.ds(n * main, main)] = value[:, :main].astype(low)
        lasts = jnp.concatenate([value[:, main:] for value in four], axis=1)
        grads[here, pl.ds(4 * main, 4 * tail)] = lasts.astype(low)

    second.tick()
    loads[13].wait()
    third.start()
    loads[11].wait()
    loads[12].wait()

    def part(block):
        return nt_dot(grads[pl.ds(pl.multiple_of(block * rows, rows), rows)], mix[...])

    def idle(point):
        second.tick()
        third.tick()
        if point == 2:
            second.tick()
        conv_sum.step()

    sum_rows(at, part, send, receive, total, sems, 70, idle=idle)
    conv_sum.finish()
    conv_all[at["t"]] = conv[3]
    conv_group.start()
    small[0, 0] = jnp.zeros((1, small.shape[3]), jnp.float32)
    small[0, 1] = gain_part[0:1]
    small[0, 2] = squares[0:1]

    @chunks_of(rows, 32)
    def _(row, size):
        here = pl.ds(row, size)
        through, term_gain = norm_back(x[here].astype(jnp.float32), total[here], row_of(gain))
        small[0, 0] += term_gain
        input_grad[here] += through

    small_sum.start()
    second.finish()
    for k in range(5):
        third.tick()
        third.tick()
        small_sum.step()
        if k == 1:
            conv_group.relay()
    conv_group.finish()
    third.finish()
    small_sum.finish()
    small_out[...] = small[5]
    conv_out[...] = conv_all[...]


def mixer_backward(
    x, gain, same, taps, gain_part, squares, dx1t, o, h2t, slopes, ends, q, k_pad, v_pad, u, p, do, mix, h1t, dx1
):
    rows, width = x.shape
    everyone, local = o.shape
    shard, ups = width // 8, slopes.shape[1]
    both = local + ends.shape[1]
    low, wide = jnp.bfloat16, jnp.float32
    vmem, hbm = specs()
    arrays = (dx1t, o, h2t, slopes, ends, q, k_pad, v_pad, u, p, do, mix)
    return pl.pallas_call(
        mixer_backward_kernel,
        out_shape=(
            shape(shard, both, kind=wide),
            shape(shard, ups, kind=wide),
            shape(shard, 4 * local, kind=wide),
            shape(rows, width, kind=wide),
            shape(CONV, 1, width, kind=wide),
            shape(4, CONV, 1, local, kind=wide),
        ),
        in_specs=[vmem] * 6 + [hbm] * 14,
        out_specs=(vmem,) * 6,
        scratch_shapes=[pltpu.VMEM(array.shape, array.dtype) for array in arrays]
        + [
            pltpu.VMEM((everyone + TILE, local), wide),
            pltpu.VMEM((everyone + TILE, local), wide),
            pltpu.VMEM((everyone, 4 * local), low),
            pltpu.VMEM((2, 8, shard // 2, both), low),
            pltpu.VMEM((2, 8, shard // 2, ups), low),
            pltpu.VMEM((2, 8, shard // 2, 4 * local), low),
            pltpu.VMEM((shard, both), wide),
            pltpu.VMEM((shard, ups), wide),
            pltpu.VMEM((shard, 4 * local), wide),
            pltpu.VMEM((3, rows, width), low),
            pltpu.VMEM((3, rows, width), low),
            pltpu.VMEM((rows, width), wide),
            pltpu.VMEM((6, 3, 1, width), wide),
            pltpu.VMEM((5, 3, 1, width), wide),
            pltpu.VMEM((4, CONV, 1, local), wide),
            pltpu.VMEM((3, CONV, 1, local), wide),
            pltpu.VMEM((4, CONV, 1, local), wide),
            dma(84),
            dma(84),
            dma(14),
        ],
        compiler_params=params(4),
    )(x, gain, same, taps, gain_part, squares, *arrays, h1t, dx1)


def finish_kernel(
    count, down_grad, gate_main, up_rest, mix_grad, out_grad, small, conv, act_in, input_in,
    loss, act, input_grad, query, key, value, mixgate, output, conv_grad, gain_one, gain_two, gate, up, down,
):
    act[...] = act_in[...]
    input_grad[...] = input_in[...]
    local = query.shape[1]
    main = local // LANES * LANES
    tail = local - main
    for n, target in enumerate((query, key, value, mixgate)):
        target[:, pl.ds(0, main)] = mix_grad[:, pl.ds(n * main, main)]
        target[:, pl.ds(main, tail)] = mix_grad[:, pl.ds(4 * main, 4 * tail)][:, n * tail : (n + 1) * tail]
    cut = gate.shape[1] // LANES * LANES
    rest, early = gate.shape[1] - cut, gate_main.shape[1] - cut
    late = cut - early
    ends = up_rest[:, pl.ds(late, 2 * rest)]
    gate[:, pl.ds(0, cut)] = gate_main[:, pl.ds(0, cut)]
    gate[:, pl.ds(cut, rest)] = ends[:, :rest]
    up[:, pl.ds(0, early)] = gate_main[:, pl.ds(cut, early)]
    up[:, pl.ds(early, late)] = up_rest[:, pl.ds(0, late)]
    up[:, pl.ds(cut, rest)] = ends[:, rest:]
    output[...] = out_grad[:, pl.ds(0, local)].T
    down[:, pl.ds(0, cut)] = down_grad[...]
    down[:, pl.ds(cut, rest)] = out_grad[:, pl.ds(local, rest)]
    for m in range(CONV):
        conv_grad[m : m + 1] = jnp.concatenate([conv[n, m] for n in range(conv.shape[0])], axis=1)
    gain_one[...] = small[0, 0]
    gain_two[...] = small[1, 0]
    total = jnp.sum(small[2], axis=1, keepdims=True) / (count[0:1, 0:1] * D)
    loss[...] = total


def finish(count, down_grad, gate_main, up_rest, mix_grad, out_grad, small, conv, act, input_grad):
    vmem, _ = specs()
    wide = jnp.float32
    shard, width = gate_main.shape[0], small.shape[2]
    hidden, local = (gate_main.shape[1] + up_rest.shape[1]) // 2, mix_grad.shape[1] // 4
    square = shape(shard, local, kind=wide)
    broad = shape(shard, hidden, kind=wide)
    return pl.pallas_call(
        finish_kernel,
        out_shape=(
            shape(1, 1, kind=wide),
            shape(*act.shape, kind=wide),
            shape(*input_grad.shape, kind=wide),
            square,
            square,
            square,
            square,
            shape(local, shard, kind=wide),
            shape(CONV, width, kind=wide),
            shape(width, kind=wide),
            shape(width, kind=wide),
            broad,
            broad,
            broad,
        ),
        in_specs=[vmem] * 10,
        out_specs=(vmem,) * 14,
        compiler_params=pltpu.CompilerParams(vmem_limit_bytes=VMEM_LIMIT),
    )(count, down_grad, gate_main, up_rest, mix_grad, out_grad, small, conv, act, input_grad)


def pack(*weights):
    main = weights[0].shape[1] // LANES * LANES
    return jnp.concatenate([w[:, :main] for w in weights] + [w[:, main:] for w in weights], axis=1)


def on_rings(
    block_input,
    cotangent,
    teacher,
    segments,
    valid_mask,
    query_weight,
    key_weight,
    value_weight,
    mixgate_weight,
    output_weight,
    conv_weight,
    gain_mixer,
    gain_feed,
    gate_weight,
    up_weight,
    down_weight,
):
    local = query_weight.shape[1]
    taps = lax.dynamic_slice_in_dim(conv_weight, lax.axis_index("tensor") * local, local, 1)
    (
        mix, last, feed, down, h1t, h2t, dybt, q, k_pad, v_pad, u, p, o, x1, dyb, slopes, active,
        outputs, dy, count, squares, same,
    ) = forward(
        block_input, valid_mask.reshape(-1, LANES), gain_mixer, gain_feed, segments.reshape(-1, LANES), taps,
        pack(query_weight, key_weight, value_weight, mixgate_weight),
        output_weight, gate_weight, up_weight, down_weight.T, cotangent, teacher,
    )
    down_grad, gate_main, gain_part, dx1, dx1t, do, slopes_up, ends = feed_backward(
        gain_feed, dyb, dybt, h2t, down, feed, active, slopes, last, x1, dy
    )
    out_grad, up_rest, mix_grad, input_grad, small, conv = mixer_backward(
        block_input, gain_mixer, same, taps, gain_part, squares, dx1t, o, h2t, slopes_up, ends, q, k_pad, v_pad,
        u, p, do, mix, h1t, dx1,
    )
    loss, *rest, down_turned = finish(
        count, down_grad, gate_main, up_rest, mix_grad, out_grad, small, conv, outputs, input_grad
    )
    return (loss.reshape(()), *rest, down_turned.T)


def on_any_mesh(
    block_input,
    cotangent,
    teacher,
    segments,
    valid_mask,
    query_weight,
    key_weight,
    value_weight,
    mixgate_weight,
    output_weight,
    conv_weight,
    gain_mixer,
    gain_feed,
    gate_weight,
    up_weight,
    down_weight,
):
    rows = block_input.shape[0]
    valid_rows = valid_mask.astype(jnp.float32)
    valid_total = sum_all(jnp.full((8, 128), jnp.sum(valid_rows), jnp.float32))[0, 0]
    local_width = query_weight.shape[1]
    local_hidden = gate_weight.shape[1]
    mixer_own = jnp.concatenate(
        [query_weight, key_weight, value_weight, mixgate_weight, output_weight.T], axis=1
    )
    feed_own = jnp.concatenate([gate_weight, up_weight], axis=1)
    mixer_all = gather_dp(mixer_own).reshape(D, -1)
    feed_all = gather_dp(feed_own).reshape(D, -1)
    full_down = gather_dp(down_weight.T).reshape(D, -1)
    full_query, full_key, full_value, full_mixgate, full_output = jnp.split(mixer_all, 5, axis=1)
    full_gate, full_upward = jnp.split(feed_all, 2, axis=1)
    column = lax.axis_index("tensor") * local_width
    conv_local = lax.dynamic_slice_in_dim(conv_weight, column, local_width, 1)
    inputs = block_input.astype(jnp.float32)
    scale_one = rms_scale(inputs)
    normed_one = inputs * scale_one
    group_one = gather_tensor((normed_one * gain_mixer).astype(jnp.bfloat16))
    queries = jnp.dot(group_one, full_query, preferred_element_type=jnp.float32).astype(
        jnp.bfloat16
    )
    key_rows = jnp.dot(group_one, full_key, preferred_element_type=jnp.float32).astype(jnp.bfloat16)
    value_rows = jnp.dot(group_one, full_value, preferred_element_type=jnp.float32).astype(
        jnp.bfloat16
    )
    mix_gate = jnp.dot(group_one, full_mixgate, preferred_element_type=jnp.float32).astype(
        jnp.bfloat16
    )
    attended, log_totals = attend_forward(queries, key_rows, value_rows, segments)
    value_float = value_rows.astype(jnp.float32)
    convolved = jnp.zeros_like(value_float)
    for offset in range(CONV):
        convolved = convolved + conv_local[offset] * shift_down(value_float, segments, offset)
    gate_float = mix_gate.astype(jnp.float32)
    mixer_out = (attended + convolved * gate_float).astype(jnp.bfloat16)
    mixer_part = cols_inner(mixer_out, full_output)
    hidden = inputs + scatter_tensor(mixer_part)
    scale_two = rms_scale(hidden)
    normed_two = hidden * scale_two
    group_two = gather_tensor((normed_two * gain_feed).astype(jnp.bfloat16))
    gate_value = jnp.dot(group_two, full_gate, preferred_element_type=jnp.float32)
    up_value = jnp.dot(group_two, full_upward, preferred_element_type=jnp.float32)
    sigmoid_gate = jax.nn.sigmoid(gate_value)
    silu_gate = gate_value * sigmoid_gate
    active = (silu_gate * up_value).astype(jnp.bfloat16)
    feed_part = cols_inner(active, full_down)
    outputs = hidden + scatter_tensor(feed_part)
    target = teacher.astype(jnp.float32)
    deviation = outputs - target
    squares = jnp.sum(valid_rows[:, None] * deviation * deviation)
    all_tokens = rows * lax.axis_size("dp") * lax.axis_size("tensor")
    grad_out = cotangent + valid_rows[:, None] * deviation * (all_tokens / valid_total)
    grad_feed = gather_tensor(grad_out.astype(jnp.bfloat16))
    down_part = rows_inner(grad_feed, active)
    down_grad = scatter_dp(down_part.astype(jnp.bfloat16).reshape(-1, down_weight.shape[1], local_hidden)).T
    grad_active = jnp.dot(grad_feed, full_down, preferred_element_type=jnp.float32)
    silu_slope = sigmoid_gate * (1.0 + gate_value * (1.0 - sigmoid_gate))
    grad_gate = (grad_active * up_value * silu_slope).astype(jnp.bfloat16)
    grad_upward = (grad_active * silu_gate).astype(jnp.bfloat16)
    grad_normed_two = cols_inner(grad_gate, full_gate) + cols_inner(grad_upward, full_upward)
    grad_rows_two = scatter_tensor(grad_normed_two)
    gate_part = rows_inner(group_two, grad_gate)
    up_part = rows_inner(group_two, grad_upward)
    shard = gate_weight.shape[0]
    gate_grad = scatter_dp(gate_part.astype(jnp.bfloat16).reshape(-1, shard, local_hidden))
    up_grad = scatter_dp(up_part.astype(jnp.bfloat16).reshape(-1, shard, local_hidden))
    gainfeed_part = jnp.sum(grad_rows_two * normed_two, axis=0)
    scaled_two = grad_rows_two * gain_feed
    grad_hidden = grad_out + scale_two * (
        scaled_two - normed_two * jnp.mean(scaled_two * normed_two, axis=1, keepdims=True)
    )
    grad_mixer = gather_tensor(grad_hidden.astype(jnp.bfloat16))
    output_part = rows_inner(grad_mixer, mixer_out)
    output_grad = scatter_dp(output_part.astype(jnp.bfloat16).reshape(-1, shard, local_width)).T
    grad_mixed = jnp.dot(grad_mixer, full_output, preferred_element_type=jnp.float32).astype(jnp.bfloat16)
    grad_mixed_float = grad_mixed.astype(jnp.float32)
    grad_mixgate = (grad_mixed_float * convolved).astype(jnp.bfloat16)
    grad_conv_out = grad_mixed_float * gate_float
    conv_rows = []
    value_from_conv = jnp.zeros_like(value_float)
    for offset in range(CONV):
        conv_rows.append(jnp.sum(grad_conv_out * shift_down(value_float, segments, offset), axis=0))
        value_from_conv = value_from_conv + conv_local[offset] * shift_up(
            grad_conv_out, segments, offset
        )
    grad_queries, key_float, value_attn = attend_backward(
        queries, key_rows, value_rows, segments, log_totals, grad_mixed
    )
    grad_keys = key_float.astype(jnp.bfloat16)
    grad_values = (value_attn + value_from_conv).astype(jnp.bfloat16)

    def project_grad(grads):
        part = rows_inner(group_one, grads).astype(jnp.bfloat16)
        return scatter_dp(part.reshape(-1, shard, local_width))

    query_grad = project_grad(grad_queries)
    key_grad = project_grad(grad_keys)
    value_grad = project_grad(grad_values)
    mixgate_grad = project_grad(grad_mixgate)
    grad_normed_one = (
        cols_inner(grad_queries, full_query)
        + cols_inner(grad_keys, full_key)
        + cols_inner(grad_values, full_value)
        + cols_inner(grad_mixgate, full_mixgate)
    )
    grad_rows_one = scatter_tensor(grad_normed_one)
    gainmix_part = jnp.sum(grad_rows_one * normed_one, axis=0)
    scaled_one = grad_rows_one * gain_mixer
    input_grad = grad_hidden + scale_one * (
        scaled_one - normed_one * jnp.mean(scaled_one * normed_one, axis=1, keepdims=True)
    )
    conv_full = lax.dynamic_update_slice_in_dim(
        jnp.zeros((CONV, D), jnp.float32), jnp.stack(conv_rows), column, 1
    )
    small = sum_all(
        jnp.concatenate(
            [
                conv_full,
                gainmix_part[None],
                gainfeed_part[None],
                jnp.full((1, D), squares, jnp.float32),
            ]
        )
    )
    conv_grad, gainmix_grad, gainfeed_grad = small[:CONV], small[CONV], small[CONV + 1]
    mean_loss = small[CONV + 2, 0] / (valid_total * D)
    return (
        mean_loss,
        outputs,
        input_grad,
        query_grad,
        key_grad,
        value_grad,
        mixgate_grad,
        output_grad,
        conv_grad,
        gainmix_grad,
        gainfeed_grad,
        gate_grad,
        up_grad,
        down_grad,
    )


def solution(mesh):
    rings = mesh.shape["dp"] == 8 and mesh.shape["tensor"] == 4
    return jax.shard_map(
        on_rings if rings else on_any_mesh,
        mesh=mesh,
        in_specs=(
            P(("dp", "tensor"), None),
            P(("dp", "tensor"), None),
            P(("dp", "tensor"), None),
            P("dp"),
            P(("dp", "tensor")),
            P("dp", "tensor"),
            P("dp", "tensor"),
            P("dp", "tensor"),
            P("dp", "tensor"),
            P("tensor", "dp"),
            P(),
            P(),
            P(),
            P("dp", "tensor"),
            P("dp", "tensor"),
            P("tensor", "dp"),
        ),
        out_specs=(
            P(),
            P(("dp", "tensor"), None),
            P(("dp", "tensor"), None),
            P("dp", "tensor"),
            P("dp", "tensor"),
            P("dp", "tensor"),
            P("dp", "tensor"),
            P("tensor", "dp"),
            P(),
            P(),
            P(),
            P("dp", "tensor"),
            P("dp", "tensor"),
            P("tensor", "dp"),
        ),
        check_vma=False,
    )
```

```python
import jax
import jax.numpy as jnp
from jax import lax
from jax.experimental import pallas as pl
from jax.experimental.pallas import tpu as pltpu
from jax.sharding import PartitionSpec as P

D = 1792
HEAD_DIM = 64
WINDOW = 64
CONV = 3
BLOCK = 512
EPS = 1e-05
MESH = pl.DeviceIdType.MESH
VMEM_LIMIT = 63 * 2**20


def rms_scale(values):
    return lax.rsqrt(jnp.mean(values * values, axis=1, keepdims=True) + EPS)


def rows_inner(matrix_left, matrix_right):
    return lax.dot_general(
        matrix_left, matrix_right, (((0,), (0,)), ((), ())), preferred_element_type=jnp.float32
    )


def cols_inner(matrix_left, matrix_right):
    return lax.dot_general(
        matrix_left, matrix_right, (((1,), (1,)), ((), ())), preferred_element_type=jnp.float32
    )


def shift_down(values, segments, offset):
    if offset == 0:
        return values
    shifted = jnp.concatenate(
        [jnp.zeros((offset, values.shape[1]), values.dtype), values[: values.shape[0] - offset]],
        axis=0,
    )
    same_doc = jnp.concatenate(
        [jnp.zeros((offset,), bool), segments[offset:] == segments[:-offset]]
    )
    return jnp.where(same_doc[:, None], shifted, 0.0)


def shift_up(values, segments, offset):
    if offset == 0:
        return values
    shifted = jnp.concatenate(
        [values[offset:], jnp.zeros((offset, values.shape[1]), values.dtype)], axis=0
    )
    same_doc = jnp.concatenate(
        [segments[:-offset] == segments[offset:], jnp.zeros((offset,), bool)]
    )
    return jnp.where(same_doc[:, None], shifted, 0.0)


def pad_front(array, fill_value):
    front = jnp.full((WINDOW,) + array.shape[1:], fill_value, array.dtype)
    return jnp.concatenate([front, array], axis=0)


def block_setup(queries, key_pad, seg_pad, segments, row_start, head_count):
    score_scale = HEAD_DIM ** (-0.5)
    query_rows = lax.dynamic_slice_in_dim(queries, row_start, BLOCK, 0).reshape(
        BLOCK, head_count, HEAD_DIM
    )
    key_block = lax.dynamic_slice_in_dim(key_pad, row_start, BLOCK + WINDOW, 0).reshape(
        BLOCK + WINDOW, head_count, HEAD_DIM
    )
    seg_rows = lax.dynamic_slice_in_dim(segments, row_start, BLOCK, 0)
    seg_keys = lax.dynamic_slice_in_dim(seg_pad, row_start, BLOCK + WINDOW, 0)
    distance = (
        jnp.arange(BLOCK, dtype=jnp.int32)[:, None]
        + WINDOW
        - jnp.arange(BLOCK + WINDOW, dtype=jnp.int32)[None, :]
    )
    allowed = (distance >= 0) & (distance < WINDOW) & (seg_rows[:, None] == seg_keys[None, :])
    scores = (
        jnp.einsum("qhd,khd->hqk", query_rows, key_block, preferred_element_type=jnp.float32)
        * score_scale
    )
    return (query_rows, key_block, jnp.where(allowed[None], scores, -1e30))


def attend_forward(queries, key_rows, value_rows, segments):
    group_rows, local_width = queries.shape
    head_count = local_width // HEAD_DIM
    key_pad = pad_front(key_rows, 0)
    value_pad = pad_front(value_rows, 0)
    seg_pad = pad_front(segments, -1)

    def one_block(block_index):
        row_start = block_index * BLOCK
        query_rows, key_block, scores = block_setup(
            queries, key_pad, seg_pad, segments, row_start, head_count
        )
        row_max = jnp.max(scores, axis=-1, keepdims=True)
        exponent = jnp.exp(scores - row_max)
        row_total = jnp.sum(exponent, axis=-1, keepdims=True)
        attention = (exponent / row_total).astype(jnp.bfloat16)
        value_block = lax.dynamic_slice_in_dim(value_pad, row_start, BLOCK + WINDOW, 0).reshape(
            BLOCK + WINDOW, head_count, HEAD_DIM
        )
        mixed_rows = jnp.einsum(
            "hqk,khd->qhd", attention, value_block, preferred_element_type=jnp.float32
        )
        return (
            mixed_rows.reshape(BLOCK, local_width),
            row_max[..., 0] + jnp.log(row_total[..., 0]),
        )

    blocks_out, log_totals = lax.map(one_block, jnp.arange(group_rows // BLOCK, dtype=jnp.int32))
    return (blocks_out.reshape(group_rows, local_width), log_totals)


def attend_backward(queries, key_rows, value_rows, segments, log_totals, grad_mixed):
    group_rows, local_width = queries.shape
    head_count = local_width // HEAD_DIM
    score_scale = HEAD_DIM ** (-0.5)
    key_pad = pad_front(key_rows, 0)
    value_pad = pad_front(value_rows, 0)
    seg_pad = pad_front(segments, -1)

    def one_block(accumulated, block_pair):
        block_index, log_block = block_pair
        row_start = block_index * BLOCK
        query_rows, key_block, scores = block_setup(
            queries, key_pad, seg_pad, segments, row_start, head_count
        )
        attention = jnp.exp(scores - log_block[..., None])
        value_block = lax.dynamic_slice_in_dim(value_pad, row_start, BLOCK + WINDOW, 0).reshape(
            BLOCK + WINDOW, head_count, HEAD_DIM
        )
        grad_block = lax.dynamic_slice_in_dim(grad_mixed, row_start, BLOCK, 0).reshape(
            BLOCK, head_count, HEAD_DIM
        )
        grad_attention = jnp.einsum(
            "qhd,khd->hqk", grad_block, value_block, preferred_element_type=jnp.float32
        )
        row_inner = jnp.sum(attention * grad_attention, axis=-1, keepdims=True)
        grad_scores = (attention * (grad_attention - row_inner)).astype(jnp.bfloat16)
        grad_query = (
            jnp.einsum("hqk,khd->qhd", grad_scores, key_block, preferred_element_type=jnp.float32)
            * score_scale
        )
        grad_key = (
            jnp.einsum("hqk,qhd->khd", grad_scores, query_rows, preferred_element_type=jnp.float32)
            * score_scale
        )
        grad_value = jnp.einsum(
            "hqk,qhd->khd",
            attention.astype(jnp.bfloat16),
            grad_block,
            preferred_element_type=jnp.float32,
        )
        key_acc, value_acc = accumulated
        key_acc = lax.dynamic_update_slice_in_dim(
            key_acc,
            lax.dynamic_slice_in_dim(key_acc, row_start, BLOCK + WINDOW, 0)
            + grad_key.reshape(BLOCK + WINDOW, local_width),
            row_start,
            0,
        )
        value_acc = lax.dynamic_update_slice_in_dim(
            value_acc,
            lax.dynamic_slice_in_dim(value_acc, row_start, BLOCK + WINDOW, 0)
            + grad_value.reshape(BLOCK + WINDOW, local_width),
            row_start,
            0,
        )
        return ((key_acc, value_acc), grad_query.astype(jnp.bfloat16).reshape(BLOCK, local_width))

    zeros_pad = jnp.zeros((group_rows + WINDOW, local_width), jnp.float32)
    block_ids = jnp.arange(group_rows // BLOCK, dtype=jnp.int32)
    (key_acc, value_acc), query_blocks = lax.scan(
        one_block, (zeros_pad, zeros_pad), (block_ids, log_totals)
    )
    return (query_blocks.reshape(group_rows, local_width), key_acc[WINDOW:], value_acc[WINDOW:])


def pairs_xor(size, mask):
    return [(i, i ^ mask) for i in range(size)]


def pairs_shift(size, step):
    return [(i, (i + step) % size) for i in range(size)]


def put(buffer, block, index):
    return lax.dynamic_update_slice_in_dim(buffer, block[None], index, 0)


def pick(blocks, index):
    return lax.dynamic_index_in_dim(blocks, index, 0, keepdims=False)


def gather_dp(own):
    size = lax.axis_size("dp")
    if size != 8:
        return lax.all_gather(own, "dp", axis=0)
    me = lax.axis_index("dp")
    over_y = pairs_xor(size, 1)
    up, down = pairs_shift(size, 2), pairs_shift(size, -2)
    mate = lax.ppermute(own, "dp", over_y)
    own_below = lax.ppermute(own, "dp", up)
    own_above = lax.ppermute(own, "dp", down)
    mate_below = lax.ppermute(mate, "dp", up)
    mate_above = lax.ppermute(mate, "dp", down)
    own_far = lax.ppermute(own_below, "dp", up)
    mate_far = lax.ppermute(mate_above, "dp", down)
    below, above, far = (me + 6) % size, (me + 2) % size, (me + 4) % size
    full = jnp.zeros((size,) + own.shape, own.dtype)
    for block, index in (
        (own, me),
        (mate, me ^ 1),
        (own_below, below),
        (own_above, above),
        (mate_below, below ^ 1),
        (mate_above, above ^ 1),
        (own_far, far),
        (mate_far, far ^ 1),
    ):
        full = put(full, block, index)
    return full


def scatter_dp(parts):
    size = lax.axis_size("dp")
    if size != 8:
        return lax.psum_scatter(parts, "dp", scatter_dimension=0).astype(jnp.float32)
    me = lax.axis_index("dp")
    over_y = pairs_xor(size, 1)
    up, down = pairs_shift(size, 2), pairs_shift(size, -2)
    below, above, far = (me + 6) % size, (me + 2) % size, (me + 4) % size

    def part(index):
        return pick(parts, index).astype(jnp.float32)

    low = jnp.bfloat16
    own_first = lax.ppermute(pick(parts, far), "dp", up)
    mate_first = lax.ppermute(pick(parts, far ^ 1), "dp", down)
    mate_from_below = lax.ppermute(pick(parts, above ^ 1), "dp", up)
    own_from_above = lax.ppermute(pick(parts, below), "dp", down)
    mate_from_above = lax.ppermute(
        (part(below ^ 1) + mate_first.astype(jnp.float32)).astype(low), "dp", down
    )
    own_from_below = lax.ppermute(
        (part(above) + own_first.astype(jnp.float32)).astype(low), "dp", up
    )
    mate_sum = (
        part(me ^ 1)
        + mate_from_below.astype(jnp.float32)
        + mate_from_above.astype(jnp.float32)
    )
    from_mate = lax.ppermute(mate_sum.astype(low), "dp", over_y)
    own_sum = part(me) + own_from_below.astype(jnp.float32) + own_from_above.astype(jnp.float32)
    return own_sum + from_mate.astype(jnp.float32)


def gather_tensor(own):
    size = lax.axis_size("tensor")
    if size != 4:
        return lax.all_gather(own, "tensor", axis=0, tiled=True)
    me = lax.axis_index("tensor")
    across = lax.ppermute(own, "tensor", pairs_xor(size, 2))
    beside = lax.ppermute(own, "tensor", pairs_xor(size, 1))
    beside_across = lax.ppermute(across, "tensor", pairs_xor(size, 1))
    full = jnp.zeros((size,) + own.shape, own.dtype)
    for block, index in ((own, me), (beside, me ^ 1), (across, me ^ 2), (beside_across, me ^ 3)):
        full = put(full, block, index)
    return full.reshape(size * own.shape[0], own.shape[1])


def scatter_tensor(parts):
    size = lax.axis_size("tensor")
    if size != 4:
        return lax.psum_scatter(
            parts.astype(jnp.bfloat16), "tensor", scatter_dimension=0, tiled=True
        ).astype(jnp.float32)
    me = lax.axis_index("tensor")
    low = jnp.bfloat16
    parts = parts.reshape(size, -1, parts.shape[1])
    beside = lax.ppermute(pick(parts, me ^ 3).astype(low), "tensor", pairs_xor(size, 1))
    sent = (pick(parts, me ^ 2).astype(jnp.float32) + beside.astype(jnp.float32)).astype(low)
    across = lax.ppermute(sent, "tensor", pairs_xor(size, 2))
    beside_own = lax.ppermute(pick(parts, me ^ 1).astype(low), "tensor", pairs_xor(size, 1))
    return (
        pick(parts, me).astype(jnp.float32)
        + beside_own.astype(jnp.float32)
        + across.astype(jnp.float32)
    )


def sum_all(values):
    dp_size, tensor_size = lax.axis_size("dp"), lax.axis_size("tensor")
    if dp_size != 8 or tensor_size != 4:
        return lax.psum(values, ("dp", "tensor"))
    for axis, size, mask in (
        ("tensor", tensor_size, 1),
        ("tensor", tensor_size, 2),
        ("dp", dp_size, 1),
        ("dp", dp_size, 2),
        ("dp", dp_size, 6),
    ):
        values = values + lax.ppermute(values, axis, pairs_xor(size, mask))
    return values


TILE = 64
LANES = 128
PIECES = 4
SHARE = 2


def neighbours():
    d, t = lax.axis_index("dp"), lax.axis_index("tensor")
    z, y = d // 2, lax.rem(d, 2)
    core = t + 1 - 2 * lax.rem(t, 2)
    place = z + y * (7 - 2 * z)

    def ring(offset):
        position = lax.rem(place + offset + 16, 8)
        side = position // 4
        return 2 * (position + side * (7 - 2 * position)) + side

    return dict(
        d=d,
        t=t,
        ring=ring,
        core=core,
        cross=lax.rem(t + 2, 4),
        cross_core=lax.rem(core + 2, 4),
        mate=d + 1 - 2 * y,
        z_pair=2 * (z + 1 - 2 * lax.rem(z, 2)) + y,
        z_mirror=2 * (3 - z) + y,
    )


def hail(at, everyone=False):
    d, t = at["d"], at["t"]
    devices = [(at["ring"](1), t), (at["ring"](-1), t), (d, at["core"]), (d, at["cross"])]
    if everyone:
        devices += [(at["mate"], t), (at["z_pair"], t), (at["z_mirror"], t)]
    for device in devices:
        pl.semaphore_signal(
            pltpu.get_barrier_semaphore(), inc=1, device_id=device, device_id_type=MESH
        )
    return len(devices)


def meet(number):
    pl.semaphore_wait(pltpu.get_barrier_semaphore(), number)


def remote(source, target, sems, index, device):
    return pltpu.make_async_remote_copy(
        src_ref=source,
        dst_ref=target,
        send_sem=sems[0].at[index],
        recv_sem=sems[1].at[index],
        device_id=device,
        device_id_type=MESH,
    )


def pieces_of(half, count):
    if count == 1:
        return [(0, half)]
    first = (half // 2 + 15) // 16 * 16
    return [(0, first), (first, half - first)]


class RingGather:
    def __init__(self, at, own, slot, sems, base, local_sem, count=2):
        half = own.shape[0] // 2
        ring, t = at["ring"], at["t"]
        self.local = pltpu.make_async_copy(own, slot(at["d"], 0, 2 * half), local_sem)
        self.sends, self.receives, self.at = [], [], 0
        for s in range(7):
            for k, (first, size) in enumerate(pieces_of(half, count)):
                sends, receives = [], []
                for way, sign in ((0, 1), (1, -1)):
                    to, row = (ring(sign), t), way * half + first
                    index = base + (s * count + k) * 2 + way
                    here = slot(ring(-sign * s), row, size)
                    there = slot(ring(-sign * (s + 1)), row, size)
                    source = own.at[pl.ds(row, size)] if s == 0 else here
                    sends.append(remote(source, here, sems, index, to))
                    receives.append(remote(there, there, sems, index, to))
                self.sends.append(sends)
                self.receives.append(receives)
        self.count = count

    def start(self):
        for copies in self.sends[: self.count]:
            for copy in copies:
                copy.start()
        self.local.start()

    def tick(self):
        if self.at < len(self.receives):
            for way in range(2):
                self.receives[self.at][way].wait_recv()
                if self.at + self.count < len(self.sends):
                    self.sends[self.at + self.count][way].start()
            self.at += 1

    def finish(self):
        while self.at < len(self.receives):
            self.tick()
        self.local.wait()

    def drain(self):
        for sends in self.sends:
            for copy in sends:
                copy.wait_send()


class RingScatter:
    def __init__(self, at, left, right, slots, term, out, sems, base, count=2, side=None):
        self.ring, self.left, self.right, self.side = at["ring"], left, right, side
        self.slots, self.term, self.out = slots, term, out
        self.half, self.columns = slots.shape[2], slots.shape[3]
        self.pieces = pieces_of(self.half, count)
        self.at = 0
        self.sends = []
        for s in range(7):
            for k, (first, size) in enumerate(self.pieces):
                rows = pl.ds(first, size)
                self.sends.append(
                    [
                        remote(
                            slots.at[way, s, rows], slots.at[way, s + 1, rows], sems,
                            base + (s * count + k) * 2 + way, (at["ring"](sign), at["t"]),
                        )
                        for way, sign in ((0, 1), (1, -1))
                    ]
                )

    def compute(self, away):
        half = self.half
        first = pl.multiple_of(self.ring(-away) * 2 * half, half)
        second = pl.multiple_of(self.ring(away) * 2 * half + half, half)
        if self.side is not None:
            left, beside = [
                jnp.concatenate([ref[pl.ds(first, half)], ref[pl.ds(second, half)]], axis=0)
                for ref in (self.left, self.side)
            ]
            self.term[...] = jnp.concatenate(
                [nn_dot(left, self.right[...]), beside.astype(jnp.float32)], axis=1
            )
            return
        width = 512
        whole = self.columns // width * width

        def block(lanes):
            left = jnp.concatenate(
                [self.left[pl.ds(first, half)], self.left[pl.ds(second, half)]], axis=0
            )
            self.term[:, lanes] = nn_dot(left, self.right[:, lanes])

        @pl.loop(0, whole // width)
        def _(i):
            block(pl.ds(pl.multiple_of(i * width, width), width))

        if whole < self.columns:
            block(pl.ds(whole, self.columns - whole))

    def prepare(self):
        self.compute(1)
        for way in range(2):
            self.slots[way, 0] = self.term[pl.ds(way * self.half, self.half)].astype(jnp.bfloat16)

    def launch(self):
        for k in range(len(self.pieces)):
            for way in range(2):
                self.sends[k][way].start()

    def start(self):
        self.prepare()
        self.launch()
        self.compute(2)

    def tick(self):
        if self.at == len(self.sends):
            return
        count = len(self.pieces)
        s, k = divmod(self.at, count)
        first, size = self.pieces[k]
        for way in range(2):
            here, rows = pl.ds(first, size), pl.ds(way * self.half + first, size)
            self.sends[self.at][way].wait_recv()
            total = self.slots[way, s + 1, here].astype(jnp.float32) + self.term[rows]
            if s < 6:
                self.slots[way, s + 1, here] = total.astype(jnp.bfloat16)
                self.sends[self.at + count][way].start()
            else:
                self.out[rows] = total
        self.at += 1
        if k == count - 1 and s < 6:
            self.compute(s + 3)

    def finish(self):
        while self.at < len(self.sends):
            self.tick()
        for sends in self.sends:
            for copy in sends:
                copy.wait_send()


class GatherTensor:
    def __init__(self, at, full, rows, sems, base):
        def block(index):
            return full.at[pl.ds(pl.multiple_of(index * rows, rows), rows)]

        mine, across = block(at["t"]), block(at["cross"])
        self.to_core = remote(mine, mine, sems, base, (at["d"], at["core"]))
        self.to_cross = remote(mine, mine, sems, base + 1, (at["d"], at["cross"]))
        self.relay_core = remote(across, across, sems, base + 2, (at["d"], at["core"]))
        places = (block(at["core"]), across, block(at["cross_core"]))
        self.receives = [
            remote(place, place, sems, base + k, (at["d"], at["core"]))
            for k, place in enumerate(places)
        ]

    def start(self):
        self.to_cross.start()
        self.to_core.start()

    def relay(self):
        self.receives[1].wait_recv()
        self.relay_core.start()

    def drain(self):
        for send in (self.to_core, self.to_cross, self.relay_core):
            send.wait_send()

    def finish(self):
        self.receives[0].wait_recv()
        self.receives[2].wait_recv()
        self.drain()


def sum_rows(at, block_part, send, receive, total, sems, base, idle=lambda point: None):
    to_core, to_cross = (at["d"], at["core"]), (at["d"], at["cross"])
    low = jnp.bfloat16
    first = remote(send.at[0], receive.at[0], sems, base, to_core)
    second = remote(send.at[1], receive.at[1], sems, base + 1, to_cross)
    third = remote(send.at[2], receive.at[2], sems, base + 2, to_core)
    send[0] = block_part(at["cross_core"]).astype(low)
    first.start()
    total[...] = block_part(at["cross"])
    first.wait_recv()
    send[1] = (total[...] + receive[0].astype(jnp.float32)).astype(low)
    second.start()
    idle(0)
    send[2] = block_part(at["core"]).astype(low)
    third.start()
    idle(1)
    total[...] = block_part(at["t"])
    third.wait_recv()
    total[...] += receive[2].astype(jnp.float32)
    idle(2)
    second.wait_recv()
    total[...] += receive[1].astype(jnp.float32)
    for copy in (first, second, third):
        copy.wait_send()


class GatherPieces:
    def __init__(self, at, full, rows, count, sems, base):
        size = rows // count
        to_core, to_cross = (at["d"], at["core"]), (at["d"], at["cross"])

        def place(block, c):
            return full.at[pl.ds(pl.multiple_of(block * rows + c * size, size), size)]

        def copies(k, block, to):
            return [
                remote(place(block, c), place(block, c), sems, base + k * count + c, to)
                for c in range(count)
            ]

        self.to_core = copies(0, at["t"], to_core)
        self.to_cross = copies(1, at["t"], to_cross)
        self.relay_core = copies(2, at["cross"], to_core)
        self.receives = [
            copies(k, block, to_core) for k, block in enumerate((at["core"], at["cross"], at["cross_core"]))
        ]

    def start(self, c):
        self.to_cross[c].start()
        self.to_core[c].start()

    def relay(self):
        for receive, send in zip(self.receives[1], self.relay_core):
            receive.wait_recv()
            send.start()

    def wait(self, k):
        for receive in self.receives[k]:
            receive.wait_recv()

    def drain(self):
        for send in self.to_core + self.to_cross + self.relay_core:
            send.wait_send()


def sum_pieces(
    at, block_part, send, receive, total, sems, base, count, done, idle=lambda: None
):
    to_core, to_cross = (at["d"], at["core"]), (at["d"], at["cross"])
    low = jnp.bfloat16
    size = total.shape[0] // count
    pieces = [pl.ds(c * size, size) for c in range(count)]

    def copies(k, to):
        return [
            remote(send.at[k, piece], receive.at[k, piece], sems, base + k * count + c, to)
            for c, piece in enumerate(pieces)
        ]

    first, second, third = copies(0, to_core), copies(1, to_cross), copies(2, to_core)
    send[0] = block_part(at["cross_core"]).astype(low)
    for copy in first:
        copy.start()
    total[...] = block_part(at["cross"])
    for c, piece in enumerate(pieces):
        first[c].wait_recv()
        send[1, piece] = (total[piece] + receive[0, piece].astype(jnp.float32)).astype(low)
        second[c].start()
    idle()
    send[2] = block_part(at["core"]).astype(low)
    for copy in third:
        copy.start()
    total[...] = block_part(at["t"])
    for c, piece in enumerate(pieces):
        idle()
        third[c].wait_recv()
        second[c].wait_recv()
        total[piece] += receive[2, piece].astype(jnp.float32) + receive[1, piece].astype(jnp.float32)
        done(c)
    for copy in first + second + third:
        copy.wait_send()


class SumAll:
    def __init__(self, at, value, received, sems, base, over=("core", "cross", "mate", "z_pair", "z_mirror")):
        d, t = at["d"], at["t"]
        self.value, self.received, self.s = value, received, 0
        self.copies = [
            remote(
                value.at[k], received.at[k], sems, base + k,
                (d, at[name]) if name in ("core", "cross") else (at[name], t),
            )
            for k, name in enumerate(over)
        ]

    def start(self):
        self.copies[0].start()

    def step(self):
        s = self.s
        if s == len(self.copies):
            return
        self.copies[s].wait_recv()
        self.value[s + 1] = self.value[s] + self.received[s]
        if s + 1 < len(self.copies):
            self.copies[s + 1].start()
        self.s += 1

    def finish(self):
        while self.s < len(self.copies):
            self.step()
        for copy in self.copies:
            copy.wait_send()


def nt_dot(left, right):
    return lax.dot_general(
        left, right, (((1,), (1,)), ((), ())), preferred_element_type=jnp.float32
    )


def nn_dot(left, right):
    return lax.dot_general(
        left, right, (((1,), (0,)), ((), ())), preferred_element_type=jnp.float32
    )


def tn_dot(left, right):
    return lax.dot_general(
        left, right, (((0,), (0,)), ((), ())), preferred_element_type=jnp.float32
    )


def head_groups(width):
    heads = width // HEAD_DIM
    return [(2 * HEAD_DIM * j, min(2, heads - 2 * j)) for j in range((heads + 1) // 2)]


def split_heads(tile, heads):
    if heads == 1:
        return tile
    lane = lax.broadcasted_iota(jnp.int32, tile.shape, 1)
    zero = jnp.zeros_like(tile)
    return jnp.concatenate(
        [jnp.where(lane < HEAD_DIM, tile, zero), jnp.where(lane < HEAD_DIM, zero, tile)], axis=0
    )


def join_heads(stacked, heads):
    if heads == 1:
        return stacked
    half = stacked.shape[0] // 2
    lane = lax.broadcasted_iota(jnp.int32, (half, stacked.shape[1]), 1)
    return jnp.where(lane < HEAD_DIM, stacked[:half], stacked[half:])


def convolve(window, taps, lanes, same_one, same_two):
    one = pltpu.roll(window, 1, axis=0)[TILE:] * same_one
    two = pltpu.roll(window, 2, axis=0)[TILE:] * same_two
    rows = (window[TILE:], one, two)
    return sum(taps[m : m + 1, lanes] * rows[m] for m in range(CONV)), rows


def attend_tile(i, q, k_pad, v_pad, u, seg_q, seg_k, same, taps, p_out, o):
    row = pl.multiple_of(i * TILE, TILE)
    at_row, at_window = pl.ds(row, TILE), pl.ds(row, 2 * TILE)
    distance = (
        lax.broadcasted_iota(jnp.int32, (TILE, 2 * TILE), 0)
        + TILE
        - lax.broadcasted_iota(jnp.int32, (TILE, 2 * TILE), 1)
    )
    allowed = (seg_q[at_row] == seg_k[i]) & (distance >= 0) & (distance < WINDOW)
    same_one, same_two = same[at_row, 0:1], same[at_row, 1:2]
    for lane, heads in head_groups(q.shape[1]):
        lanes = pl.ds(lane, heads * HEAD_DIM)
        values = v_pad[at_window, lanes]
        allow = jnp.concatenate([allowed] * heads, axis=0) if heads > 1 else allowed
        scores = nt_dot(split_heads(q[at_row, lanes], heads), k_pad[at_window, lanes])
        scores = jnp.where(allow, scores * (HEAD_DIM**-0.5), -1e30)
        exponent = jnp.exp(scores - jnp.max(scores, axis=1, keepdims=True))
        chance = exponent * (1.0 / jnp.sum(exponent, axis=1, keepdims=True))
        chance = chance.astype(jnp.bfloat16)
        p_out[i, pl.ds((lane // HEAD_DIM) * TILE, heads * TILE), :] = chance
        mixed = join_heads(nn_dot(chance, values), heads)
        convolved, _ = convolve(values.astype(jnp.float32), taps, lanes, same_one, same_two)
        o[at_row, lanes] = (mixed + convolved * u[at_row, lanes].astype(jnp.float32)).astype(
            jnp.bfloat16
        )


def attend_back_tile(
    i, q, k_pad, v_pad, u, p, same, taps, do, dk, dv, conv_sum
):
    row = pl.multiple_of(i * TILE, TILE)
    at_row, at_window = pl.ds(row, TILE), pl.ds(row, 2 * TILE)
    same_one, same_two = same[at_row, 0:1], same[at_row, 1:2]
    for lane, heads in head_groups(q.shape[1]):
        lanes = pl.ds(lane, heads * HEAD_DIM)
        keys, values = k_pad[at_window, lanes], v_pad[at_window, lanes]
        grad = do[at_row, lanes]
        grad_heads = split_heads(grad, heads)
        chance_low = p[i, pl.ds((lane // HEAD_DIM) * TILE, heads * TILE), :]
        chance = chance_low.astype(jnp.float32)
        weighted = chance * nt_dot(grad_heads, values)
        slope = weighted - chance * jnp.sum(weighted, axis=1, keepdims=True)
        slope = (slope * (HEAD_DIM**-0.5)).astype(jnp.bfloat16)
        dk[at_window, lanes] += tn_dot(slope, split_heads(q[at_row, lanes], heads))
        q[at_row, lanes] = join_heads(nn_dot(slope, keys), heads).astype(jnp.bfloat16)
        convolved, rows = convolve(values.astype(jnp.float32), taps, lanes, same_one, same_two)
        grad = grad.astype(jnp.float32)
        do[at_row, lanes] = (grad * convolved).astype(jnp.bfloat16)
        grad_conv = grad * u[at_row, lanes].astype(jnp.float32)
        back = tn_dot(chance_low, grad_heads)
        zero = jnp.zeros_like(grad_conv)
        for m, same_m in enumerate((None, same_one, same_two)):
            conv_sum[m, :, lanes] += jnp.sum(grad_conv * rows[m], axis=0, keepdims=True)
            term = taps[m : m + 1, lanes] * grad_conv
            term = term if m == 0 else term * same_m
            term = jnp.concatenate([zero, term], axis=0)
            back = back + (term if m == 0 else pltpu.roll(term, 2 * TILE - m, axis=0))
        dv[at_window, lanes] += back


def rolled(values, offset):
    turned = pltpu.roll(values, offset, axis=1)
    lane = lax.broadcasted_iota(jnp.int32, values.shape, 1)
    return jnp.where(lane < offset, pltpu.roll(turned, 1, axis=0), turned)


def make_tables(segments, seg_q, seg_k, same):
    values = segments[...]
    row = lax.broadcasted_iota(jnp.int32, values.shape, 0)
    lane = lax.broadcasted_iota(jnp.int32, values.shape, 1)
    columns = values.T
    matches = [
        jnp.where((values == rolled(values, m)) & ((row > 0) | (lane >= m)), 1.0, 0.0).astype(jnp.float32).T
        for m in range(1, CONV)
    ]
    crossing = rolled(values, TILE)
    crossing = jnp.where((row == 0) & (lane < TILE), -1, crossing)
    for n in range(values.shape[0]):
        rows = pl.ds(n * LANES, LANES)
        seg_q[rows] = columns[:, n : n + 1]
        for m, match in enumerate(matches):
            same[rows, m : m + 1] = match[:, n : n + 1]
        seg_k[2 * n] = crossing[n : n + 1]
        seg_k[2 * n + 1] = values[n : n + 1]


def row_of(gain):
    return gain[...].reshape(1, -1)


def norm_rows(values, gain):
    scale = lax.rsqrt(jnp.mean(values * values, axis=1, keepdims=True) + EPS)
    return (values * scale * gain).astype(jnp.bfloat16)


def norm_back(values, grad, gain):
    scale = lax.rsqrt(jnp.mean(values * values, axis=1, keepdims=True) + EPS)
    normed = values * scale
    scaled = grad * gain
    through = scale * (scaled - normed * jnp.mean(scaled * normed, axis=1, keepdims=True))
    return through, jnp.sum(grad * normed, axis=0, keepdims=True)


def chunks_of(rows, size=64):
    def run(body):
        @pl.loop(0, rows // size)
        def _(i):
            body(pl.multiple_of(i * size, size), size)

    return run


def forward_kernel(
    x, valid_lanes, gain_one, gain_two, segments, taps,
    gate_in, up_in, out_in, down_in, mix_own, cotangent_in, teacher_in,
    mix_out, last_out, feed_out, down_out, h1t_out, h2t_out, dybt_out, q_out, k_out, v_out, u_out, p_out,
    o_out, x1_out, dyb_out, slopes_out, active_out, act_out, dy_out, count_out, squares_out, same,
    valid, seg_q, seg_k, gate_own, up_own, out_turned, down_own, feed_own, out_own, mix, last, feed, down, h1, turned, h2, q, k_pad, v_pad, u, p, o, slopes, active, x1, side, teacher,
    send, receive, total, count, count_in,
    send_sems, recv_sems, local_sems, load_sems, out_sems,
):
    at = neighbours()
    sems = (send_sems, recv_sems)
    rows, shard = x.shape[0], mix_own.shape[0]
    low = jnp.bfloat16
    meet(hail(at, everyone=True))

    def slot_of(full):
        return lambda i, first, size: full.at[pl.ds(pl.multiple_of(i * shard + first, 16), size)]

    mix_ring = RingGather(at, mix_own, slot_of(mix), sems, 0, local_sems.at[0])
    last_ring = RingGather(at, out_own, slot_of(last), sems, 28, local_sems.at[1], count=1)
    feed_ring = RingGather(at, feed_own, slot_of(feed), sems, 42, local_sems.at[2])
    down_ring = RingGather(
        at, down_own.at[:, pl.ds(0, down.shape[1])], slot_of(down), sems, 70, local_sems.at[3]
    )
    dyb = h1
    group_one = GatherTensor(at, h1, rows, sems, 98)
    group_two = GatherTensor(at, h2, rows, sems, 101)
    group_back = GatherPieces(at, dyb, rows, PIECES, sems, 115)
    counting = SumAll(at, count, count_in, sems, 110)
    local = q.shape[1]
    main = local // LANES * LANES
    tail = local - main
    keeps = []

    def keep(source, target):
        copy = pltpu.make_async_copy(source, target, out_sems.at[len(keeps)])
        copy.start()
        keeps.append(copy)
        return copy

    def tick():
        last_ring.tick()
        if feed_ring.at < len(feed_ring.receives):
            feed_ring.tick()
            if feed_ring.at == len(feed_ring.receives) - 2:
                down_ring.start()
        else:
            down_ring.tick()

    def turn(source, block):
        here = pl.ds(pl.multiple_of(block * rows, rows), rows)
        turned[:, here] = source[here].T

    mix_ring.start()

    @chunks_of(rows)
    def _(row, size):
        h1[pl.ds(pl.multiple_of(at["t"] * rows + row, size), size)] = norm_rows(
            x[pl.ds(row, size)].astype(jnp.float32), row_of(gain_one)
        )

    group_one.start()
    flags = valid_lanes[...].astype(jnp.float32)
    count[0] = jnp.full(count.shape[1:], jnp.sum(flags), jnp.float32)
    counting.start()
    load_teacher = pltpu.make_async_copy(teacher_in, teacher, load_sems.at[0])
    load_cotangent = pltpu.make_async_copy(cotangent_in, side, load_sems.at[1])
    raw = [
        pltpu.make_async_copy(source, target, load_sems.at[2 + n])
        for n, (source, target) in enumerate(
            ((gate_in, gate_own), (up_in, up_own), (out_in, out_turned), (down_in, down_own))
        )
    ]
    for load in raw + [load_teacher, load_cotangent]:
        load.start()
    k_pad[pl.ds(0, TILE)] = jnp.zeros((TILE, local), k_pad.dtype)
    v_pad[pl.ds(0, TILE)] = jnp.zeros((TILE, local), v_pad.dtype)
    make_tables(segments, seg_q, seg_k, same)
    width = gate_own.shape[1]
    cut = width // LANES * LANES
    rest = width - cut
    for load in raw:
        load.wait()
    feed_own[:, pl.ds(0, cut)] = gate_own[:, pl.ds(0, cut)]
    feed_own[:, pl.ds(cut, cut)] = up_own[:, pl.ds(0, cut)]
    ends = [own[:, pl.ds(cut, rest)].astype(jnp.float32) for own in (gate_own, up_own)]
    feed_own[:, pl.ds(2 * cut, 2 * rest)] = jnp.concatenate(ends, axis=1).astype(low)
    ends = [out_turned[...].astype(jnp.float32).T, down_own[:, pl.ds(cut, rest)].astype(jnp.float32)]
    out_own[...] = jnp.concatenate(ends, axis=1).astype(low)
    spare = jnp.zeros((8 - flags.shape[0], LANES), jnp.float32)
    columns = jnp.concatenate([flags, spare], axis=0).T
    for n in range(flags.shape[0]):
        valid[pl.ds(n * LANES, LANES)] = columns[:, n : n + 1]
    for _ in range(6):
        mix_ring.tick()
    group_one.relay()
    mix_ring.tick()
    mix_ring.tick()
    group_one.finish()
    mix_ring.tick()
    for k in range(2):

        @pl.loop(2 * k, 2 * k + 2)
        def _(j):
            turn(h1, j)

        mix_ring.tick()
    keep_h1t = keep(turned, h1t_out)
    last_ring.start()
    mix_ring.tick()
    last_ring.tick()
    feed_ring.start()
    mix_ring.tick()
    last_ring.tick()
    mix_ring.finish()
    last_ring.tick()
    keep(mix, mix_out)

    def project(j):
        here = pl.ds(pl.multiple_of(j * rows, rows), rows)
        there = pl.ds(pl.multiple_of(j * rows + TILE, TILE), rows)
        left = h1[here]
        pair = nn_dot(left, mix[:, pl.ds(0, 2 * main)]).astype(low)
        q[here, pl.ds(0, main)] = pair[:, :main]
        k_pad[there, pl.ds(0, main)] = pair[:, main:]
        pair = nn_dot(left, mix[:, pl.ds(2 * main, 2 * main)]).astype(low)
        v_pad[there, pl.ds(0, main)] = pair[:, :main]
        u[here, pl.ds(0, main)] = pair[:, main:]
        ends = nn_dot(left, mix[:, pl.ds(4 * main, 4 * tail)])
        q[here, pl.ds(main, tail)] = ends[:, :tail].astype(low)
        k_pad[there, pl.ds(main, tail)] = ends[:, tail : 2 * tail].astype(low)
        v_pad[there, pl.ds(main, tail)] = ends[:, 2 * tail : 3 * tail].astype(low)
        u[here, pl.ds(main, tail)] = ends[:, 3 * tail :].astype(low)

    def projects(first, last_block):
        @pl.loop(first, last_block)
        def _(j):
            project(j)

    projects(0, 2)
    tick()
    counting.step()
    projects(2, 4)
    for source, target in ((q, q_out), (k_pad, k_out), (v_pad, v_out), (u, u_out)):
        keep(source, target)
    tick()
    tiles = q.shape[0] // TILE

    def attend(first, last_tile):
        @pl.loop(first, last_tile)
        def _(i):
            attend_tile(i, q, k_pad, v_pad, u, seg_q, seg_k, same, taps, p, o)

    for k in range(4):
        attend(k * tiles // 4, (k + 1) * tiles // 4)
        tick()
        if k % 2:
            counting.step()
    last_ring.finish()
    keep(last, last_out)
    keep(p, p_out)
    keep(o, o_out)

    def mixed_part(block):
        return nt_dot(o[pl.ds(pl.multiple_of(block * rows, rows), rows)], last[:, pl.ds(0, local)])

    def idle(point):
        tick()
        if point == 2:
            tick()
            tick()

    sum_rows(at, mixed_part, send, receive, total, sems, 107, idle=idle)

    @chunks_of(rows)
    def _(row, size):
        here = pl.ds(row, size)
        hidden = total[here] + x[here].astype(jnp.float32)
        x1[here] = hidden
        h2[pl.ds(pl.multiple_of(at["t"] * rows + row, size), size)] = norm_rows(hidden, row_of(gain_two))

    group_two.start()
    keep(x1, x1_out)
    for _ in range(3):
        tick()
    counting.step()
    tick()
    group_two.relay()
    tick()
    counting.finish()
    keep(count.at[5], count_out)
    group_two.finish()
    while feed_ring.at < len(feed_ring.receives):
        tick()
    feed_ring.finish()
    keep(feed, feed_out)
    parts, _ = feed_lanes(width)

    def widen(j):
        here = pl.ds(pl.multiple_of(j * (rows // 2), rows // 2), rows // 2)
        left = h2[here]
        for own, gate_lanes, up_lanes in parts:
            a, by_gate, by_up = gated(nn_dot(left, feed[:, gate_lanes]), nn_dot(left, feed[:, up_lanes]))
            active[here, own] = a.astype(low)
            slopes[here, gate_lanes] = by_gate.astype(low)
            slopes[here, up_lanes] = by_up.astype(low)
        both = nn_dot(left, feed[:, pl.ds(2 * cut, 2 * rest)])
        a, by_gate, by_up = gated(both[:, :rest], both[:, rest:])
        active[here, pl.ds(cut, rest)] = a.astype(low)
        slopes[here, pl.ds(2 * cut, 2 * rest)] = jnp.concatenate([by_gate, by_up], axis=1).astype(low)

    for k in range(8):

        @pl.loop(k, k + 1)
        def _(j):
            widen(j)

        tick()
    keep(active, active_out)
    keep(slopes, slopes_out)
    keep_h1t.wait()
    for k in range(4):

        @pl.loop(k, k + 1)
        def _(j):
            turn(h2, j)

        tick()
    keep_h2t = keep(turned, h2t_out)
    down_ring.finish()
    keep(down, down_out)
    load_teacher.wait()
    load_cotangent.wait()

    def fed_part(block):
        here = pl.ds(pl.multiple_of(block * rows, rows), rows)
        ends = nt_dot(active[here, pl.ds(cut, rest)], last[:, pl.ds(local, rest)])
        return ends + nt_dot(active[here, pl.ds(0, cut)], down[...])

    weight = (rows * 4 * 8) / count[5, 0:1, 0:1]
    squares_out[...] = jnp.zeros_like(squares_out)
    piece, step = rows // PIECES, 32

    def judge(c):
        @pl.loop(0, piece // step)
        def _(i):
            row = pl.multiple_of(c * piece + i * step, step)
            here = pl.ds(row, step)
            result = total[here] + x1[here]
            deviation = result - teacher[here].astype(jnp.float32)
            kept = valid[here, 0:1] * deviation
            total[here] = result
            squares_out[0:1] += jnp.sum(kept * deviation, axis=0, keepdims=True)
            grad = side[here] + kept * weight
            side[here] = grad
            dyb[pl.ds(pl.multiple_of(at["t"] * rows + row, step), step)] = grad.astype(low)

        group_back.start(c)

    sum_pieces(at, fed_part, send, receive, total, sems, 115 + 3 * PIECES, PIECES, judge)
    keep(total, act_out)
    keep(side, dy_out)
    keep_h2t.wait()

    def spread(block):
        here = pl.ds(pl.multiple_of(block * rows, rows), rows)
        turn(dyb, block)
        keep(dyb.at[here], dyb_out.at[here])
        keep(turned.at[:, here], dybt_out.at[:, here])

    spread(at["t"])
    group_back.wait(0)
    spread(at["core"])
    group_back.relay()
    spread(at["cross"])
    group_back.wait(2)
    spread(at["cross_core"])
    group_back.drain()
    for ring in (mix_ring, last_ring, feed_ring, down_ring):
        ring.drain()
    for copy in keeps:
        if copy is not keep_h1t and copy is not keep_h2t:
            copy.wait()


def specs():
    return pl.BlockSpec(memory_space=pltpu.VMEM), pl.BlockSpec(memory_space=pl.ANY)


def shape(*dims, kind=jnp.bfloat16):
    return jax.ShapeDtypeStruct(dims, kind)


def params(identity):
    return pltpu.CompilerParams(
        collective_id=identity, has_side_effects=True, vmem_limit_bytes=VMEM_LIMIT
    )


def dma(count):
    return pltpu.SemaphoreType.DMA((count,))


def forward(
    x, valid_lanes, gain_one, gain_two, segments, taps, mix_own, output_weight, gate_own, up_own, down_own,
    cotangent, teacher,
):
    rows, width = x.shape
    shard = mix_own.shape[0]
    local, hidden = mix_own.shape[1] // 4, gate_own.shape[1]
    cut = hidden // LANES * LANES
    both = local + hidden - cut
    everyone, depth = 4 * rows, 8 * shard
    low, wide = jnp.bfloat16, jnp.float32
    tiles, heads = everyone // TILE, local // HEAD_DIM
    vmem, hbm = specs()
    return pl.pallas_call(
        forward_kernel,
        out_shape=(
            shape(depth, 4 * local),
            shape(depth, both),
            shape(depth, 2 * hidden),
            shape(depth, cut),
            shape(width, everyone),
            shape(width, everyone),
            shape(width, everyone),
            shape(everyone, local),
            shape(everyone + TILE, local),
            shape(everyone + TILE, local),
            shape(everyone, local),
            shape(tiles, heads * TILE, 2 * TILE),
            shape(everyone, local),
            shape(rows, width, kind=wide),
            shape(everyone, width),
            shape(everyone, 2 * hidden),
            shape(everyone, hidden),
            shape(rows, width, kind=wide),
            shape(rows, width, kind=wide),
            shape(8, LANES, kind=wide),
            shape(8, width, kind=wide),
            shape(everyone, CONV - 1, kind=wide),
        ),
        in_specs=[vmem] * 6 + [hbm] * 7,
        out_specs=(hbm,) * 20 + (vmem,) * 2,
        scratch_shapes=[
            pltpu.VMEM((rows, 1), wide),
            pltpu.VMEM((everyone, 1), jnp.int32),
            pltpu.VMEM((tiles, 1, 2 * TILE), jnp.int32),
            pltpu.VMEM((shard, hidden), low),
            pltpu.VMEM((shard, hidden), low),
            pltpu.VMEM(output_weight.shape, low),
            pltpu.VMEM((shard, hidden), low),
            pltpu.VMEM((shard, 2 * hidden), low),
            pltpu.VMEM((shard, both), low),
            pltpu.VMEM((depth, 4 * local), low),
            pltpu.VMEM((depth, both), low),
            pltpu.VMEM((depth, 2 * hidden), low),
            pltpu.VMEM((depth, cut), low),
            pltpu.VMEM((everyone, width), low),
            pltpu.VMEM((width, everyone), low),
            pltpu.VMEM((everyone, width), low),
            pltpu.VMEM((everyone, local), low),
            pltpu.VMEM((everyone + TILE, local), low),
            pltpu.VMEM((everyone + TILE, local), low),
            pltpu.VMEM((everyone, local), low),
            pltpu.VMEM((tiles, heads * TILE, 2 * TILE), low),
            pltpu.VMEM((everyone, local), low),
            pltpu.VMEM((everyone, 2 * hidden), low),
            pltpu.VMEM((everyone, hidden), low),
            pltpu.VMEM((rows, width), wide),
            pltpu.VMEM((rows, width), wide),
            pltpu.VMEM((rows, width), low),
            pltpu.VMEM((3, rows, width), low),
            pltpu.VMEM((3, rows, width), low),
            pltpu.VMEM((rows, width), wide),
            pltpu.VMEM((6, 8, LANES), wide),
            pltpu.VMEM((5, 8, LANES), wide),
            dma(115 + 6 * PIECES),
            dma(115 + 6 * PIECES),
            dma(4),
            dma(6),
            dma(26),
        ],
        compiler_params=params(1),
    )(
        x, valid_lanes, gain_one, gain_two, segments, taps, gate_own, up_own, output_weight, down_own, mix_own,
        cotangent, teacher,
    )


def feed_lanes(hidden):
    main = hidden // LANES * LANES
    cut = main // 2 // LANES * LANES
    parts = [(0, cut), (cut, main - cut)]
    return [(pl.ds(a, n), pl.ds(a, n), pl.ds(main + a, n)) for a, n in parts], main


def gated(gate, up):
    sigmoid = jax.nn.sigmoid(gate)
    silu = gate * sigmoid
    return silu * up, up * sigmoid * (1.0 + gate * (1.0 - sigmoid)), silu


def feed_backward_kernel(
    gain, dyb_in, dybt_in, h2t_in, down_in, feed_in, active_in, slopes_in, last_in, x1_in, dy_in,
    down_grad, gate_grad, gain_part, dx1_out, dx1t_out, do_out, slopes_out, ends_out,
    dyb, dybt, h2t, down, feed, active, slopes, last, do, x1, dy, total, down_slots, gate_slots,
    down_term, gate_term, ends, send, receive,
    send_sems, recv_sems, load_sems, out_sems,
):
    at = neighbours()
    sems = (send_sems, recv_sems)
    rows = total.shape[0]
    low = jnp.bfloat16
    loads = [
        pltpu.make_async_copy(source, target, load_sems.at[n])
        for n, (source, target) in enumerate(
            (
                (dybt_in, dybt), (active_in, active), (dyb_in, dyb), (down_in, down), (slopes_in, slopes),
                (last_in, last), (h2t_in, h2t), (feed_in, feed), (x1_in, x1), (dy_in, dy),
            )
        )
    ]
    for load in loads[:2]:
        load.start()
    number = hail(at)
    hidden = active.shape[1]
    parts, main = feed_lanes(hidden)
    tail, share = hidden - main, gate_slots.shape[3]
    first = RingScatter(
        at, dybt, active.at[:, pl.ds(0, main)], down_slots, down_term, down_grad, sems, 0
    )
    second = RingScatter(
        at, h2t, slopes.at[:, pl.ds(0, share)], gate_slots, gate_term, gate_grad, sems, 28
    )
    group = GatherPieces(at, dyb, rows, PIECES, sems, 56)
    keeps = []

    def keep(source, target):
        copy = pltpu.make_async_copy(source, target, out_sems.at[len(keeps)])
        copy.start()
        keeps.append(copy)

    loads[0].wait()
    loads[1].wait()
    for load in loads[2:]:
        load.start()
    first.prepare()
    meet(number)
    first.launch()
    first.compute(2)
    for load in loads[2:6]:
        load.wait()

    def slope_back(first_block, last_block):
        @pl.loop(first_block, last_block)
        def _(j):
            here = pl.ds(pl.multiple_of(j * (rows // 2), rows // 2), rows // 2)
            left = dyb[here]
            for own, gate_lanes, up_lanes in parts:
                da = nn_dot(left, down[:, own])
                slopes[here, gate_lanes] = (da * slopes[here, gate_lanes].astype(jnp.float32)).astype(low)
                slopes[here, up_lanes] = (da * slopes[here, up_lanes].astype(jnp.float32)).astype(low)
            da = nn_dot(left, last[:, pl.ds(last.shape[1] - tail, tail)])
            last_lanes = pl.ds(2 * main, 2 * tail)
            both = jnp.concatenate([da, da], axis=1) * slopes[here, last_lanes].astype(jnp.float32)
            slopes[here, last_lanes] = both.astype(low)

    for k in range(8):
        slope_back(k, k + 1)
        if k % 2 or k > 3:
            first.tick()
    loads[6].wait()
    second.start()
    first.tick()
    keep(slopes.at[:, pl.ds(share, 2 * hidden - share)], slopes_out)

    @pl.loop(0, dybt.shape[0] // rows)
    def _(j):
        here = pl.ds(pl.multiple_of(j * rows, rows), rows)
        ends[here] = nn_dot(dybt[here], active[:, pl.ds(main, tail)]).astype(low)

    keep(ends, ends_out)
    first.tick()
    loads[7].wait()
    loads[8].wait()

    def part(block):
        return nt_dot(slopes[pl.ds(pl.multiple_of(block * rows, rows), rows)], feed[...])

    def idle():
        first.tick()
        second.tick()

    gain_part[...] = jnp.zeros_like(gain_part)
    loads[9].wait()
    piece, step = rows // PIECES, 32

    def through_norm(c):
        @pl.loop(0, piece // step)
        def _(i):
            row = pl.multiple_of(c * piece + i * step, step)
            here = pl.ds(row, step)
            through, term_gain = norm_back(x1[here], total[here], row_of(gain))
            gain_part[0:1] += term_gain
            grad = dy[here] + through
            total[here] = grad
            dyb[pl.ds(pl.multiple_of(at["t"] * rows + row, step), step)] = grad.astype(low)

        group.start(c)

    sum_pieces(
        at, part, send, receive, total, sems, 56 + 3 * PIECES, PIECES, through_norm, idle=idle
    )
    keep(total, dx1_out)

    def spread(block):
        here = pl.ds(pl.multiple_of(block * rows, rows), rows)
        dybt[:, here] = dyb[here].T
        do[here] = nn_dot(dyb[here], last[:, pl.ds(0, do.shape[1])]).astype(low)

    while first.at < len(first.sends):
        first.tick()
        second.tick()
    spread(at["t"])
    second.tick()
    group.wait(0)
    spread(at["core"])
    second.tick()
    group.relay()
    second.tick()
    spread(at["cross"])
    group.wait(2)
    spread(at["cross_core"])
    group.drain()
    keep(dybt, dx1t_out)
    keep(do, do_out)
    second.finish()
    first.finish()
    for copy in keeps:
        copy.wait()


def feed_backward(gain, dyb, dybt, h2t, down, feed, active, slopes, last, x1, dy):
    rows, width = x1.shape
    depth, main = down.shape
    hidden = active.shape[1]
    share = main + SHARE * LANES
    local = last.shape[1] - (hidden - main)
    everyone, shard = 4 * rows, depth // 8
    low, wide = jnp.bfloat16, jnp.float32
    vmem, hbm = specs()
    return pl.pallas_call(
        feed_backward_kernel,
        out_shape=(
            shape(shard, main, kind=wide),
            shape(shard, share, kind=wide),
            shape(8, width, kind=wide),
            shape(rows, width, kind=wide),
            shape(width, everyone),
            shape(everyone, local),
            shape(everyone, 2 * hidden - share),
            shape(width, hidden - main),
        ),
        in_specs=[vmem] + [hbm] * 10,
        out_specs=(vmem,) * 3 + (hbm,) * 5,
        scratch_shapes=[
            pltpu.VMEM((everyone, width), low),
            pltpu.VMEM((width, everyone), low),
            pltpu.VMEM((width, everyone), low),
            pltpu.VMEM((depth, main), low),
            pltpu.VMEM((depth, 2 * hidden), low),
            pltpu.VMEM((everyone, hidden), low),
            pltpu.VMEM((everyone, 2 * hidden), low),
            pltpu.VMEM(last.shape, low),
            pltpu.VMEM((everyone, local), low),
            pltpu.VMEM((rows, width), wide),
            pltpu.VMEM((rows, width), wide),
            pltpu.VMEM((rows, width), wide),
            pltpu.VMEM((2, 8, shard // 2, main), low),
            pltpu.VMEM((2, 8, shard // 2, share), low),
            pltpu.VMEM((shard, main), wide),
            pltpu.VMEM((shard, share), wide),
            pltpu.VMEM((width, hidden - main), low),
            pltpu.VMEM((3, rows, width), low),
            pltpu.VMEM((3, rows, width), low),
            dma(56 + 6 * PIECES),
            dma(56 + 6 * PIECES),
            dma(10),
            dma(5),
        ],
        compiler_params=params(3),
    )(gain, dyb, dybt, h2t, down, feed, active, slopes, last, x1, dy)


def mixer_backward_kernel(
    x, gain, same, taps, gain_part, squares,
    dx1t_in, o_in, h2t_in, slopes_in, ends_in, q_in, k_in, v_in, u_in, p_in, do_in, mix_in, h1t_in, dx1_in,
    out_grad, up_grad, mix_grad, input_grad, small_out, conv_out,
    turned, o, h2t, slopes, ends, q, k_pad, v_pad, u, p, do, mix,
    dk, dv, grads, out_slots, up_slots, mix_slots, out_term, up_term, mix_term, send, receive, total,
    small, small_in, conv, conv_in, conv_all,
    send_sems, recv_sems, load_sems,
):
    at = neighbours()
    sems = (send_sems, recv_sems)
    rows = total.shape[0]
    low = jnp.bfloat16
    loads = [
        pltpu.make_async_copy(source, target, load_sems.at[n])
        for n, (source, target) in enumerate(
            (
                (dx1t_in, turned), (o_in, o), (h2t_in, h2t), (slopes_in, slopes), (ends_in, ends), (q_in, q), (k_in, k_pad),
                (v_in, v_pad), (u_in, u), (p_in, p), (do_in, do), (mix_in, mix), (dx1_in, input_grad),
                (h1t_in, turned),
            )
        )
    ]
    for load in loads[:5]:
        load.start()
    number = hail(at, everyone=True)
    local = q.shape[1]
    main = local // LANES * LANES
    tail = local - main
    first = RingScatter(
        at, turned, o, out_slots, out_term, out_grad, sems, 0, count=1, side=ends
    )
    second = RingScatter(at, h2t, slopes, up_slots, up_term, up_grad, sems, 14)
    third = RingScatter(at, turned, grads, mix_slots, mix_term, mix_grad, sems, 42)
    small_sum = SumAll(at, small, small_in, sems, 73)
    conv_sum = SumAll(at, conv, conv_in, sems, 78, over=("mate", "z_pair", "z_mirror"))
    conv_group = GatherTensor(at, conv_all, 1, sems, 81)
    loads[0].wait()
    loads[1].wait()
    loads[4].wait()
    first.prepare()
    meet(number)
    first.launch()
    loads[2].wait()
    loads[3].wait()
    for load in loads[5:-1]:
        load.start()
    second.prepare()
    second.launch()
    first.compute(2)
    second.compute(2)
    dk[...] = jnp.zeros_like(dk)
    dv[...] = jnp.zeros_like(dv)
    conv[0] = jnp.zeros(conv.shape[1:], jnp.float32)
    first.tick()
    for load in loads[5:11]:
        load.wait()
    tiles = q.shape[0] // TILE

    def attend(a, b):
        @pl.loop(a, b)
        def _(i):
            attend_back_tile(i, q, k_pad, v_pad, u, p, same, taps, do, dk, dv, conv.at[0])

    for k in range(8):
        attend(k * tiles // 8, (k + 1) * tiles // 8)
        first.tick()
        second.tick()
    conv_sum.start()

    first.finish()
    loads[13].start()
    second.tick()

    @chunks_of(q.shape[0])
    def _(row, size):
        here, there = pl.ds(row, size), pl.ds(pl.multiple_of(row + TILE, TILE), size)
        four = [q[here].astype(jnp.float32), dk[there], dv[there], do[here].astype(jnp.float32)]
        for n, value in enumerate(four):
            grads[here, pl.ds(n * main, main)] = value[:, :main].astype(low)
        lasts = jnp.concatenate([value[:, main:] for value in four], axis=1)
        grads[here, pl.ds(4 * main, 4 * tail)] = lasts.astype(low)

    second.tick()
    loads[13].wait()
    third.start()
    loads[11].wait()
    loads[12].wait()

    def part(block):
        return nt_dot(grads[pl.ds(pl.multiple_of(block * rows, rows), rows)], mix[...])

    def idle(point):
        second.tick()
        third.tick()
        if point == 2:
            for _ in range(3):
                second.tick()
                third.tick()
        conv_sum.step()

    sum_rows(at, part, send, receive, total, sems, 70, idle=idle)
    conv_sum.finish()
    conv_all[at["t"]] = conv[3]
    conv_group.start()
    small[0, 0] = jnp.zeros((1, small.shape[3]), jnp.float32)
    small[0, 1] = gain_part[0:1]
    small[0, 2] = squares[0:1]

    @chunks_of(rows, 32)
    def _(row, size):
        here = pl.ds(row, size)
        through, term_gain = norm_back(x[here].astype(jnp.float32), total[here], row_of(gain))
        small[0, 0] += term_gain
        input_grad[here] += through

    small_sum.start()
    second.finish()
    for k in range(5):
        third.tick()
        if k < 3:
            third.tick()
        small_sum.step()
        if k == 1:
            conv_group.relay()
    conv_group.finish()
    third.finish()
    small_sum.finish()
    small_out[...] = small[5]
    conv_out[...] = conv_all[...]


def mixer_backward(
    x, gain, same, taps, gain_part, squares, dx1t, o, h2t, slopes, ends, q, k_pad, v_pad, u, p, do, mix, h1t, dx1
):
    rows, width = x.shape
    everyone, local = o.shape
    shard, ups = width // 8, slopes.shape[1]
    both = local + ends.shape[1]
    low, wide = jnp.bfloat16, jnp.float32
    vmem, hbm = specs()
    arrays = (dx1t, o, h2t, slopes, ends, q, k_pad, v_pad, u, p, do, mix)
    return pl.pallas_call(
        mixer_backward_kernel,
        out_shape=(
            shape(shard, both, kind=wide),
            shape(shard, ups, kind=wide),
            shape(shard, 4 * local, kind=wide),
            shape(rows, width, kind=wide),
            shape(CONV, 1, width, kind=wide),
            shape(4, CONV, 1, local, kind=wide),
        ),
        in_specs=[vmem] * 6 + [hbm] * 14,
        out_specs=(vmem,) * 6,
        scratch_shapes=[pltpu.VMEM(array.shape, array.dtype) for array in arrays]
        + [
            pltpu.VMEM((everyone + TILE, local), wide),
            pltpu.VMEM((everyone + TILE, local), wide),
            pltpu.VMEM((everyone, 4 * local), low),
            pltpu.VMEM((2, 8, shard // 2, both), low),
            pltpu.VMEM((2, 8, shard // 2, ups), low),
            pltpu.VMEM((2, 8, shard // 2, 4 * local), low),
            pltpu.VMEM((shard, both), wide),
            pltpu.VMEM((shard, ups), wide),
            pltpu.VMEM((shard, 4 * local), wide),
            pltpu.VMEM((3, rows, width), low),
            pltpu.VMEM((3, rows, width), low),
            pltpu.VMEM((rows, width), wide),
            pltpu.VMEM((6, 3, 1, width), wide),
            pltpu.VMEM((5, 3, 1, width), wide),
            pltpu.VMEM((4, CONV, 1, local), wide),
            pltpu.VMEM((3, CONV, 1, local), wide),
            pltpu.VMEM((4, CONV, 1, local), wide),
            dma(84),
            dma(84),
            dma(14),
        ],
        compiler_params=params(4),
    )(x, gain, same, taps, gain_part, squares, *arrays, h1t, dx1)


def finish_kernel(
    count, down_grad, gate_main, up_rest, mix_grad, out_grad, small, conv, act_in, input_in,
    loss, act, input_grad, query, key, value, mixgate, output, conv_grad, gain_one, gain_two, gate, up, down,
):
    act[...] = act_in[...]
    input_grad[...] = input_in[...]
    local = query.shape[1]
    main = local // LANES * LANES
    tail = local - main
    for n, target in enumerate((query, key, value, mixgate)):
        target[:, pl.ds(0, main)] = mix_grad[:, pl.ds(n * main, main)]
        target[:, pl.ds(main, tail)] = mix_grad[:, pl.ds(4 * main, 4 * tail)][:, n * tail : (n + 1) * tail]
    cut = gate.shape[1] // LANES * LANES
    rest, early = gate.shape[1] - cut, gate_main.shape[1] - cut
    late = cut - early
    ends = up_rest[:, pl.ds(late, 2 * rest)]
    gate[:, pl.ds(0, cut)] = gate_main[:, pl.ds(0, cut)]
    gate[:, pl.ds(cut, rest)] = ends[:, :rest]
    up[:, pl.ds(0, early)] = gate_main[:, pl.ds(cut, early)]
    up[:, pl.ds(early, late)] = up_rest[:, pl.ds(0, late)]
    up[:, pl.ds(cut, rest)] = ends[:, rest:]
    output[...] = out_grad[:, pl.ds(0, local)].T
    down[:, pl.ds(0, cut)] = down_grad[...]
    down[:, pl.ds(cut, rest)] = out_grad[:, pl.ds(local, rest)]
    for m in range(CONV):
        conv_grad[m : m + 1] = jnp.concatenate([conv[n, m] for n in range(conv.shape[0])], axis=1)
    gain_one[...] = small[0, 0]
    gain_two[...] = small[1, 0]
    total = jnp.sum(small[2], axis=1, keepdims=True) / (count[0:1, 0:1] * D)
    loss[...] = total


def finish(count, down_grad, gate_main, up_rest, mix_grad, out_grad, small, conv, act, input_grad):
    vmem, _ = specs()
    wide = jnp.float32
    shard, width = gate_main.shape[0], small.shape[2]
    hidden, local = (gate_main.shape[1] + up_rest.shape[1]) // 2, mix_grad.shape[1] // 4
    square = shape(shard, local, kind=wide)
    broad = shape(shard, hidden, kind=wide)
    return pl.pallas_call(
        finish_kernel,
        out_shape=(
            shape(1, 1, kind=wide),
            shape(*act.shape, kind=wide),
            shape(*input_grad.shape, kind=wide),
            square,
            square,
            square,
            square,
            shape(local, shard, kind=wide),
            shape(CONV, width, kind=wide),
            shape(width, kind=wide),
            shape(width, kind=wide),
            broad,
            broad,
            broad,
        ),
        in_specs=[vmem] * 10,
        out_specs=(vmem,) * 14,
        compiler_params=pltpu.CompilerParams(vmem_limit_bytes=VMEM_LIMIT),
    )(count, down_grad, gate_main, up_rest, mix_grad, out_grad, small, conv, act, input_grad)


def pack(*weights):
    main = weights[0].shape[1] // LANES * LANES
    return jnp.concatenate([w[:, :main] for w in weights] + [w[:, main:] for w in weights], axis=1)


def on_rings(
    block_input,
    cotangent,
    teacher,
    segments,
    valid_mask,
    query_weight,
    key_weight,
    value_weight,
    mixgate_weight,
    output_weight,
    conv_weight,
    gain_mixer,
    gain_feed,
    gate_weight,
    up_weight,
    down_weight,
):
    local = query_weight.shape[1]
    taps = lax.dynamic_slice_in_dim(conv_weight, lax.axis_index("tensor") * local, local, 1)
    (
        mix, last, feed, down, h1t, h2t, dybt, q, k_pad, v_pad, u, p, o, x1, dyb, slopes, active,
        outputs, dy, count, squares, same,
    ) = forward(
        block_input, valid_mask.reshape(-1, LANES), gain_mixer, gain_feed, segments.reshape(-1, LANES), taps,
        pack(query_weight, key_weight, value_weight, mixgate_weight),
        output_weight, gate_weight, up_weight, down_weight.T, cotangent, teacher,
    )
    down_grad, gate_main, gain_part, dx1, dx1t, do, slopes_up, ends = feed_backward(
        gain_feed, dyb, dybt, h2t, down, feed, active, slopes, last, x1, dy
    )
    out_grad, up_rest, mix_grad, input_grad, small, conv = mixer_backward(
        block_input, gain_mixer, same, taps, gain_part, squares, dx1t, o, h2t, slopes_up, ends, q, k_pad, v_pad,
        u, p, do, mix, h1t, dx1,
    )
    loss, *rest, down_turned = finish(
        count, down_grad, gate_main, up_rest, mix_grad, out_grad, small, conv, outputs, input_grad
    )
    return (loss.reshape(()), *rest, down_turned.T)


def on_any_mesh(
    block_input,
    cotangent,
    teacher,
    segments,
    valid_mask,
    query_weight,
    key_weight,
    value_weight,
    mixgate_weight,
    output_weight,
    conv_weight,
    gain_mixer,
    gain_feed,
    gate_weight,
    up_weight,
    down_weight,
):
    rows = block_input.shape[0]
    valid_rows = valid_mask.astype(jnp.float32)
    valid_total = sum_all(jnp.full((8, 128), jnp.sum(valid_rows), jnp.float32))[0, 0]
    local_width = query_weight.shape[1]
    local_hidden = gate_weight.shape[1]
    mixer_own = jnp.concatenate(
        [query_weight, key_weight, value_weight, mixgate_weight, output_weight.T], axis=1
    )
    feed_own = jnp.concatenate([gate_weight, up_weight], axis=1)
    mixer_all = gather_dp(mixer_own).reshape(D, -1)
    feed_all = gather_dp(feed_own).reshape(D, -1)
    full_down = gather_dp(down_weight.T).reshape(D, -1)
    full_query, full_key, full_value, full_mixgate, full_output = jnp.split(mixer_all, 5, axis=1)
    full_gate, full_upward = jnp.split(feed_all, 2, axis=1)
    column = lax.axis_index("tensor") * local_width
    conv_local = lax.dynamic_slice_in_dim(conv_weight, column, local_width, 1)
    inputs = block_input.astype(jnp.float32)
    scale_one = rms_scale(inputs)
    normed_one = inputs * scale_one
    group_one = gather_tensor((normed_one * gain_mixer).astype(jnp.bfloat16))
    queries = jnp.dot(group_one, full_query, preferred_element_type=jnp.float32).astype(
        jnp.bfloat16
    )
    key_rows = jnp.dot(group_one, full_key, preferred_element_type=jnp.float32).astype(jnp.bfloat16)
    value_rows = jnp.dot(group_one, full_value, preferred_element_type=jnp.float32).astype(
        jnp.bfloat16
    )
    mix_gate = jnp.dot(group_one, full_mixgate, preferred_element_type=jnp.float32).astype(
        jnp.bfloat16
    )
    attended, log_totals = attend_forward(queries, key_rows, value_rows, segments)
    value_float = value_rows.astype(jnp.float32)
    convolved = jnp.zeros_like(value_float)
    for offset in range(CONV):
        convolved = convolved + conv_local[offset] * shift_down(value_float, segments, offset)
    gate_float = mix_gate.astype(jnp.float32)
    mixer_out = (attended + convolved * gate_float).astype(jnp.bfloat16)
    mixer_part = cols_inner(mixer_out, full_output)
    hidden = inputs + scatter_tensor(mixer_part)
    scale_two = rms_scale(hidden)
    normed_two = hidden * scale_two
    group_two = gather_tensor((normed_two * gain_feed).astype(jnp.bfloat16))
    gate_value = jnp.dot(group_two, full_gate, preferred_element_type=jnp.float32)
    up_value = jnp.dot(group_two, full_upward, preferred_element_type=jnp.float32)
    sigmoid_gate = jax.nn.sigmoid(gate_value)
    silu_gate = gate_value * sigmoid_gate
    active = (silu_gate * up_value).astype(jnp.bfloat16)
    feed_part = cols_inner(active, full_down)
    outputs = hidden + scatter_tensor(feed_part)
    target = teacher.astype(jnp.float32)
    deviation = outputs - target
    squares = jnp.sum(valid_rows[:, None] * deviation * deviation)
    all_tokens = rows * lax.axis_size("dp") * lax.axis_size("tensor")
    grad_out = cotangent + valid_rows[:, None] * deviation * (all_tokens / valid_total)
    grad_feed = gather_tensor(grad_out.astype(jnp.bfloat16))
    down_part = rows_inner(grad_feed, active)
    down_grad = scatter_dp(down_part.astype(jnp.bfloat16).reshape(-1, down_weight.shape[1], local_hidden)).T
    grad_active = jnp.dot(grad_feed, full_down, preferred_element_type=jnp.float32)
    silu_slope = sigmoid_gate * (1.0 + gate_value * (1.0 - sigmoid_gate))
    grad_gate = (grad_active * up_value * silu_slope).astype(jnp.bfloat16)
    grad_upward = (grad_active * silu_gate).astype(jnp.bfloat16)
    grad_normed_two = cols_inner(grad_gate, full_gate) + cols_inner(grad_upward, full_upward)
    grad_rows_two = scatter_tensor(grad_normed_two)
    gate_part = rows_inner(group_two, grad_gate)
    up_part = rows_inner(group_two, grad_upward)
    shard = gate_weight.shape[0]
    gate_grad = scatter_dp(gate_part.astype(jnp.bfloat16).reshape(-1, shard, local_hidden))
    up_grad = scatter_dp(up_part.astype(jnp.bfloat16).reshape(-1, shard, local_hidden))
    gainfeed_part = jnp.sum(grad_rows_two * normed_two, axis=0)
    scaled_two = grad_rows_two * gain_feed
    grad_hidden = grad_out + scale_two * (
        scaled_two - normed_two * jnp.mean(scaled_two * normed_two, axis=1, keepdims=True)
    )
    grad_mixer = gather_tensor(grad_hidden.astype(jnp.bfloat16))
    output_part = rows_inner(grad_mixer, mixer_out)
    output_grad = scatter_dp(output_part.astype(jnp.bfloat16).reshape(-1, shard, local_width)).T
    grad_mixed = jnp.dot(grad_mixer, full_output, preferred_element_type=jnp.float32).astype(jnp.bfloat16)
    grad_mixed_float = grad_mixed.astype(jnp.float32)
    grad_mixgate = (grad_mixed_float * convolved).astype(jnp.bfloat16)
    grad_conv_out = grad_mixed_float * gate_float
    conv_rows = []
    value_from_conv = jnp.zeros_like(value_float)
    for offset in range(CONV):
        conv_rows.append(jnp.sum(grad_conv_out * shift_down(value_float, segments, offset), axis=0))
        value_from_conv = value_from_conv + conv_local[offset] * shift_up(
            grad_conv_out, segments, offset
        )
    grad_queries, key_float, value_attn = attend_backward(
        queries, key_rows, value_rows, segments, log_totals, grad_mixed
    )
    grad_keys = key_float.astype(jnp.bfloat16)
    grad_values = (value_attn + value_from_conv).astype(jnp.bfloat16)

    def project_grad(grads):
        part = rows_inner(group_one, grads).astype(jnp.bfloat16)
        return scatter_dp(part.reshape(-1, shard, local_width))

    query_grad = project_grad(grad_queries)
    key_grad = project_grad(grad_keys)
    value_grad = project_grad(grad_values)
    mixgate_grad = project_grad(grad_mixgate)
    grad_normed_one = (
        cols_inner(grad_queries, full_query)
        + cols_inner(grad_keys, full_key)
        + cols_inner(grad_values, full_value)
        + cols_inner(grad_mixgate, full_mixgate)
    )
    grad_rows_one = scatter_tensor(grad_normed_one)
    gainmix_part = jnp.sum(grad_rows_one * normed_one, axis=0)
    scaled_one = grad_rows_one * gain_mixer
    input_grad = grad_hidden + scale_one * (
        scaled_one - normed_one * jnp.mean(scaled_one * normed_one, axis=1, keepdims=True)
    )
    conv_full = lax.dynamic_update_slice_in_dim(
        jnp.zeros((CONV, D), jnp.float32), jnp.stack(conv_rows), column, 1
    )
    small = sum_all(
        jnp.concatenate(
            [
                conv_full,
                gainmix_part[None],
                gainfeed_part[None],
                jnp.full((1, D), squares, jnp.float32),
            ]
        )
    )
    conv_grad, gainmix_grad, gainfeed_grad = small[:CONV], small[CONV], small[CONV + 1]
    mean_loss = small[CONV + 2, 0] / (valid_total * D)
    return (
        mean_loss,
        outputs,
        input_grad,
        query_grad,
        key_grad,
        value_grad,
        mixgate_grad,
        output_grad,
        conv_grad,
        gainmix_grad,
        gainfeed_grad,
        gate_grad,
        up_grad,
        down_grad,
    )


def solution(mesh):
    rings = mesh.shape["dp"] == 8 and mesh.shape["tensor"] == 4
    return jax.shard_map(
        on_rings if rings else on_any_mesh,
        mesh=mesh,
        in_specs=(
            P(("dp", "tensor"), None),
            P(("dp", "tensor"), None),
            P(("dp", "tensor"), None),
            P("dp"),
            P(("dp", "tensor")),
            P("dp", "tensor"),
            P("dp", "tensor"),
            P("dp", "tensor"),
            P("dp", "tensor"),
            P("tensor", "dp"),
            P(),
            P(),
            P(),
            P("dp", "tensor"),
            P("dp", "tensor"),
            P("tensor", "dp"),
        ),
        out_specs=(
            P(),
            P(("dp", "tensor"), None),
            P(("dp", "tensor"), None),
            P("dp", "tensor"),
            P("dp", "tensor"),
            P("dp", "tensor"),
            P("dp", "tensor"),
            P("tensor", "dp"),
            P(),
            P(),
            P(),
            P("dp", "tensor"),
            P("dp", "tensor"),
            P("tensor", "dp"),
        ),
        check_vma=False,
    )
```
